32 devices in a mesh: row: 4 (over z), col: 8 (over y, x, core).
Axes of the slice: x: 2, y: 2, z: 4, core: 2. Of those that a mesh axis runs over, the one named last changes fastest.
Arguments:
- tangents: float32 [3, 256, 256, 128], P(None, 'row', 'col'), may hold values from -400 to 400
- sea_mask: int32 [256, 256], P('row', 'col'), may hold values 0 or 1
- levels: int32 [256, 256], P('row', 'col'), may hold values from 0 to 49
- current: float32 [256, 256], P('row', 'col'), may hold values from -0.6 to 0.6
Outputs:
- new_tangents: float32 [3, 256, 256, 128], P(None, 'row', 'col')
- growth: float32 [128], replicated
The draws below stay inside these ranges and needn't reach their ends.
All inputs are finite; a program needn't handle non-finite values. No bound on the sum of `sea_mask` on one device may be relied on, other than what follows from the above.
Results may differ from the reference program's by a relative error of at most 0.00014.
Values sent between devices are 32-bit elements; how exact they have to be, the bound alone decides.
No kernel may reach another device: no remote copies, remote signals or barrier semaphores. Data moves between devices by JAX's collectives and lax.ppermute only.
A program may use at most 64 MiB of HBM per device.

```python
import math
import jax
import jax.numpy as jnp
from jax import lax

MODES = 128
STEPS = 2
RENORMS = 2
LEVELS = 50
NLAT = 256
NLON = 256


def draw_tangents(key, part):
    base_key = jax.random.fold_in(key, 11)
    key_noise, key_cell, key_mode = jax.random.split(base_key, 3)
    latitude = jnp.arange(NLAT, dtype=jnp.float32)[:, None] / NLAT
    longitude = jnp.arange(NLON, dtype=jnp.float32)[None, :] / NLON
    cell_scale = jnp.exp(jax.random.uniform(key_cell, (NLAT, NLON)) * math.log(10.0))
    mode_scale = jnp.exp(jax.random.uniform(key_mode, (MODES,)) * math.log(10.0))
    trend_scale = jnp.exp((latitude + longitude) * math.log(3.0))
    random_part = jnp.clip(jax.random.normal(key_noise, (3, NLAT, NLON, MODES)), -4.0, 4.0)
    return (0.1 * random_part * (cell_scale * trend_scale)[None, :, :, None] * mode_scale).astype(jnp.float32)


def set_ends(array, key, low, top_value):
    longest = array.shape.index(max(array.shape))
    spots = []
    for shift in (0, 1):
        where = [jax.random.randint(jax.random.fold_in(key, axis), (), 0, length) for axis, length in enumerate(array.shape)]
        where[longest] = (where[longest] + shift) % array.shape[longest]
        spots.append(tuple(where))
    return array.at[spots[0]].set(low).at[spots[1]].set(top_value)


def steps_of(rng, shape, shards, low, largest):
    loudness, own = 1.0, jax.random.fold_in(rng, 6)
    for dim, shards_of in shards:
        steps = jnp.exp(jax.random.uniform(jax.random.fold_in(own, dim), (shards_of,), jnp.float32, low / len(shards), largest / len(shards)))
        loudness = loudness * jnp.repeat(steps, shape[dim] // shards_of).reshape([-1 if axis == dim else 1 for axis in range(len(shape))])
    return loudness


def setup_inputs(seed: int = 0) -> dict:
    streams_of = jax.random.split(jax.random.key(seed), 5)
    return {
        "tangents": draw_tangents(jax.random.fold_in(streams_of[4], 71), 0),
        "sea_mask": set_ends((jax.random.randint(streams_of[1], (NLAT, NLON), 0, 5) < 4).astype(jnp.int32), jax.random.fold_in(streams_of[1], 1), 0, 1),
        "levels": set_ends(jax.random.randint(streams_of[2], (NLAT, NLON), 0, LEVELS), jax.random.fold_in(streams_of[2], 1), 0, LEVELS - 1).astype(jnp.int32),
        "current": jnp.clip(jax.random.uniform(streams_of[3], (NLAT, NLON), jnp.float32, -0.6, 0.6) * steps_of(streams_of[3], (NLAT, NLON), ((0, 4), (1, 8)), -0.4, 0.0), -0.6, 0.6),
    }


viscosity = 0.15
gravity = 0.5
rotation = 0.4

def latitude_spin(rows_global, total_rows):
    angle = (-70.0 + 140.0 * (rows_global + 0.5) / total_rows) * (jnp.pi / 180.0)
    return rotation * jnp.sin(angle)

def advance(padded, sea_frac, column_depth, current, coriolis):
    middle = padded[:, 1:-1, 1:-1]
    east_side = padded[:, 1:-1, 2:]
    west_side = padded[:, 1:-1, :-2]
    north_side = padded[:, 2:, 1:-1]
    south_side = padded[:, :-2, 1:-1]
    zonal_diff = 0.5 * (east_side - west_side)
    merid_diff = 0.5 * (north_side - south_side)
    spread = east_side + west_side + north_side + south_side - 4.0 * middle
    advected = middle + viscosity * spread - current * zonal_diff
    zonal = sea_frac * (advected[0] - gravity * zonal_diff[2] + coriolis * middle[1])
    meridional = sea_frac * (advected[1] - gravity * merid_diff[2] - coriolis * middle[0])
    height = sea_frac * (advected[2] - column_depth * (zonal_diff[0] + merid_diff[1]))
    return jnp.stack([zonal, meridional, height])

def pad_global(field):
    rowed = jnp.pad(field, ((0, 0), (1, 1), (0, 0), (0, 0)))
    return jnp.concatenate([rowed[:, :, -1:], rowed, rowed[:, :, :1]], axis=2)

def reference(tangents, sea_mask, levels, current):
    sea_frac = sea_mask.astype(jnp.float32)[:, :, None]
    column_depth = ((levels + 1).astype(jnp.float32) / LEVELS)[:, :, None]
    flow = current[:, :, None]
    coriolis = latitude_spin(jnp.arange(NLAT, dtype=jnp.float32), NLAT)[:, None, None]
    group_width = MODES // 8
    growth = jnp.zeros((MODES,), jnp.float32)
    identity = jnp.eye(MODES, dtype=jnp.float32)
    for renorm in range(RENORMS):
        pieces = []
        for group in range(8):
            piece = tangents[:, :, :, group * group_width:(group + 1) * group_width]
            for substep in range(STEPS):
                piece = advance(pad_global(piece), sea_frac, column_depth, flow, coriolis)
            pieces.append(piece)
        tangents = jnp.concatenate(pieces, axis=3)
        flattened = tangents.reshape(-1, MODES)
        gram_matrix = lax.dot_general(flattened, flattened, (((0,), (0,)), ((), ())), precision=lax.Precision.HIGHEST) / (NLAT * NLON)
        lower_factor = jnp.linalg.cholesky(gram_matrix)
        inverse_factor = jax.scipy.linalg.solve_triangular(lower_factor, identity, lower=True)
        tangents = jnp.dot(flattened, inverse_factor.T, precision=lax.Precision.HIGHEST).reshape(tangents.shape)
        growth = growth + jnp.log(jnp.diagonal(lower_factor))
    return (tangents, growth)
```

```python
import functools

import jax
import jax.numpy as jnp
from jax import lax
from jax.experimental import pallas as pl
from jax.experimental.pallas import tpu as pltpu
from jax.sharding import PartitionSpec as P

STEPS = 2
RENORMS = 2
LEVELS = 50

viscosity = 0.15
gravity = 0.5
rotation = 0.4

SUB = 8
LANES = 128
WIDTH = 2
LEFT = 8
FIELDS = 3
VMEM_LIMIT = 48 * 1024 * 1024

ANY = pl.BlockSpec(memory_space=pl.ANY)
VMEM = pl.BlockSpec(memory_space=pltpu.VMEM)
SMEM = pl.BlockSpec(memory_space=pltpu.SMEM)


def params():
    return pltpu.CompilerParams(vmem_limit_bytes=VMEM_LIMIT)


def shape_of(*dims):
    return jax.ShapeDtypeStruct(dims, jnp.float32)


def lane_spread(block, lane):
    return jnp.broadcast_to(block[:, lane : lane + 1], (block.shape[0], LANES))


def pack_columns(par, t_ref, ct_ref, msg_a, msg_b, edges, sems):
    comps, rows, cols, _ = t_ref.shape
    odd = par[1] % 2
    copies = []
    for slot in (0, 1):
        east = (1 - odd) if slot == 0 else odd
        start = pl.multiple_of(east * (cols - SUB), SUB)
        copies.append(
            pltpu.make_async_copy(t_ref.at[:, :, pl.ds(start, SUB), :], edges.at[slot], sems.at[slot])
        )
        copies[-1].start()
    for slot, msg in ((0, msg_a), (1, msg_b)):
        east = (1 - odd) if slot == 0 else odd
        tail = comps * WIDTH * rows
        msg[pl.ds(tail, SUB), :] = jnp.zeros((SUB, LANES), jnp.float32)
        for field in range(FIELDS):
            msg[pl.ds(tail + field, 1), :] = ct_ref[field, pl.ds(east * (cols - 1), 1), :]
        copies[slot].wait()
        flat = edges.at[slot].reshape(comps * rows * SUB, LANES)
        for comp in range(comps):
            for j in range(WIDTH):
                for row in range(0, rows, SUB):
                    at = (comp * rows + row) * SUB + east * (SUB - WIDTH) + j
                    msg[pl.ds((comp * WIDTH + j) * rows + row, SUB), :] = flat[
                        pl.ds(at, SUB, stride=SUB), :
                    ]


def pack_rows(with_fields, par, t_ref, cn_ref, got_a, got_b, msg_a, msg_b, sems):
    comps, rows, cols, _ = t_ref.shape
    odd_row, odd_col = par[0] % 2, par[1] % 2
    lane = lax.broadcasted_iota(jnp.int32, (1, LANES), 1)
    copies = []
    for slot, msg in ((0, msg_a), (1, msg_b)):
        north = (1 - odd_row) if slot == 0 else odd_row
        copies.append(
            pltpu.make_async_copy(
                t_ref.at[:, pl.ds(north * (rows - WIDTH), WIDTH)],
                msg.at[:, :, pl.ds(0, cols), :],
                sems.at[slot],
            )
        )
        copies[-1].start()
    for slot, msg in ((0, msg_a), (1, msg_b)):
        north = (1 - odd_row) if slot == 0 else odd_row
        first = north * (rows - WIDTH)
        for comp in range(comps):
            for j in range(WIDTH):
                for side in range(WIDTH):
                    at = (comp * WIDTH + side) * rows + first + j
                    from_a, from_b = got_a[pl.ds(at, 1), :], got_b[pl.ds(at, 1), :]
                    west = jnp.where(odd_col == 1, from_a, from_b)
                    east = jnp.where(odd_col == 1, from_b, from_a)
                    msg[comp, j, pl.ds(cols + side, 1), :] = west
                    msg[comp, j, pl.ds(cols + WIDTH + side, 1), :] = east
                msg[comp, j, pl.ds(cols + 2 * WIDTH, SUB - 2 * WIDTH), :] = jnp.zeros(
                    (SUB - 2 * WIDTH, LANES), jnp.float32
                )
        if with_fields:
            edge = north * (rows - 1)
            tail = comps * WIDTH * rows
            for field in range(FIELDS):
                own = cn_ref[field, pl.ds(edge, 1), :]
                ends = [
                    jnp.sum(
                        jnp.where(lane == edge, got[pl.ds(tail + field, 1), :], 0.0),
                        axis=1,
                        keepdims=True,
                    )
                    for got in (got_a, got_b)
                ]
                west = jnp.where(odd_col == 1, ends[0], ends[1])
                east = jnp.where(odd_col == 1, ends[1], ends[0])
                own = jnp.where(lane == cols, west, own)
                own = jnp.where(lane == cols + 1, east, own)
                msg[field, 0, pl.ds(cols + 2 * WIDTH, 1), :] = own
    for copy in copies:
        copy.wait()


def split_halves(value):
    high = value.astype(jnp.bfloat16)
    low = (value - high.astype(jnp.float32)).astype(jnp.bfloat16)
    return jnp.concatenate([high, low], axis=1)


def gram_of(pair):
    return lax.dot_general(pair, pair, (((0,), (0,)), ((), ())), preferred_element_type=jnp.float32)


def fold_gram(total, scale):
    half = LANES
    whole = (total[:half, :half] + total[half:, half:]) + (total[:half, half:] + total[half:, :half])
    return whole * scale


def stencil(load, sea, flow, depth, spin):
    zonal, merid, height = (load(comp, 0, 0) for comp in range(3))
    u_e, u_w, u_n, u_s = load(0, 0, 1), load(0, 0, -1), load(0, 1, 0), load(0, -1, 0)
    v_e, v_w, v_n, v_s = load(1, 0, 1), load(1, 0, -1), load(1, 1, 0), load(1, -1, 0)
    h_e, h_w, h_n, h_s = load(2, 0, 1), load(2, 0, -1), load(2, 1, 0), load(2, -1, 0)
    keep = 1.0 - 4.0 * viscosity
    u_x, v_x, h_x = u_e - u_w, v_e - v_w, h_e - h_w
    v_y, h_y = v_n - v_s, h_n - h_s
    u_mix = keep * zonal + viscosity * ((u_e + u_w) + (u_n + u_s)) - flow * u_x
    v_mix = keep * merid + viscosity * ((v_e + v_w) + (v_n + v_s)) - flow * v_x
    h_mix = keep * height + viscosity * ((h_e + h_w) + (h_n + h_s)) - flow * h_x
    half = 0.5 * gravity
    return (
        sea * (u_mix - half * h_x + spin * merid),
        sea * (v_mix - half * h_y - spin * zonal),
        sea * (h_mix - depth * (u_x + v_y)),
    )


def two_steps(
    with_gram,
    scale,
    par,
    t_ref,
    ct_ref,
    spin_ref,
    col_a,
    col_b,
    row_a,
    row_b,
    *rest,
):
    if with_gram:
        out_ref, msg_a, msg_b, gram_ref, *rest = rest
        halo_cols, halo_rows = (col_a, col_b), (row_a, row_b)
    else:
        new_col_a, new_col_b, new_row_a, new_row_b, out_ref, *rest = rest
        halo_cols, halo_rows = (new_col_a, new_col_b), (new_row_a, new_row_b)
    buf, mid, done, coef, edge, stage, total, sem_in, sem_out = rest
    comps, rows, cols, _ = t_ref.shape
    pitch = buf.shape[2]
    tall = rows + 2 * WIDTH
    odd_row, odd_col = par[0] % 2, par[1] % 2
    norths = (1 - odd_row, odd_row)
    easts = (1 - odd_col, odd_col)

    load_in = pltpu.make_async_copy(
        t_ref, buf.at[:, pl.ds(WIDTH, rows), pl.ds(LEFT, cols), :], sem_in
    )
    load_in.start()

    for field in range(FIELDS):
        columns = ct_ref[field]
        for row in range(rows):
            coef[field, row + 1] = lane_spread(columns, row)
    tail = comps * WIDTH * rows
    for slot, col in ((0, col_a), (1, col_b)):
        upright = jnp.transpose(col[pl.ds(tail, SUB), :])
        for field in range(FIELDS):
            edge[easts[slot], field, pl.ds(1, rows), :] = lane_spread(upright[:rows], field)
    stage[...] = jnp.zeros((SUB, LANES), jnp.float32)
    for slot, row in ((0, row_a), (1, row_b)):
        for field in range(FIELDS):
            stage[pl.ds(slot * FIELDS + field, 1), :] = row[field, 0, pl.ds(cols + 2 * WIDTH, 1), :]
    upright = jnp.transpose(stage[...])
    for slot in (0, 1):
        line = norths[slot] * (rows + 1)
        for field in range(FIELDS):
            spread = lane_spread(upright[: cols + SUB], slot * FIELDS + field)
            coef[field, line] = spread[:cols]
            edge[0, field, pl.ds(line, 1), :] = spread[cols : cols + 1]
            edge[1, field, pl.ds(line, 1), :] = spread[cols + 1 : cols + 2]

    flat_buf = buf.reshape(comps * tall * pitch, LANES)
    for slot, col in enumerate(halo_cols):
        lon = LEFT - WIDTH + easts[slot] * (cols + WIDTH)
        for comp in range(comps):
            for j in range(WIDTH):
                for row in range(0, rows, SUB):
                    at = ((comp * tall) + WIDTH + row) * pitch + lon + j
                    flat_buf[pl.ds(at, SUB, stride=pitch), :] = col[
                        pl.ds((comp * WIDTH + j) * rows + row, SUB), :
                    ]
    for slot, row in enumerate(halo_rows):
        line = norths[slot] * (rows + WIDTH)
        for comp in range(comps):
            for j in range(WIDTH):
                buf[comp, line + j, pl.ds(LEFT, cols), :] = row[comp, j, pl.ds(0, cols), :]
                for side in range(WIDTH):
                    buf[comp, line + j, pl.ds(LEFT - WIDTH + side, 1), :] = row[
                        comp, j, pl.ds(cols + side, 1), :
                    ]
                    buf[comp, line + j, pl.ds(LEFT + cols + side, 1), :] = row[
                        comp, j, pl.ds(cols + WIDTH + side, 1), :
                    ]
    load_in.wait()

    flat_mid = mid.reshape(comps * tall * pitch, LANES)

    def reader(flat, at, stride):
        def load(comp, d_lat, d_lon):
            start = at + comp * tall * pitch + d_lat * pitch + d_lon
            if stride == 1:
                return flat[pl.ds(start, SUB), :]
            return flat[pl.ds(start, SUB, stride=stride), :]

        return load

    @pl.loop(0, rows + 2)
    def _(line):
        spin = jnp.broadcast_to(spin_ref[pl.ds(line, 1), :], (SUB, LANES))
        for lon in range(0, cols, SUB):
            sea, flow, depth = (coef[field, line, pl.ds(lon, SUB), :] for field in range(FIELDS))
            at = (line + 1) * pitch + LEFT + lon
            new = stencil(reader(flat_buf, at, 1), sea, flow, depth, spin)
            for comp in range(comps):
                mid[comp, line + 1, pl.ds(LEFT + lon, SUB), :] = new[comp]

    flat_edge = edge
    starts = list(range(0, rows + 2 - SUB, SUB)) + [rows + 2 - SUB]
    for side in (0, 1):
        for line in starts:
            spin = spin_ref[pl.ds(line, SUB), :]
            sea, flow, depth = (flat_edge[side, field, pl.ds(line, SUB), :] for field in range(FIELDS))
            at = (line + 1) * pitch + LEFT - 1 + side * (cols + 1)
            new = stencil(reader(flat_buf, at, pitch), sea, flow, depth, spin)
            for comp in range(comps):
                flat_mid[pl.ds(at + comp * tall * pitch, SUB, stride=pitch), :] = new[comp]

    if with_gram:
        total[...] = jnp.zeros_like(total)
    groups = rows // SUB

    def out_copy(group):
        lines = pl.ds(group * SUB, SUB)
        return pltpu.make_async_copy(done.at[:, lines], out_ref.at[:, lines], sem_out.at[group])

    @pl.loop(0, groups)
    def _(group):
        for inner in range(SUB):
            line = group * SUB + inner
            spin = jnp.broadcast_to(spin_ref[pl.ds(line + 1, 1), :], (SUB, LANES))
            for lon in range(0, cols, SUB):
                sea, flow, depth = (
                    coef[field, line + 1, pl.ds(lon, SUB), :] for field in range(FIELDS)
                )
                at = (line + WIDTH) * pitch + LEFT + lon
                new = stencil(reader(flat_mid, at, 1), sea, flow, depth, spin)
                for comp in range(comps):
                    done[comp, line, pl.ds(lon, SUB), :] = new[comp]
        if with_gram:
            cells = done[:, pl.ds(group * SUB, SUB)].reshape(comps * SUB * cols, LANES)
            total[...] += gram_of(split_halves(cells))
        out_copy(group).start()

    if with_gram:
        flat_done = done.reshape(comps * rows * cols, LANES)
        for slot, msg in ((0, msg_a), (1, msg_b)):
            lon = easts[slot] * (cols - WIDTH)
            for comp in range(comps):
                for j in range(WIDTH):
                    for row in range(0, rows, SUB):
                        at = (comp * rows + row) * cols + lon + j
                        msg[pl.ds((comp * WIDTH + j) * rows + row, SUB), :] = flat_done[
                            pl.ds(at, SUB, stride=cols), :
                        ]
        gram_ref[...] = fold_gram(total[...], scale)
    for group in range(groups):
        out_copy(group).wait()


def invert_factor(gram_ref, work):
    count = LANES // SUB
    lane = lax.broadcasted_iota(jnp.int32, (SUB, LANES), 1)
    sub = lax.broadcasted_iota(jnp.int32, (SUB, LANES), 0)
    rows = [gram_ref[pl.ds(SUB * i, SUB), :] for i in range(count)]
    for block in range(count):
        base = SUB * block
        here = (lane >= base) & (lane < base + SUB)
        spread = [lane_spread(rows[block], base + l) for l in range(SUB)]
        low = [
            [jnp.broadcast_to(spread[l][k : k + 1, :], (SUB, LANES)) for l in range(k + 1)]
            for k in range(SUB)
        ]
        pivot = jnp.where(here, jnp.where(lane - base == sub, 1.0, 0.0), rows[block])
        inv, scaled = [], []
        for k in range(SUB):
            inv.append(lax.rsqrt(low[k][k]))
            for i in range(k + 1, SUB):
                low[i][k] = low[i][k] * inv[k]
            for i in range(k + 1, SUB):
                for m in range(k + 1, i + 1):
                    low[i][m] = low[i][m] - low[i][k] * low[m][k]
            line = jnp.broadcast_to(pivot[k : k + 1, :], (SUB, LANES))
            for l in range(k):
                line = line - low[k][l] * scaled[l]
            scaled.append(line * inv[k])
        merged = scaled[0]
        for k in range(1, SUB):
            merged = jnp.where(sub == k, scaled[k], merged)
        work[pl.ds(base, SUB), :] = merged
        for i in range(block + 1, count):
            weights = []
            rest = jnp.where(here, 0.0, rows[i])
            for l in range(SUB):
                weight = lane_spread(rows[i], base + l)
                for m in range(l):
                    weight = weight - weights[m] * low[l][m]
                weights.append(weight * inv[l])
            for l in range(SUB):
                rest = rest - weights[l] * scaled[l]
            rows[i] = rest


def renorm(last, scale, gram_ref, t_ref, prior_ref, *rest):
    if last:
        out_ref, logs_ref, work, factor, cells, fresh, sem_in, sem_out = rest
    else:
        out_ref, logs_ref, next_ref, work, factor, cells, fresh, total, sem_in, sem_out = rest
    tiles, height, _ = cells.shape
    load_in = pltpu.make_async_copy(t_ref, cells, sem_in)
    load_in.start()
    invert_factor(gram_ref, work)
    row = lax.broadcasted_iota(jnp.int32, (LANES, LANES), 0)
    col = lax.broadcasted_iota(jnp.int32, (LANES, LANES), 1)
    inverse = jnp.where(row >= col, work[...], 0.0)
    diagonal = jnp.sum(jnp.where(row == col, inverse, 0.0), axis=0, keepdims=True)
    logs_ref[...] = prior_ref[...] - jnp.log(diagonal)
    high = inverse.astype(jnp.bfloat16)
    lower = (inverse - high.astype(jnp.float32)).astype(jnp.bfloat16)
    factor[...] = jnp.concatenate(
        [jnp.concatenate([high, high], axis=1), jnp.concatenate([lower, lower], axis=1)], axis=0
    )
    if not last:
        total[...] = jnp.zeros_like(total)
    load_in.wait()

    def out_copy(tile):
        return pltpu.make_async_copy(fresh.at[tile], out_ref.at[tile], sem_out.at[tile])

    @pl.loop(0, tiles)
    def _(tile):
        both = lax.dot_general(
            split_halves(cells[tile]),
            factor[...],
            (((1,), (1,)), ((), ())),
            preferred_element_type=jnp.float32,
        )
        new = both[:, :LANES] + both[:, LANES:]
        fresh[tile] = new
        out_copy(tile).start()
        if not last:
            total[...] += gram_of(split_halves(new))

    if not last:
        next_ref[...] = fold_gram(total[...], scale)
    for tile in range(tiles):
        out_copy(tile).wait()


def swap_pairs(value, axis):
    count = lax.axis_size(axis)
    near = [(i, i ^ 1) for i in range(count)]
    if axis == "col":
        far = [(i, (i + 1) % count if i % 2 else (i - 1) % count) for i in range(count)]
    else:
        far = [(i, i + 1 if i % 2 else i - 1) for i in range(1, count - 1)]
    return lax.ppermute(value[0], axis, near), lax.ppermute(value[1], axis, far)


def sum_devices(part):
    axes = ("row", "col")
    count = lax.axis_size("row") * lax.axis_size("col")
    modes = part.shape[0]
    pieces = part.reshape(count, modes // count, part.shape[1])
    pieces = lax.all_to_all(pieces, axes, 0, 0)
    mine = jnp.sum(pieces, axis=0)
    return lax.all_gather(mine, axes, axis=0, tiled=True)


def body(tangents, sea_mask, levels, current):
    comps, rows, cols, modes = tangents.shape
    total_rows = rows * lax.axis_size("row")
    total_cells = total_rows * cols * lax.axis_size("col")
    scale = 1.0 / total_cells
    row_at, col_at = lax.axis_index("row"), lax.axis_index("col")
    par = jnp.stack([row_at, col_at]).astype(jnp.int32)

    lat = (row_at * rows - 1 + jnp.arange(rows + SUB)).astype(jnp.float32)
    angle = (-70.0 + 140.0 * (lat + 0.5) / total_rows) * (jnp.pi / 180.0)
    spin = jnp.broadcast_to((rotation * jnp.sin(angle))[:, None], (rows + SUB, LANES))
    fields = jnp.stack(
        [
            sea_mask.astype(jnp.float32),
            0.5 * current,
            0.5 * ((levels + 1).astype(jnp.float32) / LEVELS),
        ]
    )
    natural = jnp.pad(fields, ((0, 0), (0, 0), (0, LANES - cols)))
    upright = jnp.pad(fields.transpose(0, 2, 1), ((0, 0), (0, 0), (0, LANES - rows)))

    message = shape_of(comps * WIDTH * rows + SUB, modes)
    row_message = shape_of(comps, WIDTH, cols + SUB, modes)
    tall, pitch = rows + 2 * WIDTH, cols + 2 * LEFT
    block = shape_of(comps, rows, cols, modes)

    def rows_packed(with_fields, cells, got):
        return pl.pallas_call(
            functools.partial(pack_rows, with_fields),
            out_shape=(row_message, row_message),
            in_specs=[SMEM, ANY, VMEM, VMEM, VMEM],
            out_specs=(VMEM, VMEM),
            scratch_shapes=[pltpu.SemaphoreType.DMA((2,))],
            compiler_params=params(),
        )(par, cells, natural, *got)

    def stepped(with_gram, cells, first, second):
        halos = first + (second or ())
        outs = (block,)
        specs = (ANY,)
        if with_gram:
            outs += (message, message, shape_of(modes, modes))
            specs += (VMEM, VMEM, VMEM)
        return pl.pallas_call(
            functools.partial(two_steps, with_gram, scale),
            out_shape=outs,
            in_specs=[SMEM, ANY, VMEM, VMEM] + [VMEM] * len(halos),
            out_specs=specs,
            scratch_shapes=[
                pltpu.VMEM((comps, tall, pitch, modes), jnp.float32),
                pltpu.VMEM((comps, tall, pitch, modes), jnp.float32),
                pltpu.VMEM((comps, rows, cols, modes), jnp.float32),
                pltpu.VMEM((FIELDS, rows + 2, cols, modes), jnp.float32),
                pltpu.VMEM((2, FIELDS, rows + SUB, modes), jnp.float32),
                pltpu.VMEM((SUB, LANES), jnp.float32),
                pltpu.VMEM((2 * modes, 2 * modes), jnp.float32),
                pltpu.SemaphoreType.DMA,
                pltpu.SemaphoreType.DMA((rows // SUB,)),
            ],
            compiler_params=params(),
        )(par, cells, upright, spin, *halos)

    tiles = 8
    height = comps * rows * cols // tiles

    def renormed(last, gram, cells, logs):
        outs = (shape_of(tiles, height, modes), shape_of(1, modes))
        specs = (ANY, VMEM)
        scratch = [
            pltpu.VMEM((modes, modes), jnp.float32),
            pltpu.VMEM((2 * modes, 2 * modes), jnp.bfloat16),
            pltpu.VMEM((tiles, height, modes), jnp.float32),
            pltpu.VMEM((tiles, height, modes), jnp.float32),
        ]
        if not last:
            outs += (shape_of(modes, modes),)
            specs += (VMEM,)
            scratch += [pltpu.VMEM((2 * modes, 2 * modes), jnp.float32)]
        return pl.pallas_call(
            functools.partial(renorm, last, scale),
            out_shape=outs,
            in_specs=[VMEM, ANY, VMEM],
            out_specs=specs,
            scratch_shapes=scratch
            + [pltpu.SemaphoreType.DMA, pltpu.SemaphoreType.DMA((tiles,))],
            compiler_params=params(),
        )(gram, cells.reshape(tiles, height, modes), logs)

    packed = pl.pallas_call(
        pack_columns,
        out_shape=(message, message),
        in_specs=[SMEM, ANY, VMEM],
        out_specs=(VMEM, VMEM),
        scratch_shapes=[
            pltpu.VMEM((2, comps, rows, SUB, modes), jnp.float32),
            pltpu.SemaphoreType.DMA((2,)),
        ],
        compiler_params=params(),
    )(par, tangents, upright)
    col_halos = swap_pairs(packed, "col")
    row_halos = swap_pairs(rows_packed(True, tangents, col_halos), "row")
    first = tuple(col_halos) + tuple(row_halos)
    advanced, *packed, gram = stepped(True, tangents, first, None)
    gram = sum_devices(gram)
    col_halos = swap_pairs(packed, "col")
    row_halos = swap_pairs(rows_packed(False, advanced, col_halos), "row")
    (advanced,) = stepped(False, advanced, first, tuple(col_halos) + tuple(row_halos))
    logs = jnp.zeros((1, modes), jnp.float32)
    advanced, logs, gram = renormed(False, gram, advanced, logs)
    gram = sum_devices(gram)
    advanced, logs = renormed(True, gram, advanced, logs)
    return advanced.reshape(tangents.shape), logs.reshape(modes)


def solution(mesh):
    placed = (P(None, "row", "col", None), P("row", "col"), P("row", "col"), P("row", "col"))
    return jax.shard_map(
        body,
        mesh=mesh,
        in_specs=placed,
        out_specs=(P(None, "row", "col", None), P()),
        check_vma=False,
    )
```

```python
import functools

import jax
import jax.numpy as jnp
from jax import lax
from jax.experimental import pallas as pl
from jax.experimental.pallas import tpu as pltpu
from jax.sharding import PartitionSpec as P

STEPS = 2
RENORMS = 2
LEVELS = 50

viscosity = 0.15
gravity = 0.5
rotation = 0.4

SUB = 8
LANES = 128
FIELDS = 3
TILES = 8
VMEM_LIMIT = 16 * 1024 * 1024

HBM = pl.BlockSpec(memory_space=pltpu.HBM)
VMEM = pl.BlockSpec(memory_space=pltpu.VMEM)
SMEM = pl.BlockSpec(memory_space=pltpu.SMEM)


def params():
    return pltpu.CompilerParams(vmem_limit_bytes=VMEM_LIMIT)


def shape_of(*dims):
    return jax.ShapeDtypeStruct(dims, jnp.float32)


def lane_spread(block, lane):
    return jnp.broadcast_to(block[:, lane : lane + 1], (block.shape[0], LANES))


def spread_fields(sea_ref, levels_ref, current_ref, out_ref):
    rows = sea_ref.shape[1]
    fields = (
        sea_ref[...].astype(jnp.float32),
        0.5 * current_ref[...],
        0.5 * ((levels_ref[...] + 1).astype(jnp.float32) / LEVELS),
    )
    for field, value in enumerate(fields):
        for row in range(rows):
            out_ref[field, row] = lane_spread(value, row)


def sides_of(par):
    odd_row, odd_col = par[0] % 2, par[1] % 2
    return (1 - odd_row, odd_row), (1 - odd_col, odd_col)


def pack_first(par, t_ref, col_a, col_b, row_a, row_b, edges, sems):
    comps, rows, cols, _ = t_ref.shape
    norths, easts = sides_of(par)
    copies = []
    for slot in (0, 1):
        start = pl.multiple_of(easts[slot] * (cols - SUB), SUB)
        copies.append(
            pltpu.make_async_copy(t_ref.at[:, :, pl.ds(start, SUB), :], edges.at[slot], sems.at[slot])
        )
        copies[-1].start()
    for slot, msg in ((0, row_a), (1, row_b)):
        copies.append(
            pltpu.make_async_copy(t_ref.at[:, norths[slot] * (rows - 1)], msg, sems.at[2 + slot])
        )
        copies[-1].start()
    for slot, msg in ((0, col_a), (1, col_b)):
        copies[slot].wait()
        flat = edges.at[slot].reshape(comps * rows * SUB, LANES)
        for comp in range(comps):
            for row in range(0, rows, SUB):
                at = (comp * rows + row) * SUB + easts[slot] * (SUB - 1)
                msg[comp, pl.ds(row, SUB), :] = flat[pl.ds(at, SUB, stride=SUB), :]
    copies[2].wait()
    copies[3].wait()


def pack_edges(par, state, col_a, col_b, row_a, row_b):
    comps, rows, cols, _ = state.shape
    norths, easts = sides_of(par)
    flat = state.reshape(comps * rows * cols, LANES)
    for slot, msg in ((0, col_a), (1, col_b)):
        for comp in range(comps):
            for row in range(0, rows, SUB):
                at = (comp * rows + row) * cols + easts[slot] * (cols - 1)
                msg[comp, pl.ds(row, SUB), :] = flat[pl.ds(at, SUB, stride=cols), :]
    for slot, msg in ((0, row_a), (1, row_b)):
        for comp in range(comps):
            msg[comp] = state[comp, norths[slot] * (rows - 1)]


def apply_inside(t_ref, coef_ref, spin_ref, out_ref):
    comps, rows, cols, _ = t_ref.shape
    flat = t_ref.reshape(comps * rows * cols, LANES)
    sub = lax.broadcasted_iota(jnp.int32, (SUB, LANES), 0)
    zero = jnp.zeros((SUB, LANES), jnp.float32)
    keep, half = 1.0 - 4.0 * viscosity, 0.5 * gravity

    def line_of(line, south, north):
        spin = jnp.broadcast_to(spin_ref[pl.ds(line, 1), :], (SUB, LANES))
        for lon in range(0, cols, SUB):
            at = [(comp * rows + line) * cols + lon for comp in range(comps)]
            sea, flow, depth = (coef_ref[field, line, pl.ds(lon, SUB), :] for field in range(FIELDS))
            own = [t_ref[comp, line, pl.ds(lon, SUB), :] for comp in range(comps)]
            if lon == 0:
                west = [jnp.where(sub == 0, 0.0, pltpu.roll(x, 1, 0)) for x in own]
            else:
                west = [flat[pl.ds(a - 1, SUB), :] for a in at]
            if lon == cols - SUB:
                east = [jnp.where(sub == SUB - 1, 0.0, pltpu.roll(x, SUB - 1, 0)) for x in own]
            else:
                east = [flat[pl.ds(a + 1, SUB), :] for a in at]
            above = [
                t_ref[comp, line + 1, pl.ds(lon, SUB), :] if north else zero for comp in range(comps)
            ]
            below = [
                t_ref[comp, line - 1, pl.ds(lon, SUB), :] if south else zero for comp in range(comps)
            ]
            x_diff = [e - w for e, w in zip(east, west)]
            mixed = [
                keep * c + viscosity * ((e + w) + (n + s)) - flow * x
                for c, e, w, n, s, x in zip(own, east, west, above, below, x_diff)
            ]
            v_y, h_y = above[1] - below[1], above[2] - below[2]
            out_ref[0, line, pl.ds(lon, SUB), :] = sea * (mixed[0] - half * x_diff[2] + spin * own[1])
            out_ref[1, line, pl.ds(lon, SUB), :] = sea * (mixed[1] - half * h_y - spin * own[0])
            out_ref[2, line, pl.ds(lon, SUB), :] = sea * (mixed[2] - depth * (x_diff[0] + v_y))

    line_of(0, False, True)
    line_of(rows - 1, True, False)

    @pl.loop(0, (rows - 2) // 2)
    def _(pair):
        line_of(1 + 2 * pair, True, True)
        line_of(2 + 2 * pair, True, True)


def add_halos(par, state, coef_ref, col_a, col_b, row_a, row_b):
    comps, rows, cols, _ = state.shape
    norths, easts = sides_of(par)
    half = 0.5 * gravity
    flat = state.reshape(comps * rows * cols, LANES)
    flat_coef = coef_ref.reshape(FIELDS * rows * cols, LANES)
    for slot, halo in ((0, col_a), (1, col_b)):
        sign = (1 - 2 * easts[slot]).astype(jnp.float32)
        for row in range(0, rows, SUB):
            spots = [
                pl.ds((comp * rows + row) * cols + easts[slot] * (cols - 1), SUB, stride=cols)
                for comp in range(comps)
            ]
            sea, flow, depth = (flat_coef[spot, :] for spot in spots)
            u, v, h = (halo[comp, pl.ds(row, SUB), :] for comp in range(comps))
            mix = viscosity + sign * flow
            flat[spots[0], :] += sea * (mix * u + (sign * half) * h)
            flat[spots[1], :] += sea * (mix * v)
            flat[spots[2], :] += sea * (mix * h + (sign * depth) * u)
    for slot, halo in ((0, row_a), (1, row_b)):
        sign = (1 - 2 * norths[slot]).astype(jnp.float32)
        line = norths[slot] * (rows - 1)
        for lon in range(0, cols, SUB):
            cells = pl.ds(lon, SUB)
            sea, _, depth = (coef_ref[field, line, cells, :] for field in range(FIELDS))
            u, v, h = (halo[comp, cells, :] for comp in range(comps))
            state[0, line, cells, :] += sea * (viscosity * u)
            state[1, line, cells, :] += sea * (viscosity * v + (sign * half) * h)
            state[2, line, cells, :] += sea * (viscosity * h + (sign * depth) * v)


def join_step(par, state_in, coef_ref, a, b, c, d, state, col_a, col_b, row_a, row_b):
    add_halos(par, state, coef_ref, a, b, c, d)
    pack_edges(par, state, col_a, col_b, row_a, row_b)


def join_gram(
    scale, par, state_in, coef_ref, a, b, c, d, state, col_a, col_b, row_a, row_b, kept, sent, total
):
    add_halos(par, state, coef_ref, a, b, c, d)
    pack_edges(par, state, col_a, col_b, row_a, row_b)
    total[...] = jnp.zeros_like(total)
    flat = state.reshape(state.shape[0] * state.shape[1] * state.shape[2], LANES)
    height = flat.shape[0] // TILES

    @pl.loop(0, TILES)
    def _(tile):
        total[...] += gram_of(split_halves(flat[pl.ds(tile * height, height), :]))

    write_halves(par, total, scale, kept, sent)


def split_halves(value):
    high = value.astype(jnp.bfloat16)
    low = (value - high.astype(jnp.float32)).astype(jnp.bfloat16)
    return jnp.concatenate([high, low], axis=1)


def gram_of(pair):
    return lax.dot_general(pair, pair, (((0,), (0,)), ((), ())), preferred_element_type=jnp.float32)


def write_halves(par, total, scale, kept, sent):
    odd = par[1] % 2
    rows = LANES // 2
    for out, start in ((kept, odd * rows), (sent, (1 - odd) * rows)):
        top, low = pl.ds(start, rows), pl.ds(LANES + start, rows)
        out[...] = scale * (
            (total[top, :LANES] + total[low, LANES:]) + (total[top, LANES:] + total[low, :LANES])
        )


def invert_factor(gram_ref, work):
    count = LANES // SUB
    lane = lax.broadcasted_iota(jnp.int32, (SUB, LANES), 1)
    sub = lax.broadcasted_iota(jnp.int32, (SUB, LANES), 0)
    rows = [gram_ref[pl.ds(SUB * i, SUB), :] for i in range(count)]
    for block in range(count):
        base = SUB * block
        here = (lane >= base) & (lane < base + SUB)
        spread = [lane_spread(rows[block], base + l) for l in range(SUB)]
        low = [
            [jnp.broadcast_to(spread[l][k : k + 1, :], (SUB, LANES)) for l in range(k + 1)]
            for k in range(SUB)
        ]
        pivot = jnp.where(here, jnp.where(lane - base == sub, 1.0, 0.0), rows[block])
        inv, scaled = [], []
        for k in range(SUB):
            inv.append(lax.rsqrt(low[k][k]))
            for i in range(k + 1, SUB):
                low[i][k] = low[i][k] * inv[k]
            for i in range(k + 1, SUB):
                for m in range(k + 1, i + 1):
                    low[i][m] = low[i][m] - low[i][k] * low[m][k]
            line = jnp.broadcast_to(pivot[k : k + 1, :], (SUB, LANES))
            for l in range(k):
                line = line - low[k][l] * scaled[l]
            scaled.append(line * inv[k])
        merged = scaled[0]
        for k in range(1, SUB):
            merged = jnp.where(sub == k, scaled[k], merged)
        work[pl.ds(base, SUB), :] = merged
        for i in range(block + 1, count):
            weights = []
            rest = jnp.where(here, 0.0, rows[i])
            for l in range(SUB):
                weight = lane_spread(rows[i], base + l)
                for m in range(l):
                    weight = weight - weights[m] * low[l][m]
                weights.append(weight * inv[l])
            for l in range(SUB):
                rest = rest - weights[l] * scaled[l]
            rows[i] = rest


def factorize(par, mine_ref, other_ref, gram, work):
    rows = LANES // 2
    odd = par[1] % 2
    gram[pl.ds(odd * rows, rows), :] = mine_ref[...]
    gram[pl.ds((1 - odd) * rows, rows), :] = other_ref[...]
    invert_factor(gram, work)
    row = lax.broadcasted_iota(jnp.int32, (LANES, LANES), 0)
    col = lax.broadcasted_iota(jnp.int32, (LANES, LANES), 1)
    inverse = jnp.where(row >= col, work[...], 0.0)
    diagonal = jnp.sum(jnp.where(row == col, inverse, 0.0), axis=0, keepdims=True)
    return inverse, diagonal


def paired(inverse):
    high = inverse.astype(jnp.bfloat16)
    low = (inverse - high.astype(jnp.float32)).astype(jnp.bfloat16)
    return jnp.concatenate(
        [jnp.concatenate([high, high], axis=1), jnp.concatenate([low, low], axis=1)], axis=0
    )


def times_factor(cells, factor):
    both = lax.dot_general(
        split_halves(cells), factor, (((1,), (1,)), ((), ())), preferred_element_type=jnp.float32
    )
    return both[:, :LANES] + both[:, LANES:]


def factor_only(par, mine_ref, other_ref, prior_ref, inverse_ref, logs_ref, gram, work):
    inverse, diagonal = factorize(par, mine_ref, other_ref, gram, work)
    inverse_ref[...] = inverse
    logs_ref[...] = prior_ref[...] - jnp.log(diagonal)


def join_update(
    scale, par, state_in, coef_ref, a, b, c, d, inverse_ref, state, kept, sent, factor, total
):
    add_halos(par, state, coef_ref, a, b, c, d)
    factor[...] = paired(inverse_ref[...])
    total[...] = jnp.zeros_like(total)
    flat = state.reshape(state.shape[0] * state.shape[1] * state.shape[2], LANES)
    height = flat.shape[0] // TILES

    @pl.loop(0, TILES)
    def _(tile):
        cells = pl.ds(tile * height, height)
        new = times_factor(flat[cells, :], factor[...])
        flat[cells, :] = new
        total[...] += gram_of(split_halves(new))

    write_halves(par, total, scale, kept, sent)


def finish(par, mine_ref, other_ref, prior_ref, t_ref, out_ref, logs_ref, gram, work, factor, fresh, sems):
    inverse, diagonal = factorize(par, mine_ref, other_ref, gram, work)
    logs_ref[...] = prior_ref[...] - jnp.log(diagonal)
    factor[...] = paired(inverse)

    def out_copy(tile):
        return pltpu.make_async_copy(fresh.at[tile], out_ref.at[tile], sems.at[tile])

    @pl.loop(0, TILES)
    def _(tile):
        fresh[tile] = times_factor(t_ref[tile], factor[...])
        out_copy(tile).start()

    for tile in range(TILES):
        out_copy(tile).wait()


def swap_pairs(near_value, far_value, axis, closed):
    count = lax.axis_size(axis)
    near = [(i, i ^ 1) for i in range(count)]
    far = [(i, (i + 1 if i % 2 else i - 1) % count) for i in range(count)]
    if not closed:
        far = far[1:-1]
    return lax.ppermute(near_value, axis, near), lax.ppermute(far_value, axis, far)


def exchanged(messages):
    col_a, col_b, row_a, row_b = messages
    return swap_pairs(col_a, col_b, "col", True) + swap_pairs(row_a, row_b, "row", False)


def swapped(value, axis, mask):
    return lax.ppermute(value, axis, [(i, i ^ mask) for i in range(lax.axis_size(axis))])


def sum_over(value, axis, first_bit):
    bits = lax.axis_size(axis).bit_length() - 1
    while first_bit < bits:
        low = 1 << first_bit
        if first_bit + 1 < bits:
            high = low << 1
            one, two, three = (swapped(value, axis, mask) for mask in (low, high, low | high))
            value = (value + one) + (two + three)
            first_bit += 2
        else:
            value = value + swapped(value, axis, low)
            first_bit += 1
    return value


def sum_devices(kept, sent):
    mine = kept + swapped(sent, "col", 1)
    mine = sum_over(mine, "col", 1)
    mine = sum_over(mine, "row", 0)
    return mine, swapped(mine, "col", 1)


def body(tangents, sea_mask, levels, current):
    comps, rows, cols, modes = tangents.shape
    total_rows = rows * lax.axis_size("row")
    total_cells = total_rows * cols * lax.axis_size("col")
    scale = 1.0 / total_cells
    row_at, col_at = lax.axis_index("row"), lax.axis_index("col")
    par = jnp.stack([row_at, col_at]).astype(jnp.int32)

    lat = (row_at * rows + jnp.arange(rows)).astype(jnp.float32)
    angle = (-70.0 + 140.0 * (lat + 0.5) / total_rows) * (jnp.pi / 180.0)
    spin = jnp.broadcast_to((rotation * jnp.sin(angle))[:, None], (rows, LANES))

    block = shape_of(comps, rows, cols, modes)
    messages = (shape_of(comps, rows, modes),) * 2 + (shape_of(comps, cols, modes),) * 2
    halves = (shape_of(modes // 2, modes),) * 2
    square = pltpu.VMEM((modes, modes), jnp.float32)
    factor = pltpu.VMEM((2 * modes, 2 * modes), jnp.bfloat16)
    total = pltpu.VMEM((2 * modes, 2 * modes), jnp.float32)

    def call(kernel, outs, *operands, specs=None, out_specs=None, scratch=(), aliases=None):
        return pl.pallas_call(
            kernel,
            out_shape=outs,
            in_specs=specs or [SMEM] + [VMEM] * (len(operands) - 1),
            out_specs=out_specs or (VMEM,) * len(outs),
            scratch_shapes=scratch,
            input_output_aliases=aliases or {},
            compiler_params=params(),
        )(*operands)

    coef = call(
        spread_fields,
        (shape_of(FIELDS, rows, cols, LANES),),
        sea_mask.T,
        levels.T,
        current.T,
        specs=[VMEM] * 3,
    )[0]

    def inside(state):
        return call(apply_inside, (block,), state, coef, spin, specs=[VMEM] * 3)[0]

    packed = call(
        pack_first,
        messages,
        par,
        tangents,
        specs=[SMEM, HBM],
        scratch=[
            pltpu.VMEM((2, comps, rows, SUB, modes), jnp.float32),
            pltpu.SemaphoreType.DMA((4,)),
        ],
    )
    halos = exchanged(packed)
    state, *packed = call(
        join_step, (block,) + messages, par, inside(tangents), coef, *halos, aliases={1: 0}
    )
    halos = exchanged(packed)
    state, *packed, kept, sent = call(
        functools.partial(join_gram, scale),
        (block,) + messages + halves,
        par,
        inside(state),
        coef,
        *halos,
        scratch=[total],
        aliases={1: 0},
    )
    halos = exchanged(packed)
    mine, other = sum_devices(kept, sent)
    state, *packed = call(
        join_step, (block,) + messages, par, inside(state), coef, *halos, aliases={1: 0}
    )
    halos = exchanged(packed)
    logs = jnp.zeros((1, modes), jnp.float32)
    inverse, logs = call(
        factor_only,
        (shape_of(modes, modes), shape_of(1, modes)),
        par,
        mine,
        other,
        logs,
        scratch=[square, square],
    )
    state, kept, sent = call(
        functools.partial(join_update, scale),
        (block,) + halves,
        par,
        inside(state),
        coef,
        *halos,
        inverse,
        scratch=[factor, total],
        aliases={1: 0},
    )
    mine, other = sum_devices(kept, sent)
    height = comps * rows * cols // TILES
    tiled = shape_of(TILES, height, modes)
    out, logs = call(
        finish,
        (tiled, shape_of(1, modes)),
        par,
        mine,
        other,
        logs,
        state.reshape(TILES, height, modes),
        out_specs=(HBM, VMEM),
        scratch=[
            square,
            square,
            factor,
            pltpu.VMEM((TILES, height, modes), jnp.float32),
            pltpu.SemaphoreType.DMA((TILES,)),
        ],
    )
    return out.reshape(tangents.shape), logs.reshape(modes)


def solution(mesh):
    placed = (P(None, "row", "col", None), P("row", "col"), P("row", "col"), P("row", "col"))
    return jax.shard_map(
        body,
        mesh=mesh,
        in_specs=placed,
        out_specs=(P(None, "row", "col", None), P()),
        check_vma=False,
    )
```

```python
import functools

import jax
import jax.numpy as jnp
from jax import lax
from jax.experimental import pallas as pl
from jax.experimental.pallas import tpu as pltpu
from jax.sharding import PartitionSpec as P

STEPS = 2
RENORMS = 2
LEVELS = 50

viscosity = 0.15
gravity = 0.5
rotation = 0.4

SUB = 8
LANES = 128
FIELDS = 3
HALO = STEPS * RENORMS
TILES = 6
VMEM_LIMIT = 16 * 1024 * 1024

HBM = pl.BlockSpec(memory_space=pltpu.HBM)
VMEM = pl.BlockSpec(memory_space=pltpu.VMEM)
SMEM = pl.BlockSpec(memory_space=pltpu.SMEM)


def params():
    return pltpu.CompilerParams(vmem_limit_bytes=VMEM_LIMIT)


def shape_of(*dims):
    return jax.ShapeDtypeStruct(dims, jnp.float32)


def lane_spread(block, lane):
    return jnp.broadcast_to(block[:, lane : lane + 1], (block.shape[0], LANES))


def fields_of(sea_ref, levels_ref, current_ref):
    return (
        sea_ref[...].astype(jnp.float32),
        0.5 * current_ref[...],
        0.5 * ((levels_ref[...] + 1).astype(jnp.float32) / LEVELS),
    )


def sides_of(par):
    odd_row, odd_col = par[0] % 2, par[1] % 2
    return (1 - odd_row, odd_row), (1 - odd_col, odd_col)


def pack_rows(par, t_ref, sea_ref, levels_ref, current_ref, row_a, row_b, wide, sems):
    comps, rows, cols, _ = t_ref.shape
    norths, _ = sides_of(par)
    copies = []
    for slot, msg in ((0, row_a), (1, row_b)):
        for comp in range(comps):
            copies.append(
                pltpu.make_async_copy(
                    t_ref.at[comp, pl.ds(norths[slot] * (rows - HALO), HALO)],
                    msg.at[pl.ds(comp * HALO, HALO)],
                    sems.at[slot * comps + comp],
                )
            )
            copies[-1].start()
    lane = lax.broadcasted_iota(jnp.int32, (cols, LANES), 1)
    wide[...] = jnp.zeros_like(wide)
    packed = [jnp.zeros((cols, LANES), jnp.float32)] * 2
    for field, value in enumerate(fields_of(sea_ref, levels_ref, current_ref)):
        wide[:, pl.ds(0, rows)] = value
        whole = wide[...]
        for north in (0, 1):
            shift = (field * SUB - north * (rows - HALO)) % LANES
            moved = pltpu.roll(whole, shift, 1) if shift else whole
            here = (lane >= field * SUB) & (lane < field * SUB + HALO)
            packed[north] = jnp.where(here, moved, packed[north])
    for slot, msg in ((0, row_a), (1, row_b)):
        msg[comps * HALO] = jnp.where(norths[slot] == 1, packed[1], packed[0])
    for copy in copies:
        copy.wait()


def spread_fields(t_ref, sea_ref, levels_ref, current_ref, state, coef, sems):
    comps, rows, _, _ = t_ref.shape
    copies = [
        pltpu.make_async_copy(t_ref.at[comp], state.at[comp, pl.ds(HALO, rows)], sems.at[comp])
        for comp in range(comps)
    ]
    for copy in copies:
        copy.start()
    for field, value in enumerate(fields_of(sea_ref, levels_ref, current_ref)):
        for row in range(rows):
            coef[field, HALO + row] = lane_spread(value, row)
    for copy in copies:
        copy.wait()


def pack_columns(par, state, col_a, col_b):
    comps, tall, cols, _ = state.shape
    _, easts = sides_of(par)
    flat = state.reshape(comps * tall * cols, LANES)
    for slot, msg in ((0, col_a), (1, col_b)):
        for comp in range(comps):
            for row in range(0, tall, SUB):
                at = (comp * tall + row) * cols + easts[slot] * (cols - 1)
                msg[comp, pl.ds(row, SUB), :] = flat[pl.ds(at, SUB, stride=cols), :]


def join_rows(par, state_in, coef_in, row_a, row_b, state, coef, col_a, col_b):
    comps, tall, _, _ = state.shape
    norths, _ = sides_of(par)
    for slot, msg in ((0, row_a), (1, row_b)):
        line = norths[slot] * (tall - HALO)
        fields = msg[comps * HALO]
        for h in range(HALO):
            for comp in range(comps):
                state[comp, line + h] = msg[comp * HALO + h]
            for field in range(FIELDS):
                coef[field, line + h] = lane_spread(fields, field * SUB + h)
    pack_columns(par, state, col_a, col_b)


def apply_inside(step, t_ref, coef_ref, spin_ref, out_ref):
    comps, tall, cols, _ = t_ref.shape
    flat = t_ref.reshape(comps * tall * cols, LANES)
    sub = lax.broadcasted_iota(jnp.int32, (SUB, LANES), 0)
    keep, half = 1.0 - 4.0 * viscosity, 0.5 * gravity
    first, last = step + 1, tall - step - 1

    def line_of(line):
        spin = jnp.broadcast_to(spin_ref[pl.ds(line, 1), :], (SUB, LANES))
        for lon in range(0, cols, SUB):
            at = [(comp * tall + line) * cols + lon for comp in range(comps)]
            cells = pl.ds(lon, SUB)
            sea, flow, depth = (coef_ref[field, line, cells, :] for field in range(FIELDS))
            own = [t_ref[comp, line, cells, :] for comp in range(comps)]
            if lon == 0:
                west = [jnp.where(sub == 0, 0.0, pltpu.roll(x, 1, 0)) for x in own]
            else:
                west = [flat[pl.ds(a - 1, SUB), :] for a in at]
            if lon == cols - SUB:
                east = [jnp.where(sub == SUB - 1, 0.0, pltpu.roll(x, SUB - 1, 0)) for x in own]
            else:
                east = [flat[pl.ds(a + 1, SUB), :] for a in at]
            above = [t_ref[comp, line + 1, cells, :] for comp in range(comps)]
            below = [t_ref[comp, line - 1, cells, :] for comp in range(comps)]
            x_diff = [e - w for e, w in zip(east, west)]
            mixed = [
                keep * c + viscosity * ((e + w) + (n + s)) - flow * x
                for c, e, w, n, s, x in zip(own, east, west, above, below, x_diff)
            ]
            v_y, h_y = above[1] - below[1], above[2] - below[2]
            out_ref[0, line, cells, :] = sea * (mixed[0] - half * x_diff[2] + spin * own[1])
            out_ref[1, line, cells, :] = sea * (mixed[1] - half * h_y - spin * own[0])
            out_ref[2, line, cells, :] = sea * (mixed[2] - depth * (x_diff[0] + v_y))

    @pl.loop(0, (last - first) // 2)
    def _(pair):
        line_of(first + 2 * pair)
        line_of(first + 1 + 2 * pair)


def add_columns(par, state, coef_ref, col_a, col_b):
    comps, tall, cols, _ = state.shape
    _, easts = sides_of(par)
    half = 0.5 * gravity
    flat = state.reshape(comps * tall * cols, LANES)
    flat_coef = coef_ref.reshape(FIELDS * tall * cols, LANES)
    for slot, halo in ((0, col_a), (1, col_b)):
        sign = (1 - 2 * easts[slot]).astype(jnp.float32)
        for row in range(0, tall, SUB):
            spots = [
                pl.ds((comp * tall + row) * cols + easts[slot] * (cols - 1), SUB, stride=cols)
                for comp in range(comps)
            ]
            sea, flow, depth = (flat_coef[spot, :] for spot in spots)
            u, v, h = (halo[comp, pl.ds(row, SUB), :] for comp in range(comps))
            mix = viscosity + sign * flow
            flat[spots[0], :] += sea * (mix * u + (sign * half) * h)
            flat[spots[1], :] += sea * (mix * v)
            flat[spots[2], :] += sea * (mix * h + (sign * depth) * u)


def tiles_of(state):
    comps, tall, cols, _ = state.shape
    flat = state.reshape(comps * tall * cols, LANES)
    parts = TILES // comps
    height = (tall - 2 * HALO) * cols // parts
    for tile in range(TILES):
        start = ((tile // parts) * tall + HALO) * cols + (tile % parts) * height
        yield flat, pl.ds(start, height)


def join_step(par, state_in, coef_ref, a, b, state, col_a, col_b):
    add_columns(par, state, coef_ref, a, b)
    pack_columns(par, state, col_a, col_b)


def join_gram(scale, par, state_in, coef_ref, a, b, state, col_a, col_b, kept, sent, total):
    add_columns(par, state, coef_ref, a, b)
    pack_columns(par, state, col_a, col_b)
    gram = sum(gram_of(*split_halves(flat[cells, :])) for flat, cells in tiles_of(state))
    write_halves(par, gram, scale, kept, sent, total)


def split_halves(value):
    high = value.astype(jnp.bfloat16)
    return high, (value - high.astype(jnp.float32)).astype(jnp.bfloat16)


def gram_of(high, low):
    return lax.dot_general(
        high,
        jnp.concatenate([high, low], axis=1),
        (((0,), (0,)), ((), ())),
        preferred_element_type=jnp.float32,
    )


def write_halves(par, gram, scale, kept, sent, total):
    odd = par[1] % 2
    rows = LANES // 2
    mixed = gram[:, LANES:]
    total[...] = scale * (gram[:, :LANES] + (mixed + jnp.transpose(mixed)))
    kept[...] = total[pl.ds(odd * rows, rows), :]
    sent[...] = total[pl.ds((1 - odd) * rows, rows), :]


def invert_factor(gram_ref, work):
    count = LANES // SUB
    lane = lax.broadcasted_iota(jnp.int32, (SUB, LANES), 1)
    sub = lax.broadcasted_iota(jnp.int32, (SUB, LANES), 0)
    rows = [gram_ref[pl.ds(SUB * i, SUB), :] for i in range(count)]
    for block in range(count):
        base = SUB * block
        here = (lane >= base) & (lane < base + SUB)
        spread = [lane_spread(rows[block], base + l) for l in range(SUB)]
        low = [
            [jnp.broadcast_to(spread[l][k : k + 1, :], (SUB, LANES)) for l in range(k + 1)]
            for k in range(SUB)
        ]
        pivot = jnp.where(here, jnp.where(lane - base == sub, 1.0, 0.0), rows[block])
        inv, scaled = [], []
        for k in range(SUB):
            inv.append(lax.rsqrt(low[k][k]))
            for i in range(k + 1, SUB):
                low[i][k] = low[i][k] * inv[k]
            for i in range(k + 1, SUB):
                for m in range(k + 1, i + 1):
                    low[i][m] = low[i][m] - low[i][k] * low[m][k]
            line = jnp.broadcast_to(pivot[k : k + 1, :], (SUB, LANES))
            for l in range(k):
                line = line - low[k][l] * scaled[l]
            scaled.append(line * inv[k])
        merged = scaled[0]
        for k in range(1, SUB):
            merged = jnp.where(sub == k, scaled[k], merged)
        work[pl.ds(base, SUB), :] = merged
        for i in range(block + 1, count):
            weights = []
            rest = jnp.where(here, 0.0, rows[i])
            for l in range(SUB):
                weight = lane_spread(rows[i], base + l)
                for m in range(l):
                    weight = weight - weights[m] * low[l][m]
                weights.append(weight * inv[l])
            for l in range(SUB):
                rest = rest - weights[l] * scaled[l]
            rows[i] = rest


def factorize(par, mine_ref, other_ref, gram, work):
    rows = LANES // 2
    odd = par[1] % 2
    gram[pl.ds(odd * rows, rows), :] = mine_ref[...]
    gram[pl.ds((1 - odd) * rows, rows), :] = other_ref[...]
    invert_factor(gram, work)
    row = lax.broadcasted_iota(jnp.int32, (LANES, LANES), 0)
    col = lax.broadcasted_iota(jnp.int32, (LANES, LANES), 1)
    inverse = jnp.where(row >= col, work[...], 0.0)
    diagonal = jnp.sum(jnp.where(row == col, inverse, 0.0), axis=0, keepdims=True)
    return inverse, diagonal


def paired(inverse):
    high = inverse.astype(jnp.bfloat16)
    low = (inverse - high.astype(jnp.float32)).astype(jnp.bfloat16)
    return jnp.concatenate(
        [jnp.concatenate([high, high], axis=1), jnp.concatenate([low, low], axis=1)], axis=0
    )


def times_factor(cells, factor):
    pair = jnp.concatenate(split_halves(cells), axis=1)
    both = lax.dot_general(
        pair, factor, (((1,), (1,)), ((), ())), preferred_element_type=jnp.float32
    )
    return both[:, :LANES] + both[:, LANES:]


def factor_only(par, mine_ref, other_ref, prior_ref, inverse_ref, logs_ref, gram, work):
    inverse, diagonal = factorize(par, mine_ref, other_ref, gram, work)
    inverse_ref[...] = inverse
    logs_ref[...] = prior_ref[...] - jnp.log(diagonal)


def join_update(
    scale, par, state_in, coef_ref, a, b, inverse_ref, state, out_ref, kept, sent, factor, total
):
    add_columns(par, state, coef_ref, a, b)
    factor[...] = paired(inverse_ref[...])
    gram = 0.0
    for tile, (flat, cells) in enumerate(tiles_of(state)):
        new = times_factor(flat[cells, :], factor[...])
        out_ref[tile] = new
        gram += gram_of(*split_halves(new))
    write_halves(par, gram, scale, kept, sent, total)


def finish(par, mine_ref, other_ref, prior_ref, t_ref, out_ref, logs_ref, gram, work, factor, fresh, sems):
    inverse, diagonal = factorize(par, mine_ref, other_ref, gram, work)
    logs_ref[...] = prior_ref[...] - jnp.log(diagonal)
    factor[...] = paired(inverse)

    def out_copy(tile):
        return pltpu.make_async_copy(fresh.at[tile], out_ref.at[tile], sems.at[tile])

    for tile in range(TILES):
        fresh[tile] = times_factor(t_ref[tile], factor[...])
        out_copy(tile).start()

    for tile in range(TILES):
        out_copy(tile).wait()


def swap_pairs(near_value, far_value, axis, closed):
    count = lax.axis_size(axis)
    near = [(i, i ^ 1) for i in range(count)]
    far = [(i, (i + 1 if i % 2 else i - 1) % count) for i in range(count)]
    if not closed:
        far = far[1:-1]
    return lax.ppermute(near_value, axis, near), lax.ppermute(far_value, axis, far)


def swapped(value, axis, mask):
    return lax.ppermute(value, axis, [(i, i ^ mask) for i in range(lax.axis_size(axis))])


def sum_over(value, axis, first_bit):
    bits = lax.axis_size(axis).bit_length() - 1
    while first_bit < bits:
        low = 1 << first_bit
        if first_bit + 1 < bits:
            high = low << 1
            one, two, three = (swapped(value, axis, mask) for mask in (low, high, low | high))
            value = (value + one) + (two + three)
            first_bit += 2
        else:
            value = value + swapped(value, axis, low)
            first_bit += 1
    return value


def sum_devices(kept, sent):
    mine = kept + swapped(sent, "col", 1)
    mine = sum_over(mine, "col", 1)
    mine = sum_over(mine, "row", 0)
    return mine, swapped(mine, "col", 1)


def body(tangents, sea_mask, levels, current):
    comps, rows, cols, modes = tangents.shape
    total_rows = rows * lax.axis_size("row")
    total_cells = total_rows * cols * lax.axis_size("col")
    scale = 1.0 / total_cells
    row_at, col_at = lax.axis_index("row"), lax.axis_index("col")
    par = jnp.stack([row_at, col_at]).astype(jnp.int32)

    tall = rows + 2 * HALO
    lat = (row_at * rows - HALO + jnp.arange(tall)).astype(jnp.float32)
    angle = (-70.0 + 140.0 * (lat + 0.5) / total_rows) * (jnp.pi / 180.0)
    spin = jnp.broadcast_to((rotation * jnp.sin(angle))[:, None], (tall, LANES))

    height = comps * rows * cols // TILES
    block = shape_of(comps, tall, cols, modes)
    columns = (shape_of(comps, tall, modes),) * 2
    rows_sent = (shape_of(comps * HALO + 1, cols, modes),) * 2
    halves = (shape_of(modes // 2, modes),) * 2
    tiled = shape_of(TILES, height, modes)
    square = pltpu.VMEM((modes, modes), jnp.float32)
    factor = pltpu.VMEM((2 * modes, 2 * modes), jnp.bfloat16)

    def call(kernel, outs, *operands, specs=None, out_specs=None, scratch=(), aliases=None):
        return pl.pallas_call(
            kernel,
            out_shape=outs,
            in_specs=specs or [SMEM] + [VMEM] * (len(operands) - 1),
            out_specs=out_specs or (VMEM,) * len(outs),
            scratch_shapes=scratch,
            input_output_aliases=aliases or {},
            compiler_params=params(),
        )(*operands)

    def inside(step, state):
        kernel = functools.partial(apply_inside, step)
        return call(kernel, (block,), state, coef, spin, specs=[VMEM] * 3)[0]

    def swap_columns(packed):
        return swap_pairs(*packed, "col", True)

    source = pltpu.with_memory_space_constraint(tangents, pltpu.HBM)
    fields = (sea_mask.T, levels.T, current.T)
    packed = call(
        pack_rows,
        rows_sent,
        par,
        source,
        *fields,
        specs=[SMEM, HBM] + [VMEM] * 3,
        scratch=[pltpu.VMEM((cols, LANES), jnp.float32), pltpu.SemaphoreType.DMA((2 * comps,))],
    )
    row_halos = swap_pairs(*packed, "row", False)
    state, coef = call(
        spread_fields,
        (block, shape_of(FIELDS, tall, cols, LANES)),
        source,
        *fields,
        specs=[HBM] + [VMEM] * 3,
        scratch=[pltpu.SemaphoreType.DMA((comps,))],
    )
    state, coef, *packed = call(
        join_rows,
        (block, shape_of(FIELDS, tall, cols, LANES)) + columns,
        par,
        state,
        coef,
        *row_halos,
        aliases={1: 0, 2: 1},
    )
    logs = jnp.zeros((1, modes), jnp.float32)
    for step in range(STEPS * RENORMS):
        halos = swap_columns(packed)
        state = inside(step, state)
        if step == STEPS * RENORMS - 1:
            break
        if step == STEPS - 1:
            state, *packed, kept, sent = call(
                functools.partial(join_gram, scale),
                (block,) + columns + halves,
                par,
                state,
                coef,
                *halos,
                scratch=[square],
                aliases={1: 0},
            )
            mine, other = sum_devices(kept, sent)
            inverse, logs = call(
                factor_only,
                (shape_of(modes, modes), shape_of(1, modes)),
                par,
                mine,
                other,
                logs,
                scratch=[square, square],
            )
        else:
            state, *packed = call(
                join_step, (block,) + columns, par, state, coef, *halos, aliases={1: 0}
            )
    _, state, kept, sent = call(
        functools.partial(join_update, scale),
        (block, tiled) + halves,
        par,
        state,
        coef,
        *halos,
        inverse,
        scratch=[factor, square],
        aliases={1: 0},
    )
    mine, other = sum_devices(kept, sent)
    out, logs = call(
        finish,
        (tiled, shape_of(1, modes)),
        par,
        mine,
        other,
        logs,
        state,
        out_specs=(HBM, VMEM),
        scratch=[
            square,
            square,
            factor,
            pltpu.VMEM((TILES, height, modes), jnp.float32),
            pltpu.SemaphoreType.DMA((TILES,)),
        ],
    )
    return out.reshape(tangents.shape), logs.reshape(modes)


def solution(mesh):
    placed = (P(None, "row", "col", None), P("row", "col"), P("row", "col"), P("row", "col"))
    return jax.shard_map(
        body,
        mesh=mesh,
        in_specs=placed,
        out_specs=(P(None, "row", "col", None), P()),
        check_vma=False,
    )
```

```python
import functools

import jax
import jax.numpy as jnp
from jax import lax
from jax.experimental import pallas as pl
from jax.experimental.pallas import tpu as pltpu
from jax.sharding import PartitionSpec as P

STEPS = 2
RENORMS = 2
LEVELS = 50

viscosity = 0.15
gravity = 0.5
rotation = 0.4

SUB = 8
LANES = 128
FIELDS = 3
HALO = STEPS * RENORMS
TILES = 12
VMEM_LIMIT = 16 * 1024 * 1024

HBM = pl.BlockSpec(memory_space=pltpu.HBM)
VMEM = pl.BlockSpec(memory_space=pltpu.VMEM)
SMEM = pl.BlockSpec(memory_space=pltpu.SMEM)


def params():
    return pltpu.CompilerParams(vmem_limit_bytes=VMEM_LIMIT)


def shape_of(*dims):
    return jax.ShapeDtypeStruct(dims, jnp.float32)


def lane_spread(block, lane):
    return jnp.broadcast_to(block[:, lane : lane + 1], (block.shape[0], LANES))


def fetch(sources, places, sems):
    copies = [
        pltpu.make_async_copy(source, place, sems.at[i])
        for i, (source, place) in enumerate(zip(sources, places))
    ]
    for copy in copies:
        copy.start()
    return copies


def finish_all(copies):
    for copy in copies:
        copy.wait()


def fields_of(sea_ref, levels_ref, current_ref):
    return (
        sea_ref[...].astype(jnp.float32),
        0.5 * current_ref[...],
        0.5 * ((levels_ref[...] + 1).astype(jnp.float32) / LEVELS),
    )


def sides_of(par):
    odd_row, odd_col = par[0] % 2, par[1] % 2
    return (1 - odd_row, odd_row), (1 - odd_col, odd_col)


def pack_rows(
    par, t_ref, sea_ref, levels_ref, current_ref, row_a, row_b, sea, levels, current, wide, sems, field_sems
):
    comps, rows, cols, _ = t_ref.shape
    norths, _ = sides_of(par)
    field_copies = fetch((sea_ref, levels_ref, current_ref), (sea, levels, current), field_sems)
    slots = [(slot, msg, comp) for slot, msg in ((0, row_a), (1, row_b)) for comp in range(comps)]
    copies = fetch(
        [t_ref.at[comp, pl.ds(norths[slot] * (rows - HALO), HALO)] for slot, _, comp in slots],
        [msg.at[pl.ds(comp * HALO, HALO)] for _, msg, comp in slots],
        sems,
    )
    lane = lax.broadcasted_iota(jnp.int32, (cols, LANES), 1)
    wide[...] = jnp.zeros_like(wide)
    packed = [jnp.zeros((cols, LANES), jnp.float32)] * 2
    finish_all(field_copies)
    for field, value in enumerate(fields_of(sea, levels, current)):
        wide[:, pl.ds(0, rows)] = value
        whole = wide[...]
        for north in (0, 1):
            shift = (field * SUB - north * (rows - HALO)) % LANES
            moved = pltpu.roll(whole, shift, 1) if shift else whole
            here = (lane >= field * SUB) & (lane < field * SUB + HALO)
            packed[north] = jnp.where(here, moved, packed[north])
    for slot, msg in ((0, row_a), (1, row_b)):
        msg[comps * HALO] = jnp.where(norths[slot] == 1, packed[1], packed[0])
    finish_all(copies)


def spread_fields(sea_ref, levels_ref, current_ref, coef, sea, levels, current, sems):
    rows = sea_ref.shape[1]
    finish_all(fetch((sea_ref, levels_ref, current_ref), (sea, levels, current), sems))
    for field, value in enumerate(fields_of(sea, levels, current)):
        for row in range(rows):
            coef[field, HALO + row] = lane_spread(value, row)


def pack_columns(par, state, col_a, col_b):
    comps, tall, cols, _ = state.shape
    _, easts = sides_of(par)
    flat = state.reshape(comps * tall * cols, LANES)
    for slot, msg in ((0, col_a), (1, col_b)):
        for comp in range(comps):
            for row in range(0, tall, SUB):
                at = (comp * tall + row) * cols + easts[slot] * (cols - 1)
                msg[comp, pl.ds(row, SUB), :] = flat[pl.ds(at, SUB, stride=cols), :]


def join_rows(par, t_ref, coef_in, row_a, row_b, state, coef, col_a, col_b, sems):
    comps, tall, _, _ = state.shape
    rows = tall - 2 * HALO
    norths, _ = sides_of(par)
    copies = fetch(
        [t_ref.at[comp] for comp in range(comps)],
        [state.at[comp, pl.ds(HALO, rows)] for comp in range(comps)],
        sems,
    )
    for slot, msg in ((0, row_a), (1, row_b)):
        line = norths[slot] * (tall - HALO)
        fields = msg[comps * HALO]
        for h in range(HALO):
            for comp in range(comps):
                state[comp, line + h] = msg[comp * HALO + h]
            for field in range(FIELDS):
                coef[field, line + h] = lane_spread(fields, field * SUB + h)
    finish_all(copies)
    pack_columns(par, state, col_a, col_b)


def apply_inside(step, t_ref, coef_ref, spin_ref, out_ref):
    comps, tall, cols, _ = t_ref.shape
    flat = t_ref.reshape(comps * tall * cols, LANES)
    sub = lax.broadcasted_iota(jnp.int32, (SUB, LANES), 0)
    keep, half = 1.0 - 4.0 * viscosity, 0.5 * gravity
    first, last = step + 1, tall - step - 1

    def line_of(line):
        spin = jnp.broadcast_to(spin_ref[pl.ds(line, 1), :], (SUB, LANES))
        for lon in range(0, cols, SUB):
            at = [(comp * tall + line) * cols + lon for comp in range(comps)]
            cells = pl.ds(lon, SUB)
            sea, flow, depth = (coef_ref[field, line, cells, :] for field in range(FIELDS))
            own = [t_ref[comp, line, cells, :] for comp in range(comps)]
            if lon == 0:
                west = [jnp.where(sub == 0, 0.0, pltpu.roll(x, 1, 0)) for x in own]
            else:
                west = [flat[pl.ds(a - 1, SUB), :] for a in at]
            if lon == cols - SUB:
                east = [jnp.where(sub == SUB - 1, 0.0, pltpu.roll(x, SUB - 1, 0)) for x in own]
            else:
                east = [flat[pl.ds(a + 1, SUB), :] for a in at]
            above = [t_ref[comp, line + 1, cells, :] for comp in range(comps)]
            below = [t_ref[comp, line - 1, cells, :] for comp in range(comps)]
            x_diff = [e - w for e, w in zip(east, west)]
            mixed = [
                keep * c + viscosity * ((e + w) + (n + s)) - flow * x
                for c, e, w, n, s, x in zip(own, east, west, above, below, x_diff)
            ]
            v_y, h_y = above[1] - below[1], above[2] - below[2]
            out_ref[0, line, cells, :] = sea * (mixed[0] - half * x_diff[2] + spin * own[1])
            out_ref[1, line, cells, :] = sea * (mixed[1] - half * h_y - spin * own[0])
            out_ref[2, line, cells, :] = sea * (mixed[2] - depth * (x_diff[0] + v_y))

    @pl.loop(0, (last - first) // 2)
    def _(pair):
        line_of(first + 2 * pair)
        line_of(first + 1 + 2 * pair)


def add_columns(par, state, coef_ref, col_a, col_b):
    comps, tall, cols, _ = state.shape
    _, easts = sides_of(par)
    half = 0.5 * gravity
    flat = state.reshape(comps * tall * cols, LANES)
    flat_coef = coef_ref.reshape(FIELDS * tall * cols, LANES)
    for slot, halo in ((0, col_a), (1, col_b)):
        sign = (1 - 2 * easts[slot]).astype(jnp.float32)
        for row in range(0, tall, SUB):
            spots = [
                pl.ds((comp * tall + row) * cols + easts[slot] * (cols - 1), SUB, stride=cols)
                for comp in range(comps)
            ]
            sea, flow, depth = (flat_coef[spot, :] for spot in spots)
            u, v, h = (halo[comp, pl.ds(row, SUB), :] for comp in range(comps))
            mix = viscosity + sign * flow
            flat[spots[0], :] += sea * (mix * u + (sign * half) * h)
            flat[spots[1], :] += sea * (mix * v)
            flat[spots[2], :] += sea * (mix * h + (sign * depth) * u)


def tiles_of(state):
    comps, tall, cols, _ = state.shape
    flat = state.reshape(comps * tall * cols, LANES)
    parts = TILES // comps
    height = (tall - 2 * HALO) * cols // parts
    for tile in range(TILES):
        start = ((tile // parts) * tall + HALO) * cols + (tile % parts) * height
        yield flat, pl.ds(start, height)


def join_step(par, state_in, coef_ref, a, b, state, col_a, col_b):
    add_columns(par, state, coef_ref, a, b)
    pack_columns(par, state, col_a, col_b)


def join_gram(scale, par, state_in, coef_ref, a, b, state, col_a, col_b, kept, sent, total):
    add_columns(par, state, coef_ref, a, b)
    pack_columns(par, state, col_a, col_b)
    gram = sum(gram_of(*split_halves(flat[cells, :])) for flat, cells in tiles_of(state))
    write_halves(par, gram, scale, kept, sent, total)


def split_halves(value):
    high = value.astype(jnp.bfloat16)
    return high, (value - high.astype(jnp.float32)).astype(jnp.bfloat16)


def gram_of(high, low):
    return lax.dot_general(
        high,
        jnp.concatenate([high, low], axis=1),
        (((0,), (0,)), ((), ())),
        preferred_element_type=jnp.float32,
    )


def write_halves(par, gram, scale, kept, sent, total):
    odd = par[1] % 2
    rows = LANES // 2
    mixed = gram[:, LANES:]
    total[...] = scale * (gram[:, :LANES] + (mixed + jnp.transpose(mixed)))
    kept[...] = total[pl.ds(odd * rows, rows), :]
    sent[...] = total[pl.ds((1 - odd) * rows, rows), :]


def invert_factor(gram_ref, work):
    count = LANES // SUB
    lane = lax.broadcasted_iota(jnp.int32, (SUB, LANES), 1)
    sub = lax.broadcasted_iota(jnp.int32, (SUB, LANES), 0)
    rows = [gram_ref[pl.ds(SUB * i, SUB), :] for i in range(count)]
    for block in range(count):
        base = SUB * block
        here = (lane >= base) & (lane < base + SUB)
        spread = [lane_spread(rows[block], base + l) for l in range(SUB)]
        low = [
            [jnp.broadcast_to(spread[l][k : k + 1, :], (SUB, LANES)) for l in range(k + 1)]
            for k in range(SUB)
        ]
        pivot = jnp.where(here, jnp.where(lane - base == sub, 1.0, 0.0), rows[block])
        inv, scaled = [], []
        for k in range(SUB):
            inv.append(lax.rsqrt(low[k][k]))
            for i in range(k + 1, SUB):
                low[i][k] = low[i][k] * inv[k]
            for i in range(k + 1, SUB):
                for m in range(k + 1, i + 1):
                    low[i][m] = low[i][m] - low[i][k] * low[m][k]
            line = jnp.broadcast_to(pivot[k : k + 1, :], (SUB, LANES))
            for l in range(k):
                line = line - low[k][l] * scaled[l]
            scaled.append(line * inv[k])
        merged = scaled[0]
        for k in range(1, SUB):
            merged = jnp.where(sub == k, scaled[k], merged)
        work[pl.ds(base, SUB), :] = merged
        for i in range(block + 1, count):
            weights = []
            rest = jnp.where(here, 0.0, rows[i])
            for l in range(SUB):
                weight = lane_spread(rows[i], base + l)
                for m in range(l):
                    weight = weight - weights[m] * low[l][m]
                weights.append(weight * inv[l])
            for l in range(SUB):
                rest = rest - weights[l] * scaled[l]
            rows[i] = rest


def factorize(par, mine_ref, other_ref, gram, work):
    rows = LANES // 2
    odd = par[1] % 2
    gram[pl.ds(odd * rows, rows), :] = mine_ref[...]
    gram[pl.ds((1 - odd) * rows, rows), :] = other_ref[...]
    invert_factor(gram, work)
    row = lax.broadcasted_iota(jnp.int32, (LANES, LANES), 0)
    col = lax.broadcasted_iota(jnp.int32, (LANES, LANES), 1)
    inverse = jnp.where(row >= col, work[...], 0.0)
    diagonal = jnp.sum(jnp.where(row == col, inverse, 0.0), axis=0, keepdims=True)
    return inverse, diagonal


def paired(inverse):
    high = inverse.astype(jnp.bfloat16)
    low = (inverse - high.astype(jnp.float32)).astype(jnp.bfloat16)
    return jnp.concatenate(
        [jnp.concatenate([high, high], axis=1), jnp.concatenate([low, low], axis=1)], axis=0
    )


def times_factor(cells, factor):
    pair = jnp.concatenate(split_halves(cells), axis=1)
    both = lax.dot_general(
        pair, factor, (((1,), (1,)), ((), ())), preferred_element_type=jnp.float32
    )
    return both[:, :LANES] + both[:, LANES:]


def factor_only(par, mine_ref, other_ref, prior_ref, inverse_ref, logs_ref, gram, work):
    inverse, diagonal = factorize(par, mine_ref, other_ref, gram, work)
    inverse_ref[...] = inverse
    logs_ref[...] = prior_ref[...] - jnp.log(diagonal)


def join_update(
    scale, par, state_in, coef_ref, a, b, inverse_ref, state, out_ref, kept, sent, factor, total
):
    add_columns(par, state, coef_ref, a, b)
    factor[...] = paired(inverse_ref[...])
    gram = 0.0
    for tile, (flat, cells) in enumerate(tiles_of(state)):
        new = times_factor(flat[cells, :], factor[...])
        out_ref[tile] = new
        gram += gram_of(*split_halves(new))
    write_halves(par, gram, scale, kept, sent, total)


def finish(par, mine_ref, other_ref, prior_ref, t_ref, out_ref, logs_ref, gram, work, factor, fresh, sems):
    inverse, diagonal = factorize(par, mine_ref, other_ref, gram, work)
    logs_ref[...] = prior_ref[...] - jnp.log(diagonal)
    factor[...] = paired(inverse)

    def out_copy(tile):
        return pltpu.make_async_copy(fresh.at[tile], out_ref.at[tile], sems.at[tile])

    for tile in range(TILES):
        fresh[tile] = times_factor(t_ref[tile], factor[...])
        out_copy(tile).start()

    for tile in range(TILES):
        out_copy(tile).wait()


def swap_pairs(near_value, far_value, axis, closed):
    count = lax.axis_size(axis)
    near = [(i, i ^ 1) for i in range(count)]
    far = [(i, (i + 1 if i % 2 else i - 1) % count) for i in range(count)]
    if not closed:
        far = far[1:-1]
    return lax.ppermute(near_value, axis, near), lax.ppermute(far_value, axis, far)


def swapped(value, axis, mask):
    return lax.ppermute(value, axis, [(i, i ^ mask) for i in range(lax.axis_size(axis))])


def sum_over(value, axis, first_bit):
    bits = lax.axis_size(axis).bit_length() - 1
    while first_bit < bits:
        low = 1 << first_bit
        if first_bit + 1 < bits:
            high = low << 1
            one, two, three = (swapped(value, axis, mask) for mask in (low, high, low | high))
            value = (value + one) + (two + three)
            first_bit += 2
        else:
            value = value + swapped(value, axis, low)
            first_bit += 1
    return value


def sum_groups(value, axis, low_bits, bits):
    count = lax.axis_size(axis)
    low, size = 1 << low_bits, 1 << bits
    groups = [
        [high * low * size + i * low + rest for i in range(size)]
        for high in range(count // (low * size))
        for rest in range(low)
    ]
    copies = jnp.broadcast_to(value, (size,) + value.shape)
    if size == count:
        groups = None
    got = lax.all_to_all(copies, axis, 0, 0, axis_index_groups=groups)
    return jnp.sum(got, axis=0)


def sum_devices(kept, sent, grouped):
    mine = kept + swapped(sent, "col", 1)
    if grouped:
        mine = sum_groups(mine, "col", 1, lax.axis_size("col").bit_length() - 2)
        mine = sum_groups(mine, "row", 0, lax.axis_size("row").bit_length() - 1)
    else:
        mine = sum_over(mine, "col", 1)
        mine = sum_over(mine, "row", 0)
    return mine, swapped(mine, "col", 1)


def body(tangents, sea_mask, levels, current):
    comps, rows, cols, modes = tangents.shape
    total_rows = rows * lax.axis_size("row")
    total_cells = total_rows * cols * lax.axis_size("col")
    scale = 1.0 / total_cells
    row_at, col_at = lax.axis_index("row"), lax.axis_index("col")
    par = jnp.stack([row_at, col_at]).astype(jnp.int32)

    tall = rows + 2 * HALO
    lat = (row_at * rows - HALO + jnp.arange(tall)).astype(jnp.float32)
    angle = (-70.0 + 140.0 * (lat + 0.5) / total_rows) * (jnp.pi / 180.0)
    spin = jnp.broadcast_to((rotation * jnp.sin(angle))[:, None], (tall, LANES))

    height = comps * rows * cols // TILES
    block = shape_of(comps, tall, cols, modes)
    columns = (shape_of(comps, tall, modes),) * 2
    rows_sent = (shape_of(comps * HALO + 1, cols, modes),) * 2
    halves = (shape_of(modes // 2, modes),) * 2
    tiled = shape_of(TILES, height, modes)
    square = pltpu.VMEM((modes, modes), jnp.float32)
    factor = pltpu.VMEM((2 * modes, 2 * modes), jnp.bfloat16)

    def call(kernel, outs, *operands, specs=None, out_specs=None, scratch=(), aliases=None):
        return pl.pallas_call(
            kernel,
            out_shape=outs,
            in_specs=specs or [SMEM] + [VMEM] * (len(operands) - 1),
            out_specs=out_specs or (VMEM,) * len(outs),
            scratch_shapes=scratch,
            input_output_aliases=aliases or {},
            compiler_params=params(),
        )(*operands)

    def inside(step, state):
        kernel = functools.partial(apply_inside, step)
        return call(kernel, (block,), state, coef, spin, specs=[VMEM] * 3)[0]

    def swap_columns(packed):
        return swap_pairs(*packed, "col", True)

    source, *fields = (
        pltpu.with_memory_space_constraint(x, pltpu.HBM)
        for x in (tangents, sea_mask.T, levels.T, current.T)
    )
    upright = [pltpu.VMEM(x.shape, x.dtype) for x in fields]
    packed = call(
        pack_rows,
        rows_sent,
        par,
        source,
        *fields,
        specs=[SMEM] + [HBM] * 4,
        scratch=upright
        + [
            pltpu.VMEM((cols, LANES), jnp.float32),
            pltpu.SemaphoreType.DMA((2 * comps,)),
            pltpu.SemaphoreType.DMA((FIELDS,)),
        ],
    )
    row_halos = swap_pairs(*packed, "row", False)
    coef = call(
        spread_fields,
        (shape_of(FIELDS, tall, cols, LANES),),
        *fields,
        specs=[HBM] * 3,
        scratch=upright + [pltpu.SemaphoreType.DMA((FIELDS,))],
    )[0]
    state, coef, *packed = call(
        join_rows,
        (block, shape_of(FIELDS, tall, cols, LANES)) + columns,
        par,
        source,
        coef,
        *row_halos,
        specs=[SMEM, HBM] + [VMEM] * 3,
        scratch=[pltpu.SemaphoreType.DMA((comps,))],
        aliases={2: 1},
    )
    logs = jnp.zeros((1, modes), jnp.float32)
    for step in range(STEPS * RENORMS):
        halos = swap_columns(packed)
        state = inside(step, state)
        if step == STEPS * RENORMS - 1:
            break
        if step == STEPS - 1:
            state, *packed, kept, sent = call(
                functools.partial(join_gram, scale),
                (block,) + columns + halves,
                par,
                state,
                coef,
                *halos,
                scratch=[square],
                aliases={1: 0},
            )
            mine, other = sum_devices(kept, sent, False)
            inverse, logs = call(
                factor_only,
                (shape_of(modes, modes), shape_of(1, modes)),
                par,
                mine,
                other,
                logs,
                scratch=[square, square],
            )
        else:
            state, *packed = call(
                join_step, (block,) + columns, par, state, coef, *halos, aliases={1: 0}
            )
    _, state, kept, sent = call(
        functools.partial(join_update, scale),
        (block, tiled) + halves,
        par,
        state,
        coef,
        *halos,
        inverse,
        scratch=[factor, square],
        aliases={1: 0},
    )
    mine, other = sum_devices(kept, sent, True)
    out, logs = call(
        finish,
        (tiled, shape_of(1, modes)),
        par,
        mine,
        other,
        logs,
        state,
        out_specs=(HBM, VMEM),
        scratch=[
            square,
            square,
            factor,
            pltpu.VMEM((TILES, height, modes), jnp.float32),
            pltpu.SemaphoreType.DMA((TILES,)),
        ],
    )
    return out.reshape(tangents.shape), logs.reshape(modes)


def solution(mesh):
    placed = (P(None, "row", "col", None), P("row", "col"), P("row", "col"), P("row", "col"))
    return jax.shard_map(
        body,
        mesh=mesh,
        in_specs=placed,
        out_specs=(P(None, "row", "col", None), P()),
        check_vma=False,
    )
```

```python
import functools

import jax
import jax.numpy as jnp
from jax import lax
from jax.experimental import pallas as pl
from jax.experimental.pallas import tpu as pltpu
from jax.sharding import PartitionSpec as P

STEPS = 2
RENORMS = 2
LEVELS = 50

viscosity = 0.15
gravity = 0.5
rotation = 0.4

SUB = 8
LANES = 128
FIELDS = 3
HALO = STEPS * RENORMS
SIDE = STEPS
STRIP = 2 * STEPS + 2
TILES = 12
VMEM_LIMIT = 16 * 1024 * 1024

HBM = pl.BlockSpec(memory_space=pltpu.HBM)
VMEM = pl.BlockSpec(memory_space=pltpu.VMEM)
SMEM = pl.BlockSpec(memory_space=pltpu.SMEM)


def params():
    return pltpu.CompilerParams(vmem_limit_bytes=VMEM_LIMIT)


def shape_of(*dims):
    return jax.ShapeDtypeStruct(dims, jnp.float32)


def lane_spread(block, lane):
    return jnp.broadcast_to(block[:, lane : lane + 1], (block.shape[0], LANES))


def fetch(sources, places, sems):
    copies = [
        pltpu.make_async_copy(source, place, sems.at[i])
        for i, (source, place) in enumerate(zip(sources, places))
    ]
    for copy in copies:
        copy.start()
    return copies


def finish_all(copies):
    for copy in copies:
        copy.wait()


def fields_of(sea_ref, levels_ref, current_ref):
    return (
        sea_ref[...].astype(jnp.float32),
        0.5 * current_ref[...],
        0.5 * ((levels_ref[...] + 1).astype(jnp.float32) / LEVELS),
    )


def sides_of(par):
    odd_row, odd_col = par[0] % 2, par[1] % 2
    return (1 - odd_row, odd_row), (1 - odd_col, odd_col)


def pack_rows(
    par, t_ref, sea_ref, levels_ref, current_ref, row_a, row_b, sea, levels, current, wide, sems, field_sems
):
    comps, rows, cols, _ = t_ref.shape
    norths, _ = sides_of(par)
    field_copies = fetch((sea_ref, levels_ref, current_ref), (sea, levels, current), field_sems)
    slots = [(slot, msg, comp) for slot, msg in ((0, row_a), (1, row_b)) for comp in range(comps)]
    copies = fetch(
        [t_ref.at[comp, pl.ds(norths[slot] * (rows - HALO), HALO)] for slot, _, comp in slots],
        [msg.at[pl.ds(comp * HALO, HALO)] for _, msg, comp in slots],
        sems,
    )
    lane = lax.broadcasted_iota(jnp.int32, (cols, LANES), 1)
    wide[...] = jnp.zeros_like(wide)
    packed = [jnp.zeros((cols, LANES), jnp.float32)] * 2
    finish_all(field_copies)
    for field, value in enumerate(fields_of(sea, levels, current)):
        wide[:, pl.ds(0, rows)] = value
        whole = wide[...]
        for north in (0, 1):
            shift = (field * SUB - north * (rows - HALO)) % LANES
            moved = pltpu.roll(whole, shift, 1) if shift else whole
            here = (lane >= field * SUB) & (lane < field * SUB + HALO)
            packed[north] = jnp.where(here, moved, packed[north])
    for slot, msg in ((0, row_a), (1, row_b)):
        msg[comps * HALO] = jnp.where(norths[slot] == 1, packed[1], packed[0])
    finish_all(copies)


def spread_fields(sea_ref, levels_ref, current_ref, coef, wide, sea, levels, current, sems):
    rows = sea_ref.shape[1]
    finish_all(fetch((sea_ref, levels_ref, current_ref), (sea, levels, current), sems))
    wide[...] = jnp.zeros_like(wide)
    for field, value in enumerate(fields_of(sea, levels, current)):
        wide[field, :, pl.ds(0, rows)] = value
        for row in range(rows):
            coef[field, HALO + row] = lane_spread(value, row)


def column_at(east, cols, depth):
    return depth + east * (cols - 1 - 2 * depth)


def join_rows(par, t_ref, coef_in, wide, row_a, row_b, state, coef, col_a, col_b, sems):
    comps, tall, cols, _ = state.shape
    rows = tall - 2 * HALO
    norths, easts = sides_of(par)
    copies = fetch(
        [t_ref.at[comp] for comp in range(comps)],
        [state.at[comp, pl.ds(HALO, rows)] for comp in range(comps)],
        sems,
    )
    for slot, msg in ((0, row_a), (1, row_b)):
        line = norths[slot] * (tall - HALO)
        fields = msg[comps * HALO]
        for h in range(HALO):
            for comp in range(comps):
                state[comp, line + h] = msg[comp * HALO + h]
            for field in range(FIELDS):
                coef[field, line + h] = lane_spread(fields, field * SUB + h)
    tail = comps * SIDE * tall
    for slot, msg in ((0, col_a), (1, col_b)):
        lon = column_at(easts[slot], cols, 0)
        msg[pl.ds(tail, SUB), :] = jnp.zeros((SUB, LANES), jnp.float32)
        for field in range(FIELDS):
            msg[pl.ds(tail + field, 1), :] = wide[field, pl.ds(lon, 1), :]
        for i, got in enumerate((row_a, row_b)):
            msg[pl.ds(tail + FIELDS + i, 1), :] = got[comps * HALO, pl.ds(lon, 1), :]
    finish_all(copies)
    flat = state.reshape(comps * tall * cols, LANES)
    for slot, msg in ((0, col_a), (1, col_b)):
        for comp in range(comps):
            for j in range(SIDE):
                for row in range(0, tall, SUB):
                    at = (comp * tall + row) * cols + column_at(easts[slot], cols, j)
                    msg[pl.ds((comp * SIDE + j) * tall + row, SUB), :] = flat[
                        pl.ds(at, SUB, stride=cols), :
                    ]


def model(own, x_diff, x_sum, above, below, sea, flow, depth, spin):
    keep, half = 1.0 - 4.0 * viscosity, 0.5 * gravity
    mixed = [
        keep * c + viscosity * (x + (n + s)) - flow * d
        for c, d, x, n, s in zip(own, x_diff, x_sum, above, below)
    ]
    v_y, h_y = above[1] - below[1], above[2] - below[2]
    return (
        sea * (mixed[0] - half * x_diff[2] + spin * own[1]),
        sea * (mixed[1] - half * h_y - spin * own[0]),
        sea * (mixed[2] - depth * (x_diff[0] + v_y)),
    )


def apply_inside(step, t_ref, coef_ref, spin_ref, out_ref):
    comps, tall, cols, _ = t_ref.shape
    flat = t_ref.reshape(comps * tall * cols, LANES)
    sub = lax.broadcasted_iota(jnp.int32, (SUB, LANES), 0)
    first, last = step + 1, tall - step - 1

    def line_of(line):
        spin = jnp.broadcast_to(spin_ref[pl.ds(line, 1), :], (SUB, LANES))
        for lon in range(0, cols, SUB):
            at = [(comp * tall + line) * cols + lon for comp in range(comps)]
            cells = pl.ds(lon, SUB)
            sea, flow, depth = (coef_ref[field, line, cells, :] for field in range(FIELDS))
            own = [t_ref[comp, line, cells, :] for comp in range(comps)]
            if lon == 0:
                west = [jnp.where(sub == 0, 0.0, pltpu.roll(x, 1, 0)) for x in own]
            else:
                west = [flat[pl.ds(a - 1, SUB), :] for a in at]
            if lon == cols - SUB:
                east = [jnp.where(sub == SUB - 1, 0.0, pltpu.roll(x, SUB - 1, 0)) for x in own]
            else:
                east = [flat[pl.ds(a + 1, SUB), :] for a in at]
            above = [t_ref[comp, line + 1, cells, :] for comp in range(comps)]
            below = [t_ref[comp, line - 1, cells, :] for comp in range(comps)]
            x_diff = [e - w for e, w in zip(east, west)]
            x_sum = [e + w for e, w in zip(east, west)]
            new = model(own, x_diff, x_sum, above, below, sea, flow, depth, spin)
            for comp in range(comps):
                out_ref[comp, line, cells, :] = new[comp]

    @pl.loop(0, (last - first) // 2)
    def _(pair):
        line_of(first + 2 * pair)
        line_of(first + 1 + 2 * pair)


def fill_edge(par, coef_ref, cols_got, edge):
    _, tall, cols, _ = coef_ref.shape
    rows = tall - 2 * HALO
    norths, easts = sides_of(par)
    flat = coef_ref.reshape(FIELDS * tall * cols, LANES)
    for slot, msg in enumerate(cols_got):
        upright = jnp.transpose(msg[pl.ds(msg.shape[0] - SUB, SUB), :])
        for field in range(FIELDS):
            edge[slot, field, 0, pl.ds(HALO, rows), :] = lane_spread(upright[:rows], field)
            for i in (0, 1):
                beyond = lane_spread(upright[field * SUB : (field + 1) * SUB], FIELDS + i)
                line = norths[i] * (tall - HALO)
                edge[slot, field, 0, pl.ds(line, HALO), :] = beyond[:HALO]
            for depth in range(STRIP - 3):
                lon = column_at(easts[slot], cols, depth)
                for row in range(0, tall, SUB):
                    at = (field * tall + row) * cols + lon
                    edge[slot, field, 1 + depth, pl.ds(row, SUB), :] = flat[
                        pl.ds(at, SUB, stride=cols), :
                    ]


def mend_columns(par, old, state, spin_ref, edge, cols_got, sent, strips):
    comps, tall, cols, _ = state.shape
    _, easts = sides_of(par)
    flat_old = old.reshape(comps * tall * cols, LANES)
    flat = state.reshape(comps * tall * cols, LANES)
    signs = [(1 - 2 * east).astype(jnp.float32) for east in easts]
    first, second = strips

    def neighbours(strip, slot, column, row):
        def load(comp, shift, lat):
            return strip[slot, comp, column + shift, pl.ds(SUB + row + lat, SUB), :]

        inner, outer = ([load(comp, shift, 0) for comp in range(comps)] for shift in (1, -1))
        return (
            [load(comp, 0, 0) for comp in range(comps)],
            [signs[slot] * (i - o) for i, o in zip(inner, outer)],
            [i + o for i, o in zip(inner, outer)],
            [load(comp, 0, 1) for comp in range(comps)],
            [load(comp, 0, -1) for comp in range(comps)],
        )

    def coefs(slot, column, row):
        return [edge[slot, field, column, pl.ds(row, SUB), :] for field in range(FIELDS)]

    @pl.loop(0, tall // SUB)
    def _(group):
        row = pl.multiple_of(group * SUB, SUB)
        for slot, got in enumerate(cols_got):
            for comp in range(comps):
                for j in range(SIDE):
                    first[slot, comp, SIDE - 1 - j, pl.ds(SUB + row, SUB), :] = got[
                        pl.ds((comp * SIDE + j) * tall + row, SUB), :
                    ]
                for depth in range(STRIP - SIDE):
                    at = (comp * tall + row) * cols + column_at(easts[slot], cols, depth)
                    first[slot, comp, SIDE + depth, pl.ds(SUB + row, SUB), :] = flat_old[
                        pl.ds(at, SUB, stride=cols), :
                    ]

    @pl.loop(0, tall // SUB)
    def _(group):
        row = pl.multiple_of(group * SUB, SUB)
        spin = spin_ref[pl.ds(row, SUB), :]
        for slot in (0, 1):
            for column in range(STRIP - 2):
                new = model(
                    *neighbours(first, slot, column + 1, row), *coefs(slot, column, row), spin
                )
                for comp in range(comps):
                    second[slot, comp, column, pl.ds(SUB + row, SUB), :] = new[comp]

    @pl.loop(0, tall // SUB)
    def _(group):
        row = pl.multiple_of(group * SUB, SUB)
        spin = spin_ref[pl.ds(row, SUB), :]
        for slot in (0, 1):
            for j in range(SIDE):
                new = model(
                    *neighbours(second, slot, j + 1, row), *coefs(slot, j + 1, row), spin
                )
                for comp in range(comps):
                    at = (comp * tall + row) * cols + column_at(easts[slot], cols, j)
                    flat[pl.ds(at, SUB, stride=cols), :] = new[comp]
                    if sent is not None:
                        sent[slot][pl.ds((comp * SIDE + j) * tall + row, SUB), :] = new[comp]


def tiles_of(state):
    comps, tall, cols, _ = state.shape
    flat = state.reshape(comps * tall * cols, LANES)
    parts = TILES // comps
    height = (tall - 2 * HALO) * cols // parts
    for tile in range(TILES):
        start = ((tile // parts) * tall + HALO) * cols + (tile % parts) * height
        yield flat, pl.ds(start, height)


def join_gram(
    scale, par, old, state_in, coef_ref, spin_ref, a, b, state, edge, col_a, col_b, kept, sent, total, *strips
):
    fill_edge(par, coef_ref, (a, b), edge)
    mend_columns(par, old, state, spin_ref, edge, (a, b), (col_a, col_b), strips)
    gram = sum(gram_of(*split_halves(flat[cells, :])) for flat, cells in tiles_of(state))
    write_halves(par, gram, scale, kept, sent, total)


def split_halves(value):
    high = value.astype(jnp.bfloat16)
    return high, (value - high.astype(jnp.float32)).astype(jnp.bfloat16)


def gram_of(high, low):
    return lax.dot_general(
        high,
        jnp.concatenate([high, low], axis=1),
        (((0,), (0,)), ((), ())),
        preferred_element_type=jnp.float32,
    )


def write_halves(par, gram, scale, kept, sent, total):
    odd = par[1] % 2
    rows = LANES // 2
    mixed = gram[:, LANES:]
    total[...] = scale * (gram[:, :LANES] + (mixed + jnp.transpose(mixed)))
    kept[...] = total[pl.ds(odd * rows, rows), :]
    sent[...] = total[pl.ds((1 - odd) * rows, rows), :]


def invert_factor(gram_ref, work):
    count = LANES // SUB
    lane = lax.broadcasted_iota(jnp.int32, (SUB, LANES), 1)
    sub = lax.broadcasted_iota(jnp.int32, (SUB, LANES), 0)
    rows = [gram_ref[pl.ds(SUB * i, SUB), :] for i in range(count)]
    for block in range(count):
        base = SUB * block
        here = (lane >= base) & (lane < base + SUB)
        spread = [lane_spread(rows[block], base + l) for l in range(SUB)]
        low = [
            [jnp.broadcast_to(spread[l][k : k + 1, :], (SUB, LANES)) for l in range(k + 1)]
            for k in range(SUB)
        ]
        pivot = jnp.where(here, jnp.where(lane - base == sub, 1.0, 0.0), rows[block])
        inv, scaled = [], []
        for k in range(SUB):
            inv.append(lax.rsqrt(low[k][k]))
            for i in range(k + 1, SUB):
                low[i][k] = low[i][k] * inv[k]
            for i in range(k + 1, SUB):
                for m in range(k + 1, i + 1):
                    low[i][m] = low[i][m] - low[i][k] * low[m][k]
            line = jnp.broadcast_to(pivot[k : k + 1, :], (SUB, LANES))
            for l in range(k):
                line = line - low[k][l] * scaled[l]
            scaled.append(line * inv[k])
        merged = scaled[0]
        for k in range(1, SUB):
            merged = jnp.where(sub == k, scaled[k], merged)
        work[pl.ds(base, SUB), :] = merged
        for i in range(block + 1, count):
            weights = []
            rest = jnp.where(here, 0.0, rows[i])
            for l in range(SUB):
                weight = lane_spread(rows[i], base + l)
                for m in range(l):
                    weight = weight - weights[m] * low[l][m]
                weights.append(weight * inv[l])
            for l in range(SUB):
                rest = rest - weights[l] * scaled[l]
            rows[i] = rest


def factorize(par, mine_ref, other_ref, gram, work):
    rows = LANES // 2
    odd = par[1] % 2
    gram[pl.ds(odd * rows, rows), :] = mine_ref[...]
    gram[pl.ds((1 - odd) * rows, rows), :] = other_ref[...]
    invert_factor(gram, work)
    row = lax.broadcasted_iota(jnp.int32, (LANES, LANES), 0)
    col = lax.broadcasted_iota(jnp.int32, (LANES, LANES), 1)
    inverse = jnp.where(row >= col, work[...], 0.0)
    diagonal = jnp.sum(jnp.where(row == col, inverse, 0.0), axis=0, keepdims=True)
    return inverse, diagonal


def paired(inverse):
    high = inverse.astype(jnp.bfloat16)
    low = (inverse - high.astype(jnp.float32)).astype(jnp.bfloat16)
    return jnp.concatenate(
        [jnp.concatenate([high, high], axis=1), jnp.concatenate([low, low], axis=1)], axis=0
    )


def times_factor(cells, factor):
    pair = jnp.concatenate(split_halves(cells), axis=1)
    both = lax.dot_general(
        pair, factor, (((1,), (1,)), ((), ())), preferred_element_type=jnp.float32
    )
    return both[:, :LANES] + both[:, LANES:]


def factor_only(par, mine_ref, other_ref, prior_ref, inverse_ref, logs_ref, gram, work):
    inverse, diagonal = factorize(par, mine_ref, other_ref, gram, work)
    inverse_ref[...] = inverse
    logs_ref[...] = prior_ref[...] - jnp.log(diagonal)


def join_update(
    scale,
    par,
    old,
    state_in,
    edge,
    spin_ref,
    a,
    b,
    inverse_ref,
    state,
    out_ref,
    kept,
    sent,
    factor,
    total,
    *strips,
):
    factor[...] = paired(inverse_ref[...])
    mend_columns(par, old, state, spin_ref, edge, (a, b), None, strips)
    gram = 0.0
    for tile, (flat, cells) in enumerate(tiles_of(state)):
        new = times_factor(flat[cells, :], factor[...])
        out_ref[tile] = new
        gram += gram_of(*split_halves(new))
    write_halves(par, gram, scale, kept, sent, total)


def finish(par, mine_ref, other_ref, prior_ref, t_ref, out_ref, logs_ref, gram, work, factor, fresh, sems):
    inverse, diagonal = factorize(par, mine_ref, other_ref, gram, work)
    logs_ref[...] = prior_ref[...] - jnp.log(diagonal)
    factor[...] = paired(inverse)

    def out_copy(tile):
        return pltpu.make_async_copy(fresh.at[tile], out_ref.at[tile], sems.at[tile])

    for tile in range(TILES):
        fresh[tile] = times_factor(t_ref[tile], factor[...])
        out_copy(tile).start()

    for tile in range(TILES):
        out_copy(tile).wait()


def swap_pairs(near_value, far_value, axis, closed):
    count = lax.axis_size(axis)
    near = [(i, i ^ 1) for i in range(count)]
    far = [(i, (i + 1 if i % 2 else i - 1) % count) for i in range(count)]
    if not closed:
        far = far[1:-1]
    return lax.ppermute(near_value, axis, near), lax.ppermute(far_value, axis, far)


def swapped(value, axis, mask):
    return lax.ppermute(value, axis, [(i, i ^ mask) for i in range(lax.axis_size(axis))])


def sum_over(value, axis, first_bit):
    bits = lax.axis_size(axis).bit_length() - 1
    while first_bit < bits:
        low = 1 << first_bit
        if first_bit + 1 < bits:
            high = low << 1
            one, two, three = (swapped(value, axis, mask) for mask in (low, high, low | high))
            value = (value + one) + (two + three)
            first_bit += 2
        else:
            value = value + swapped(value, axis, low)
            first_bit += 1
    return value


def sum_devices(kept, sent):
    mine = kept + swapped(sent, "col", 1)
    mine = sum_over(mine, "col", 1)
    mine = sum_over(mine, "row", 0)
    return mine, swapped(mine, "col", 1)


def body(tangents, sea_mask, levels, current):
    comps, rows, cols, modes = tangents.shape
    total_rows = rows * lax.axis_size("row")
    total_cells = total_rows * cols * lax.axis_size("col")
    scale = 1.0 / total_cells
    row_at, col_at = lax.axis_index("row"), lax.axis_index("col")
    par = jnp.stack([row_at, col_at]).astype(jnp.int32)

    tall = rows + 2 * HALO
    lat = (row_at * rows - HALO + jnp.arange(tall)).astype(jnp.float32)
    angle = (-70.0 + 140.0 * (lat + 0.5) / total_rows) * (jnp.pi / 180.0)
    spin = jnp.broadcast_to((rotation * jnp.sin(angle))[:, None], (tall, LANES))

    height = comps * rows * cols // TILES
    block = shape_of(comps, tall, cols, modes)
    columns = (shape_of(comps * SIDE * tall, modes),) * 2
    first_columns = (shape_of(comps * SIDE * tall + SUB, modes),) * 2
    edges = shape_of(2, FIELDS, STRIP - 2, tall, LANES)
    strips = [
        pltpu.VMEM((2, comps, columns_of, tall + 2 * SUB, modes), jnp.float32)
        for columns_of in (STRIP, STRIP - 2)
    ]
    rows_sent = (shape_of(comps * HALO + 1, cols, modes),) * 2
    halves = (shape_of(modes // 2, modes),) * 2
    tiled = shape_of(TILES, height, modes)
    square = pltpu.VMEM((modes, modes), jnp.float32)
    factor = pltpu.VMEM((2 * modes, 2 * modes), jnp.bfloat16)

    def call(kernel, outs, *operands, specs=None, out_specs=None, scratch=(), aliases=None):
        return pl.pallas_call(
            kernel,
            out_shape=outs,
            in_specs=specs or [SMEM] + [VMEM] * (len(operands) - 1),
            out_specs=out_specs or (VMEM,) * len(outs),
            scratch_shapes=scratch,
            input_output_aliases=aliases or {},
            compiler_params=params(),
        )(*operands)

    def inside(step, state):
        kernel = functools.partial(apply_inside, step)
        return call(kernel, (block,), state, coef, spin, specs=[VMEM] * 3)[0]

    def swap_columns(packed):
        return swap_pairs(*packed, "col", True)

    source, *fields = (
        pltpu.with_memory_space_constraint(x, pltpu.HBM)
        for x in (tangents, sea_mask.T, levels.T, current.T)
    )
    upright = [pltpu.VMEM(x.shape, x.dtype) for x in fields]
    packed = call(
        pack_rows,
        rows_sent,
        par,
        source,
        *fields,
        specs=[SMEM] + [HBM] * 4,
        scratch=upright
        + [
            pltpu.VMEM((cols, LANES), jnp.float32),
            pltpu.SemaphoreType.DMA((2 * comps,)),
            pltpu.SemaphoreType.DMA((FIELDS,)),
        ],
    )
    row_halos = swap_pairs(*packed, "row", False)
    coef, wide = call(
        spread_fields,
        (shape_of(FIELDS, tall, cols, LANES), shape_of(FIELDS, cols, LANES)),
        *fields,
        specs=[HBM] * 3,
        scratch=upright + [pltpu.SemaphoreType.DMA((FIELDS,))],
    )
    start, coef, *packed = call(
        join_rows,
        (block, shape_of(FIELDS, tall, cols, LANES)) + first_columns,
        par,
        tangents,
        coef,
        wide,
        *row_halos,
        scratch=[pltpu.SemaphoreType.DMA((comps,))],
        aliases={2: 1},
    )
    logs = jnp.zeros((1, modes), jnp.float32)

    halos = swap_columns(packed)
    state = inside(1, inside(0, start))
    start, edge, *packed, kept, sent = call(
        functools.partial(join_gram, scale),
        (block, edges) + columns + halves,
        par,
        start,
        state,
        coef,
        spin,
        *halos,
        scratch=[square] + strips,
        aliases={2: 0},
    )
    halos = swap_columns(packed)
    mine, other = sum_devices(kept, sent)
    state = inside(3, inside(2, start))
    inverse, logs = call(
        factor_only,
        (shape_of(modes, modes), shape_of(1, modes)),
        par,
        mine,
        other,
        logs,
        scratch=[square, square],
    )
    _, state, kept, sent = call(
        functools.partial(join_update, scale),
        (block, tiled) + halves,
        par,
        start,
        state,
        edge,
        spin,
        *halos,
        inverse,
        scratch=[factor, square] + strips,
        aliases={2: 0},
    )
    mine, other = sum_devices(kept, sent)
    out, logs = call(
        finish,
        (tiled, shape_of(1, modes)),
        par,
        mine,
        other,
        logs,
        state,
        out_specs=(HBM, VMEM),
        scratch=[
            square,
            square,
            factor,
            pltpu.VMEM((TILES, height, modes), jnp.float32),
            pltpu.SemaphoreType.DMA((TILES,)),
        ],
    )
    return out.reshape(tangents.shape), logs.reshape(modes)


def solution(mesh):
    placed = (P(None, "row", "col", None), P("row", "col"), P("row", "col"), P("row", "col"))
    return jax.shard_map(
        body,
        mesh=mesh,
        in_specs=placed,
        out_specs=(P(None, "row", "col", None), P()),
        check_vma=False,
    )
```

```python
import functools

import jax
import jax.numpy as jnp
from jax import lax
from jax.experimental import pallas as pl
from jax.experimental.pallas import tpu as pltpu
from jax.sharding import PartitionSpec as P

STEPS = 2
RENORMS = 2
LEVELS = 50

viscosity = 0.15
gravity = 0.5
rotation = 0.4

SUB = 8
LANES = 128
FIELDS = 3
HALO = STEPS * RENORMS
SIDE = STEPS
STRIP = 2 * STEPS + 2
TILES = 12
VMEM_LIMIT = 16 * 1024 * 1024

HBM = pl.BlockSpec(memory_space=pltpu.HBM)
VMEM = pl.BlockSpec(memory_space=pltpu.VMEM)
SMEM = pl.BlockSpec(memory_space=pltpu.SMEM)


def params():
    return pltpu.CompilerParams(vmem_limit_bytes=VMEM_LIMIT)


def shape_of(*dims):
    return jax.ShapeDtypeStruct(dims, jnp.float32)


def lane_spread(block, lane):
    return jnp.broadcast_to(block[:, lane : lane + 1], (block.shape[0], LANES))


def fetch(sources, places, sems):
    copies = [
        pltpu.make_async_copy(source, place, sems.at[i])
        for i, (source, place) in enumerate(zip(sources, places))
    ]
    for copy in copies:
        copy.start()
    return copies


def finish_all(copies):
    for copy in copies:
        copy.wait()


def fields_of(sea_ref, levels_ref, current_ref):
    return (
        sea_ref[...].astype(jnp.float32),
        0.5 * current_ref[...],
        0.5 * ((levels_ref[...] + 1).astype(jnp.float32) / LEVELS),
    )


def sides_of(par):
    odd_row, odd_col = par[0] % 2, par[1] % 2
    return (1 - odd_row, odd_row), (1 - odd_col, odd_col)


def pack_rows(
    par, t_ref, sea_ref, levels_ref, current_ref, row_a, row_b, sea, levels, current, wide, sems, field_sems
):
    comps, rows, cols, _ = t_ref.shape
    norths, _ = sides_of(par)
    field_copies = fetch((sea_ref, levels_ref, current_ref), (sea, levels, current), field_sems)
    slots = [(slot, msg, comp) for slot, msg in ((0, row_a), (1, row_b)) for comp in range(comps)]
    copies = fetch(
        [t_ref.at[comp, pl.ds(norths[slot] * (rows - HALO), HALO)] for slot, _, comp in slots],
        [msg.at[pl.ds(comp * HALO, HALO)] for _, msg, comp in slots],
        sems,
    )
    lane = lax.broadcasted_iota(jnp.int32, (cols, LANES), 1)
    wide[...] = jnp.zeros_like(wide)
    packed = [jnp.zeros((cols, LANES), jnp.float32)] * 2
    finish_all(field_copies)
    for field, value in enumerate(fields_of(sea, levels, current)):
        wide[:, pl.ds(0, rows)] = value
        whole = wide[...]
        for north in (0, 1):
            shift = (field * SUB - north * (rows - HALO)) % LANES
            moved = pltpu.roll(whole, shift, 1) if shift else whole
            here = (lane >= field * SUB) & (lane < field * SUB + HALO)
            packed[north] = jnp.where(here, moved, packed[north])
    for slot, msg in ((0, row_a), (1, row_b)):
        msg[comps * HALO] = jnp.where(norths[slot] == 1, packed[1], packed[0])
    finish_all(copies)


def spread_fields(
    total_rows, par, sea_ref, levels_ref, current_ref, coef, wide, spin, sea, levels, current, sems
):
    rows = sea_ref.shape[1]
    copies = fetch((sea_ref, levels_ref, current_ref), (sea, levels, current), sems)
    line = lax.broadcasted_iota(jnp.int32, spin.shape, 0)
    latitude = (par[0] * rows - HALO + line).astype(jnp.float32)
    angle = (-70.0 + 140.0 * (latitude + 0.5) / total_rows) * (jnp.pi / 180.0)
    spin[...] = rotation * jnp.sin(angle)
    finish_all(copies)
    wide[...] = jnp.zeros_like(wide)
    for field, value in enumerate(fields_of(sea, levels, current)):
        wide[field, :, pl.ds(0, rows)] = value
        for row in range(rows):
            coef[field, HALO + row] = lane_spread(value, row)


def column_at(east, cols, depth):
    return depth + east * (cols - 1 - 2 * depth)


def join_rows(par, t_ref, coef_in, wide, row_a, row_b, state, coef, col_a, col_b, sems):
    comps, tall, cols, _ = state.shape
    rows = tall - 2 * HALO
    norths, easts = sides_of(par)
    copies = fetch(
        [t_ref.at[comp] for comp in range(comps)],
        [state.at[comp, pl.ds(HALO, rows)] for comp in range(comps)],
        sems,
    )
    for slot, msg in ((0, row_a), (1, row_b)):
        line = norths[slot] * (tall - HALO)
        fields = msg[comps * HALO]
        for h in range(HALO):
            for comp in range(comps):
                state[comp, line + h] = msg[comp * HALO + h]
            for field in range(FIELDS):
                coef[field, line + h] = lane_spread(fields, field * SUB + h)
    tail = comps * SIDE * tall
    for slot, msg in ((0, col_a), (1, col_b)):
        lon = column_at(easts[slot], cols, 0)
        msg[pl.ds(tail, SUB), :] = jnp.zeros((SUB, LANES), jnp.float32)
        for field in range(FIELDS):
            msg[pl.ds(tail + field, 1), :] = wide[field, pl.ds(lon, 1), :]
        for i, got in enumerate((row_a, row_b)):
            msg[pl.ds(tail + FIELDS + i, 1), :] = got[comps * HALO, pl.ds(lon, 1), :]
    finish_all(copies)
    flat = state.reshape(comps * tall * cols, LANES)
    for slot, msg in ((0, col_a), (1, col_b)):
        for comp in range(comps):
            for j in range(SIDE):
                for row in range(0, tall, SUB):
                    at = (comp * tall + row) * cols + column_at(easts[slot], cols, j)
                    msg[pl.ds((comp * SIDE + j) * tall + row, SUB), :] = flat[
                        pl.ds(at, SUB, stride=cols), :
                    ]


def model(own, x_diff, x_sum, above, below, sea, flow, depth, spin):
    keep, half = 1.0 - 4.0 * viscosity, 0.5 * gravity
    mixed = [
        keep * c + viscosity * (x + (n + s)) - flow * d
        for c, d, x, n, s in zip(own, x_diff, x_sum, above, below)
    ]
    v_y, h_y = above[1] - below[1], above[2] - below[2]
    return (
        sea * (mixed[0] - half * x_diff[2] + spin * own[1]),
        sea * (mixed[1] - half * h_y - spin * own[0]),
        sea * (mixed[2] - depth * (x_diff[0] + v_y)),
    )


def apply_inside(step, t_ref, coef_ref, spin_ref, out_ref):
    comps, tall, cols, _ = t_ref.shape
    flat = t_ref.reshape(comps * tall * cols, LANES)
    sub = lax.broadcasted_iota(jnp.int32, (SUB, LANES), 0)
    first, last = step + 1, tall - step - 1

    def line_of(line):
        spin = jnp.broadcast_to(spin_ref[pl.ds(line, 1), :], (SUB, LANES))
        for lon in range(0, cols, SUB):
            at = [(comp * tall + line) * cols + lon for comp in range(comps)]
            cells = pl.ds(lon, SUB)
            sea, flow, depth = (coef_ref[field, line, cells, :] for field in range(FIELDS))
            own = [t_ref[comp, line, cells, :] for comp in range(comps)]
            if lon == 0:
                west = [jnp.where(sub == 0, 0.0, pltpu.roll(x, 1, 0)) for x in own]
            else:
                west = [flat[pl.ds(a - 1, SUB), :] for a in at]
            if lon == cols - SUB:
                east = [jnp.where(sub == SUB - 1, 0.0, pltpu.roll(x, SUB - 1, 0)) for x in own]
            else:
                east = [flat[pl.ds(a + 1, SUB), :] for a in at]
            above = [t_ref[comp, line + 1, cells, :] for comp in range(comps)]
            below = [t_ref[comp, line - 1, cells, :] for comp in range(comps)]
            x_diff = [e - w for e, w in zip(east, west)]
            x_sum = [e + w for e, w in zip(east, west)]
            new = model(own, x_diff, x_sum, above, below, sea, flow, depth, spin)
            for comp in range(comps):
                out_ref[comp, line, cells, :] = new[comp]

    @pl.loop(0, (last - first) // 2)
    def _(pair):
        line_of(first + 2 * pair)
        line_of(first + 1 + 2 * pair)


def fill_edge(par, coef_ref, cols_got, edge):
    _, tall, cols, _ = coef_ref.shape
    rows = tall - 2 * HALO
    norths, easts = sides_of(par)
    flat = coef_ref.reshape(FIELDS * tall * cols, LANES)
    for slot, msg in enumerate(cols_got):
        upright = jnp.transpose(msg[pl.ds(msg.shape[0] - SUB, SUB), :])
        for field in range(FIELDS):
            edge[slot, field, 0, pl.ds(HALO, rows), :] = lane_spread(upright[:rows], field)
            for i in (0, 1):
                beyond = lane_spread(upright[field * SUB : (field + 1) * SUB], FIELDS + i)
                line = norths[i] * (tall - HALO)
                edge[slot, field, 0, pl.ds(line, HALO), :] = beyond[:HALO]
            for depth in range(STRIP - 3):
                lon = column_at(easts[slot], cols, depth)
                for row in range(0, tall, SUB):
                    at = (field * tall + row) * cols + lon
                    edge[slot, field, 1 + depth, pl.ds(row, SUB), :] = flat[
                        pl.ds(at, SUB, stride=cols), :
                    ]


def mend_columns(par, old, state, spin_ref, edge, cols_got, sent, strips):
    comps, tall, cols, _ = state.shape
    _, easts = sides_of(par)
    flat_old = old.reshape(comps * tall * cols, LANES)
    flat = state.reshape(comps * tall * cols, LANES)
    signs = [(1 - 2 * east).astype(jnp.float32) for east in easts]
    first, second = strips

    def neighbours(strip, slot, column, row):
        def load(comp, shift, lat):
            return strip[slot, comp, column + shift, pl.ds(SUB + row + lat, SUB), :]

        inner, outer = ([load(comp, shift, 0) for comp in range(comps)] for shift in (1, -1))
        return (
            [load(comp, 0, 0) for comp in range(comps)],
            [signs[slot] * (i - o) for i, o in zip(inner, outer)],
            [i + o for i, o in zip(inner, outer)],
            [load(comp, 0, 1) for comp in range(comps)],
            [load(comp, 0, -1) for comp in range(comps)],
        )

    def coefs(slot, column, row):
        return [edge[slot, field, column, pl.ds(row, SUB), :] for field in range(FIELDS)]

    @pl.loop(0, tall // SUB)
    def _(group):
        row = pl.multiple_of(group * SUB, SUB)
        for slot, got in enumerate(cols_got):
            for comp in range(comps):
                for j in range(SIDE):
                    first[slot, comp, SIDE - 1 - j, pl.ds(SUB + row, SUB), :] = got[
                        pl.ds((comp * SIDE + j) * tall + row, SUB), :
                    ]
                for depth in range(STRIP - SIDE):
                    at = (comp * tall + row) * cols + column_at(easts[slot], cols, depth)
                    first[slot, comp, SIDE + depth, pl.ds(SUB + row, SUB), :] = flat_old[
                        pl.ds(at, SUB, stride=cols), :
                    ]

    @pl.loop(0, tall // SUB)
    def _(group):
        row = pl.multiple_of(group * SUB, SUB)
        spin = spin_ref[pl.ds(row, SUB), :]
        for slot in (0, 1):
            for column in range(STRIP - 2):
                new = model(
                    *neighbours(first, slot, column + 1, row), *coefs(slot, column, row), spin
                )
                for comp in range(comps):
                    second[slot, comp, column, pl.ds(SUB + row, SUB), :] = new[comp]

    @pl.loop(0, tall // SUB)
    def _(group):
        row = pl.multiple_of(group * SUB, SUB)
        spin = spin_ref[pl.ds(row, SUB), :]
        for slot in (0, 1):
            for j in range(SIDE):
                new = model(
                    *neighbours(second, slot, j + 1, row), *coefs(slot, j + 1, row), spin
                )
                for comp in range(comps):
                    at = (comp * tall + row) * cols + column_at(easts[slot], cols, j)
                    flat[pl.ds(at, SUB, stride=cols), :] = new[comp]
                    if sent is not None:
                        sent[slot][pl.ds((comp * SIDE + j) * tall + row, SUB), :] = new[comp]


def tiles_of(state):
    comps, tall, cols, _ = state.shape
    flat = state.reshape(comps * tall * cols, LANES)
    parts = TILES // comps
    height = (tall - 2 * HALO) * cols // parts
    for tile in range(TILES):
        start = ((tile // parts) * tall + HALO) * cols + (tile % parts) * height
        yield flat, pl.ds(start, height)


def join_gram(
    scale, par, old, state_in, coef_ref, spin_ref, a, b, state, edge, col_a, col_b, kept, sent, total, *strips
):
    fill_edge(par, coef_ref, (a, b), edge)
    mend_columns(par, old, state, spin_ref, edge, (a, b), (col_a, col_b), strips)
    gram = sum(gram_of(*split_halves(flat[cells, :])) for flat, cells in tiles_of(state))
    write_halves(par, gram, scale, kept, sent, total)


def split_halves(value):
    high = value.astype(jnp.bfloat16)
    return high, (value - high.astype(jnp.float32)).astype(jnp.bfloat16)


def gram_of(high, low):
    return lax.dot_general(
        high,
        jnp.concatenate([high, low], axis=1),
        (((0,), (0,)), ((), ())),
        preferred_element_type=jnp.float32,
    )


def write_halves(par, gram, scale, kept, sent, total):
    odd = par[1] % 2
    rows = LANES // 2
    mixed = gram[:, LANES:]
    total[...] = scale * (gram[:, :LANES] + (mixed + jnp.transpose(mixed)))
    kept[...] = total[pl.ds(odd * rows, rows), :]
    sent[...] = total[pl.ds((1 - odd) * rows, rows), :]


def invert_factor(gram_ref, work):
    count = LANES // SUB
    lane = lax.broadcasted_iota(jnp.int32, (SUB, LANES), 1)
    sub = lax.broadcasted_iota(jnp.int32, (SUB, LANES), 0)
    rows = [gram_ref[pl.ds(SUB * i, SUB), :] for i in range(count)]
    for block in range(count):
        base = SUB * block
        here = (lane >= base) & (lane < base + SUB)
        spread = [lane_spread(rows[block], base + l) for l in range(SUB)]
        low = [
            [jnp.broadcast_to(spread[l][k : k + 1, :], (SUB, LANES)) for l in range(k + 1)]
            for k in range(SUB)
        ]
        pivot = jnp.where(here, jnp.where(lane - base == sub, 1.0, 0.0), rows[block])
        inv, scaled = [], []
        for k in range(SUB):
            inv.append(lax.rsqrt(low[k][k]))
            for i in range(k + 1, SUB):
                low[i][k] = low[i][k] * inv[k]
            for i in range(k + 1, SUB):
                for m in range(k + 1, i + 1):
                    low[i][m] = low[i][m] - low[i][k] * low[m][k]
            line = jnp.broadcast_to(pivot[k : k + 1, :], (SUB, LANES))
            for l in range(k):
                line = line - low[k][l] * scaled[l]
            scaled.append(line * inv[k])
        merged = scaled[0]
        for k in range(1, SUB):
            merged = jnp.where(sub == k, scaled[k], merged)
        work[pl.ds(base, SUB), :] = merged
        for i in range(block + 1, count):
            weights = []
            rest = jnp.where(here, 0.0, rows[i])
            for l in range(SUB):
                weight = lane_spread(rows[i], base + l)
                for m in range(l):
                    weight = weight - weights[m] * low[l][m]
                weights.append(weight * inv[l])
            for l in range(SUB):
                rest = rest - weights[l] * scaled[l]
            rows[i] = rest


def factorize(par, mine_ref, other_ref, gram, work):
    rows = LANES // 2
    odd = par[1] % 2
    gram[pl.ds(odd * rows, rows), :] = mine_ref[...]
    gram[pl.ds((1 - odd) * rows, rows), :] = other_ref[...]
    invert_factor(gram, work)
    row = lax.broadcasted_iota(jnp.int32, (LANES, LANES), 0)
    col = lax.broadcasted_iota(jnp.int32, (LANES, LANES), 1)
    inverse = jnp.where(row >= col, work[...], 0.0)
    diagonal = jnp.sum(jnp.where(row == col, inverse, 0.0), axis=0, keepdims=True)
    return inverse, diagonal


def paired(inverse):
    high = inverse.astype(jnp.bfloat16)
    low = (inverse - high.astype(jnp.float32)).astype(jnp.bfloat16)
    return jnp.concatenate(
        [jnp.concatenate([high, high], axis=1), jnp.concatenate([low, low], axis=1)], axis=0
    )


def times_factor(cells, factor):
    pair = jnp.concatenate(split_halves(cells), axis=1)
    both = lax.dot_general(
        pair, factor, (((1,), (1,)), ((), ())), preferred_element_type=jnp.float32
    )
    return both[:, :LANES] + both[:, LANES:]


def factor_only(par, mine_ref, other_ref, prior_ref, inverse_ref, logs_ref, gram, work):
    inverse, diagonal = factorize(par, mine_ref, other_ref, gram, work)
    inverse_ref[...] = inverse
    logs_ref[...] = prior_ref[...] - jnp.log(diagonal)


def join_update(
    scale,
    par,
    old,
    state_in,
    edge,
    spin_ref,
    a,
    b,
    inverse_ref,
    state,
    out_ref,
    kept,
    sent,
    factor,
    total,
    *strips,
):
    factor[...] = paired(inverse_ref[...])
    mend_columns(par, old, state, spin_ref, edge, (a, b), None, strips)
    gram = 0.0
    for tile, (flat, cells) in enumerate(tiles_of(state)):
        new = times_factor(flat[cells, :], factor[...])
        out_ref[tile] = new
        gram += gram_of(*split_halves(new))
    write_halves(par, gram, scale, kept, sent, total)


def finish(par, mine_ref, other_ref, prior_ref, t_ref, out_ref, logs_ref, gram, work, factor, fresh, sems):
    inverse, diagonal = factorize(par, mine_ref, other_ref, gram, work)
    logs_ref[...] = prior_ref[...] - jnp.log(diagonal)
    factor[...] = paired(inverse)

    def out_copy(tile):
        return pltpu.make_async_copy(fresh.at[tile], out_ref.at[tile], sems.at[tile])

    for tile in range(TILES):
        fresh[tile] = times_factor(t_ref[tile], factor[...])
        out_copy(tile).start()

    for tile in range(TILES):
        out_copy(tile).wait()


def swap_pairs(near_value, far_value, axis, closed):
    count = lax.axis_size(axis)
    near = [(i, i ^ 1) for i in range(count)]
    far = [(i, (i + 1 if i % 2 else i - 1) % count) for i in range(count)]
    if not closed:
        far = far[1:-1]
    return lax.ppermute(near_value, axis, near), lax.ppermute(far_value, axis, far)


def swapped(value, axis, mask):
    return lax.ppermute(value, axis, [(i, i ^ mask) for i in range(lax.axis_size(axis))])


def sum_over(value, axis, first_bit):
    bits = lax.axis_size(axis).bit_length() - 1
    while first_bit < bits:
        low = 1 << first_bit
        if first_bit + 1 < bits:
            high = low << 1
            one, two, three = (swapped(value, axis, mask) for mask in (low, high, low | high))
            value = (value + one) + (two + three)
            first_bit += 2
        else:
            value = value + swapped(value, axis, low)
            first_bit += 1
    return value


def sum_devices(kept, sent):
    mine = kept + swapped(sent, "col", 1)
    mine = sum_over(mine, "col", 1)
    mine = sum_over(mine, "row", 0)
    return mine, swapped(mine, "col", 1)


def body(tangents, sea_mask, levels, current):
    comps, rows, cols, modes = tangents.shape
    total_rows = rows * lax.axis_size("row")
    total_cells = total_rows * cols * lax.axis_size("col")
    scale = 1.0 / total_cells
    row_at, col_at = lax.axis_index("row"), lax.axis_index("col")
    par = jnp.stack([row_at, col_at]).astype(jnp.int32)

    tall = rows + 2 * HALO
    height = comps * rows * cols // TILES
    block = shape_of(comps, tall, cols, modes)
    columns = (shape_of(comps * SIDE * tall, modes),) * 2
    first_columns = (shape_of(comps * SIDE * tall + SUB, modes),) * 2
    edges = shape_of(2, FIELDS, STRIP - 2, tall, LANES)
    strips = [
        pltpu.VMEM((2, comps, columns_of, tall + 2 * SUB, modes), jnp.float32)
        for columns_of in (STRIP, STRIP - 2)
    ]
    rows_sent = (shape_of(comps * HALO + 1, cols, modes),) * 2
    halves = (shape_of(modes // 2, modes),) * 2
    tiled = shape_of(TILES, height, modes)
    square = pltpu.VMEM((modes, modes), jnp.float32)
    factor = pltpu.VMEM((2 * modes, 2 * modes), jnp.bfloat16)

    def call(kernel, outs, *operands, specs=None, out_specs=None, scratch=(), aliases=None):
        return pl.pallas_call(
            kernel,
            out_shape=outs,
            in_specs=specs or [SMEM] + [VMEM] * (len(operands) - 1),
            out_specs=out_specs or (VMEM,) * len(outs),
            scratch_shapes=scratch,
            input_output_aliases=aliases or {},
            compiler_params=params(),
        )(*operands)

    def inside(step, state):
        kernel = functools.partial(apply_inside, step)
        return call(kernel, (block,), state, coef, spin, specs=[VMEM] * 3)[0]

    def swap_columns(packed):
        return swap_pairs(*packed, "col", True)

    source, *fields = (
        pltpu.with_memory_space_constraint(x, pltpu.HBM)
        for x in (tangents, sea_mask.T, levels.T, current.T)
    )
    upright = [pltpu.VMEM(x.shape, x.dtype) for x in fields]
    packed = call(
        pack_rows,
        rows_sent,
        par,
        source,
        *fields,
        specs=[SMEM] + [HBM] * 4,
        scratch=upright
        + [
            pltpu.VMEM((cols, LANES), jnp.float32),
            pltpu.SemaphoreType.DMA((2 * comps,)),
            pltpu.SemaphoreType.DMA((FIELDS,)),
        ],
    )
    row_halos = swap_pairs(*packed, "row", False)
    coef, wide, spin = call(
        functools.partial(spread_fields, total_rows),
        (
            shape_of(FIELDS, tall, cols, LANES),
            shape_of(FIELDS, cols, LANES),
            shape_of(tall, LANES),
        ),
        par,
        *fields,
        specs=[SMEM] + [HBM] * 3,
        scratch=upright + [pltpu.SemaphoreType.DMA((FIELDS,))],
    )
    start, coef, *packed = call(
        join_rows,
        (block, shape_of(FIELDS, tall, cols, LANES)) + first_columns,
        par,
        tangents,
        coef,
        wide,
        *row_halos,
        scratch=[pltpu.SemaphoreType.DMA((comps,))],
        aliases={2: 1},
    )
    logs = jnp.zeros((1, modes), jnp.float32)

    halos = swap_columns(packed)
    state = inside(1, inside(0, start))
    start, edge, *packed, kept, sent = call(
        functools.partial(join_gram, scale),
        (block, edges) + columns + halves,
        par,
        start,
        state,
        coef,
        spin,
        *halos,
        scratch=[square] + strips,
        aliases={2: 0},
    )
    halos = swap_columns(packed)
    mine, other = sum_devices(kept, sent)
    state = inside(3, inside(2, start))
    inverse, logs = call(
        factor_only,
        (shape_of(modes, modes), shape_of(1, modes)),
        par,
        mine,
        other,
        logs,
        scratch=[square, square],
    )
    _, state, kept, sent = call(
        functools.partial(join_update, scale),
        (block, tiled) + halves,
        par,
        start,
        state,
        edge,
        spin,
        *halos,
        inverse,
        scratch=[factor, square] + strips,
        aliases={2: 0},
    )
    mine, other = sum_devices(kept, sent)
    out, logs = call(
        finish,
        (tiled, shape_of(1, modes)),
        par,
        mine,
        other,
        logs,
        state,
        out_specs=(HBM, VMEM),
        scratch=[
            square,
            square,
            factor,
            pltpu.VMEM((TILES, height, modes), jnp.float32),
            pltpu.SemaphoreType.DMA((TILES,)),
        ],
    )
    return out.reshape(tangents.shape), logs.reshape(modes)


def solution(mesh):
    placed = (P(None, "row", "col", None), P("row", "col"), P("row", "col"), P("row", "col"))
    return jax.shard_map(
        body,
        mesh=mesh,
        in_specs=placed,
        out_specs=(P(None, "row", "col", None), P()),
        check_vma=False,
    )
```

```python
import functools

import jax
import jax.numpy as jnp
from jax import lax
from jax.experimental import pallas as pl
from jax.experimental.pallas import tpu as pltpu
from jax.sharding import PartitionSpec as P

STEPS = 2
RENORMS = 2
LEVELS = 50

viscosity = 0.15
gravity = 0.5
rotation = 0.4

SUB = 8
LANES = 128
FIELDS = 3
HALO = STEPS * RENORMS
SIDE = STEPS
TILES = 12
VMEM_LIMIT = 16 * 1024 * 1024

HBM = pl.BlockSpec(memory_space=pltpu.HBM)
VMEM = pl.BlockSpec(memory_space=pltpu.VMEM)
SMEM = pl.BlockSpec(memory_space=pltpu.SMEM)


def params():
    return pltpu.CompilerParams(vmem_limit_bytes=VMEM_LIMIT)


def shape_of(*dims):
    return jax.ShapeDtypeStruct(dims, jnp.float32)


def lane_spread(block, lane):
    return jnp.broadcast_to(block[:, lane : lane + 1], (block.shape[0], LANES))


def fetch(sources, places, sems):
    copies = [
        pltpu.make_async_copy(source, place, sems.at[i])
        for i, (source, place) in enumerate(zip(sources, places))
    ]
    for copy in copies:
        copy.start()
    return copies


def finish_all(copies):
    for copy in copies:
        copy.wait()


def fields_of(sea_ref, levels_ref, current_ref):
    return (
        sea_ref[...].astype(jnp.float32),
        0.5 * current_ref[...],
        0.5 * ((levels_ref[...] + 1).astype(jnp.float32) / LEVELS),
    )


def sides_of(par):
    odd_row, odd_col = par[0] % 2, par[1] % 2
    return (1 - odd_row, odd_row), (1 - odd_col, odd_col)


def pack_rows(
    par, t_ref, sea_ref, levels_ref, current_ref, row_a, row_b, sea, levels, current, wide, sems, field_sems
):
    comps, rows, cols, _ = t_ref.shape
    norths, _ = sides_of(par)
    field_copies = fetch((sea_ref, levels_ref, current_ref), (sea, levels, current), field_sems)
    slots = [(slot, msg, comp) for slot, msg in ((0, row_a), (1, row_b)) for comp in range(comps)]
    copies = fetch(
        [t_ref.at[comp, pl.ds(norths[slot] * (rows - HALO), HALO)] for slot, _, comp in slots],
        [msg.at[pl.ds(comp * HALO, HALO)] for _, msg, comp in slots],
        sems,
    )
    lane = lax.broadcasted_iota(jnp.int32, (cols, LANES), 1)
    wide[...] = jnp.zeros_like(wide)
    packed = [jnp.zeros((cols, LANES), jnp.float32)] * 2
    finish_all(field_copies)
    for field, value in enumerate(fields_of(sea, levels, current)):
        wide[:, pl.ds(0, rows)] = value
        whole = wide[...]
        for north in (0, 1):
            shift = (field * SUB - north * (rows - HALO)) % LANES
            moved = pltpu.roll(whole, shift, 1) if shift else whole
            here = (lane >= field * SUB) & (lane < field * SUB + HALO)
            packed[north] = jnp.where(here, moved, packed[north])
    for slot, msg in ((0, row_a), (1, row_b)):
        msg[comps * HALO] = jnp.where(norths[slot] == 1, packed[1], packed[0])
    finish_all(copies)


def spread_fields(
    total_rows, par, t_ref, sea_ref, levels_ref, current_ref, state, coef, wide, spin, sea, levels, current, sems, field_sems
):
    comps, rows, cols, _ = t_ref.shape
    field_copies = fetch((sea_ref, levels_ref, current_ref), (sea, levels, current), field_sems)
    cells = [(comp, lon) for comp in range(comps) for lon in range(cols)]
    copies = fetch(
        [t_ref.at[comp, :, lon] for comp, lon in cells],
        [state.at[comp, SIDE + lon, pl.ds(0, rows)] for comp, lon in cells],
        sems,
    )
    line = lax.broadcasted_iota(jnp.int32, spin.shape, 0)
    line = jnp.where(line < rows + HALO, line, line - (rows + 2 * HALO))
    latitude = (par[0] * rows + line).astype(jnp.float32)
    angle = (-70.0 + 140.0 * (latitude + 0.5) / total_rows) * (jnp.pi / 180.0)
    spin[...] = rotation * jnp.sin(angle)
    wide[...] = jnp.zeros_like(wide)
    finish_all(field_copies)
    for field, value in enumerate(fields_of(sea, levels, current)):
        wide[field, :, pl.ds(0, rows)] = value
        natural = jnp.transpose(wide[field])[:rows]
        for lon in range(cols):
            coef[field, SIDE + lon, pl.ds(0, rows), :] = lane_spread(natural, lon)
    finish_all(copies)


def column_at(east, cols, depth):
    return SIDE + depth + east * (cols - 1 - 2 * depth)


def send_columns(par, state, cols_sent):
    comps, wide, tall, _ = state.shape
    _, easts = sides_of(par)
    for slot, msg in enumerate(cols_sent):
        for comp in range(comps):
            for j in range(SIDE):
                column = column_at(easts[slot], wide - 2 * SIDE, j)
                msg[pl.ds((comp * SIDE + j) * tall, tall), :] = state[comp, column]


def join_rows(par, state_in, coef_in, wide, row_a, row_b, state, coef, col_a, col_b):
    comps, length, tall, _ = state.shape
    cols, rows = length - 2 * SIDE, tall - 2 * HALO
    norths, easts = sides_of(par)
    flat = state.reshape(comps * length * tall, LANES)
    for slot, msg in ((0, row_a), (1, row_b)):
        line = rows + HALO * (1 - norths[slot])
        for comp in range(comps):
            for h in range(HALO):
                for lon in range(0, cols, SUB):
                    at = (comp * length + SIDE + lon) * tall + line + h
                    flat[pl.ds(at, SUB, stride=tall), :] = msg[comp * HALO + h, pl.ds(lon, SUB), :]
    lane = lax.broadcasted_iota(jnp.int32, (cols, LANES), 1)
    north = jnp.where(norths[0] == 1, row_a[comps * HALO], row_b[comps * HALO])
    south = jnp.where(norths[0] == 1, row_b[comps * HALO], row_a[comps * HALO])
    beyond = jnp.where(lane % SUB < HALO, north, pltpu.roll(south, HALO, 1))
    natural = jnp.transpose(beyond)
    for field in range(FIELDS):
        block = natural[field * SUB : (field + 1) * SUB]
        for lon in range(cols):
            coef[field, SIDE + lon, pl.ds(rows, SUB), :] = lane_spread(block, lon)
    tail = comps * SIDE * tall
    whole = [
        jnp.where(lane < rows, wide[field], pltpu.roll(beyond, rows - field * SUB, 1))
        for field in range(FIELDS)
    ]
    for slot, msg in ((0, col_a), (1, col_b)):
        msg[pl.ds(tail, SUB), :] = jnp.zeros((SUB, LANES), jnp.float32)
        for field in range(FIELDS):
            msg[pl.ds(tail + field, 1), :] = jnp.where(
                easts[slot] == 1, whole[field][cols - 1 :], whole[field][:1]
            )
    send_columns(par, state, (col_a, col_b))


def model(own, x_diff, x_sum, above, below, sea, flow, depth, spin):
    keep, half = 1.0 - 4.0 * viscosity, 0.5 * gravity
    mixed = [
        keep * c + viscosity * (x + (n + s)) - flow * d
        for c, d, x, n, s in zip(own, x_diff, x_sum, above, below)
    ]
    v_y, h_y = above[1] - below[1], above[2] - below[2]
    return (
        sea * (mixed[0] - half * x_diff[2] + spin * own[1]),
        sea * (mixed[1] - half * h_y - spin * own[0]),
        sea * (mixed[2] - depth * (x_diff[0] + v_y)),
    )


def advance_column(source, target, coef_ref, spin_ref, lon):
    comps, length, tall, _ = source.shape
    flat = source.reshape(comps * length * tall, LANES)
    sub = lax.broadcasted_iota(jnp.int32, (SUB, LANES), 0)
    tiles = tall // SUB
    for tile in range(tiles):
        lines = pl.ds(SUB * tile, SUB)
        own, east, west = (
            [source[comp, lon + shift, lines, :] for comp in range(comps)] for shift in (0, 1, -1)
        )
        starts = [(comp * length + lon) * tall + SUB * tile for comp in range(comps)]
        if tile < tiles - 1:
            above = [flat[pl.ds(start + 1, SUB), :] for start in starts]
        else:
            wrap = [source[comp, lon, pl.ds(0, SUB), :] for comp in range(comps)]
            above = [
                jnp.where(sub == SUB - 1, pltpu.roll(w, SUB - 1, 0), pltpu.roll(o, SUB - 1, 0))
                for w, o in zip(wrap, own)
            ]
        if tile > 0:
            below = [flat[pl.ds(start - 1, SUB), :] for start in starts]
        else:
            wrap = [source[comp, lon, pl.ds(tall - SUB, SUB), :] for comp in range(comps)]
            below = [
                jnp.where(sub == 0, pltpu.roll(w, 1, 0), pltpu.roll(o, 1, 0))
                for w, o in zip(wrap, own)
            ]
        new = model(
            own,
            [e - w for e, w in zip(east, west)],
            [e + w for e, w in zip(east, west)],
            above,
            below,
            *(coef_ref[field, lon, lines, :] for field in range(FIELDS)),
            spin_ref[lines, :],
        )
        for comp in range(comps):
            target[comp, lon, lines, :] = new[comp]


def apply_inside(step, source, coef_ref, spin_ref, target):
    first = SIDE + step + 1
    count = source.shape[1] - 2 * first

    @pl.loop(0, count // 2)
    def _(pair):
        advance_column(source, target, coef_ref, spin_ref, first + 2 * pair)
        advance_column(source, target, coef_ref, spin_ref, first + 2 * pair + 1)


def mend_columns(par, states, coef_ref, spin_ref, cols_got):
    comps, length, tall, _ = states[0].shape
    _, easts = sides_of(par)
    for slot, msg in enumerate(cols_got):
        for comp in range(comps):
            for j in range(SIDE):
                column = column_at(easts[slot], length - 2 * SIDE, -1 - j)
                states[0][comp, column] = msg[pl.ds((comp * SIDE + j) * tall, tall), :]
    for step in range(STEPS):
        first = step + 1
        skip = length - 2 * first - 2 * SIDE

        @pl.loop(0, 2 * SIDE)
        def _(i):
            lon = first + i + (i // SIDE) * skip
            advance_column(states[step], states[step + 1], coef_ref, spin_ref, lon)


def join_gram(
    scale, par, start_in, middle_in, state_in, coef_in, spin_ref, a, b, start, middle, state, coef, col_a, col_b, kept, sent, total
):
    _, length, tall, _ = state.shape
    _, easts = sides_of(par)
    for slot, msg in enumerate((a, b)):
        upright = jnp.transpose(msg[pl.ds(msg.shape[0] - SUB, SUB), :])
        for field in range(FIELDS):
            column = column_at(easts[slot], length - 2 * SIDE, -1)
            coef[field, column] = lane_spread(upright[:tall], field)
    mend_columns(par, (start, middle, state), coef, spin_ref, (a, b))
    send_columns(par, state, (col_a, col_b))
    gram = sum(gram_of(*split_halves(cells)) for _, _, cells in tiles_of(state))
    write_halves(par, gram, scale, kept, sent, total)


def tiles_of(state):
    comps, length, tall, _ = state.shape
    rows = tall - 2 * HALO
    for comp in range(comps):
        for lon in range(0, length - 2 * SIDE, SUB):
            cells = state[comp, pl.ds(SIDE + lon, SUB), pl.ds(0, rows), :]
            yield comp, lon, cells.reshape(SUB * rows, LANES)


def split_halves(value):
    high = value.astype(jnp.bfloat16)
    return high, (value - high.astype(jnp.float32)).astype(jnp.bfloat16)


def gram_of(high, low):
    return lax.dot_general(
        high,
        jnp.concatenate([high, low], axis=1),
        (((0,), (0,)), ((), ())),
        preferred_element_type=jnp.float32,
    )


def write_halves(par, gram, scale, kept, sent, total):
    odd = par[1] % 2
    rows = LANES // 2
    mixed = gram[:, LANES:]
    total[...] = scale * (gram[:, :LANES] + (mixed + jnp.transpose(mixed)))
    kept[...] = total[pl.ds(odd * rows, rows), :]
    sent[...] = total[pl.ds((1 - odd) * rows, rows), :]


def invert_factor(gram_ref, work):
    count = LANES // SUB
    lane = lax.broadcasted_iota(jnp.int32, (SUB, LANES), 1)
    sub = lax.broadcasted_iota(jnp.int32, (SUB, LANES), 0)
    rows = [gram_ref[pl.ds(SUB * i, SUB), :] for i in range(count)]
    for block in range(count):
        base = SUB * block
        here = (lane >= base) & (lane < base + SUB)
        spread = [lane_spread(rows[block], base + l) for l in range(SUB)]
        low = [
            [jnp.broadcast_to(spread[l][k : k + 1, :], (SUB, LANES)) for l in range(k + 1)]
            for k in range(SUB)
        ]
        pivot = jnp.where(here, jnp.where(lane - base == sub, 1.0, 0.0), rows[block])
        inv, scaled = [], []
        for k in range(SUB):
            inv.append(lax.rsqrt(low[k][k]))
            for i in range(k + 1, SUB):
                low[i][k] = low[i][k] * inv[k]
            for i in range(k + 1, SUB):
                for m in range(k + 1, i + 1):
                    low[i][m] = low[i][m] - low[i][k] * low[m][k]
            line = jnp.broadcast_to(pivot[k : k + 1, :], (SUB, LANES))
            for l in range(k):
                line = line - low[k][l] * scaled[l]
            scaled.append(line * inv[k])
        merged = scaled[0]
        for k in range(1, SUB):
            merged = jnp.where(sub == k, scaled[k], merged)
        work[pl.ds(base, SUB), :] = merged
        for i in range(block + 1, count):
            weights = []
            rest = jnp.where(here, 0.0, rows[i])
            for l in range(SUB):
                weight = lane_spread(rows[i], base + l)
                for m in range(l):
                    weight = weight - weights[m] * low[l][m]
                weights.append(weight * inv[l])
            for l in range(SUB):
                rest = rest - weights[l] * scaled[l]
            rows[i] = rest


def factorize(par, mine_ref, other_ref, gram, work):
    rows = LANES // 2
    odd = par[1] % 2
    gram[pl.ds(odd * rows, rows), :] = mine_ref[...]
    gram[pl.ds((1 - odd) * rows, rows), :] = other_ref[...]
    invert_factor(gram, work)
    row = lax.broadcasted_iota(jnp.int32, (LANES, LANES), 0)
    col = lax.broadcasted_iota(jnp.int32, (LANES, LANES), 1)
    inverse = jnp.where(row >= col, work[...], 0.0)
    diagonal = jnp.sum(jnp.where(row == col, inverse, 0.0), axis=0, keepdims=True)
    return inverse, diagonal


def paired(inverse):
    high = inverse.astype(jnp.bfloat16)
    low = (inverse - high.astype(jnp.float32)).astype(jnp.bfloat16)
    return jnp.concatenate(
        [jnp.concatenate([high, high], axis=1), jnp.concatenate([low, low], axis=1)], axis=0
    )


def times_factor(cells, factor):
    pair = jnp.concatenate(split_halves(cells), axis=1)
    both = lax.dot_general(
        pair, factor, (((1,), (1,)), ((), ())), preferred_element_type=jnp.float32
    )
    return both[:, :LANES] + both[:, LANES:]


def factor_only(par, mine_ref, other_ref, prior_ref, inverse_ref, logs_ref, gram, work):
    inverse, diagonal = factorize(par, mine_ref, other_ref, gram, work)
    inverse_ref[...] = inverse
    logs_ref[...] = prior_ref[...] - jnp.log(diagonal)


def join_update(
    scale, par, start_in, middle_in, state_in, coef_ref, spin_ref, a, b, inverse_ref, start, middle, state, out_ref, kept, sent, factor, total, fresh, sems
):
    factor[...] = paired(inverse_ref[...])
    mend_columns(par, (start, middle, state), coef_ref, spin_ref, (a, b))
    cols = fresh.shape[1]

    def back_copy(comp, lon):
        return pltpu.make_async_copy(
            fresh.at[comp, lon], out_ref.at[comp, :, lon], sems.at[comp * cols + lon]
        )

    gram = 0.0
    copies = []
    for comp, lon, cells in tiles_of(state):
        new = times_factor(cells, factor[...])
        fresh[comp, pl.ds(lon, SUB)] = new.reshape((SUB,) + fresh.shape[2:])
        for i in range(SUB):
            copies.append(back_copy(comp, lon + i))
            copies[-1].start()
        gram += gram_of(*split_halves(new))
    write_halves(par, gram, scale, kept, sent, total)
    finish_all(copies)


def finish(par, mine_ref, other_ref, prior_ref, t_ref, out_ref, logs_ref, gram, work, factor, fresh, sems):
    inverse, diagonal = factorize(par, mine_ref, other_ref, gram, work)
    logs_ref[...] = prior_ref[...] - jnp.log(diagonal)
    factor[...] = paired(inverse)

    def out_copy(tile):
        return pltpu.make_async_copy(fresh.at[tile], out_ref.at[tile], sems.at[tile])

    for tile in range(TILES):
        fresh[tile] = times_factor(t_ref[tile], factor[...])
        out_copy(tile).start()

    for tile in range(TILES):
        out_copy(tile).wait()


def swap_pairs(near_value, far_value, axis, closed):
    count = lax.axis_size(axis)
    near = [(i, i ^ 1) for i in range(count)]
    far = [(i, (i + 1 if i % 2 else i - 1) % count) for i in range(count)]
    if not closed:
        far = far[1:-1]
    return lax.ppermute(near_value, axis, near), lax.ppermute(far_value, axis, far)


def swapped(value, axis, mask):
    return lax.ppermute(value, axis, [(i, i ^ mask) for i in range(lax.axis_size(axis))])


def sum_over(value, axis, first_bit):
    bits = lax.axis_size(axis).bit_length() - 1
    while first_bit < bits:
        low = 1 << first_bit
        if first_bit + 1 < bits:
            high = low << 1
            one, two, three = (swapped(value, axis, mask) for mask in (low, high, low | high))
            value = (value + one) + (two + three)
            first_bit += 2
        else:
            value = value + swapped(value, axis, low)
            first_bit += 1
    return value


def sum_devices(kept, sent):
    mine = kept + swapped(sent, "col", 1)
    mine = sum_over(mine, "col", 1)
    mine = sum_over(mine, "row", 0)
    return mine, swapped(mine, "col", 1)


def body(tangents, sea_mask, levels, current):
    comps, rows, cols, modes = tangents.shape
    total_rows = rows * lax.axis_size("row")
    total_cells = total_rows * cols * lax.axis_size("col")
    scale = 1.0 / total_cells
    row_at, col_at = lax.axis_index("row"), lax.axis_index("col")
    par = jnp.stack([row_at, col_at]).astype(jnp.int32)

    tall, length = rows + 2 * HALO, cols + 2 * SIDE

    block = shape_of(comps, length, tall, modes)
    coefs = shape_of(FIELDS, length, tall, LANES)
    columns = (shape_of(comps * SIDE * tall, modes),) * 2
    first_columns = (shape_of(comps * SIDE * tall + SUB, modes),) * 2
    rows_sent = (shape_of(comps * HALO + 1, cols, modes),) * 2
    halves = (shape_of(modes // 2, modes),) * 2
    square = pltpu.VMEM((modes, modes), jnp.float32)
    factor = pltpu.VMEM((2 * modes, 2 * modes), jnp.bfloat16)

    def call(
        kernel, outs, *operands, specs=None, out_specs=None, scratch=(), aliases=None, cost=1.0
    ):
        return pl.pallas_call(
            kernel,
            out_shape=outs,
            in_specs=specs or [SMEM] + [VMEM] * (len(operands) - 1),
            out_specs=out_specs or (VMEM,) * len(outs),
            scratch_shapes=scratch,
            input_output_aliases=aliases or {},
            compiler_params=params(),
            cost_estimate=pl.CostEstimate(
                flops=int(cost * 1e9), bytes_accessed=int(cost * 3e6), transcendentals=0
            ),
        )(*operands)

    def inside(step, state):
        kernel = functools.partial(apply_inside, step)
        return call(kernel, (block,), state, coef, spin, specs=[VMEM] * 3, cost=2.0)[0]

    def swap_columns(packed):
        return swap_pairs(*packed, "col", True)

    source, *fields = (
        pltpu.with_memory_space_constraint(x, pltpu.HBM)
        for x in (tangents, sea_mask.T, levels.T, current.T)
    )
    upright = [pltpu.VMEM(x.shape, x.dtype) for x in fields]
    packed = call(
        pack_rows,
        rows_sent,
        par,
        source,
        *fields,
        specs=[SMEM] + [HBM] * 4,
        scratch=upright
        + [
            pltpu.VMEM((cols, LANES), jnp.float32),
            pltpu.SemaphoreType.DMA((2 * comps,)),
            pltpu.SemaphoreType.DMA((FIELDS,)),
        ],
    )
    row_halos = swap_pairs(*packed, "row", False)
    start, coef, wide, spin = call(
        functools.partial(spread_fields, total_rows),
        (block, coefs, shape_of(FIELDS, cols, LANES), shape_of(tall, LANES)),
        par,
        source,
        *fields,
        specs=[SMEM] + [HBM] * 4,
        scratch=upright
        + [pltpu.SemaphoreType.DMA((comps * cols,)), pltpu.SemaphoreType.DMA((FIELDS,))],
        cost=3.0,
    )
    start, coef, *packed = call(
        join_rows,
        (block, coefs) + first_columns,
        par,
        start,
        coef,
        wide,
        *row_halos,
        aliases={1: 0, 2: 1},
    )
    logs = jnp.zeros((1, modes), jnp.float32)

    halos = swap_columns(packed)
    middle = inside(0, start)
    state = inside(1, middle)
    _, _, start, coef, *packed, kept, sent = call(
        functools.partial(join_gram, scale),
        (block, block, block, coefs) + columns + halves,
        par,
        start,
        middle,
        state,
        coef,
        spin,
        *halos,
        scratch=[square],
        aliases={1: 0, 2: 1, 3: 2, 4: 3},
        cost=2.0,
    )
    halos = swap_columns(packed)
    mine, other = sum_devices(kept, sent)
    middle = inside(0, start)
    state = inside(1, middle)
    inverse, logs = call(
        factor_only,
        (shape_of(modes, modes), shape_of(1, modes)),
        par,
        mine,
        other,
        logs,
        scratch=[square, square],
        cost=4.4,
    )
    _, _, _, state, kept, sent = call(
        functools.partial(join_update, scale),
        (block, block, block, shape_of(comps, rows, cols, modes)) + halves,
        par,
        start,
        middle,
        state,
        coef,
        spin,
        *halos,
        inverse,
        scratch=[
            factor,
            square,
            pltpu.VMEM((comps, cols, rows, modes), jnp.float32),
            pltpu.SemaphoreType.DMA((comps * cols,)),
        ],
        aliases={1: 0, 2: 1, 3: 2},
        cost=3.0,
    )
    height = comps * rows * cols // TILES
    tiled = shape_of(TILES, height, modes)
    mine, other = sum_devices(kept, sent)
    out, logs = call(
        finish,
        (tiled, shape_of(1, modes)),
        par,
        mine,
        other,
        logs,
        state.reshape(TILES, height, modes),
        out_specs=(HBM, VMEM),
        scratch=[
            square,
            square,
            factor,
            pltpu.VMEM((TILES, height, modes), jnp.float32),
            pltpu.SemaphoreType.DMA((TILES,)),
        ],
    )
    return out.reshape(tangents.shape), logs.reshape(modes)


def solution(mesh):
    placed = (P(None, "row", "col", None), P("row", "col"), P("row", "col"), P("row", "col"))
    return jax.shard_map(
        body,
        mesh=mesh,
        in_specs=placed,
        out_specs=(P(None, "row", "col", None), P()),
        check_vma=False,
    )
```

```python
import functools

import jax
import jax.numpy as jnp
from jax import lax
from jax.experimental import pallas as pl
from jax.experimental.pallas import tpu as pltpu
from jax.sharding import PartitionSpec as P

STEPS = 2
RENORMS = 2
LEVELS = 50

viscosity = 0.15
gravity = 0.5
rotation = 0.4

SUB = 8
LANES = 128
FIELDS = 3
HALO = STEPS * RENORMS
SIDE = STEPS
TILES = 12
VMEM_LIMIT = 16 * 1024 * 1024

HBM = pl.BlockSpec(memory_space=pltpu.HBM)
VMEM = pl.BlockSpec(memory_space=pltpu.VMEM)
SMEM = pl.BlockSpec(memory_space=pltpu.SMEM)


def params():
    return pltpu.CompilerParams(vmem_limit_bytes=VMEM_LIMIT)


def shape_of(*dims):
    return jax.ShapeDtypeStruct(dims, jnp.float32)


def lane_spread(block, lane):
    return jnp.broadcast_to(block[:, lane : lane + 1], (block.shape[0], LANES))


def fetch(sources, places, sems):
    copies = [
        pltpu.make_async_copy(source, place, sems.at[i])
        for i, (source, place) in enumerate(zip(sources, places))
    ]
    for copy in copies:
        copy.start()
    return copies


def finish_all(copies):
    for copy in copies:
        copy.wait()


def fields_of(sea_ref, levels_ref, current_ref):
    return (
        sea_ref[...].astype(jnp.float32),
        0.5 * current_ref[...],
        0.5 * ((levels_ref[...] + 1).astype(jnp.float32) / LEVELS),
    )


def sides_of(par):
    odd_row, odd_col = par[0] % 2, par[1] % 2
    return (1 - odd_row, odd_row), (1 - odd_col, odd_col)


def pack_rows(
    par, t_ref, sea_ref, levels_ref, current_ref, row_a, row_b, sea, levels, current, wide, sems, field_sems
):
    comps, rows, cols, _ = t_ref.shape
    norths, _ = sides_of(par)
    field_copies = fetch((sea_ref, levels_ref, current_ref), (sea, levels, current), field_sems)
    slots = [(slot, msg, comp) for slot, msg in ((0, row_a), (1, row_b)) for comp in range(comps)]
    copies = fetch(
        [t_ref.at[comp, pl.ds(norths[slot] * (rows - HALO), HALO)] for slot, _, comp in slots],
        [msg.at[pl.ds(comp * HALO, HALO)] for _, msg, comp in slots],
        sems,
    )
    lane = lax.broadcasted_iota(jnp.int32, (cols, LANES), 1)
    wide[...] = jnp.zeros_like(wide)
    packed = [jnp.zeros((cols, LANES), jnp.float32)] * 2
    finish_all(field_copies)
    for field, value in enumerate(fields_of(sea, levels, current)):
        wide[:, pl.ds(0, rows)] = value
        whole = wide[...]
        for north in (0, 1):
            shift = (field * SUB - north * (rows - HALO)) % LANES
            moved = pltpu.roll(whole, shift, 1) if shift else whole
            here = (lane >= field * SUB) & (lane < field * SUB + HALO)
            packed[north] = jnp.where(here, moved, packed[north])
    for slot, msg in ((0, row_a), (1, row_b)):
        msg[comps * HALO] = jnp.where(norths[slot] == 1, packed[1], packed[0])
    finish_all(copies)


def spread_fields(
    total_rows, par, t_ref, sea_ref, levels_ref, current_ref, state, coef, wide, spin, sea, levels, current, sems, field_sems
):
    comps, rows, cols, _ = t_ref.shape
    field_copies = fetch((sea_ref, levels_ref, current_ref), (sea, levels, current), field_sems)
    cells = [(comp, lon) for comp in range(comps) for lon in range(cols)]
    copies = fetch(
        [t_ref.at[comp, :, lon] for comp, lon in cells],
        [state.at[comp, SIDE + lon, pl.ds(0, rows)] for comp, lon in cells],
        sems,
    )
    line = lax.broadcasted_iota(jnp.int32, spin.shape, 0)
    line = jnp.where(line < rows + HALO, line, line - (rows + 2 * HALO))
    latitude = (par[0] * rows + line).astype(jnp.float32)
    angle = (-70.0 + 140.0 * (latitude + 0.5) / total_rows) * (jnp.pi / 180.0)
    spin[...] = rotation * jnp.sin(angle)
    wide[...] = jnp.zeros_like(wide)
    finish_all(field_copies)
    for field, value in enumerate(fields_of(sea, levels, current)):
        wide[field, :, pl.ds(0, rows)] = value
        natural = jnp.transpose(wide[field])[:rows]
        for lon in range(cols):
            coef[field, SIDE + lon, pl.ds(0, rows), :] = lane_spread(natural, lon)
    finish_all(copies)


def column_at(east, cols, depth):
    return SIDE + depth + east * (cols - 1 - 2 * depth)


def send_columns(par, state, cols_sent):
    comps, wide, tall, _ = state.shape
    _, easts = sides_of(par)
    for slot, msg in enumerate(cols_sent):
        for comp in range(comps):
            for j in range(SIDE):
                column = column_at(easts[slot], wide - 2 * SIDE, j)
                msg[pl.ds((comp * SIDE + j) * tall, tall), :] = state[comp, column]


def join_rows(par, state_in, coef_in, wide, row_a, row_b, state, coef, col_a, col_b):
    comps, length, tall, _ = state.shape
    cols, rows = length - 2 * SIDE, tall - 2 * HALO
    norths, easts = sides_of(par)
    flat = state.reshape(comps * length * tall, LANES)
    for slot, msg in ((0, row_a), (1, row_b)):
        line = rows + HALO * (1 - norths[slot])
        for comp in range(comps):
            for h in range(HALO):
                for lon in range(0, cols, SUB):
                    at = (comp * length + SIDE + lon) * tall + line + h
                    flat[pl.ds(at, SUB, stride=tall), :] = msg[comp * HALO + h, pl.ds(lon, SUB), :]
    lane = lax.broadcasted_iota(jnp.int32, (cols, LANES), 1)
    north = jnp.where(norths[0] == 1, row_a[comps * HALO], row_b[comps * HALO])
    south = jnp.where(norths[0] == 1, row_b[comps * HALO], row_a[comps * HALO])
    beyond = jnp.where(lane % SUB < HALO, north, pltpu.roll(south, HALO, 1))
    natural = jnp.transpose(beyond)
    for field in range(FIELDS):
        block = natural[field * SUB : (field + 1) * SUB]
        for lon in range(cols):
            coef[field, SIDE + lon, pl.ds(rows, SUB), :] = lane_spread(block, lon)
    tail = comps * SIDE * tall
    whole = [
        jnp.where(lane < rows, wide[field], pltpu.roll(beyond, rows - field * SUB, 1))
        for field in range(FIELDS)
    ]
    for slot, msg in ((0, col_a), (1, col_b)):
        msg[pl.ds(tail, SUB), :] = jnp.zeros((SUB, LANES), jnp.float32)
        for field in range(FIELDS):
            msg[pl.ds(tail + field, 1), :] = jnp.where(
                easts[slot] == 1, whole[field][cols - 1 :], whole[field][:1]
            )
    send_columns(par, state, (col_a, col_b))


def model(own, x_diff, x_sum, above, below, sea, flow, depth, spin):
    keep, half = 1.0 - 4.0 * viscosity, 0.5 * gravity
    mixed = [
        keep * c + viscosity * (x + (n + s)) - flow * d
        for c, d, x, n, s in zip(own, x_diff, x_sum, above, below)
    ]
    v_y, h_y = above[1] - below[1], above[2] - below[2]
    return (
        sea * (mixed[0] - half * x_diff[2] + spin * own[1]),
        sea * (mixed[1] - half * h_y - spin * own[0]),
        sea * (mixed[2] - depth * (x_diff[0] + v_y)),
    )


def advance_column(source, target, coef_ref, spin_ref, lon):
    comps, length, tall, _ = source.shape
    flat = source.reshape(comps * length * tall, LANES)
    sub = lax.broadcasted_iota(jnp.int32, (SUB, LANES), 0)
    tiles = tall // SUB
    for tile in range(tiles):
        lines = pl.ds(SUB * tile, SUB)
        own, east, west = (
            [source[comp, lon + shift, lines, :] for comp in range(comps)] for shift in (0, 1, -1)
        )
        starts = [(comp * length + lon) * tall + SUB * tile for comp in range(comps)]
        if tile < tiles - 1:
            above = [flat[pl.ds(start + 1, SUB), :] for start in starts]
        else:
            wrap = [source[comp, lon, pl.ds(0, SUB), :] for comp in range(comps)]
            above = [
                jnp.where(sub == SUB - 1, pltpu.roll(w, SUB - 1, 0), pltpu.roll(o, SUB - 1, 0))
                for w, o in zip(wrap, own)
            ]
        if tile > 0:
            below = [flat[pl.ds(start - 1, SUB), :] for start in starts]
        else:
            wrap = [source[comp, lon, pl.ds(tall - SUB, SUB), :] for comp in range(comps)]
            below = [
                jnp.where(sub == 0, pltpu.roll(w, 1, 0), pltpu.roll(o, 1, 0))
                for w, o in zip(wrap, own)
            ]
        new = model(
            own,
            [e - w for e, w in zip(east, west)],
            [e + w for e, w in zip(east, west)],
            above,
            below,
            *(coef_ref[field, lon, lines, :] for field in range(FIELDS)),
            spin_ref[lines, :],
        )
        for comp in range(comps):
            target[comp, lon, lines, :] = new[comp]


def apply_inside(step, source, coef_ref, spin_ref, target):
    first = SIDE + step + 1
    count = source.shape[1] - 2 * first

    @pl.loop(0, count // 2)
    def _(pair):
        advance_column(source, target, coef_ref, spin_ref, first + 2 * pair)
        advance_column(source, target, coef_ref, spin_ref, first + 2 * pair + 1)


def mend_columns(par, states, coef_ref, spin_ref, cols_got):
    comps, length, tall, _ = states[0].shape
    _, easts = sides_of(par)
    for slot, msg in enumerate(cols_got):
        for comp in range(comps):
            for j in range(SIDE):
                column = column_at(easts[slot], length - 2 * SIDE, -1 - j)
                states[0][comp, column] = msg[pl.ds((comp * SIDE + j) * tall, tall), :]
    for step in range(STEPS):
        first = step + 1
        skip = length - 2 * first - 2 * SIDE

        @pl.loop(0, 2 * SIDE)
        def _(i):
            lon = first + i + (i // SIDE) * skip
            advance_column(states[step], states[step + 1], coef_ref, spin_ref, lon)


def join_gram(
    scale, par, start_in, middle_in, state_in, coef_in, spin_ref, a, b, start, middle, state, coef, col_a, col_b, kept, sent, total
):
    _, length, tall, _ = state.shape
    _, easts = sides_of(par)
    for slot, msg in enumerate((a, b)):
        upright = jnp.transpose(msg[pl.ds(msg.shape[0] - SUB, SUB), :])
        for field in range(FIELDS):
            column = column_at(easts[slot], length - 2 * SIDE, -1)
            coef[field, column] = lane_spread(upright[:tall], field)
    mend_columns(par, (start, middle, state), coef, spin_ref, (a, b))
    send_columns(par, state, (col_a, col_b))
    gram = sum(gram_of(*split_halves(cells)) for _, _, cells in tiles_of(state))
    write_halves(par, gram, scale, kept, sent, total)


def tiles_of(state):
    comps, length, tall, _ = state.shape
    rows = tall - 2 * HALO
    for comp in range(comps):
        for lon in range(0, length - 2 * SIDE, SUB):
            cells = state[comp, pl.ds(SIDE + lon, SUB), pl.ds(0, rows), :]
            yield comp, lon, cells.reshape(SUB * rows, LANES)


def split_halves(value):
    high = value.astype(jnp.bfloat16)
    return high, (value - high.astype(jnp.float32)).astype(jnp.bfloat16)


def gram_of(high, low):
    return lax.dot_general(
        high,
        jnp.concatenate([high, low], axis=1),
        (((0,), (0,)), ((), ())),
        preferred_element_type=jnp.float32,
    )


def write_halves(par, gram, scale, kept, sent, total):
    odd = par[1] % 2
    rows = LANES // 2
    mixed = gram[:, LANES:]
    total[...] = scale * (gram[:, :LANES] + (mixed + jnp.transpose(mixed)))
    kept[...] = total[pl.ds(odd * rows, rows), :]
    sent[...] = total[pl.ds((1 - odd) * rows, rows), :]


def invert_factor(gram_ref, work, board):
    count = LANES // SUB
    lane = lax.broadcasted_iota(jnp.int32, (SUB, LANES), 1)
    sub = lax.broadcasted_iota(jnp.int32, (SUB, LANES), 0)
    rows = [gram_ref[pl.ds(SUB * i, SUB), :] for i in range(count)]
    for block in range(count):
        base = SUB * block
        here = (lane >= base) & (lane < base + SUB)
        shelf = 2 * SUB * base
        for l in range(SUB):
            board[pl.ds(shelf + SUB * l, SUB), :] = lane_spread(rows[block], base + l)
        low = [
            [board[pl.ds(shelf + SUB * l + k, SUB, stride=0), :] for l in range(k + 1)]
            for k in range(SUB)
        ]
        shelf += SUB * SUB
        board[pl.ds(shelf, SUB), :] = jnp.where(
            here, jnp.where(lane - base == sub, 1.0, 0.0), rows[block]
        )
        inv, scaled = [], []
        for k in range(SUB):
            inv.append(lax.rsqrt(low[k][k]))
            for i in range(k + 1, SUB):
                low[i][k] = low[i][k] * inv[k]
            for i in range(k + 1, SUB):
                for m in range(k + 1, i + 1):
                    low[i][m] = low[i][m] - low[i][k] * low[m][k]
            line = board[pl.ds(shelf + k, SUB, stride=0), :]
            for l in range(k):
                line = line - low[k][l] * scaled[l]
            scaled.append(line * inv[k])
        merged = scaled[0]
        for k in range(1, SUB):
            merged = jnp.where(sub == k, scaled[k], merged)
        work[pl.ds(base, SUB), :] = merged
        for i in range(block + 1, count):
            weights = []
            rest = jnp.where(here, 0.0, rows[i])
            for l in range(SUB):
                weight = lane_spread(rows[i], base + l)
                for m in range(l):
                    weight = weight - weights[m] * low[l][m]
                weights.append(weight * inv[l])
            for l in range(SUB):
                rest = rest - weights[l] * scaled[l]
            rows[i] = rest


def factorize(par, mine_ref, other_ref, gram, work, board):
    rows = LANES // 2
    odd = par[1] % 2
    gram[pl.ds(odd * rows, rows), :] = mine_ref[...]
    gram[pl.ds((1 - odd) * rows, rows), :] = other_ref[...]
    invert_factor(gram, work, board)
    row = lax.broadcasted_iota(jnp.int32, (LANES, LANES), 0)
    col = lax.broadcasted_iota(jnp.int32, (LANES, LANES), 1)
    inverse = jnp.where(row >= col, work[...], 0.0)
    diagonal = jnp.sum(jnp.where(row == col, inverse, 0.0), axis=0, keepdims=True)
    return inverse, diagonal


def paired(inverse):
    high = inverse.astype(jnp.bfloat16)
    low = (inverse - high.astype(jnp.float32)).astype(jnp.bfloat16)
    return jnp.concatenate(
        [jnp.concatenate([high, high], axis=1), jnp.concatenate([low, low], axis=1)], axis=0
    )


def times_factor(cells, factor):
    pair = jnp.concatenate(split_halves(cells), axis=1)
    both = lax.dot_general(
        pair, factor, (((1,), (1,)), ((), ())), preferred_element_type=jnp.float32
    )
    return both[:, :LANES] + both[:, LANES:]


def factor_only(par, mine_ref, other_ref, prior_ref, inverse_ref, logs_ref, gram, work, board):
    inverse, diagonal = factorize(par, mine_ref, other_ref, gram, work, board)
    inverse_ref[...] = inverse
    logs_ref[...] = prior_ref[...] - jnp.log(diagonal)


def join_update(
    scale, par, start_in, middle_in, state_in, coef_ref, spin_ref, a, b, inverse_ref, start, middle, state, out_ref, kept, sent, factor, total
):
    factor[...] = paired(inverse_ref[...])
    mend_columns(par, (start, middle, state), coef_ref, spin_ref, (a, b))
    gram = 0.0
    for comp, lon, cells in tiles_of(state):
        new = times_factor(cells, factor[...])
        out_ref[comp, pl.ds(lon, SUB)] = new.reshape((SUB,) + out_ref.shape[2:])
        gram += gram_of(*split_halves(new))
    write_halves(par, gram, scale, kept, sent, total)


def restore_order(turned, out_ref):
    comps, cols, _, _ = turned.shape
    for comp in range(comps):
        for lon in range(0, cols, SUB):
            cells = turned[comp, pl.ds(lon, SUB)]
            out_ref[comp, :, pl.ds(lon, SUB), :] = jnp.transpose(cells, (1, 0, 2))


def finish(
    par, mine_ref, other_ref, prior_ref, t_ref, out_ref, logs_ref, gram, work, board, factor, fresh, sems
):
    inverse, diagonal = factorize(par, mine_ref, other_ref, gram, work, board)
    logs_ref[...] = prior_ref[...] - jnp.log(diagonal)
    factor[...] = paired(inverse)

    def out_copy(tile):
        return pltpu.make_async_copy(fresh.at[tile], out_ref.at[tile], sems.at[tile])

    for tile in range(TILES):
        fresh[tile] = times_factor(t_ref[tile], factor[...])
        out_copy(tile).start(priority=tile % 2)

    for tile in range(TILES):
        out_copy(tile).wait()


def swap_pairs(near_value, far_value, axis, closed):
    count = lax.axis_size(axis)
    near = [(i, i ^ 1) for i in range(count)]
    far = [(i, (i + 1 if i % 2 else i - 1) % count) for i in range(count)]
    if not closed:
        far = far[1:-1]
    return lax.ppermute(near_value, axis, near), lax.ppermute(far_value, axis, far)


def swapped(value, axis, mask):
    return lax.ppermute(value, axis, [(i, i ^ mask) for i in range(lax.axis_size(axis))])


def sum_over(value, axis, first_bit):
    bits = lax.axis_size(axis).bit_length() - 1
    while first_bit < bits:
        low = 1 << first_bit
        if first_bit + 1 < bits:
            high = low << 1
            one, two, three = (swapped(value, axis, mask) for mask in (low, high, low | high))
            value = (value + one) + (two + three)
            first_bit += 2
        else:
            value = value + swapped(value, axis, low)
            first_bit += 1
    return value


def sum_devices(kept, sent):
    mine = kept + swapped(sent, "col", 1)
    mine = sum_over(mine, "col", 1)
    mine = sum_over(mine, "row", 0)
    return mine, swapped(mine, "col", 1)


def body(tangents, sea_mask, levels, current):
    comps, rows, cols, modes = tangents.shape
    total_rows = rows * lax.axis_size("row")
    total_cells = total_rows * cols * lax.axis_size("col")
    scale = 1.0 / total_cells
    row_at, col_at = lax.axis_index("row"), lax.axis_index("col")
    par = jnp.stack([row_at, col_at]).astype(jnp.int32)

    tall, length = rows + 2 * HALO, cols + 2 * SIDE

    block = shape_of(comps, length, tall, modes)
    coefs = shape_of(FIELDS, length, tall, LANES)
    columns = (shape_of(comps * SIDE * tall, modes),) * 2
    first_columns = (shape_of(comps * SIDE * tall + SUB, modes),) * 2
    rows_sent = (shape_of(comps * HALO + 1, cols, modes),) * 2
    halves = (shape_of(modes // 2, modes),) * 2
    square = pltpu.VMEM((modes, modes), jnp.float32)
    board = pltpu.VMEM((2 * SUB * modes, LANES), jnp.float32)
    factor = pltpu.VMEM((2 * modes, 2 * modes), jnp.bfloat16)

    def call(
        kernel, outs, *operands, specs=None, out_specs=None, scratch=(), aliases=None, cost=1.0
    ):
        return pl.pallas_call(
            kernel,
            out_shape=outs,
            in_specs=specs or [SMEM] + [VMEM] * (len(operands) - 1),
            out_specs=out_specs or (VMEM,) * len(outs),
            scratch_shapes=scratch,
            input_output_aliases=aliases or {},
            compiler_params=params(),
            cost_estimate=pl.CostEstimate(
                flops=int(cost * 1e9), bytes_accessed=int(cost * 3e6), transcendentals=0
            ),
        )(*operands)

    def inside(step, state):
        kernel = functools.partial(apply_inside, step)
        return call(kernel, (block,), state, coef, spin, specs=[VMEM] * 3, cost=2.0)[0]

    def swap_columns(packed):
        return swap_pairs(*packed, "col", True)

    source, *fields = (
        pltpu.with_memory_space_constraint(x, pltpu.HBM)
        for x in (tangents, sea_mask.T, levels.T, current.T)
    )
    upright = [pltpu.VMEM(x.shape, x.dtype) for x in fields]
    packed = call(
        pack_rows,
        rows_sent,
        par,
        source,
        *fields,
        specs=[SMEM] + [HBM] * 4,
        scratch=upright
        + [
            pltpu.VMEM((cols, LANES), jnp.float32),
            pltpu.SemaphoreType.DMA((2 * comps,)),
            pltpu.SemaphoreType.DMA((FIELDS,)),
        ],
    )
    row_halos = swap_pairs(*packed, "row", False)
    start, coef, wide, spin = call(
        functools.partial(spread_fields, total_rows),
        (block, coefs, shape_of(FIELDS, cols, LANES), shape_of(tall, LANES)),
        par,
        source,
        *fields,
        specs=[SMEM] + [HBM] * 4,
        scratch=upright
        + [pltpu.SemaphoreType.DMA((comps * cols,)), pltpu.SemaphoreType.DMA((FIELDS,))],
        cost=3.0,
    )
    start, coef, *packed = call(
        join_rows,
        (block, coefs) + first_columns,
        par,
        start,
        coef,
        wide,
        *row_halos,
        aliases={1: 0, 2: 1},
    )
    logs = jnp.zeros((1, modes), jnp.float32)

    halos = swap_columns(packed)
    middle = inside(0, start)
    state = inside(1, middle)
    _, _, start, coef, *packed, kept, sent = call(
        functools.partial(join_gram, scale),
        (block, block, block, coefs) + columns + halves,
        par,
        start,
        middle,
        state,
        coef,
        spin,
        *halos,
        scratch=[square],
        aliases={1: 0, 2: 1, 3: 2, 4: 3},
        cost=2.0,
    )
    halos = swap_columns(packed)
    mine, other = sum_devices(kept, sent)
    middle = inside(0, start)
    state = inside(1, middle)
    inverse, logs = call(
        factor_only,
        (shape_of(modes, modes), shape_of(1, modes)),
        par,
        mine,
        other,
        logs,
        scratch=[square, square, board],
        cost=0.01,
    )
    _, _, _, state, kept, sent = call(
        functools.partial(join_update, scale),
        (block, block, block, shape_of(comps, cols, rows, modes)) + halves,
        par,
        start,
        middle,
        state,
        coef,
        spin,
        *halos,
        inverse,
        scratch=[factor, square],
        aliases={1: 0, 2: 1, 3: 2},
        cost=3.0,
    )
    state = call(
        restore_order, (shape_of(comps, rows, cols, modes),), state, specs=[VMEM], cost=2.0
    )[0]
    height = comps * rows * cols // TILES
    tiled = shape_of(TILES, height, modes)
    mine, other = sum_devices(kept, sent)
    out, logs = call(
        finish,
        (tiled, shape_of(1, modes)),
        par,
        mine,
        other,
        logs,
        state.reshape(TILES, height, modes),
        out_specs=(HBM, VMEM),
        scratch=[
            square,
            square,
            board,
            factor,
            pltpu.VMEM((TILES, height, modes), jnp.float32),
            pltpu.SemaphoreType.DMA((TILES,)),
        ],
    )
    return out.reshape(tangents.shape), logs.reshape(modes)


def solution(mesh):
    placed = (P(None, "row", "col", None), P("row", "col"), P("row", "col"), P("row", "col"))
    return jax.shard_map(
        body,
        mesh=mesh,
        in_specs=placed,
        out_specs=(P(None, "row", "col", None), P()),
        check_vma=False,
    )
```

```python
import functools

import jax
import jax.numpy as jnp
from jax import lax
from jax.experimental import pallas as pl
from jax.experimental.pallas import tpu as pltpu
from jax.sharding import PartitionSpec as P

STEPS = 2
RENORMS = 2
LEVELS = 50

viscosity = 0.15
gravity = 0.5
rotation = 0.4

SUB = 8
LANES = 128
FIELDS = 3
HALO = STEPS * RENORMS
SIDE = STEPS
TILES = 12
VMEM_LIMIT = 16 * 1024 * 1024

HBM = pl.BlockSpec(memory_space=pltpu.HBM)
VMEM = pl.BlockSpec(memory_space=pltpu.VMEM)
SMEM = pl.BlockSpec(memory_space=pltpu.SMEM)


def params():
    return pltpu.CompilerParams(vmem_limit_bytes=VMEM_LIMIT)


def shape_of(*dims):
    return jax.ShapeDtypeStruct(dims, jnp.float32)


def lane_spread(block, lane):
    return jnp.broadcast_to(block[:, lane : lane + 1], (block.shape[0], LANES))


def fetch(sources, places, sems):
    copies = [
        pltpu.make_async_copy(source, place, sems.at[i])
        for i, (source, place) in enumerate(zip(sources, places))
    ]
    for copy in copies:
        copy.start()
    return copies


def finish_all(copies):
    for copy in copies:
        copy.wait()


def fields_of(sea_ref, levels_ref, current_ref):
    return (
        sea_ref[...].astype(jnp.float32),
        0.5 * current_ref[...],
        0.5 * ((levels_ref[...] + 1).astype(jnp.float32) / LEVELS),
    )


def sides_of(par):
    odd_row, odd_col = par[0] % 2, par[1] % 2
    return (1 - odd_row, odd_row), (1 - odd_col, odd_col)


def pack_rows(
    par, t_ref, sea_ref, levels_ref, current_ref, row_a, row_b, sea, levels, current, wide, sems, field_sems
):
    comps, rows, cols, _ = t_ref.shape
    norths, _ = sides_of(par)
    field_copies = fetch((sea_ref, levels_ref, current_ref), (sea, levels, current), field_sems)
    slots = [(slot, msg, comp) for slot, msg in ((0, row_a), (1, row_b)) for comp in range(comps)]
    copies = fetch(
        [t_ref.at[comp, pl.ds(norths[slot] * (rows - HALO), HALO)] for slot, _, comp in slots],
        [msg.at[pl.ds(comp * HALO, HALO)] for _, msg, comp in slots],
        sems,
    )
    lane = lax.broadcasted_iota(jnp.int32, (cols, LANES), 1)
    wide[...] = jnp.zeros_like(wide)
    packed = [jnp.zeros((cols, LANES), jnp.float32)] * 2
    finish_all(field_copies)
    for field, value in enumerate(fields_of(sea, levels, current)):
        wide[:, pl.ds(0, rows)] = value
        whole = wide[...]
        for north in (0, 1):
            shift = (field * SUB - north * (rows - HALO)) % LANES
            moved = pltpu.roll(whole, shift, 1) if shift else whole
            here = (lane >= field * SUB) & (lane < field * SUB + HALO)
            packed[north] = jnp.where(here, moved, packed[north])
    for slot, msg in ((0, row_a), (1, row_b)):
        msg[comps * HALO] = jnp.where(norths[slot] == 1, packed[1], packed[0])
    finish_all(copies)


def spread_fields(
    total_rows, par, t_ref, sea_ref, levels_ref, current_ref, state, coef, wide, spin, block, sea, levels, current, sems, field_sems
):
    comps, rows, cols, _ = t_ref.shape
    field_copies = fetch((sea_ref, levels_ref, current_ref), (sea, levels, current), field_sems)
    copies = fetch(
        [t_ref.at[comp] for comp in range(comps)], [block.at[comp] for comp in range(comps)], sems
    )
    line = lax.broadcasted_iota(jnp.int32, spin.shape, 0)
    line = jnp.where(line < rows + HALO, line, line - (rows + 2 * HALO))
    latitude = (par[0] * rows + line).astype(jnp.float32)
    angle = (-70.0 + 140.0 * (latitude + 0.5) / total_rows) * (jnp.pi / 180.0)
    spin[...] = rotation * jnp.sin(angle)
    wide[...] = jnp.zeros_like(wide)
    finish_all(field_copies)
    for field, value in enumerate(fields_of(sea, levels, current)):
        wide[field, :, pl.ds(0, rows)] = value
        natural = jnp.transpose(wide[field])[:rows]
        for lon in range(cols):
            coef[field, SIDE + lon, pl.ds(0, rows), :] = lane_spread(natural, lon)
    for comp in range(comps):
        copies[comp].wait()
        for row in range(0, rows, SUB):
            cells = block[comp, pl.ds(row, SUB)]
            state[comp, pl.ds(SIDE, cols), pl.ds(row, SUB), :] = jnp.transpose(cells, (1, 0, 2))


def column_at(east, cols, depth):
    return SIDE + depth + east * (cols - 1 - 2 * depth)


def send_columns(par, state, cols_sent):
    comps, wide, tall, _ = state.shape
    _, easts = sides_of(par)
    for slot, msg in enumerate(cols_sent):
        for comp in range(comps):
            for j in range(SIDE):
                column = column_at(easts[slot], wide - 2 * SIDE, j)
                msg[pl.ds((comp * SIDE + j) * tall, tall), :] = state[comp, column]


def join_rows(par, state_in, coef_in, wide, row_a, row_b, state, coef, col_a, col_b):
    comps, length, tall, _ = state.shape
    cols, rows = length - 2 * SIDE, tall - 2 * HALO
    norths, easts = sides_of(par)
    flat = state.reshape(comps * length * tall, LANES)
    for slot, msg in ((0, row_a), (1, row_b)):
        line = rows + HALO * (1 - norths[slot])
        for comp in range(comps):
            for h in range(HALO):
                for lon in range(0, cols, SUB):
                    at = (comp * length + SIDE + lon) * tall + line + h
                    flat[pl.ds(at, SUB, stride=tall), :] = msg[comp * HALO + h, pl.ds(lon, SUB), :]
    lane = lax.broadcasted_iota(jnp.int32, (cols, LANES), 1)
    north = jnp.where(norths[0] == 1, row_a[comps * HALO], row_b[comps * HALO])
    south = jnp.where(norths[0] == 1, row_b[comps * HALO], row_a[comps * HALO])
    beyond = jnp.where(lane % SUB < HALO, north, pltpu.roll(south, HALO, 1))
    natural = jnp.transpose(beyond)
    for field in range(FIELDS):
        block = natural[field * SUB : (field + 1) * SUB]
        for lon in range(cols):
            coef[field, SIDE + lon, pl.ds(rows, SUB), :] = lane_spread(block, lon)
    tail = comps * SIDE * tall
    whole = [
        jnp.where(lane < rows, wide[field], pltpu.roll(beyond, rows - field * SUB, 1))
        for field in range(FIELDS)
    ]
    for slot, msg in ((0, col_a), (1, col_b)):
        msg[pl.ds(tail, SUB), :] = jnp.zeros((SUB, LANES), jnp.float32)
        for field in range(FIELDS):
            msg[pl.ds(tail + field, 1), :] = jnp.where(
                easts[slot] == 1, whole[field][cols - 1 :], whole[field][:1]
            )
    send_columns(par, state, (col_a, col_b))


def model(own, x_diff, x_sum, above, below, sea, flow, depth, spin):
    keep, half = 1.0 - 4.0 * viscosity, 0.5 * gravity
    mixed = [
        keep * c + viscosity * (x + (n + s)) - flow * d
        for c, d, x, n, s in zip(own, x_diff, x_sum, above, below)
    ]
    v_y, h_y = above[1] - below[1], above[2] - below[2]
    return (
        sea * (mixed[0] - half * x_diff[2] + spin * own[1]),
        sea * (mixed[1] - half * h_y - spin * own[0]),
        sea * (mixed[2] - depth * (x_diff[0] + v_y)),
    )


def advance_column(source, target, coef_ref, spin_ref, lon):
    comps, length, tall, _ = source.shape
    flat = source.reshape(comps * length * tall, LANES)
    sub = lax.broadcasted_iota(jnp.int32, (SUB, LANES), 0)
    tiles = tall // SUB
    for tile in range(tiles):
        lines = pl.ds(SUB * tile, SUB)
        own, east, west = (
            [source[comp, lon + shift, lines, :] for comp in range(comps)] for shift in (0, 1, -1)
        )
        starts = [(comp * length + lon) * tall + SUB * tile for comp in range(comps)]
        if tile < tiles - 1:
            above = [flat[pl.ds(start + 1, SUB), :] for start in starts]
        else:
            wrap = [source[comp, lon, pl.ds(0, SUB), :] for comp in range(comps)]
            above = [
                jnp.where(sub == SUB - 1, pltpu.roll(w, SUB - 1, 0), pltpu.roll(o, SUB - 1, 0))
                for w, o in zip(wrap, own)
            ]
        if tile > 0:
            below = [flat[pl.ds(start - 1, SUB), :] for start in starts]
        else:
            wrap = [source[comp, lon, pl.ds(tall - SUB, SUB), :] for comp in range(comps)]
            below = [
                jnp.where(sub == 0, pltpu.roll(w, 1, 0), pltpu.roll(o, 1, 0))
                for w, o in zip(wrap, own)
            ]
        new = model(
            own,
            [e - w for e, w in zip(east, west)],
            [e + w for e, w in zip(east, west)],
            above,
            below,
            *(coef_ref[field, lon, lines, :] for field in range(FIELDS)),
            spin_ref[lines, :],
        )
        for comp in range(comps):
            target[comp, lon, lines, :] = new[comp]


def apply_inside(step, source, coef_ref, spin_ref, target):
    first = SIDE + step + 1
    count = source.shape[1] - 2 * first

    @pl.loop(0, count // 2)
    def _(pair):
        advance_column(source, target, coef_ref, spin_ref, first + 2 * pair)
        advance_column(source, target, coef_ref, spin_ref, first + 2 * pair + 1)


def mend_columns(par, states, coef_ref, spin_ref, cols_got):
    comps, length, tall, _ = states[0].shape
    _, easts = sides_of(par)
    for slot, msg in enumerate(cols_got):
        for comp in range(comps):
            for j in range(SIDE):
                column = column_at(easts[slot], length - 2 * SIDE, -1 - j)
                states[0][comp, column] = msg[pl.ds((comp * SIDE + j) * tall, tall), :]
    for step in range(STEPS):
        first = step + 1
        skip = length - 2 * first - 2 * SIDE

        @pl.loop(0, 2 * SIDE)
        def _(i):
            lon = first + i + (i // SIDE) * skip
            advance_column(states[step], states[step + 1], coef_ref, spin_ref, lon)


def join_gram(
    scale, par, start_in, middle_in, state_in, coef_in, spin_ref, a, b, start, middle, state, coef, col_a, col_b, kept, sent, total
):
    _, length, tall, _ = state.shape
    _, easts = sides_of(par)
    for slot, msg in enumerate((a, b)):
        upright = jnp.transpose(msg[pl.ds(msg.shape[0] - SUB, SUB), :])
        for field in range(FIELDS):
            column = column_at(easts[slot], length - 2 * SIDE, -1)
            coef[field, column] = lane_spread(upright[:tall], field)
    mend_columns(par, (start, middle, state), coef, spin_ref, (a, b))
    send_columns(par, state, (col_a, col_b))
    gram = sum(gram_of(*split_halves(cells)) for _, _, cells in tiles_of(state))
    write_halves(par, gram, scale, kept, sent, total)


def tiles_of(state):
    comps, length, tall, _ = state.shape
    rows = tall - 2 * HALO
    for comp in range(comps):
        for lon in range(0, length - 2 * SIDE, SUB):
            cells = state[comp, pl.ds(SIDE + lon, SUB), pl.ds(0, rows), :]
            yield comp, lon, cells.reshape(SUB * rows, LANES)


def split_halves(value):
    high = value.astype(jnp.bfloat16)
    return high, (value - high.astype(jnp.float32)).astype(jnp.bfloat16)


def gram_of(high, low):
    return lax.dot_general(
        high,
        jnp.concatenate([high, low], axis=1),
        (((0,), (0,)), ((), ())),
        preferred_element_type=jnp.float32,
    )


def write_halves(par, gram, scale, kept, sent, total):
    half, rows = LANES // 2, kept.shape[0]
    mixed = gram[:, LANES:]
    whole = scale * (gram[:, :LANES] + (mixed + jnp.transpose(mixed)))
    row = lax.broadcasted_iota(jnp.int32, (half, LANES), 0)
    col = lax.broadcasted_iota(jnp.int32, (half, LANES), 1)
    total[pl.ds(0, half), :] = jnp.where(
        (col < half) | (col - half > row), whole[half:], pltpu.roll(whole[:half], half, 1)
    )
    row = lax.broadcasted_iota(jnp.int32, (LANES, LANES), 0)
    col = lax.broadcasted_iota(jnp.int32, (LANES, LANES), 1)
    total[pl.ds(half, 2 * rows - half), :] = jnp.zeros((2 * rows - half, LANES), jnp.float32)
    total[pl.ds(half, 1), :] = jnp.sum(jnp.where(row == col, whole, 0.0), axis=0, keepdims=True)
    odd = par[1] % 2
    kept[...] = total[pl.ds(odd * rows, rows), :]
    sent[...] = total[pl.ds((1 - odd) * rows, rows), :]


def factor_pair(low, p):
    q, size = p + 1, len(low)
    a, b, c = low[p][p], low[q][p], low[q][q]
    root_a, root_det = lax.rsqrt(a), lax.rsqrt(a * c - b * b)
    both = root_a * root_det
    turned = [a * low[i][q] - b * low[i][p] for i in range(q + 1, size)]
    low[q][p] = b * root_a
    for i, value in zip(range(q + 1, size), turned):
        low[i][p] = low[i][p] * root_a
        low[i][q] = value * both
    for i in range(q + 1, size):
        for m in range(q + 1, i + 1):
            low[i][m] = (low[i][m] - low[i][p] * low[m][p]) - low[i][q] * low[m][q]
    return root_a, a * both


def invert_factor(gram, work, board):
    count = LANES // SUB
    lane = lax.broadcasted_iota(jnp.int32, (SUB, LANES), 1)
    sub = lax.broadcasted_iota(jnp.int32, (SUB, LANES), 0)
    rows = [gram[SUB * i : SUB * (i + 1)] for i in range(count)]
    for block in range(count):
        base = SUB * block
        here = (lane >= base) & (lane < base + SUB)
        shelf = 2 * SUB * base
        for l in range(SUB):
            board[pl.ds(shelf + SUB * l, SUB), :] = lane_spread(rows[block], base + l)
        low = [
            [board[pl.ds(shelf + SUB * l + k, SUB, stride=0), :] for l in range(k + 1)]
            for k in range(SUB)
        ]
        shelf += SUB * SUB
        board[pl.ds(shelf, SUB), :] = jnp.where(
            here, jnp.where(lane - base == sub, 1.0, 0.0), rows[block]
        )
        inv = []
        for p in range(0, SUB, 2):
            inv.extend(factor_pair(low, p))
        scaled = []
        for k in range(SUB):
            line = board[pl.ds(shelf + k, SUB, stride=0), :]
            for l in range(k):
                line = line - low[k][l] * scaled[l]
            scaled.append(line * inv[k])
        merged = scaled[0]
        for k in range(1, SUB):
            merged = jnp.where(sub == k, scaled[k], merged)
        work[pl.ds(base, SUB), :] = merged
        for i in range(block + 1, count):
            weights = []
            rest = jnp.where(here, 0.0, rows[i])
            for l in range(SUB):
                weight = lane_spread(rows[i], base + l)
                for m in range(l):
                    weight = weight - weights[m] * low[l][m]
                weights.append(weight * inv[l])
            for l in range(SUB):
                rest = rest - weights[l] * scaled[l]
            rows[i] = rest


def factorize(par, mine_ref, other_ref, gram, work, board):
    half, rows = LANES // 2, mine_ref.shape[0]
    odd = par[1] % 2
    gram[pl.ds(odd * rows, rows), :] = mine_ref[...]
    gram[pl.ds((1 - odd) * rows, rows), :] = other_ref[...]
    packed, diagonal = gram[pl.ds(0, half), :], gram[pl.ds(half, 1), :]
    row = lax.broadcasted_iota(jnp.int32, (half, LANES), 0)
    col = lax.broadcasted_iota(jnp.int32, (half, LANES), 1)
    triangles = jnp.concatenate(
        [
            jnp.where(col < row, pltpu.roll(packed, half, 1), 0.0),
            jnp.where((col < half) | (col - half > row), packed, 0.0),
        ],
        axis=0,
    )
    row = lax.broadcasted_iota(jnp.int32, (LANES, LANES), 0)
    col = lax.broadcasted_iota(jnp.int32, (LANES, LANES), 1)
    size = jnp.broadcast_to(lax.rsqrt(diagonal), (LANES, LANES))
    whole = jnp.where(row == col, diagonal, triangles + jnp.transpose(triangles))
    invert_factor((whole * size) * jnp.transpose(size), work, board)
    inverse = jnp.where(row >= col, work[...], 0.0) * size
    diagonal = jnp.sum(jnp.where(row == col, inverse, 0.0), axis=0, keepdims=True)
    return inverse, diagonal


def paired(inverse):
    high = inverse.astype(jnp.bfloat16)
    low = (inverse - high.astype(jnp.float32)).astype(jnp.bfloat16)
    return jnp.concatenate(
        [jnp.concatenate([high, high], axis=1), jnp.concatenate([low, low], axis=1)], axis=0
    )


def times_factor(cells, factor):
    pair = jnp.concatenate(split_halves(cells), axis=1)
    both = lax.dot_general(
        pair, factor, (((1,), (1,)), ((), ())), preferred_element_type=jnp.float32
    )
    return both[:, :LANES] + both[:, LANES:]


def factor_only(par, mine_ref, other_ref, prior_ref, inverse_ref, logs_ref, gram, work, board):
    inverse, diagonal = factorize(par, mine_ref, other_ref, gram, work, board)
    inverse_ref[...] = inverse
    logs_ref[...] = prior_ref[...] - jnp.log(diagonal)


def join_update(
    scale, par, start_in, middle_in, state_in, coef_ref, spin_ref, a, b, inverse_ref, start, middle, state, out_ref, kept, sent, factor, total
):
    factor[...] = paired(inverse_ref[...])
    mend_columns(par, (start, middle, state), coef_ref, spin_ref, (a, b))
    gram = 0.0
    for comp, lon, cells in tiles_of(state):
        new = times_factor(cells, factor[...])
        out_ref[comp, pl.ds(lon, SUB)] = new.reshape((SUB,) + out_ref.shape[2:])
        gram += gram_of(*split_halves(new))
    write_halves(par, gram, scale, kept, sent, total)


def restore_order(turned, out_ref):
    comps, cols, _, _ = turned.shape
    for comp in range(comps):
        for lon in range(0, cols, SUB):
            cells = turned[comp, pl.ds(lon, SUB)]
            out_ref[comp, :, pl.ds(lon, SUB), :] = jnp.transpose(cells, (1, 0, 2))


def finish(
    par, mine_ref, other_ref, prior_ref, t_ref, out_ref, logs_ref, gram, work, board, factor, fresh, sems
):
    inverse, diagonal = factorize(par, mine_ref, other_ref, gram, work, board)
    logs_ref[...] = prior_ref[...] - jnp.log(diagonal)
    factor[...] = paired(inverse)

    def out_copy(tile):
        return pltpu.make_async_copy(fresh.at[tile], out_ref.at[tile], sems.at[tile])

    for tile in range(TILES):
        fresh[tile] = times_factor(t_ref[tile], factor[...])
        out_copy(tile).start(priority=tile % 2)

    for tile in range(TILES):
        out_copy(tile).wait()


def swap_pairs(near_value, far_value, axis, closed):
    count = lax.axis_size(axis)
    near = [(i, i ^ 1) for i in range(count)]
    far = [(i, (i + 1 if i % 2 else i - 1) % count) for i in range(count)]
    if not closed:
        far = far[1:-1]
    return lax.ppermute(near_value, axis, near), lax.ppermute(far_value, axis, far)


def swapped(value, axis, mask):
    return lax.ppermute(value, axis, [(i, i ^ mask) for i in range(lax.axis_size(axis))])


def add_four(first, second, third, fourth, *rest):
    out_ref = rest[len(rest) // 2]
    out_ref[...] = (first[...] + second[...]) + (third[...] + fourth[...])


def sum_over(value, axis, first_bit, beside=None, held=()):
    bits = lax.axis_size(axis).bit_length() - 1
    while first_bit < bits:
        low = 1 << first_bit
        if first_bit + 1 < bits:
            high = low << 1
            one, two, three = (swapped(value, axis, mask) for mask in (low, high, low | high))
            if beside is None:
                value = (value + one) + (two + three)
            else:
                anywhere = pl.BlockSpec(memory_space=pl.ANY)
                value, *held = pl.pallas_call(
                    add_four,
                    out_shape=[jax.ShapeDtypeStruct(x.shape, x.dtype) for x in (value, *held)],
                    in_specs=[VMEM] * 4 + [anywhere] * (1 + len(held)),
                    out_specs=[VMEM] + [anywhere] * len(held),
                    input_output_aliases={5 + i: 1 + i for i in range(len(held))},
                    compiler_params=params(),
                )(value, one, two, three, beside, *held)
                beside = None
            first_bit += 2
        else:
            value = value + swapped(value, axis, low)
            first_bit += 1
    return value, held


def sum_devices(kept, sent, beside=(None, None), held=()):
    mine = kept + swapped(sent, "col", 1)
    mine, held = sum_over(mine, "col", 1, beside[0], held)
    mine, _ = sum_over(mine, "row", 0, beside[1])
    return mine, swapped(mine, "col", 1), held


def body(tangents, sea_mask, levels, current):
    comps, rows, cols, modes = tangents.shape
    total_rows = rows * lax.axis_size("row")
    total_cells = total_rows * cols * lax.axis_size("col")
    scale = 1.0 / total_cells
    row_at, col_at = lax.axis_index("row"), lax.axis_index("col")
    par = jnp.stack([row_at, col_at]).astype(jnp.int32)

    tall, length = rows + 2 * HALO, cols + 2 * SIDE

    block = shape_of(comps, length, tall, modes)
    coefs = shape_of(FIELDS, length, tall, LANES)
    columns = (shape_of(comps * SIDE * tall, modes),) * 2
    first_columns = (shape_of(comps * SIDE * tall + SUB, modes),) * 2
    rows_sent = (shape_of(comps * HALO + 1, cols, modes),) * 2
    halves = (shape_of(modes // 4 + SUB, modes),) * 2
    square = pltpu.VMEM((modes, modes), jnp.float32)
    board = pltpu.VMEM((2 * SUB * modes, LANES), jnp.float32)
    factor = pltpu.VMEM((2 * modes, 2 * modes), jnp.bfloat16)

    def call(
        kernel, outs, *operands, specs=None, out_specs=None, scratch=(), aliases=None, cost=1.0
    ):
        return pl.pallas_call(
            kernel,
            out_shape=outs,
            in_specs=specs or [SMEM] + [VMEM] * (len(operands) - 1),
            out_specs=out_specs or (VMEM,) * len(outs),
            scratch_shapes=scratch,
            input_output_aliases=aliases or {},
            compiler_params=params(),
            cost_estimate=pl.CostEstimate(
                flops=int(cost * 1e9), bytes_accessed=int(cost * 3e6), transcendentals=0
            ),
        )(*operands)

    def inside(step, state):
        kernel = functools.partial(apply_inside, step)
        return call(kernel, (block,), state, coef, spin, specs=[VMEM] * 3, cost=2.0)[0]

    def swap_columns(packed):
        return swap_pairs(*packed, "col", True)

    source, *fields = (
        pltpu.with_memory_space_constraint(x, pltpu.HBM)
        for x in (tangents, sea_mask.T, levels.T, current.T)
    )
    upright = [pltpu.VMEM(x.shape, x.dtype) for x in fields]
    packed = call(
        pack_rows,
        rows_sent,
        par,
        source,
        *fields,
        specs=[SMEM] + [HBM] * 4,
        scratch=upright
        + [
            pltpu.VMEM((cols, LANES), jnp.float32),
            pltpu.SemaphoreType.DMA((2 * comps,)),
            pltpu.SemaphoreType.DMA((FIELDS,)),
        ],
    )
    row_halos = swap_pairs(*packed, "row", False)
    start, coef, wide, spin = call(
        functools.partial(spread_fields, total_rows),
        (block, coefs, shape_of(FIELDS, cols, LANES), shape_of(tall, LANES)),
        par,
        source,
        *fields,
        specs=[SMEM] + [HBM] * 4,
        scratch=[pltpu.VMEM(tangents.shape, jnp.float32)]
        + upright
        + [pltpu.SemaphoreType.DMA((comps,)), pltpu.SemaphoreType.DMA((FIELDS,))],
        cost=3.0,
    )
    start, coef, *packed = call(
        join_rows,
        (block, coefs) + first_columns,
        par,
        start,
        coef,
        wide,
        *row_halos,
        aliases={1: 0, 2: 1},
    )
    logs = jnp.zeros((1, modes), jnp.float32)

    halos = swap_columns(packed)
    middle = inside(0, start)
    state = inside(1, middle)
    _, _, start, coef, *packed, kept, sent = call(
        functools.partial(join_gram, scale),
        (block, block, block, coefs) + columns + halves,
        par,
        start,
        middle,
        state,
        coef,
        spin,
        *halos,
        scratch=[square],
        aliases={1: 0, 2: 1, 3: 2, 4: 3},
        cost=2.0,
    )
    middle = inside(0, start)
    state = inside(1, middle)
    mine, other, packed = sum_devices(kept, sent, (middle, state), packed)
    halos = swap_columns(packed)
    inverse, logs = call(
        factor_only,
        (shape_of(modes, modes), shape_of(1, modes)),
        par,
        mine,
        other,
        logs,
        scratch=[square, square, board],
        cost=0.01,
    )
    _, _, _, state, kept, sent = call(
        functools.partial(join_update, scale),
        (block, block, block, shape_of(comps, cols, rows, modes)) + halves,
        par,
        start,
        middle,
        state,
        coef,
        spin,
        *halos,
        inverse,
        scratch=[factor, square],
        aliases={1: 0, 2: 1, 3: 2},
        cost=3.0,
    )
    state = call(
        restore_order, (shape_of(comps, rows, cols, modes),), state, specs=[VMEM], cost=2.0
    )[0]
    height = comps * rows * cols // TILES
    tiled = shape_of(TILES, height, modes)
    mine, other, _ = sum_devices(kept, sent)
    out, logs = call(
        finish,
        (tiled, shape_of(1, modes)),
        par,
        mine,
        other,
        logs,
        state.reshape(TILES, height, modes),
        out_specs=(HBM, VMEM),
        scratch=[
            square,
            square,
            board,
            factor,
            pltpu.VMEM((TILES, height, modes), jnp.float32),
            pltpu.SemaphoreType.DMA((TILES,)),
        ],
    )
    return out.reshape(tangents.shape), logs.reshape(modes)


def solution(mesh):
    placed = (P(None, "row", "col", None), P("row", "col"), P("row", "col"), P("row", "col"))
    return jax.shard_map(
        body,
        mesh=mesh,
        in_specs=placed,
        out_specs=(P(None, "row", "col", None), P()),
        check_vma=False,
    )
```

```python
import functools

import jax
import jax.numpy as jnp
from jax import lax
from jax.experimental import pallas as pl
from jax.experimental.pallas import tpu as pltpu
from jax.sharding import PartitionSpec as P

STEPS = 2
RENORMS = 2
LEVELS = 50

viscosity = 0.15
gravity = 0.5
rotation = 0.4

SUB = 8
LANES = 128
FIELDS = 3
HALO = STEPS * RENORMS
SIDE = STEPS
TILES = 12
VMEM_LIMIT = 16 * 1024 * 1024

HBM = pl.BlockSpec(memory_space=pltpu.HBM)
VMEM = pl.BlockSpec(memory_space=pltpu.VMEM)
SMEM = pl.BlockSpec(memory_space=pltpu.SMEM)


def params():
    return pltpu.CompilerParams(vmem_limit_bytes=VMEM_LIMIT)


def shape_of(*dims):
    return jax.ShapeDtypeStruct(dims, jnp.float32)


def lane_spread(block, lane):
    return jnp.broadcast_to(block[:, lane : lane + 1], (block.shape[0], LANES))


def fetch(sources, places, sems):
    copies = [
        pltpu.make_async_copy(source, place, sems.at[i])
        for i, (source, place) in enumerate(zip(sources, places))
    ]
    for copy in copies:
        copy.start()
    return copies


def finish_all(copies):
    for copy in copies:
        copy.wait()


def fields_of(sea_ref, levels_ref, current_ref):
    return (
        sea_ref[...].astype(jnp.float32),
        0.5 * current_ref[...],
        0.5 * ((levels_ref[...] + 1).astype(jnp.float32) / LEVELS),
    )


def sides_of(par):
    odd_row, odd_col = par[0] % 2, par[1] % 2
    return (1 - odd_row, odd_row), (1 - odd_col, odd_col)


def pack_rows(
    par, t_ref, sea_ref, levels_ref, current_ref, row_a, row_b, sea, levels, current, wide, sems, field_sems
):
    comps, rows, cols, _ = t_ref.shape
    norths, _ = sides_of(par)
    field_copies = fetch((sea_ref, levels_ref, current_ref), (sea, levels, current), field_sems)
    slots = [(slot, msg, comp) for slot, msg in ((0, row_a), (1, row_b)) for comp in range(comps)]
    copies = fetch(
        [t_ref.at[comp, pl.ds(norths[slot] * (rows - HALO), HALO)] for slot, _, comp in slots],
        [msg.at[pl.ds(comp * HALO, HALO)] for _, msg, comp in slots],
        sems,
    )
    lane = lax.broadcasted_iota(jnp.int32, (cols, LANES), 1)
    wide[...] = jnp.zeros_like(wide)
    packed = [jnp.zeros((cols, LANES), jnp.float32)] * 2
    finish_all(field_copies)
    for field, value in enumerate(fields_of(sea, levels, current)):
        wide[:, pl.ds(0, rows)] = value
        whole = wide[...]
        for north in (0, 1):
            shift = (field * SUB - north * (rows - HALO)) % LANES
            moved = pltpu.roll(whole, shift, 1) if shift else whole
            here = (lane >= field * SUB) & (lane < field * SUB + HALO)
            packed[north] = jnp.where(here, moved, packed[north])
    for slot, msg in ((0, row_a), (1, row_b)):
        msg[comps * HALO] = jnp.where(norths[slot] == 1, packed[1], packed[0])
    finish_all(copies)


def spread_fields(
    total_rows, par, t_ref, sea_ref, levels_ref, current_ref, state, coef, wide, spin, block, sea, levels, current, sems, field_sems
):
    comps, rows, cols, _ = t_ref.shape
    field_copies = fetch((sea_ref, levels_ref, current_ref), (sea, levels, current), field_sems)
    copies = fetch(
        [t_ref.at[comp] for comp in range(comps)], [block.at[comp] for comp in range(comps)], sems
    )
    line = lax.broadcasted_iota(jnp.int32, spin.shape, 0)
    line = jnp.where(line < rows + HALO, line, line - (rows + 2 * HALO))
    latitude = (par[0] * rows + line).astype(jnp.float32)
    angle = (-70.0 + 140.0 * (latitude + 0.5) / total_rows) * (jnp.pi / 180.0)
    spin[...] = rotation * jnp.sin(angle)
    wide[...] = jnp.zeros_like(wide)
    finish_all(field_copies)
    for field, value in enumerate(fields_of(sea, levels, current)):
        wide[field, :, pl.ds(0, rows)] = value
        natural = jnp.transpose(wide[field])[:rows]
        for lon in range(cols):
            coef[field, SIDE + lon, pl.ds(0, rows), :] = lane_spread(natural, lon)
    for comp in range(comps):
        copies[comp].wait()
        for row in range(0, rows, SUB):
            cells = block[comp, pl.ds(row, SUB)]
            state[comp, pl.ds(SIDE, cols), pl.ds(row, SUB), :] = jnp.transpose(cells, (1, 0, 2))


def column_at(east, cols, depth):
    return SIDE + depth + east * (cols - 1 - 2 * depth)


def send_columns(par, state, cols_sent):
    comps, wide, tall, _ = state.shape
    _, easts = sides_of(par)
    for slot, msg in enumerate(cols_sent):
        for comp in range(comps):
            for j in range(SIDE):
                column = column_at(easts[slot], wide - 2 * SIDE, j)
                msg[pl.ds((comp * SIDE + j) * tall, tall), :] = state[comp, column]


def join_rows(par, state_in, coef_in, wide, row_a, row_b, state, coef, col_a, col_b):
    comps, length, tall, _ = state.shape
    cols, rows = length - 2 * SIDE, tall - 2 * HALO
    norths, easts = sides_of(par)
    flat = state.reshape(comps * length * tall, LANES)
    for slot, msg in ((0, row_a), (1, row_b)):
        line = rows + HALO * (1 - norths[slot])
        for comp in range(comps):
            for h in range(HALO):
                for lon in range(0, cols, SUB):
                    at = (comp * length + SIDE + lon) * tall + line + h
                    flat[pl.ds(at, SUB, stride=tall), :] = msg[comp * HALO + h, pl.ds(lon, SUB), :]
    lane = lax.broadcasted_iota(jnp.int32, (cols, LANES), 1)
    north = jnp.where(norths[0] == 1, row_a[comps * HALO], row_b[comps * HALO])
    south = jnp.where(norths[0] == 1, row_b[comps * HALO], row_a[comps * HALO])
    beyond = jnp.where(lane % SUB < HALO, north, pltpu.roll(south, HALO, 1))
    natural = jnp.transpose(beyond)
    for field in range(FIELDS):
        block = natural[field * SUB : (field + 1) * SUB]
        for lon in range(cols):
            coef[field, SIDE + lon, pl.ds(rows, SUB), :] = lane_spread(block, lon)
    tail = comps * SIDE * tall
    whole = [
        jnp.where(lane < rows, wide[field], pltpu.roll(beyond, rows - field * SUB, 1))
        for field in range(FIELDS)
    ]
    for slot, msg in ((0, col_a), (1, col_b)):
        msg[pl.ds(tail, SUB), :] = jnp.zeros((SUB, LANES), jnp.float32)
        for field in range(FIELDS):
            msg[pl.ds(tail + field, 1), :] = jnp.where(
                easts[slot] == 1, whole[field][cols - 1 :], whole[field][:1]
            )
    send_columns(par, state, (col_a, col_b))


def model(own, x_diff, x_sum, above, below, sea, flow, depth, spin):
    keep, half = 1.0 - 4.0 * viscosity, 0.5 * gravity
    mixed = [
        keep * c + viscosity * (x + (n + s)) - flow * d
        for c, d, x, n, s in zip(own, x_diff, x_sum, above, below)
    ]
    v_y, h_y = above[1] - below[1], above[2] - below[2]
    return (
        sea * (mixed[0] - half * x_diff[2] + spin * own[1]),
        sea * (mixed[1] - half * h_y - spin * own[0]),
        sea * (mixed[2] - depth * (x_diff[0] + v_y)),
    )


def advance_column(source, target, coef_ref, spin_ref, lon):
    comps, length, tall, _ = source.shape
    flat = source.reshape(comps * length * tall, LANES)
    sub = lax.broadcasted_iota(jnp.int32, (SUB, LANES), 0)
    tiles = tall // SUB
    for tile in range(tiles):
        lines = pl.ds(SUB * tile, SUB)
        own, east, west = (
            [source[comp, lon + shift, lines, :] for comp in range(comps)] for shift in (0, 1, -1)
        )
        starts = [(comp * length + lon) * tall + SUB * tile for comp in range(comps)]
        if tile < tiles - 1:
            above = [flat[pl.ds(start + 1, SUB), :] for start in starts]
        else:
            wrap = [source[comp, lon, pl.ds(0, SUB), :] for comp in range(comps)]
            above = [
                jnp.where(sub == SUB - 1, pltpu.roll(w, SUB - 1, 0), pltpu.roll(o, SUB - 1, 0))
                for w, o in zip(wrap, own)
            ]
        if tile > 0:
            below = [flat[pl.ds(start - 1, SUB), :] for start in starts]
        else:
            wrap = [source[comp, lon, pl.ds(tall - SUB, SUB), :] for comp in range(comps)]
            below = [
                jnp.where(sub == 0, pltpu.roll(w, 1, 0), pltpu.roll(o, 1, 0))
                for w, o in zip(wrap, own)
            ]
        new = model(
            own,
            [e - w for e, w in zip(east, west)],
            [e + w for e, w in zip(east, west)],
            above,
            below,
            *(coef_ref[field, lon, lines, :] for field in range(FIELDS)),
            spin_ref[lines, :],
        )
        for comp in range(comps):
            target[comp, lon, lines, :] = new[comp]


def apply_inside(step, source, coef_ref, spin_ref, target):
    first = SIDE + step + 1
    count = source.shape[1] - 2 * first

    @pl.loop(0, count // 2)
    def _(pair):
        advance_column(source, target, coef_ref, spin_ref, first + 2 * pair)
        advance_column(source, target, coef_ref, spin_ref, first + 2 * pair + 1)


def mend_columns(par, states, coef_ref, spin_ref, cols_got):
    comps, length, tall, _ = states[0].shape
    _, easts = sides_of(par)
    for slot, msg in enumerate(cols_got):
        for comp in range(comps):
            for j in range(SIDE):
                column = column_at(easts[slot], length - 2 * SIDE, -1 - j)
                states[0][comp, column] = msg[pl.ds((comp * SIDE + j) * tall, tall), :]
    for step in range(STEPS):
        first = step + 1
        skip = length - 2 * first - 2 * SIDE

        @pl.loop(0, 2 * SIDE)
        def _(i):
            lon = first + i + (i // SIDE) * skip
            advance_column(states[step], states[step + 1], coef_ref, spin_ref, lon)


def join_gram(
    scale, par, start_in, middle_in, state_in, coef_in, spin_ref, a, b, start, middle, state, coef, col_a, col_b, kept, sent, total
):
    _, length, tall, _ = state.shape
    _, easts = sides_of(par)
    for slot, msg in enumerate((a, b)):
        upright = jnp.transpose(msg[pl.ds(msg.shape[0] - SUB, SUB), :])
        for field in range(FIELDS):
            column = column_at(easts[slot], length - 2 * SIDE, -1)
            coef[field, column] = lane_spread(upright[:tall], field)
    mend_columns(par, (start, middle, state), coef, spin_ref, (a, b))
    send_columns(par, state, (col_a, col_b))
    gram = sum(gram_of(*split_halves(cells)) for _, _, cells in tiles_of(state))
    write_halves(par, gram, scale, kept, sent, total)


def tiles_of(state):
    comps, length, tall, _ = state.shape
    rows = tall - 2 * HALO
    for comp in range(comps):
        for lon in range(0, length - 2 * SIDE, SUB):
            cells = state[comp, pl.ds(SIDE + lon, SUB), pl.ds(0, rows), :]
            yield comp, lon, cells.reshape(SUB * rows, LANES)


def split_halves(value):
    high = value.astype(jnp.bfloat16)
    return high, (value - high.astype(jnp.float32)).astype(jnp.bfloat16)


def gram_of(high, low):
    return lax.dot_general(
        high,
        jnp.concatenate([high, low], axis=1),
        (((0,), (0,)), ((), ())),
        preferred_element_type=jnp.float32,
    )


def write_halves(par, gram, scale, kept, sent, total):
    half, rows = LANES // 2, kept.shape[0]
    mixed = gram[:, LANES:]
    whole = scale * (gram[:, :LANES] + (mixed + jnp.transpose(mixed)))
    row = lax.broadcasted_iota(jnp.int32, (half, LANES), 0)
    col = lax.broadcasted_iota(jnp.int32, (half, LANES), 1)
    total[pl.ds(0, half), :] = jnp.where(
        (col < half) | (col - half > row), whole[half:], pltpu.roll(whole[:half], half, 1)
    )
    row = lax.broadcasted_iota(jnp.int32, (LANES, LANES), 0)
    col = lax.broadcasted_iota(jnp.int32, (LANES, LANES), 1)
    total[pl.ds(half, 2 * rows - half), :] = jnp.zeros((2 * rows - half, LANES), jnp.float32)
    total[pl.ds(half, 1), :] = jnp.sum(jnp.where(row == col, whole, 0.0), axis=0, keepdims=True)
    odd = par[1] % 2
    kept[...] = total[pl.ds(odd * rows, rows), :]
    sent[...] = total[pl.ds((1 - odd) * rows, rows), :]


def factor_pair(low, p):
    q, size = p + 1, len(low)
    a, b, c = low[p][p], low[q][p], low[q][q]
    root_a, root_det = lax.rsqrt(a), lax.rsqrt(a * c - b * b)
    both = root_a * root_det
    turned = [a * low[i][q] - b * low[i][p] for i in range(q + 1, size)]
    low[q][p] = b * root_a
    for i, value in zip(range(q + 1, size), turned):
        low[i][p] = low[i][p] * root_a
        low[i][q] = value * both
    for i in range(q + 1, size):
        for m in range(q + 1, i + 1):
            low[i][m] = (low[i][m] - low[i][p] * low[m][p]) - low[i][q] * low[m][q]
    return root_a, a * both


def invert_factor(gram, work, board):
    count = LANES // SUB
    lane = lax.broadcasted_iota(jnp.int32, (SUB, LANES), 1)
    sub = lax.broadcasted_iota(jnp.int32, (SUB, LANES), 0)
    rows = [gram[SUB * i : SUB * (i + 1)] for i in range(count)]
    for block in range(count):
        base = SUB * block
        here = (lane >= base) & (lane < base + SUB)
        shelf = 2 * SUB * base
        for l in range(SUB):
            board[pl.ds(shelf + SUB * l, SUB), :] = lane_spread(rows[block], base + l)
        low = [
            [board[pl.ds(shelf + SUB * l + k, SUB, stride=0), :] for l in range(k + 1)]
            for k in range(SUB)
        ]
        shelf += SUB * SUB
        board[pl.ds(shelf, SUB), :] = jnp.where(
            here, jnp.where(lane - base == sub, 1.0, 0.0), rows[block]
        )
        inv = []
        for p in range(0, SUB, 2):
            inv.extend(factor_pair(low, p))
        scaled = []
        for k in range(SUB):
            line = board[pl.ds(shelf + k, SUB, stride=0), :]
            for l in range(k):
                line = line - low[k][l] * scaled[l]
            scaled.append(line * inv[k])
        merged = scaled[0]
        for k in range(1, SUB):
            merged = jnp.where(sub == k, scaled[k], merged)
        work[pl.ds(base, SUB), :] = merged
        turned = jnp.transpose(merged)
        for i in range(block + 1, count):
            rest = jnp.where(here, 0.0, rows[i])
            if i == block + 1:
                weights = []
                for l in range(SUB):
                    weight = lane_spread(rows[i], base + l)
                    for m in range(l):
                        weight = weight - weights[m] * low[l][m]
                    weights.append(weight * inv[l])
            else:
                weights = [lane_spread(turned[SUB * i : SUB * (i + 1)], l) for l in range(SUB)]
            for l in range(SUB):
                rest = rest - weights[l] * scaled[l]
            rows[i] = rest


def factorize(par, mine_ref, other_ref, gram, work, board):
    half, rows = LANES // 2, mine_ref.shape[0]
    odd = par[1] % 2
    gram[pl.ds(odd * rows, rows), :] = mine_ref[...]
    gram[pl.ds((1 - odd) * rows, rows), :] = other_ref[...]
    packed, diagonal = gram[pl.ds(0, half), :], gram[pl.ds(half, 1), :]
    row = lax.broadcasted_iota(jnp.int32, (half, LANES), 0)
    col = lax.broadcasted_iota(jnp.int32, (half, LANES), 1)
    triangles = jnp.concatenate(
        [
            jnp.where(col < row, pltpu.roll(packed, half, 1), 0.0),
            jnp.where((col < half) | (col - half > row), packed, 0.0),
        ],
        axis=0,
    )
    row = lax.broadcasted_iota(jnp.int32, (LANES, LANES), 0)
    col = lax.broadcasted_iota(jnp.int32, (LANES, LANES), 1)
    size = jnp.broadcast_to(lax.rsqrt(diagonal), (LANES, LANES))
    whole = jnp.where(row == col, diagonal, triangles + jnp.transpose(triangles))
    invert_factor((whole * size) * jnp.transpose(size), work, board)
    inverse = jnp.where(row >= col, work[...], 0.0) * size
    diagonal = jnp.sum(jnp.where(row == col, inverse, 0.0), axis=0, keepdims=True)
    return inverse, diagonal


def paired(inverse):
    high = inverse.astype(jnp.bfloat16)
    low = (inverse - high.astype(jnp.float32)).astype(jnp.bfloat16)
    return jnp.concatenate(
        [jnp.concatenate([high, high], axis=1), jnp.concatenate([low, low], axis=1)], axis=0
    )


def times_factor(pair, factor):
    both = lax.dot_general(
        pair, factor, (((1,), (1,)), ((), ())), preferred_element_type=jnp.float32
    )
    return both[:, :LANES] + both[:, LANES:]


def factor_only(par, mine_ref, other_ref, prior_ref, _, inverse_ref, logs_ref, gram, work, board):
    inverse, diagonal = factorize(par, mine_ref, other_ref, gram, work, board)
    inverse_ref[...] = inverse
    logs_ref[...] = prior_ref[...] - jnp.log(diagonal)


def mend_only(par, start_in, middle_in, state_in, coef_ref, spin_ref, a, b, start, middle, state):
    mend_columns(par, (start, middle, state), coef_ref, spin_ref, (a, b))


def update(scale, par, state, inverse_ref, out_ref, kept, sent, factor, total):
    factor[...] = paired(inverse_ref[...])
    gram = 0.0
    for comp, lon, cells in tiles_of(state):
        new = times_factor(jnp.concatenate(split_halves(cells), axis=1), factor[...])
        out_ref[comp, pl.ds(lon, SUB)] = new.reshape((SUB,) + out_ref.shape[2:])
        gram += gram_of(*split_halves(new))
    write_halves(par, gram, scale, kept, sent, total)


def restore_order(turned, out_ref):
    comps, cols, _, _ = turned.shape
    for comp in range(comps):
        for lon in range(0, cols, 2 * SUB):
            cells = jnp.concatenate(
                [
                    jnp.transpose(turned[comp, pl.ds(lon + shift, SUB)], (1, 0, 2))
                    for shift in (0, SUB)
                ],
                axis=1,
            )
            high = cells.astype(jnp.bfloat16)
            low = (cells - high.astype(jnp.float32)).astype(jnp.bfloat16)
            out_ref[comp, :, pl.ds(lon, 2 * SUB), pl.ds(0, LANES)] = high
            out_ref[comp, :, pl.ds(lon, 2 * SUB), pl.ds(LANES, LANES)] = low


def finish(
    par, mine_ref, other_ref, prior_ref, t_ref, out_ref, logs_ref, gram, work, board, factor, fresh, sems
):
    inverse, diagonal = factorize(par, mine_ref, other_ref, gram, work, board)
    logs_ref[...] = prior_ref[...] - jnp.log(diagonal)
    factor[...] = paired(inverse)

    def out_copy(tile):
        return pltpu.make_async_copy(fresh.at[tile], out_ref.at[tile], sems.at[tile])

    for tile in range(TILES):
        fresh[tile] = times_factor(t_ref[tile], factor[...])
        out_copy(tile).start(priority=tile % 2)

    for tile in range(TILES):
        out_copy(tile).wait()


def swap_pairs(near_value, far_value, axis, closed):
    count = lax.axis_size(axis)
    near = [(i, i ^ 1) for i in range(count)]
    far = [(i, (i + 1 if i % 2 else i - 1) % count) for i in range(count)]
    if not closed:
        far = far[1:-1]
    return lax.ppermute(near_value, axis, near), lax.ppermute(far_value, axis, far)


def swapped(value, axis, mask):
    return lax.ppermute(value, axis, [(i, i ^ mask) for i in range(lax.axis_size(axis))])


def add_four(first, second, third, fourth, *rest):
    out_ref = rest[len(rest) // 2]
    out_ref[...] = (first[...] + fourth[...]) + (third[...] + second[...])


def sum_over(value, axis, first_bit, beside=None, held=()):
    bits = lax.axis_size(axis).bit_length() - 1
    while first_bit < bits:
        low = 1 << first_bit
        if first_bit + 1 < bits:
            high = low << 1
            three, two, one = (swapped(value, axis, mask) for mask in (low | high, high, low))
            if beside is None:
                value = (three + two) + (one + value)
            else:
                anywhere = pl.BlockSpec(memory_space=pl.ANY)
                value, *held = pl.pallas_call(
                    add_four,
                    out_shape=[jax.ShapeDtypeStruct(x.shape, x.dtype) for x in (value, *held)],
                    in_specs=[VMEM] * 4 + [anywhere] * (1 + len(held)),
                    out_specs=[VMEM] + [anywhere] * len(held),
                    input_output_aliases={5 + i: 1 + i for i in range(len(held))},
                    compiler_params=params(),
                )(value, three, two, one, beside, *held)
                beside = None
            first_bit += 2
        else:
            value = value + swapped(value, axis, low)
            first_bit += 1
    return value, held


def sum_devices(kept, sent, beside=(None, None), held=()):
    mine = kept + swapped(sent, "col", 1)
    mine, held = sum_over(mine, "col", 1, beside[0], held)
    mine, _ = sum_over(mine, "row", 0, beside[1])
    return mine, swapped(mine, "col", 1), held


def body(tangents, sea_mask, levels, current):
    comps, rows, cols, modes = tangents.shape
    total_rows = rows * lax.axis_size("row")
    total_cells = total_rows * cols * lax.axis_size("col")
    scale = 1.0 / total_cells
    row_at, col_at = lax.axis_index("row"), lax.axis_index("col")
    par = jnp.stack([row_at, col_at]).astype(jnp.int32)

    tall, length = rows + 2 * HALO, cols + 2 * SIDE

    block = shape_of(comps, length, tall, modes)
    coefs = shape_of(FIELDS, length, tall, LANES)
    columns = (shape_of(comps * SIDE * tall, modes),) * 2
    first_columns = (shape_of(comps * SIDE * tall + SUB, modes),) * 2
    rows_sent = (shape_of(comps * HALO + 1, cols, modes),) * 2
    halves = (shape_of(modes // 4 + SUB, modes),) * 2
    square = pltpu.VMEM((modes, modes), jnp.float32)
    board = pltpu.VMEM((2 * SUB * modes, LANES), jnp.float32)
    factor = pltpu.VMEM((2 * modes, 2 * modes), jnp.bfloat16)

    def call(
        kernel, outs, *operands, specs=None, out_specs=None, scratch=(), aliases=None, cost=1.0
    ):
        return pl.pallas_call(
            kernel,
            out_shape=outs,
            in_specs=specs or [SMEM] + [VMEM] * (len(operands) - 1),
            out_specs=out_specs or (VMEM,) * len(outs),
            scratch_shapes=scratch,
            input_output_aliases=aliases or {},
            compiler_params=params(),
            cost_estimate=pl.CostEstimate(
                flops=int(cost * 1e9), bytes_accessed=int(cost * 3e6), transcendentals=0
            ),
        )(*operands)

    def inside(step, state):
        kernel = functools.partial(apply_inside, step)
        return call(kernel, (block,), state, coef, spin, specs=[VMEM] * 3, cost=2.0)[0]

    def swap_columns(packed):
        return swap_pairs(*packed, "col", True)

    source, *fields = (
        pltpu.with_memory_space_constraint(x, pltpu.HBM)
        for x in (tangents, sea_mask.T, levels.T, current.T)
    )
    upright = [pltpu.VMEM(x.shape, x.dtype) for x in fields]
    packed = call(
        pack_rows,
        rows_sent,
        par,
        source,
        *fields,
        specs=[SMEM] + [HBM] * 4,
        scratch=upright
        + [
            pltpu.VMEM((cols, LANES), jnp.float32),
            pltpu.SemaphoreType.DMA((2 * comps,)),
            pltpu.SemaphoreType.DMA((FIELDS,)),
        ],
    )
    row_halos = swap_pairs(*packed, "row", False)
    start, coef, wide, spin = call(
        functools.partial(spread_fields, total_rows),
        (block, coefs, shape_of(FIELDS, cols, LANES), shape_of(tall, LANES)),
        par,
        source,
        *fields,
        specs=[SMEM] + [HBM] * 4,
        scratch=[pltpu.VMEM(tangents.shape, jnp.float32)]
        + upright
        + [pltpu.SemaphoreType.DMA((comps,)), pltpu.SemaphoreType.DMA((FIELDS,))],
        cost=3.0,
    )
    start, coef, *packed = call(
        join_rows,
        (block, coefs) + first_columns,
        par,
        start,
        coef,
        wide,
        *row_halos,
        aliases={1: 0, 2: 1},
    )
    logs = jnp.zeros((1, modes), jnp.float32)

    halos = swap_columns(packed)
    middle = inside(0, start)
    state = inside(1, middle)
    _, _, start, coef, *packed, kept, sent = call(
        functools.partial(join_gram, scale),
        (block, block, block, coefs) + columns + halves,
        par,
        start,
        middle,
        state,
        coef,
        spin,
        *halos,
        scratch=[square],
        aliases={1: 0, 2: 1, 3: 2, 4: 3},
        cost=2.0,
    )
    middle = inside(0, start)
    state = inside(1, middle)
    mine, other, packed = sum_devices(kept, sent, (middle, state), packed)
    halos = swap_columns(packed)
    _, _, state = call(
        mend_only,
        (block,) * 3,
        par,
        start,
        middle,
        state,
        coef,
        spin,
        *halos,
        aliases={1: 0, 2: 1, 3: 2},
    )
    inverse, logs = call(
        factor_only,
        (shape_of(modes, modes), shape_of(1, modes)),
        par,
        mine,
        other,
        logs,
        state,
        specs=[SMEM] + [VMEM] * 3 + [pl.BlockSpec(memory_space=pl.ANY)],
        scratch=[square, square, board],
        cost=0.01,
    )
    state, kept, sent = call(
        functools.partial(update, scale),
        (shape_of(comps, cols, rows, modes),) + halves,
        par,
        state,
        inverse,
        scratch=[factor, square],
        cost=2.0,
    )
    state = call(
        restore_order,
        (jax.ShapeDtypeStruct((comps, rows, cols, 2 * modes), jnp.bfloat16),),
        state,
        specs=[VMEM],
        cost=1.0,
    )[0]
    height = comps * rows * cols // TILES
    tiled = shape_of(TILES, height, modes)
    mine, other, _ = sum_devices(kept, sent)
    out, logs = call(
        finish,
        (tiled, shape_of(1, modes)),
        par,
        mine,
        other,
        logs,
        state.reshape(TILES, height, 2 * modes),
        out_specs=(HBM, VMEM),
        scratch=[
            square,
            square,
            board,
            factor,
            pltpu.VMEM((TILES, height, modes), jnp.float32),
            pltpu.SemaphoreType.DMA((TILES,)),
        ],
    )
    return out.reshape(tangents.shape), logs.reshape(modes)


def solution(mesh):
    placed = (P(None, "row", "col", None), P("row", "col"), P("row", "col"), P("row", "col"))
    return jax.shard_map(
        body,
        mesh=mesh,
        in_specs=placed,
        out_specs=(P(None, "row", "col", None), P()),
        check_vma=False,
    )
```

```python
import functools

import jax
import jax.numpy as jnp
from jax import lax
from jax.experimental import pallas as pl
from jax.experimental.pallas import tpu as pltpu
from jax.sharding import PartitionSpec as P

STEPS = 2
RENORMS = 2
LEVELS = 50

viscosity = 0.15
gravity = 0.5
rotation = 0.4

SUB = 8
LANES = 128
FIELDS = 3
HALO = STEPS * RENORMS
SIDE = STEPS
TILES = 12
VMEM_LIMIT = 16 * 1024 * 1024

HBM = pl.BlockSpec(memory_space=pltpu.HBM)
VMEM = pl.BlockSpec(memory_space=pltpu.VMEM)
SMEM = pl.BlockSpec(memory_space=pltpu.SMEM)


def params():
    return pltpu.CompilerParams(vmem_limit_bytes=VMEM_LIMIT)


def shape_of(*dims):
    return jax.ShapeDtypeStruct(dims, jnp.float32)


def lane_spread(block, lane):
    return jnp.broadcast_to(block[:, lane : lane + 1], (block.shape[0], LANES))


def fetch(sources, places, sems):
    copies = [
        pltpu.make_async_copy(source, place, sems.at[i])
        for i, (source, place) in enumerate(zip(sources, places))
    ]
    for copy in copies:
        copy.start()
    return copies


def finish_all(copies):
    for copy in copies:
        copy.wait()


def fields_of(sea_ref, levels_ref, current_ref):
    return (
        sea_ref[...].astype(jnp.float32),
        0.5 * current_ref[...],
        0.5 * ((levels_ref[...] + 1).astype(jnp.float32) / LEVELS),
    )


def sides_of(par):
    odd_row, odd_col = par[0] % 2, par[1] % 2
    return (1 - odd_row, odd_row), (1 - odd_col, odd_col)


def pack_rows(
    par, t_ref, sea_ref, levels_ref, current_ref, row_a, row_b, sea, levels, current, wide, sems, field_sems
):
    comps, rows, cols, _ = t_ref.shape
    norths, _ = sides_of(par)
    field_copies = fetch((sea_ref, levels_ref, current_ref), (sea, levels, current), field_sems)
    slots = [(slot, msg, comp) for slot, msg in ((0, row_a), (1, row_b)) for comp in range(comps)]
    copies = fetch(
        [t_ref.at[comp, pl.ds(norths[slot] * (rows - HALO), HALO)] for slot, _, comp in slots],
        [msg.at[pl.ds(comp * HALO, HALO)] for _, msg, comp in slots],
        sems,
    )
    lane = lax.broadcasted_iota(jnp.int32, (cols, LANES), 1)
    wide[...] = jnp.zeros_like(wide)
    packed = [jnp.zeros((cols, LANES), jnp.float32)] * 2
    finish_all(field_copies)
    for field, value in enumerate(fields_of(sea, levels, current)):
        wide[:, pl.ds(0, rows)] = value
        whole = wide[...]
        for north in (0, 1):
            shift = (field * SUB - north * (rows - HALO)) % LANES
            moved = pltpu.roll(whole, shift, 1) if shift else whole
            here = (lane >= field * SUB) & (lane < field * SUB + HALO)
            packed[north] = jnp.where(here, moved, packed[north])
    for slot, msg in ((0, row_a), (1, row_b)):
        msg[comps * HALO] = jnp.where(norths[slot] == 1, packed[1], packed[0])
    finish_all(copies)


def spread_fields(
    total_rows, par, t_ref, sea_ref, levels_ref, current_ref, state, coef, spin, col_a, col_b, wide, block, sea, levels, current, sems, field_sems
):
    comps, rows, cols, _ = t_ref.shape
    field_copies = fetch((sea_ref, levels_ref, current_ref), (sea, levels, current), field_sems)
    copies = fetch(
        [t_ref.at[comp] for comp in range(comps)], [block.at[comp] for comp in range(comps)], sems
    )
    line = lax.broadcasted_iota(jnp.int32, spin.shape, 0)
    line = jnp.where(line < rows + HALO, line, line - (rows + 2 * HALO))
    latitude = (par[0] * rows + line).astype(jnp.float32)
    angle = (-70.0 + 140.0 * (latitude + 0.5) / total_rows) * (jnp.pi / 180.0)
    spin[...] = rotation * jnp.sin(angle)
    wide[...] = jnp.zeros_like(wide)
    finish_all(field_copies)
    for field, value in enumerate(fields_of(sea, levels, current)):
        wide[field, :, pl.ds(0, rows)] = value
        natural = jnp.transpose(wide[field])[:rows]
        for lon in range(cols):
            coef[field, SIDE + lon, pl.ds(0, rows), :] = lane_spread(natural, lon)
    for comp in range(comps):
        copies[comp].wait()
        for row in range(0, rows, SUB):
            cells = block[comp, pl.ds(row, SUB)]
            state[comp, pl.ds(SIDE, cols), pl.ds(row, SUB), :] = jnp.transpose(cells, (1, 0, 2))
    send_columns(par, state, (col_a, col_b), 0, rows)
    tail = comps * SIDE * rows
    _, easts = sides_of(par)
    for slot, msg in enumerate((col_a, col_b)):
        msg[pl.ds(tail, SUB), :] = jnp.zeros((SUB, LANES), jnp.float32)
        for field in range(FIELDS):
            msg[pl.ds(tail + field, 1), :] = wide[field, pl.ds(easts[slot] * (cols - 1), 1), :]


def column_at(east, cols, depth):
    return SIDE + depth + east * (cols - 1 - 2 * depth)


def send_columns(par, state, cols_sent, first, count):
    comps, length, _, _ = state.shape
    _, easts = sides_of(par)
    for slot, msg in enumerate(cols_sent):
        for comp in range(comps):
            for j in range(SIDE):
                column = column_at(easts[slot], length - 2 * SIDE, j)
                msg[pl.ds((comp * SIDE + j) * count, count), :] = state[
                    comp, column, pl.ds(first, count), :
                ]


def join_rows(par, state_in, coef_in, row_a, row_b, state, coef, col_a, col_b):
    comps, length, tall, _ = state.shape
    cols, rows = length - 2 * SIDE, tall - 2 * HALO
    norths, easts = sides_of(par)
    flat = state.reshape(comps * length * tall, LANES)
    for slot, msg in ((0, row_a), (1, row_b)):
        line = rows + HALO * (1 - norths[slot])
        for comp in range(comps):
            for h in range(HALO):
                for lon in range(0, cols, SUB):
                    at = (comp * length + SIDE + lon) * tall + line + h
                    flat[pl.ds(at, SUB, stride=tall), :] = msg[comp * HALO + h, pl.ds(lon, SUB), :]
    lane = lax.broadcasted_iota(jnp.int32, (cols, LANES), 1)
    north = jnp.where(norths[0] == 1, row_a[comps * HALO], row_b[comps * HALO])
    south = jnp.where(norths[0] == 1, row_b[comps * HALO], row_a[comps * HALO])
    beyond = jnp.where(lane % SUB < HALO, north, pltpu.roll(south, HALO, 1))
    natural = jnp.transpose(beyond)
    for field in range(FIELDS):
        block = natural[field * SUB : (field + 1) * SUB]
        for lon in range(cols):
            coef[field, SIDE + lon, pl.ds(rows, SUB), :] = lane_spread(block, lon)
    send_columns(par, state, (col_a, col_b), rows, SUB)
    tail = comps * SIDE * SUB
    for slot, msg in ((0, col_a), (1, col_b)):
        msg[pl.ds(tail, SUB), :] = jnp.zeros((SUB, LANES), jnp.float32)
        msg[pl.ds(tail, 1), :] = jnp.where(easts[slot] == 1, beyond[cols - 1 :], beyond[:1])


def model(own, x_diff, x_sum, above, below, sea, flow, depth, spin):
    keep, half = 1.0 - 4.0 * viscosity, 0.5 * gravity
    mixed = [
        keep * c + viscosity * (x + (n + s)) - flow * d
        for c, d, x, n, s in zip(own, x_diff, x_sum, above, below)
    ]
    v_y, h_y = above[1] - below[1], above[2] - below[2]
    return (
        sea * (mixed[0] - half * x_diff[2] + spin * own[1]),
        sea * (mixed[1] - half * h_y - spin * own[0]),
        sea * (mixed[2] - depth * (x_diff[0] + v_y)),
    )


def advance_column(source, target, coef_ref, spin_ref, lon):
    comps, length, tall, _ = source.shape
    flat = source.reshape(comps * length * tall, LANES)
    sub = lax.broadcasted_iota(jnp.int32, (SUB, LANES), 0)
    tiles = tall // SUB
    for tile in range(tiles):
        lines = pl.ds(SUB * tile, SUB)
        own, east, west = (
            [source[comp, lon + shift, lines, :] for comp in range(comps)] for shift in (0, 1, -1)
        )
        starts = [(comp * length + lon) * tall + SUB * tile for comp in range(comps)]
        if tile < tiles - 1:
            above = [flat[pl.ds(start + 1, SUB), :] for start in starts]
        else:
            wrap = [source[comp, lon, pl.ds(0, SUB), :] for comp in range(comps)]
            above = [
                jnp.where(sub == SUB - 1, pltpu.roll(w, SUB - 1, 0), pltpu.roll(o, SUB - 1, 0))
                for w, o in zip(wrap, own)
            ]
        if tile > 0:
            below = [flat[pl.ds(start - 1, SUB), :] for start in starts]
        else:
            wrap = [source[comp, lon, pl.ds(tall - SUB, SUB), :] for comp in range(comps)]
            below = [
                jnp.where(sub == 0, pltpu.roll(w, 1, 0), pltpu.roll(o, 1, 0))
                for w, o in zip(wrap, own)
            ]
        new = model(
            own,
            [e - w for e, w in zip(east, west)],
            [e + w for e, w in zip(east, west)],
            above,
            below,
            *(coef_ref[field, lon, lines, :] for field in range(FIELDS)),
            spin_ref[lines, :],
        )
        for comp in range(comps):
            target[comp, lon, lines, :] = new[comp]


def apply_inside(step, source, coef_ref, spin_ref, target):
    first = SIDE + step + 1
    count = source.shape[1] - 2 * first

    @pl.loop(0, count // 2)
    def _(pair):
        advance_column(source, target, coef_ref, spin_ref, first + 2 * pair)
        advance_column(source, target, coef_ref, spin_ref, first + 2 * pair + 1)


def mend_columns(par, states, coef_ref, spin_ref, pieces):
    comps, length, _, _ = states[0].shape
    _, easts = sides_of(par)
    for first, count, cols_got in pieces:
        for slot, msg in enumerate(cols_got):
            for comp in range(comps):
                for j in range(SIDE):
                    column = column_at(easts[slot], length - 2 * SIDE, -1 - j)
                    states[0][comp, column, pl.ds(first, count), :] = msg[
                        pl.ds((comp * SIDE + j) * count, count), :
                    ]
    for step in range(STEPS):
        first = step + 1
        skip = length - 2 * first - 2 * SIDE

        @pl.loop(0, 2 * SIDE)
        def _(i):
            lon = first + i + (i // SIDE) * skip
            advance_column(states[step], states[step + 1], coef_ref, spin_ref, lon)


def join_gram(
    scale, par, start_in, middle_in, state_in, coef_in, spin_ref, a, b, c, d, start, middle, state, coef, col_a, col_b, kept, sent, total
):
    _, length, tall, _ = state.shape
    rows = tall - 2 * HALO
    _, easts = sides_of(par)
    for slot, (own, beyond) in enumerate(((a, c), (b, d))):
        own, beyond = (jnp.transpose(x[pl.ds(x.shape[0] - SUB, SUB), :]) for x in (own, beyond))
        column = column_at(easts[slot], length - 2 * SIDE, -1)
        for field in range(FIELDS):
            coef[field, column, pl.ds(0, rows), :] = lane_spread(own[:rows], field)
            coef[field, column, pl.ds(rows, SUB), :] = lane_spread(
                beyond[field * SUB : (field + 1) * SUB], 0
            )
    mend_columns(
        par, (start, middle, state), coef, spin_ref, ((0, rows, (a, b)), (rows, SUB, (c, d)))
    )
    send_columns(par, state, (col_a, col_b), 0, tall)
    gram = sum(gram_of(*split_halves(cells)) for _, _, cells in tiles_of(state))
    write_halves(par, gram, scale, kept, sent, total)


def tiles_of(state):
    comps, length, tall, _ = state.shape
    rows = tall - 2 * HALO
    for comp in range(comps):
        for lon in range(0, length - 2 * SIDE, SUB):
            cells = state[comp, pl.ds(SIDE + lon, SUB), pl.ds(0, rows), :]
            yield comp, lon, cells.reshape(SUB * rows, LANES)


def split_halves(value):
    high = value.astype(jnp.bfloat16)
    return high, (value - high.astype(jnp.float32)).astype(jnp.bfloat16)


def gram_of(high, low):
    return lax.dot_general(
        high,
        jnp.concatenate([high, low], axis=1),
        (((0,), (0,)), ((), ())),
        preferred_element_type=jnp.float32,
    )


def write_halves(par, gram, scale, kept, sent, total):
    half, rows = LANES // 2, kept.shape[0]
    mixed = gram[:, LANES:]
    whole = scale * (gram[:, :LANES] + (mixed + jnp.transpose(mixed)))
    row = lax.broadcasted_iota(jnp.int32, (half, LANES), 0)
    col = lax.broadcasted_iota(jnp.int32, (half, LANES), 1)
    total[pl.ds(0, half), :] = jnp.where(
        (col < half) | (col - half > row), whole[half:], pltpu.roll(whole[:half], half, 1)
    )
    row = lax.broadcasted_iota(jnp.int32, (LANES, LANES), 0)
    col = lax.broadcasted_iota(jnp.int32, (LANES, LANES), 1)
    total[pl.ds(half, 2 * rows - half), :] = jnp.zeros((2 * rows - half, LANES), jnp.float32)
    total[pl.ds(half, 1), :] = jnp.sum(jnp.where(row == col, whole, 0.0), axis=0, keepdims=True)
    odd = par[1] % 2
    kept[...] = total[pl.ds(odd * rows, rows), :]
    sent[...] = total[pl.ds((1 - odd) * rows, rows), :]


def factor_pair(low, p):
    q, size = p + 1, len(low)
    a, b, c = low[p][p], low[q][p], low[q][q]
    root_a, root_det = lax.rsqrt(a), lax.rsqrt(a * c - b * b)
    both = root_a * root_det
    turned = [a * low[i][q] - b * low[i][p] for i in range(q + 1, size)]
    low[q][p] = b * root_a
    for i, value in zip(range(q + 1, size), turned):
        low[i][p] = low[i][p] * root_a
        low[i][q] = value * both
    for i in range(q + 1, size):
        for m in range(q + 1, i + 1):
            low[i][m] = (low[i][m] - low[i][p] * low[m][p]) - low[i][q] * low[m][q]
    return root_a, a * both


def invert_factor(gram, work, board):
    count = LANES // SUB
    lane = lax.broadcasted_iota(jnp.int32, (SUB, LANES), 1)
    sub = lax.broadcasted_iota(jnp.int32, (SUB, LANES), 0)
    rows = [gram[SUB * i : SUB * (i + 1)] for i in range(count)]
    for block in range(count):
        base = SUB * block
        here = (lane >= base) & (lane < base + SUB)
        shelf = 2 * SUB * base
        for l in range(SUB):
            board[pl.ds(shelf + SUB * l, SUB), :] = lane_spread(rows[block], base + l)
        low = [
            [board[pl.ds(shelf + SUB * l + k, SUB, stride=0), :] for l in range(k + 1)]
            for k in range(SUB)
        ]
        shelf += SUB * SUB
        board[pl.ds(shelf, SUB), :] = jnp.where(
            here, jnp.where(lane - base == sub, 1.0, 0.0), rows[block]
        )
        inv = []
        for p in range(0, SUB, 2):
            inv.extend(factor_pair(low, p))
        scaled = []
        for k in range(SUB):
            line = board[pl.ds(shelf + k, SUB, stride=0), :]
            for l in range(k):
                line = line - low[k][l] * scaled[l]
            scaled.append(line * inv[k])
        merged = scaled[0]
        for k in range(1, SUB):
            merged = jnp.where(sub == k, scaled[k], merged)
        work[pl.ds(base, SUB), :] = merged
        for i in range(block + 1, count):
            weights = []
            rest = jnp.where(here, 0.0, rows[i])
            for l in range(SUB):
                weight = lane_spread(rows[i], base + l)
                for m in range(l):
                    weight = weight - weights[m] * low[l][m]
                weights.append(weight * inv[l])
            for l in range(SUB):
                rest = rest - weights[l] * scaled[l]
            rows[i] = rest


def factorize(par, mine_ref, other_ref, gram, work, board):
    half, rows = LANES // 2, mine_ref.shape[0]
    odd = par[1] % 2
    gram[pl.ds(odd * rows, rows), :] = mine_ref[...]
    gram[pl.ds((1 - odd) * rows, rows), :] = other_ref[...]
    packed, diagonal = gram[pl.ds(0, half), :], gram[pl.ds(half, 1), :]
    row = lax.broadcasted_iota(jnp.int32, (half, LANES), 0)
    col = lax.broadcasted_iota(jnp.int32, (half, LANES), 1)
    triangles = jnp.concatenate(
        [
            jnp.where(col < row, pltpu.roll(packed, half, 1), 0.0),
            jnp.where((col < half) | (col - half > row), packed, 0.0),
        ],
        axis=0,
    )
    row = lax.broadcasted_iota(jnp.int32, (LANES, LANES), 0)
    col = lax.broadcasted_iota(jnp.int32, (LANES, LANES), 1)
    size = jnp.broadcast_to(lax.rsqrt(diagonal), (LANES, LANES))
    whole = jnp.where(row == col, diagonal, triangles + jnp.transpose(triangles))
    invert_factor((whole * size) * jnp.transpose(size), work, board)
    inverse = jnp.where(row >= col, work[...], 0.0) * size
    diagonal = jnp.sum(jnp.where(row == col, inverse, 0.0), axis=0, keepdims=True)
    return inverse, diagonal


def paired(inverse):
    high = inverse.astype(jnp.bfloat16)
    low = (inverse - high.astype(jnp.float32)).astype(jnp.bfloat16)
    return jnp.concatenate(
        [jnp.concatenate([high, high], axis=1), jnp.concatenate([low, low], axis=1)], axis=0
    )


def times_factor(pair, factor):
    both = lax.dot_general(
        pair, factor, (((1,), (1,)), ((), ())), preferred_element_type=jnp.float32
    )
    return both[:, :LANES] + both[:, LANES:]


def factor_only(par, mine_ref, other_ref, prior_ref, _, inverse_ref, logs_ref, gram, work, board):
    inverse, diagonal = factorize(par, mine_ref, other_ref, gram, work, board)
    inverse_ref[...] = inverse
    logs_ref[...] = prior_ref[...] - jnp.log(diagonal)


def mend_only(par, start_in, middle_in, state_in, coef_ref, spin_ref, a, b, start, middle, state):
    tall = state.shape[2]
    mend_columns(par, (start, middle, state), coef_ref, spin_ref, ((0, tall, (a, b)),))


def update(scale, par, state, inverse_ref, out_ref, kept, sent, factor, total):
    factor[...] = paired(inverse_ref[...])
    gram = 0.0
    for comp, lon, cells in tiles_of(state):
        new = times_factor(jnp.concatenate(split_halves(cells), axis=1), factor[...])
        out_ref[comp, pl.ds(lon, SUB)] = new.reshape((SUB,) + out_ref.shape[2:])
        gram += gram_of(*split_halves(new))
    write_halves(par, gram, scale, kept, sent, total)


def restore_order(turned, out_ref):
    comps, cols, _, _ = turned.shape
    for comp in range(comps):
        for lon in range(0, cols, 2 * SUB):
            cells = jnp.concatenate(
                [
                    jnp.transpose(turned[comp, pl.ds(lon + shift, SUB)], (1, 0, 2))
                    for shift in (0, SUB)
                ],
                axis=1,
            )
            high = cells.astype(jnp.bfloat16)
            low = (cells - high.astype(jnp.float32)).astype(jnp.bfloat16)
            out_ref[comp, :, pl.ds(lon, 2 * SUB), pl.ds(0, LANES)] = high
            out_ref[comp, :, pl.ds(lon, 2 * SUB), pl.ds(LANES, LANES)] = low


def finish(
    par, mine_ref, other_ref, prior_ref, t_ref, out_ref, logs_ref, gram, work, board, factor, fresh, sems
):
    inverse, diagonal = factorize(par, mine_ref, other_ref, gram, work, board)
    logs_ref[...] = prior_ref[...] - jnp.log(diagonal)
    factor[...] = paired(inverse)

    def out_copy(tile):
        return pltpu.make_async_copy(fresh.at[tile], out_ref.at[tile], sems.at[tile])

    for tile in range(TILES):
        fresh[tile] = times_factor(t_ref[tile], factor[...])
        out_copy(tile).start(priority=tile % 2)

    for tile in range(TILES):
        out_copy(tile).wait()


def swap_pairs(near_value, far_value, axis, closed):
    count = lax.axis_size(axis)
    near = [(i, i ^ 1) for i in range(count)]
    far = [(i, (i + 1 if i % 2 else i - 1) % count) for i in range(count)]
    if not closed:
        far = far[1:-1]
    return lax.ppermute(near_value, axis, near), lax.ppermute(far_value, axis, far)


def swapped(value, axis, mask):
    return lax.ppermute(value, axis, [(i, i ^ mask) for i in range(lax.axis_size(axis))])


def add_four(first, second, third, fourth, *rest):
    out_ref = rest[len(rest) // 2]
    out_ref[...] = (first[...] + fourth[...]) + (third[...] + second[...])


def sum_over(value, axis, first_bit, beside=None, held=()):
    bits = lax.axis_size(axis).bit_length() - 1
    while first_bit < bits:
        low = 1 << first_bit
        if first_bit + 1 < bits:
            high = low << 1
            three, two, one = (swapped(value, axis, mask) for mask in (low | high, high, low))
            if beside is None:
                value = (three + two) + (one + value)
            else:
                anywhere = pl.BlockSpec(memory_space=pl.ANY)
                value, *held = pl.pallas_call(
                    add_four,
                    out_shape=[jax.ShapeDtypeStruct(x.shape, x.dtype) for x in (value, *held)],
                    in_specs=[VMEM] * 4 + [anywhere] * (1 + len(held)),
                    out_specs=[VMEM] + [anywhere] * len(held),
                    input_output_aliases={5 + i: 1 + i for i in range(len(held))},
                    compiler_params=params(),
                )(value, three, two, one, beside, *held)
                beside = None
            first_bit += 2
        else:
            value = value + swapped(value, axis, low)
            first_bit += 1
    return value, held


def sum_devices(kept, sent, beside=(None, None), held=()):
    mine = kept + swapped(sent, "col", 1)
    mine, held = sum_over(mine, "col", 1, beside[0], held)
    mine, _ = sum_over(mine, "row", 0, beside[1])
    return mine, swapped(mine, "col", 1), held


def body(tangents, sea_mask, levels, current):
    comps, rows, cols, modes = tangents.shape
    total_rows = rows * lax.axis_size("row")
    total_cells = total_rows * cols * lax.axis_size("col")
    scale = 1.0 / total_cells
    row_at, col_at = lax.axis_index("row"), lax.axis_index("col")
    par = jnp.stack([row_at, col_at]).astype(jnp.int32)

    tall, length = rows + 2 * HALO, cols + 2 * SIDE

    block = shape_of(comps, length, tall, modes)
    coefs = shape_of(FIELDS, length, tall, LANES)
    columns = (shape_of(comps * SIDE * tall, modes),) * 2
    own_columns = (shape_of(comps * SIDE * rows + SUB, modes),) * 2
    corners = (shape_of(comps * SIDE * SUB + SUB, modes),) * 2
    rows_sent = (shape_of(comps * HALO + 1, cols, modes),) * 2
    halves = (shape_of(modes // 4 + SUB, modes),) * 2
    square = pltpu.VMEM((modes, modes), jnp.float32)
    board = pltpu.VMEM((2 * SUB * modes, LANES), jnp.float32)
    factor = pltpu.VMEM((2 * modes, 2 * modes), jnp.bfloat16)

    def call(
        kernel, outs, *operands, specs=None, out_specs=None, scratch=(), aliases=None, cost=1.0
    ):
        return pl.pallas_call(
            kernel,
            out_shape=outs,
            in_specs=specs or [SMEM] + [VMEM] * (len(operands) - 1),
            out_specs=out_specs or (VMEM,) * len(outs),
            scratch_shapes=scratch,
            input_output_aliases=aliases or {},
            compiler_params=params(),
            cost_estimate=pl.CostEstimate(
                flops=int(cost * 1e9), bytes_accessed=int(cost * 3e6), transcendentals=0
            ),
        )(*operands)

    def inside(step, state):
        kernel = functools.partial(apply_inside, step)
        return call(kernel, (block,), state, coef, spin, specs=[VMEM] * 3, cost=2.0)[0]

    def swap_columns(packed):
        return swap_pairs(*packed, "col", True)

    source, *fields = (
        pltpu.with_memory_space_constraint(x, pltpu.HBM)
        for x in (tangents, sea_mask.T, levels.T, current.T)
    )
    upright = [pltpu.VMEM(x.shape, x.dtype) for x in fields]
    packed = call(
        pack_rows,
        rows_sent,
        par,
        source,
        *fields,
        specs=[SMEM] + [HBM] * 4,
        scratch=upright
        + [
            pltpu.VMEM((cols, LANES), jnp.float32),
            pltpu.SemaphoreType.DMA((2 * comps,)),
            pltpu.SemaphoreType.DMA((FIELDS,)),
        ],
    )
    row_halos = swap_pairs(*packed, "row", False)
    start, coef, spin, *packed = call(
        functools.partial(spread_fields, total_rows),
        (block, coefs, shape_of(tall, LANES)) + own_columns,
        par,
        source,
        *fields,
        specs=[SMEM] + [HBM] * 4,
        scratch=[
            pltpu.VMEM((FIELDS, cols, LANES), jnp.float32),
            pltpu.VMEM(tangents.shape, jnp.float32),
        ]
        + upright
        + [pltpu.SemaphoreType.DMA((comps,)), pltpu.SemaphoreType.DMA((FIELDS,))],
        cost=3.0,
    )
    halos = swap_columns(packed)
    start, coef, *packed = call(
        join_rows,
        (block, coefs) + corners,
        par,
        start,
        coef,
        *row_halos,
        aliases={1: 0, 2: 1},
    )
    halos += swap_columns(packed)
    logs = jnp.zeros((1, modes), jnp.float32)

    middle = inside(0, start)
    state = inside(1, middle)
    _, _, start, coef, *packed, kept, sent = call(
        functools.partial(join_gram, scale),
        (block, block, block, coefs) + columns + halves,
        par,
        start,
        middle,
        state,
        coef,
        spin,
        *halos,
        scratch=[square],
        aliases={1: 0, 2: 1, 3: 2, 4: 3},
        cost=2.0,
    )
    middle = inside(0, start)
    state = inside(1, middle)
    mine, other, packed = sum_devices(kept, sent, (middle, state), packed)
    halos = swap_columns(packed)
    _, _, state = call(
        mend_only,
        (block,) * 3,
        par,
        start,
        middle,
        state,
        coef,
        spin,
        *halos,
        aliases={1: 0, 2: 1, 3: 2},
    )
    inverse, logs = call(
        factor_only,
        (shape_of(modes, modes), shape_of(1, modes)),
        par,
        mine,
        other,
        logs,
        state,
        specs=[SMEM] + [VMEM] * 3 + [pl.BlockSpec(memory_space=pl.ANY)],
        scratch=[square, square, board],
        cost=0.01,
    )
    state, kept, sent = call(
        functools.partial(update, scale),
        (shape_of(comps, cols, rows, modes),) + halves,
        par,
        state,
        inverse,
        scratch=[factor, square],
        cost=2.0,
    )
    state = call(
        restore_order,
        (jax.ShapeDtypeStruct((comps, rows, cols, 2 * modes), jnp.bfloat16),),
        state,
        specs=[VMEM],
        cost=1.0,
    )[0]
    height = comps * rows * cols // TILES
    tiled = shape_of(TILES, height, modes)
    mine, other, _ = sum_devices(kept, sent)
    out, logs = call(
        finish,
        (tiled, shape_of(1, modes)),
        par,
        mine,
        other,
        logs,
        state.reshape(TILES, height, 2 * modes),
        out_specs=(HBM, VMEM),
        scratch=[
            square,
            square,
            board,
            factor,
            pltpu.VMEM((TILES, height, modes), jnp.float32),
            pltpu.SemaphoreType.DMA((TILES,)),
        ],
    )
    return out.reshape(tangents.shape), logs.reshape(modes)


def solution(mesh):
    placed = (P(None, "row", "col", None), P("row", "col"), P("row", "col"), P("row", "col"))
    return jax.shard_map(
        body,
        mesh=mesh,
        in_specs=placed,
        out_specs=(P(None, "row", "col", None), P()),
        check_vma=False,
    )
```

```python
import functools

import jax
import jax.numpy as jnp
from jax import lax
from jax.experimental import pallas as pl
from jax.experimental.pallas import tpu as pltpu
from jax.sharding import PartitionSpec as P

STEPS = 2
RENORMS = 2
LEVELS = 50

viscosity = 0.15
gravity = 0.5
rotation = 0.4

SUB = 8
LANES = 128
FIELDS = 3
HALO = STEPS * RENORMS
SIDE = STEPS
TILES = 12
VMEM_LIMIT = 16 * 1024 * 1024

HBM = pl.BlockSpec(memory_space=pltpu.HBM)
VMEM = pl.BlockSpec(memory_space=pltpu.VMEM)
SMEM = pl.BlockSpec(memory_space=pltpu.SMEM)


def params():
    return pltpu.CompilerParams(vmem_limit_bytes=VMEM_LIMIT)


def shape_of(*dims):
    return jax.ShapeDtypeStruct(dims, jnp.float32)


def lane_spread(block, lane):
    return jnp.broadcast_to(block[:, lane : lane + 1], (block.shape[0], LANES))


def fetch(sources, places, sems):
    copies = [
        pltpu.make_async_copy(source, place, sems.at[i])
        for i, (source, place) in enumerate(zip(sources, places))
    ]
    for copy in copies:
        copy.start()
    return copies


def finish_all(copies):
    for copy in copies:
        copy.wait()


def fields_of(sea_ref, levels_ref, current_ref):
    return (
        sea_ref[...].astype(jnp.float32),
        0.5 * current_ref[...],
        0.5 * ((levels_ref[...] + 1).astype(jnp.float32) / LEVELS),
    )


def sides_of(par):
    odd_row, odd_col = par[0] % 2, par[1] % 2
    return (1 - odd_row, odd_row), (1 - odd_col, odd_col)


def pack_rows(
    par, t_ref, sea_ref, levels_ref, current_ref, row_a, row_b, sea, levels, current, wide, sems, field_sems
):
    comps, rows, cols, _ = t_ref.shape
    norths, _ = sides_of(par)
    field_copies = fetch((sea_ref, levels_ref, current_ref), (sea, levels, current), field_sems)
    slots = [(slot, msg, comp) for slot, msg in ((0, row_a), (1, row_b)) for comp in range(comps)]
    copies = fetch(
        [t_ref.at[comp, pl.ds(norths[slot] * (rows - HALO), HALO)] for slot, _, comp in slots],
        [msg.at[pl.ds(comp * HALO, HALO)] for _, msg, comp in slots],
        sems,
    )
    lane = lax.broadcasted_iota(jnp.int32, (cols, LANES), 1)
    wide[...] = jnp.zeros_like(wide)
    packed = [jnp.zeros((cols, LANES), jnp.float32)] * 2
    finish_all(field_copies)
    for field, value in enumerate(fields_of(sea, levels, current)):
        wide[:, pl.ds(0, rows)] = value
        whole = wide[...]
        for north in (0, 1):
            shift = (field * SUB - north * (rows - HALO)) % LANES
            moved = pltpu.roll(whole, shift, 1) if shift else whole
            here = (lane >= field * SUB) & (lane < field * SUB + HALO)
            packed[north] = jnp.where(here, moved, packed[north])
    for slot, msg in ((0, row_a), (1, row_b)):
        msg[comps * HALO] = jnp.where(norths[slot] == 1, packed[1], packed[0])
    finish_all(copies)


def spread_fields(
    total_rows, par, t_ref, sea_ref, levels_ref, current_ref, state, coef, spin, col_a, col_b, wide, block, sea, levels, current, sems, field_sems
):
    comps, rows, cols, _ = t_ref.shape
    field_copies = fetch((sea_ref, levels_ref, current_ref), (sea, levels, current), field_sems)
    copies = fetch(
        [t_ref.at[comp] for comp in range(comps)], [block.at[comp] for comp in range(comps)], sems
    )
    line = lax.broadcasted_iota(jnp.int32, spin.shape, 0)
    line = jnp.where(line < rows + HALO, line, line - (rows + 2 * HALO))
    latitude = (par[0] * rows + line).astype(jnp.float32)
    angle = (-70.0 + 140.0 * (latitude + 0.5) / total_rows) * (jnp.pi / 180.0)
    spin[...] = rotation * jnp.sin(angle)
    wide[...] = jnp.zeros_like(wide)
    finish_all(field_copies)
    for field, value in enumerate(fields_of(sea, levels, current)):
        wide[field, :, pl.ds(0, rows)] = value
        natural = jnp.transpose(wide[field])[:rows]
        for lon in range(cols):
            coef[field, SIDE + lon, pl.ds(0, rows), :] = lane_spread(natural, lon)
    for comp in range(comps):
        copies[comp].wait()
        for row in range(0, rows, SUB):
            cells = block[comp, pl.ds(row, SUB)]
            state[comp, pl.ds(SIDE, cols), pl.ds(row, SUB), :] = jnp.transpose(cells, (1, 0, 2))
    send_columns(par, state, (col_a, col_b), 0, rows)
    tail = comps * SIDE * rows
    _, easts = sides_of(par)
    for slot, msg in enumerate((col_a, col_b)):
        msg[pl.ds(tail, SUB), :] = jnp.zeros((SUB, LANES), jnp.float32)
        for field in range(FIELDS):
            msg[pl.ds(tail + field, 1), :] = wide[field, pl.ds(easts[slot] * (cols - 1), 1), :]


def column_at(east, cols, depth):
    return SIDE + depth + east * (cols - 1 - 2 * depth)


def send_columns(par, state, cols_sent, first, count):
    comps, length, _, _ = state.shape
    _, easts = sides_of(par)
    for slot, msg in enumerate(cols_sent):
        for comp in range(comps):
            for j in range(SIDE):
                column = column_at(easts[slot], length - 2 * SIDE, j)
                msg[pl.ds((comp * SIDE + j) * count, count), :] = state[
                    comp, column, pl.ds(first, count), :
                ]


def join_rows(par, state_in, coef_in, row_a, row_b, _, state, coef, col_a, col_b):
    comps, length, tall, _ = state.shape
    cols, rows = length - 2 * SIDE, tall - 2 * HALO
    norths, easts = sides_of(par)
    flat = state.reshape(comps * length * tall, LANES)
    for slot, msg in ((0, row_a), (1, row_b)):
        line = rows + HALO * (1 - norths[slot])
        for comp in range(comps):
            for h in range(HALO):
                for lon in range(0, cols, SUB):
                    at = (comp * length + SIDE + lon) * tall + line + h
                    flat[pl.ds(at, SUB, stride=tall), :] = msg[comp * HALO + h, pl.ds(lon, SUB), :]
    lane = lax.broadcasted_iota(jnp.int32, (cols, LANES), 1)
    north = jnp.where(norths[0] == 1, row_a[comps * HALO], row_b[comps * HALO])
    south = jnp.where(norths[0] == 1, row_b[comps * HALO], row_a[comps * HALO])
    beyond = jnp.where(lane % SUB < HALO, north, pltpu.roll(south, HALO, 1))
    natural = jnp.transpose(beyond)
    for field in range(FIELDS):
        block = natural[field * SUB : (field + 1) * SUB]
        for lon in range(cols):
            coef[field, SIDE + lon, pl.ds(rows, SUB), :] = lane_spread(block, lon)
    send_columns(par, state, (col_a, col_b), rows, SUB)
    tail = comps * SIDE * SUB
    for slot, msg in ((0, col_a), (1, col_b)):
        msg[pl.ds(tail, SUB), :] = jnp.zeros((SUB, LANES), jnp.float32)
        msg[pl.ds(tail, 1), :] = jnp.where(easts[slot] == 1, beyond[cols - 1 :], beyond[:1])


def model(own, x_diff, x_sum, above, below, sea, flow, depth, spin):
    keep, half = 1.0 - 4.0 * viscosity, 0.5 * gravity
    mixed = [
        keep * c + viscosity * (x + (n + s)) - flow * d
        for c, d, x, n, s in zip(own, x_diff, x_sum, above, below)
    ]
    v_y, h_y = above[1] - below[1], above[2] - below[2]
    return (
        sea * (mixed[0] - half * x_diff[2] + spin * own[1]),
        sea * (mixed[1] - half * h_y - spin * own[0]),
        sea * (mixed[2] - depth * (x_diff[0] + v_y)),
    )


def advance_column(source, target, coef_ref, spin_ref, lon, chosen=None):
    comps, length, tall, _ = source.shape
    flat = source.reshape(comps * length * tall, LANES)
    sub = lax.broadcasted_iota(jnp.int32, (SUB, LANES), 0)
    tiles = tall // SUB
    for tile in chosen or range(tiles):
        lines = pl.ds(SUB * tile, SUB)
        own, east, west = (
            [source[comp, lon + shift, lines, :] for comp in range(comps)] for shift in (0, 1, -1)
        )
        starts = [(comp * length + lon) * tall + SUB * tile for comp in range(comps)]
        if tile < tiles - 1:
            above = [flat[pl.ds(start + 1, SUB), :] for start in starts]
        else:
            wrap = [source[comp, lon, pl.ds(0, SUB), :] for comp in range(comps)]
            above = [
                jnp.where(sub == SUB - 1, pltpu.roll(w, SUB - 1, 0), pltpu.roll(o, SUB - 1, 0))
                for w, o in zip(wrap, own)
            ]
        if tile > 0:
            below = [flat[pl.ds(start - 1, SUB), :] for start in starts]
        else:
            wrap = [source[comp, lon, pl.ds(tall - SUB, SUB), :] for comp in range(comps)]
            below = [
                jnp.where(sub == 0, pltpu.roll(w, 1, 0), pltpu.roll(o, 1, 0))
                for w, o in zip(wrap, own)
            ]
        new = model(
            own,
            [e - w for e, w in zip(east, west)],
            [e + w for e, w in zip(east, west)],
            above,
            below,
            *(coef_ref[field, lon, lines, :] for field in range(FIELDS)),
            spin_ref[lines, :],
        )
        for comp in range(comps):
            target[comp, lon, lines, :] = new[comp]


def apply_inside(step, chosen, source, coef_ref, spin_ref, *refs):
    first = SIDE + step + 1
    count = source.shape[1] - 2 * first
    target = refs[-1]

    @pl.loop(0, count // 2)
    def _(pair):
        for lon in (first + 2 * pair, first + 2 * pair + 1):
            advance_column(source, target, coef_ref, spin_ref, lon, chosen)


def mend_columns(par, states, coef_ref, spin_ref, pieces):
    comps, length, _, _ = states[0].shape
    _, easts = sides_of(par)
    for first, count, cols_got in pieces:
        for slot, msg in enumerate(cols_got):
            for comp in range(comps):
                for j in range(SIDE):
                    column = column_at(easts[slot], length - 2 * SIDE, -1 - j)
                    states[0][comp, column, pl.ds(first, count), :] = msg[
                        pl.ds((comp * SIDE + j) * count, count), :
                    ]
    for step in range(STEPS):
        first = step + 1
        skip = length - 2 * first - 2 * SIDE

        @pl.loop(0, 2 * SIDE)
        def _(i):
            lon = first + i + (i // SIDE) * skip
            advance_column(states[step], states[step + 1], coef_ref, spin_ref, lon)


def join_gram(
    scale, par, start_in, middle_in, state_in, coef_in, spin_ref, a, b, c, d, start, middle, state, coef, col_a, col_b, kept, sent, total
):
    _, length, tall, _ = state.shape
    rows = tall - 2 * HALO
    _, easts = sides_of(par)
    for slot, (own, beyond) in enumerate(((a, c), (b, d))):
        own, beyond = (jnp.transpose(x[pl.ds(x.shape[0] - SUB, SUB), :]) for x in (own, beyond))
        column = column_at(easts[slot], length - 2 * SIDE, -1)
        for field in range(FIELDS):
            coef[field, column, pl.ds(0, rows), :] = lane_spread(own[:rows], field)
            coef[field, column, pl.ds(rows, SUB), :] = lane_spread(
                beyond[field * SUB : (field + 1) * SUB], 0
            )
    mend_columns(
        par, (start, middle, state), coef, spin_ref, ((0, rows, (a, b)), (rows, SUB, (c, d)))
    )
    send_columns(par, state, (col_a, col_b), 0, tall)
    gram = sum(gram_of(*split_halves(cells)) for _, _, cells in tiles_of(state))
    write_halves(par, gram, scale, kept, sent, total)


def tiles_of(state):
    comps, length, tall, _ = state.shape
    rows = tall - 2 * HALO
    for comp in range(comps):
        for lon in range(0, length - 2 * SIDE, SUB):
            cells = state[comp, pl.ds(SIDE + lon, SUB), pl.ds(0, rows), :]
            yield comp, lon, cells.reshape(SUB * rows, LANES)


def split_halves(value):
    high = value.astype(jnp.bfloat16)
    return high, (value - high.astype(jnp.float32)).astype(jnp.bfloat16)


def gram_of(high, low):
    return lax.dot_general(
        high,
        jnp.concatenate([high, low], axis=1),
        (((0,), (0,)), ((), ())),
        preferred_element_type=jnp.float32,
    )


def write_halves(par, gram, scale, kept, sent, total):
    half, rows = LANES // 2, kept.shape[0]
    mixed = gram[:, LANES:]
    whole = scale * (gram[:, :LANES] + (mixed + jnp.transpose(mixed)))
    row = lax.broadcasted_iota(jnp.int32, (half, LANES), 0)
    col = lax.broadcasted_iota(jnp.int32, (half, LANES), 1)
    total[pl.ds(0, half), :] = jnp.where(
        (col < half) | (col - half > row), whole[half:], pltpu.roll(whole[:half], half, 1)
    )
    row = lax.broadcasted_iota(jnp.int32, (LANES, LANES), 0)
    col = lax.broadcasted_iota(jnp.int32, (LANES, LANES), 1)
    total[pl.ds(half, 2 * rows - half), :] = jnp.zeros((2 * rows - half, LANES), jnp.float32)
    total[pl.ds(half, 1), :] = jnp.sum(jnp.where(row == col, whole, 0.0), axis=0, keepdims=True)
    odd = par[1] % 2
    kept[...] = total[pl.ds(odd * rows, rows), :]
    sent[...] = total[pl.ds((1 - odd) * rows, rows), :]


def factor_pair(low, p):
    q, size = p + 1, len(low)
    a, b, c = low[p][p], low[q][p], low[q][q]
    root_a, root_det = lax.rsqrt(a), lax.rsqrt(a * c - b * b)
    both = root_a * root_det
    turned = [a * low[i][q] - b * low[i][p] for i in range(q + 1, size)]
    low[q][p] = b * root_a
    for i, value in zip(range(q + 1, size), turned):
        low[i][p] = low[i][p] * root_a
        low[i][q] = value * both
    for i in range(q + 1, size):
        for m in range(q + 1, i + 1):
            low[i][m] = (low[i][m] - low[i][p] * low[m][p]) - low[i][q] * low[m][q]
    return root_a, a * both


def invert_factor(gram, work, board):
    count = LANES // SUB
    lane = lax.broadcasted_iota(jnp.int32, (SUB, LANES), 1)
    sub = lax.broadcasted_iota(jnp.int32, (SUB, LANES), 0)
    rows = [gram[SUB * i : SUB * (i + 1)] for i in range(count)]
    for block in range(count):
        base = SUB * block
        here = (lane >= base) & (lane < base + SUB)
        shelf = 2 * SUB * base
        for l in range(SUB):
            board[pl.ds(shelf + SUB * l, SUB), :] = lane_spread(rows[block], base + l)
        low = [
            [board[pl.ds(shelf + SUB * l + k, SUB, stride=0), :] for l in range(k + 1)]
            for k in range(SUB)
        ]
        shelf += SUB * SUB
        board[pl.ds(shelf, SUB), :] = jnp.where(
            here, jnp.where(lane - base == sub, 1.0, 0.0), rows[block]
        )
        inv = []
        for p in range(0, SUB, 2):
            inv.extend(factor_pair(low, p))
        scaled = []
        for k in range(SUB):
            line = board[pl.ds(shelf + k, SUB, stride=0), :]
            for l in range(k):
                line = line - low[k][l] * scaled[l]
            scaled.append(line * inv[k])
        merged = scaled[0]
        for k in range(1, SUB):
            merged = jnp.where(sub == k, scaled[k], merged)
        work[pl.ds(base, SUB), :] = merged
        for i in range(block + 1, count):
            weights = []
            rest = jnp.where(here, 0.0, rows[i])
            for l in range(SUB):
                weight = lane_spread(rows[i], base + l)
                for m in range(l):
                    weight = weight - weights[m] * low[l][m]
                weights.append(weight * inv[l])
            for l in range(SUB):
                rest = rest - weights[l] * scaled[l]
            rows[i] = rest


def factorize(par, mine_ref, other_ref, gram, work, board):
    half, rows = LANES // 2, mine_ref.shape[0]
    odd = par[1] % 2
    gram[pl.ds(odd * rows, rows), :] = mine_ref[...]
    gram[pl.ds((1 - odd) * rows, rows), :] = other_ref[...]
    packed, diagonal = gram[pl.ds(0, half), :], gram[pl.ds(half, 1), :]
    row = lax.broadcasted_iota(jnp.int32, (half, LANES), 0)
    col = lax.broadcasted_iota(jnp.int32, (half, LANES), 1)
    triangles = jnp.concatenate(
        [
            jnp.where(col < row, pltpu.roll(packed, half, 1), 0.0),
            jnp.where((col < half) | (col - half > row), packed, 0.0),
        ],
        axis=0,
    )
    row = lax.broadcasted_iota(jnp.int32, (LANES, LANES), 0)
    col = lax.broadcasted_iota(jnp.int32, (LANES, LANES), 1)
    size = jnp.broadcast_to(lax.rsqrt(diagonal), (LANES, LANES))
    whole = jnp.where(row == col, diagonal, triangles + jnp.transpose(triangles))
    invert_factor((whole * size) * jnp.transpose(size), work, board)
    inverse = jnp.where(row >= col, work[...], 0.0) * size
    diagonal = jnp.sum(jnp.where(row == col, inverse, 0.0), axis=0, keepdims=True)
    return inverse, diagonal


def paired(inverse):
    high = inverse.astype(jnp.bfloat16)
    low = (inverse - high.astype(jnp.float32)).astype(jnp.bfloat16)
    return jnp.concatenate(
        [jnp.concatenate([high, high], axis=1), jnp.concatenate([low, low], axis=1)], axis=0
    )


def times_factor(pair, factor):
    both = lax.dot_general(
        pair, factor, (((1,), (1,)), ((), ())), preferred_element_type=jnp.float32
    )
    return both[:, :LANES] + both[:, LANES:]


def factor_only(par, mine_ref, other_ref, prior_ref, _, inverse_ref, logs_ref, gram, work, board):
    inverse, diagonal = factorize(par, mine_ref, other_ref, gram, work, board)
    inverse_ref[...] = inverse
    logs_ref[...] = prior_ref[...] - jnp.log(diagonal)


def mend_only(par, start_in, middle_in, state_in, coef_ref, spin_ref, a, b, start, middle, state):
    tall = state.shape[2]
    mend_columns(par, (start, middle, state), coef_ref, spin_ref, ((0, tall, (a, b)),))


def update(scale, par, state, inverse_ref, out_ref, kept, sent, factor, total):
    factor[...] = paired(inverse_ref[...])
    gram = 0.0
    for comp, lon, cells in tiles_of(state):
        new = times_factor(jnp.concatenate(split_halves(cells), axis=1), factor[...])
        out_ref[comp, pl.ds(lon, SUB)] = new.reshape((SUB,) + out_ref.shape[2:])
        gram += gram_of(*split_halves(new))
    write_halves(par, gram, scale, kept, sent, total)


def restore_order(turned, out_ref):
    comps, cols, _, _ = turned.shape
    for comp in range(comps):
        for lon in range(0, cols, 2 * SUB):
            cells = jnp.concatenate(
                [
                    jnp.transpose(turned[comp, pl.ds(lon + shift, SUB)], (1, 0, 2))
                    for shift in (0, SUB)
                ],
                axis=1,
            )
            high = cells.astype(jnp.bfloat16)
            low = (cells - high.astype(jnp.float32)).astype(jnp.bfloat16)
            out_ref[comp, :, pl.ds(lon, 2 * SUB), pl.ds(0, LANES)] = high
            out_ref[comp, :, pl.ds(lon, 2 * SUB), pl.ds(LANES, LANES)] = low


def finish(
    par, mine_ref, other_ref, prior_ref, t_ref, out_ref, logs_ref, gram, work, board, factor, fresh, sems
):
    inverse, diagonal = factorize(par, mine_ref, other_ref, gram, work, board)
    logs_ref[...] = prior_ref[...] - jnp.log(diagonal)
    factor[...] = paired(inverse)

    def out_copy(tile):
        return pltpu.make_async_copy(fresh.at[tile], out_ref.at[tile], sems.at[tile])

    for tile in range(TILES):
        fresh[tile] = times_factor(t_ref[tile], factor[...])
        out_copy(tile).start(priority=tile % 2)

    for tile in range(TILES):
        out_copy(tile).wait()


def swap_pairs(near_value, far_value, axis, closed):
    count = lax.axis_size(axis)
    near = [(i, i ^ 1) for i in range(count)]
    far = [(i, (i + 1 if i % 2 else i - 1) % count) for i in range(count)]
    if not closed:
        far = far[1:-1]
    return lax.ppermute(near_value, axis, near), lax.ppermute(far_value, axis, far)


def swapped(value, axis, mask):
    return lax.ppermute(value, axis, [(i, i ^ mask) for i in range(lax.axis_size(axis))])


def add_two(first, second, _, out_ref):
    out_ref[...] = first[...] + second[...]


def add_beside(value, other, beside):
    return pl.pallas_call(
        add_two,
        out_shape=jax.ShapeDtypeStruct(value.shape, value.dtype),
        in_specs=[VMEM] * 2 + [pl.BlockSpec(memory_space=pl.ANY)],
        out_specs=VMEM,
        compiler_params=params(),
    )(value, other, beside)


def sum_over(value, axis, first_bit):
    bits = lax.axis_size(axis).bit_length() - 1
    while first_bit < bits:
        low = 1 << first_bit
        if first_bit + 1 < bits:
            high = low << 1
            three, two, one = (swapped(value, axis, mask) for mask in (low | high, high, low))
            value = (three + two) + (one + value)
            first_bit += 2
        else:
            value = value + swapped(value, axis, low)
            first_bit += 1
    return value


def sum_devices(kept, sent):
    mine = kept + swapped(sent, "col", 1)
    mine = sum_over(mine, "col", 1)
    mine = sum_over(mine, "row", 0)
    return mine, swapped(mine, "col", 1)


def sum_devices_beside(kept, sent, work):
    mine = kept + swapped(sent, "col", 1)
    for axis, first_bit in (("row", 0), ("col", 1)):
        for bit in range(first_bit, lax.axis_size(axis).bit_length() - 1):
            other = swapped(mine, axis, 1 << bit)
            mine = add_beside(mine, other, work.pop(0)) if work else mine + other
    return mine, swapped(mine, "col", 1)


def body(tangents, sea_mask, levels, current):
    comps, rows, cols, modes = tangents.shape
    total_rows = rows * lax.axis_size("row")
    total_cells = total_rows * cols * lax.axis_size("col")
    scale = 1.0 / total_cells
    row_at, col_at = lax.axis_index("row"), lax.axis_index("col")
    par = jnp.stack([row_at, col_at]).astype(jnp.int32)

    tall, length = rows + 2 * HALO, cols + 2 * SIDE

    block = shape_of(comps, length, tall, modes)
    coefs = shape_of(FIELDS, length, tall, LANES)
    columns = (shape_of(comps * SIDE * tall, modes),) * 2
    own_columns = (shape_of(comps * SIDE * rows + SUB, modes),) * 2
    corners = (shape_of(comps * SIDE * SUB + SUB, modes),) * 2
    rows_sent = (shape_of(comps * HALO + 1, cols, modes),) * 2
    halves = (shape_of(modes // 4 + SUB, modes),) * 2
    square = pltpu.VMEM((modes, modes), jnp.float32)
    board = pltpu.VMEM((2 * SUB * modes, LANES), jnp.float32)
    factor = pltpu.VMEM((2 * modes, 2 * modes), jnp.bfloat16)

    def call(
        kernel, outs, *operands, specs=None, out_specs=None, scratch=(), aliases=None, cost=1.0
    ):
        return pl.pallas_call(
            kernel,
            out_shape=outs,
            in_specs=specs or [SMEM] + [VMEM] * (len(operands) - 1),
            out_specs=out_specs or (VMEM,) * len(outs),
            scratch_shapes=scratch,
            input_output_aliases=aliases or {},
            compiler_params=params(),
            cost_estimate=pl.CostEstimate(
                flops=int(cost * 1e9), bytes_accessed=int(cost * 3e6), transcendentals=0
            ),
        )(*operands)

    def inside(step, state, chosen=None, partly=()):
        return call(
            functools.partial(apply_inside, step, chosen),
            (block,),
            state,
            coef,
            spin,
            *partly,
            specs=[VMEM] * (3 + len(partly)),
            aliases={3: 0} if partly else None,
            cost=2.0,
        )[0]

    def swap_columns(packed):
        return swap_pairs(*packed, "col", True)

    source, *fields = (
        pltpu.with_memory_space_constraint(x, pltpu.HBM)
        for x in (tangents, sea_mask.T, levels.T, current.T)
    )
    upright = [pltpu.VMEM(x.shape, x.dtype) for x in fields]
    packed = call(
        pack_rows,
        rows_sent,
        par,
        source,
        *fields,
        specs=[SMEM] + [HBM] * 4,
        scratch=upright
        + [
            pltpu.VMEM((cols, LANES), jnp.float32),
            pltpu.SemaphoreType.DMA((2 * comps,)),
            pltpu.SemaphoreType.DMA((FIELDS,)),
        ],
    )
    row_halos = swap_pairs(*packed, "row", False)
    start, coef, spin, *packed = call(
        functools.partial(spread_fields, total_rows),
        (block, coefs, shape_of(tall, LANES)) + own_columns,
        par,
        source,
        *fields,
        specs=[SMEM] + [HBM] * 4,
        scratch=[
            pltpu.VMEM((FIELDS, cols, LANES), jnp.float32),
            pltpu.VMEM(tangents.shape, jnp.float32),
        ]
        + upright
        + [pltpu.SemaphoreType.DMA((comps,)), pltpu.SemaphoreType.DMA((FIELDS,))],
        cost=3.0,
    )
    halos = swap_columns(packed)
    middle_tiles = tuple(range(1, rows // SUB - 1))
    outer_tiles = (0,) + tuple(range(rows // SUB - 1, tall // SUB))
    middle = inside(0, start, middle_tiles)
    start, coef, *packed = call(
        join_rows,
        (block, coefs) + corners,
        par,
        start,
        coef,
        *row_halos,
        middle,
        specs=[SMEM] + [VMEM] * 4 + [pl.BlockSpec(memory_space=pl.ANY)],
        aliases={1: 0, 2: 1},
    )
    halos += swap_columns(packed)
    logs = jnp.zeros((1, modes), jnp.float32)

    middle = inside(0, start, outer_tiles, (middle,))
    state = inside(1, middle)
    _, _, start, coef, *packed, kept, sent = call(
        functools.partial(join_gram, scale),
        (block, block, block, coefs) + columns + halves,
        par,
        start,
        middle,
        state,
        coef,
        spin,
        *halos,
        scratch=[square],
        aliases={1: 0, 2: 1, 3: 2, 4: 3},
        cost=2.0,
    )
    middle = inside(0, start)
    state = inside(1, middle)

    halos = swap_columns(packed)
    _, _, mended = call(
        mend_only,
        (block,) * 3,
        par,
        start,
        middle,
        state,
        coef,
        spin,
        *halos,
        aliases={1: 0, 2: 1, 3: 2},
    )
    mine, other = sum_devices_beside(kept, sent, [middle, state, mended])
    state = mended
    inverse, logs = call(
        factor_only,
        (shape_of(modes, modes), shape_of(1, modes)),
        par,
        mine,
        other,
        logs,
        state,
        specs=[SMEM] + [VMEM] * 3 + [pl.BlockSpec(memory_space=pl.ANY)],
        scratch=[square, square, board],
        cost=0.01,
    )
    state, kept, sent = call(
        functools.partial(update, scale),
        (shape_of(comps, cols, rows, modes),) + halves,
        par,
        state,
        inverse,
        scratch=[factor, square],
        cost=2.0,
    )
    state = call(
        restore_order,
        (jax.ShapeDtypeStruct((comps, rows, cols, 2 * modes), jnp.bfloat16),),
        state,
        specs=[VMEM],
        cost=1.0,
    )[0]
    height = comps * rows * cols // TILES
    tiled = shape_of(TILES, height, modes)
    mine, other = sum_devices(kept, sent)
    out, logs = call(
        finish,
        (tiled, shape_of(1, modes)),
        par,
        mine,
        other,
        logs,
        state.reshape(TILES, height, 2 * modes),
        out_specs=(HBM, VMEM),
        scratch=[
            square,
            square,
            board,
            factor,
            pltpu.VMEM((TILES, height, modes), jnp.float32),
            pltpu.SemaphoreType.DMA((TILES,)),
        ],
    )
    return out.reshape(tangents.shape), logs.reshape(modes)


def solution(mesh):
    placed = (P(None, "row", "col", None), P("row", "col"), P("row", "col"), P("row", "col"))
    return jax.shard_map(
        body,
        mesh=mesh,
        in_specs=placed,
        out_specs=(P(None, "row", "col", None), P()),
        check_vma=False,
    )
```

```python
import functools

import jax
import jax.numpy as jnp
from jax import lax
from jax.experimental import pallas as pl
from jax.experimental.pallas import tpu as pltpu
from jax.sharding import PartitionSpec as P

STEPS = 2
RENORMS = 2
LEVELS = 50

viscosity = 0.15
gravity = 0.5
rotation = 0.4

SUB = 8
LANES = 128
FIELDS = 3
HALO = STEPS * RENORMS
SIDE = STEPS
TILES = 24
BATCH = 16
VMEM_LIMIT = 16 * 1024 * 1024

HBM = pl.BlockSpec(memory_space=pltpu.HBM)
VMEM = pl.BlockSpec(memory_space=pltpu.VMEM)
SMEM = pl.BlockSpec(memory_space=pltpu.SMEM)


def params():
    return pltpu.CompilerParams(vmem_limit_bytes=VMEM_LIMIT)


def shape_of(*dims):
    return jax.ShapeDtypeStruct(dims, jnp.float32)


def lane_spread(block, lane):
    return jnp.broadcast_to(block[:, lane : lane + 1], (block.shape[0], LANES))


def fetch(sources, places, sems):
    copies = [
        pltpu.make_async_copy(source, place, sems.at[i])
        for i, (source, place) in enumerate(zip(sources, places))
    ]
    for copy in copies:
        copy.start()
    return copies


def finish_all(copies):
    for copy in copies:
        copy.wait()


def fields_of(sea_ref, levels_ref, current_ref):
    return (
        sea_ref[...].astype(jnp.float32),
        0.5 * current_ref[...],
        0.5 * ((levels_ref[...] + 1).astype(jnp.float32) / LEVELS),
    )


def sides_of(par):
    odd_row, odd_col = par[0] % 2, par[1] % 2
    return (1 - odd_row, odd_row), (1 - odd_col, odd_col)


def pack_rows(
    par, t_ref, sea_ref, levels_ref, current_ref, row_a, row_b, sea, levels, current, wide, sems, field_sems
):
    comps, rows, cols, _ = t_ref.shape
    norths, _ = sides_of(par)
    field_copies = fetch((sea_ref, levels_ref, current_ref), (sea, levels, current), field_sems)
    slots = [(slot, msg, comp) for slot, msg in ((0, row_a), (1, row_b)) for comp in range(comps)]
    copies = fetch(
        [t_ref.at[comp, pl.ds(norths[slot] * (rows - HALO), HALO)] for slot, _, comp in slots],
        [msg.at[pl.ds(comp * HALO, HALO)] for _, msg, comp in slots],
        sems,
    )
    lane = lax.broadcasted_iota(jnp.int32, (cols, LANES), 1)
    wide[...] = jnp.zeros_like(wide)
    packed = [jnp.zeros((cols, LANES), jnp.float32)] * 2
    finish_all(field_copies)
    for field, value in enumerate(fields_of(sea, levels, current)):
        wide[:, pl.ds(0, rows)] = value
        whole = wide[...]
        for north in (0, 1):
            shift = (field * SUB - north * (rows - HALO)) % LANES
            moved = pltpu.roll(whole, shift, 1) if shift else whole
            here = (lane >= field * SUB) & (lane < field * SUB + HALO)
            packed[north] = jnp.where(here, moved, packed[north])
    for slot, msg in ((0, row_a), (1, row_b)):
        msg[comps * HALO] = jnp.where(norths[slot] == 1, packed[1], packed[0])
    finish_all(copies)


def spread_fields(
    total_rows, par, t_ref, sea_ref, levels_ref, current_ref, state, coef, spin, col_a, col_b, wide, sea, levels, current, field_sems
):
    comps, rows, cols, _ = t_ref.shape
    field_copies = fetch((sea_ref, levels_ref, current_ref), (sea, levels, current), field_sems)
    line = lax.broadcasted_iota(jnp.int32, spin.shape, 0)
    line = jnp.where(line < rows + HALO, line, line - (rows + 2 * HALO))
    latitude = (par[0] * rows + line).astype(jnp.float32)
    angle = (-70.0 + 140.0 * (latitude + 0.5) / total_rows) * (jnp.pi / 180.0)
    spin[...] = rotation * jnp.sin(angle)
    wide[...] = jnp.zeros_like(wide)
    finish_all(field_copies)
    for field, value in enumerate(fields_of(sea, levels, current)):
        wide[field, :, pl.ds(0, rows)] = value
        natural = jnp.transpose(wide[field])[:rows]
        for lon in range(cols):
            coef[field, SIDE + lon, pl.ds(0, rows), :] = lane_spread(natural, lon)
    for comp in range(comps):
        for row in range(0, rows, SUB):
            cells = t_ref[comp, pl.ds(row, SUB)]
            state[comp, pl.ds(SIDE, cols), pl.ds(row, SUB), :] = jnp.transpose(cells, (1, 0, 2))
    send_columns(par, state, (col_a, col_b), 0, rows)
    tail = comps * SIDE * rows
    _, easts = sides_of(par)
    for slot, msg in enumerate((col_a, col_b)):
        msg[pl.ds(tail, SUB), :] = jnp.zeros((SUB, LANES), jnp.float32)
        for field in range(FIELDS):
            msg[pl.ds(tail + field, 1), :] = wide[field, pl.ds(easts[slot] * (cols - 1), 1), :]


def column_at(east, cols, depth):
    return SIDE + depth + east * (cols - 1 - 2 * depth)


def send_columns(par, state, cols_sent, first, count):
    comps, length, _, _ = state.shape
    _, easts = sides_of(par)
    for slot, msg in enumerate(cols_sent):
        for comp in range(comps):
            for j in range(SIDE):
                column = column_at(easts[slot], length - 2 * SIDE, j)
                msg[pl.ds((comp * SIDE + j) * count, count), :] = state[
                    comp, column, pl.ds(first, count), :
                ]


def join_rows(par, state_in, coef_in, row_a, row_b, _, state, coef, col_a, col_b):
    comps, length, tall, _ = state.shape
    cols, rows = length - 2 * SIDE, tall - 2 * HALO
    norths, easts = sides_of(par)
    flat = state.reshape(comps * length * tall, LANES)
    for slot, msg in ((0, row_a), (1, row_b)):
        line = rows + HALO * (1 - norths[slot])
        for comp in range(comps):
            for h in range(HALO):
                for lon in range(0, cols, SUB):
                    at = (comp * length + SIDE + lon) * tall + line + h
                    flat[pl.ds(at, SUB, stride=tall), :] = msg[comp * HALO + h, pl.ds(lon, SUB), :]
    lane = lax.broadcasted_iota(jnp.int32, (cols, LANES), 1)
    north = jnp.where(norths[0] == 1, row_a[comps * HALO], row_b[comps * HALO])
    south = jnp.where(norths[0] == 1, row_b[comps * HALO], row_a[comps * HALO])
    beyond = jnp.where(lane % SUB < HALO, north, pltpu.roll(south, HALO, 1))
    natural = jnp.transpose(beyond)
    for field in range(FIELDS):
        block = natural[field * SUB : (field + 1) * SUB]
        for lon in range(cols):
            coef[field, SIDE + lon, pl.ds(rows, SUB), :] = lane_spread(block, lon)
    send_columns(par, state, (col_a, col_b), rows, SUB)
    tail = comps * SIDE * SUB
    for slot, msg in ((0, col_a), (1, col_b)):
        msg[pl.ds(tail, SUB), :] = jnp.zeros((SUB, LANES), jnp.float32)
        msg[pl.ds(tail, 1), :] = jnp.where(easts[slot] == 1, beyond[cols - 1 :], beyond[:1])


def model(own, x_diff, x_sum, above, below, sea, flow, depth, spin):
    keep, half = 1.0 - 4.0 * viscosity, 0.5 * gravity
    mixed = [
        keep * c + viscosity * (x + (n + s)) - flow * d
        for c, d, x, n, s in zip(own, x_diff, x_sum, above, below)
    ]
    v_y, h_y = above[1] - below[1], above[2] - below[2]
    return (
        sea * (mixed[0] - half * x_diff[2] + spin * own[1]),
        sea * (mixed[1] - half * h_y - spin * own[0]),
        sea * (mixed[2] - depth * (x_diff[0] + v_y)),
    )


def advance_column(source, target, coef_ref, spin_ref, lon, chosen=None):
    comps, length, tall, _ = source.shape
    flat = source.reshape(comps * length * tall, LANES)
    sub = lax.broadcasted_iota(jnp.int32, (SUB, LANES), 0)
    tiles = tall // SUB
    for tile in chosen or range(tiles):
        lines = pl.ds(SUB * tile, SUB)
        own, east, west = (
            [source[comp, lon + shift, lines, :] for comp in range(comps)] for shift in (0, 1, -1)
        )
        starts = [(comp * length + lon) * tall + SUB * tile for comp in range(comps)]
        if tile < tiles - 1:
            above = [flat[pl.ds(start + 1, SUB), :] for start in starts]
        else:
            wrap = [source[comp, lon, pl.ds(0, SUB), :] for comp in range(comps)]
            above = [
                jnp.where(sub == SUB - 1, pltpu.roll(w, SUB - 1, 0), pltpu.roll(o, SUB - 1, 0))
                for w, o in zip(wrap, own)
            ]
        if tile > 0:
            below = [flat[pl.ds(start - 1, SUB), :] for start in starts]
        else:
            wrap = [source[comp, lon, pl.ds(tall - SUB, SUB), :] for comp in range(comps)]
            below = [
                jnp.where(sub == 0, pltpu.roll(w, 1, 0), pltpu.roll(o, 1, 0))
                for w, o in zip(wrap, own)
            ]
        new = model(
            own,
            [e - w for e, w in zip(east, west)],
            [e + w for e, w in zip(east, west)],
            above,
            below,
            *(coef_ref[field, lon, lines, :] for field in range(FIELDS)),
            spin_ref[lines, :],
        )
        for comp in range(comps):
            target[comp, lon, lines, :] = new[comp]


def apply_inside(step, chosen, source, coef_ref, spin_ref, *refs):
    first = SIDE + step + 1
    count = source.shape[1] - 2 * first
    target = refs[-1]

    @pl.loop(0, count // 2)
    def _(pair):
        for lon in (first + 2 * pair, first + 2 * pair + 1):
            advance_column(source, target, coef_ref, spin_ref, lon, chosen)


def mend_columns(par, states, coef_ref, spin_ref, pieces):
    comps, length, _, _ = states[0].shape
    _, easts = sides_of(par)
    for first, count, cols_got in pieces:
        for slot, msg in enumerate(cols_got):
            for comp in range(comps):
                for j in range(SIDE):
                    column = column_at(easts[slot], length - 2 * SIDE, -1 - j)
                    states[0][comp, column, pl.ds(first, count), :] = msg[
                        pl.ds((comp * SIDE + j) * count, count), :
                    ]
    for step in range(STEPS):
        first = step + 1
        skip = length - 2 * first - 2 * SIDE

        @pl.loop(0, 2 * SIDE)
        def _(i):
            lon = first + i + (i // SIDE) * skip
            advance_column(states[step], states[step + 1], coef_ref, spin_ref, lon)


def join_gram(
    scale, par, start_in, middle_in, state_in, coef_in, spin_ref, a, b, c, d, start, middle, state, coef, col_a, col_b, kept, sent, total
):
    _, length, tall, _ = state.shape
    rows = tall - 2 * HALO
    _, easts = sides_of(par)
    for slot, (own, beyond) in enumerate(((a, c), (b, d))):
        own, beyond = (jnp.transpose(x[pl.ds(x.shape[0] - SUB, SUB), :]) for x in (own, beyond))
        column = column_at(easts[slot], length - 2 * SIDE, -1)
        for field in range(FIELDS):
            coef[field, column, pl.ds(0, rows), :] = lane_spread(own[:rows], field)
            coef[field, column, pl.ds(rows, SUB), :] = lane_spread(
                beyond[field * SUB : (field + 1) * SUB], 0
            )
    mend_columns(
        par, (start, middle, state), coef, spin_ref, ((0, rows, (a, b)), (rows, SUB, (c, d)))
    )
    send_columns(par, state, (col_a, col_b), 0, tall)
    gram = sum(gram_of(*split_halves(cells)) for _, _, cells in tiles_of(state))
    write_halves(par, gram, scale, kept, sent, total)


def tiles_of(state):
    comps, length, tall, _ = state.shape
    rows = tall - 2 * HALO
    for comp in range(comps):
        for lon in range(0, length - 2 * SIDE, BATCH):
            cells = state[comp, pl.ds(SIDE + lon, BATCH), pl.ds(0, rows), :]
            yield comp, lon, cells.reshape(BATCH * rows, LANES)


def split_halves(value):
    high = value.astype(jnp.bfloat16)
    return high, (value - high.astype(jnp.float32)).astype(jnp.bfloat16)


def gram_of(high, low):
    return lax.dot_general(
        high,
        jnp.concatenate([high, low], axis=1),
        (((0,), (0,)), ((), ())),
        preferred_element_type=jnp.float32,
    )


def write_halves(par, gram, scale, kept, sent, total):
    half, rows = LANES // 2, kept.shape[0]
    mixed = gram[:, LANES:]
    whole = scale * (gram[:, :LANES] + (mixed + jnp.transpose(mixed)))
    row = lax.broadcasted_iota(jnp.int32, (half, LANES), 0)
    col = lax.broadcasted_iota(jnp.int32, (half, LANES), 1)
    total[pl.ds(0, half), :] = jnp.where(
        (col < half) | (col - half > row), whole[half:], pltpu.roll(whole[:half], half, 1)
    )
    row = lax.broadcasted_iota(jnp.int32, (LANES, LANES), 0)
    col = lax.broadcasted_iota(jnp.int32, (LANES, LANES), 1)
    total[pl.ds(half, 2 * rows - half), :] = jnp.zeros((2 * rows - half, LANES), jnp.float32)
    total[pl.ds(half, 1), :] = jnp.sum(jnp.where(row == col, whole, 0.0), axis=0, keepdims=True)
    odd = par[1] % 2
    kept[...] = total[pl.ds(odd * rows, rows), :]
    sent[...] = total[pl.ds((1 - odd) * rows, rows), :]


def factor_pair(low, p):
    q, size = p + 1, len(low)
    a, b, c = low[p][p], low[q][p], low[q][q]
    root_a, root_det = lax.rsqrt(a), lax.rsqrt(a * c - b * b)
    both = root_a * root_det
    turned = [a * low[i][q] - b * low[i][p] for i in range(q + 1, size)]
    low[q][p] = b * root_a
    for i, value in zip(range(q + 1, size), turned):
        low[i][p] = low[i][p] * root_a
        low[i][q] = value * both
    for i in range(q + 1, size):
        for m in range(q + 1, i + 1):
            low[i][m] = (low[i][m] - low[i][p] * low[m][p]) - low[i][q] * low[m][q]
    return root_a, a * both


def invert_factor(gram, work, board):
    count = LANES // SUB
    lane = lax.broadcasted_iota(jnp.int32, (SUB, LANES), 1)
    sub = lax.broadcasted_iota(jnp.int32, (SUB, LANES), 0)
    rows = [gram[SUB * i : SUB * (i + 1)] for i in range(count)]
    columns = [lane_spread(rows[0], l) for l in range(SUB)]
    for block in range(count):
        base = SUB * block
        here = (lane >= base) & (lane < base + SUB)
        shelf = 3 * SUB * base
        for l in range(SUB):
            board[pl.ds(shelf + SUB * l, SUB), :] = columns[l]
        low = [
            [board[pl.ds(shelf + SUB * l + k, SUB, stride=0), :] for l in range(k + 1)]
            for k in range(SUB)
        ]
        shelf += SUB * SUB
        board[pl.ds(shelf, SUB), :] = jnp.where(
            here, jnp.where(lane - base == sub, 1.0, 0.0), rows[block]
        )
        inv = []
        for p in range(0, SUB, 2):
            inv.extend(factor_pair(low, p))
        scaled = []
        for k in range(SUB):
            line = board[pl.ds(shelf + k, SUB, stride=0), :]
            for l in range(k):
                line = line - low[k][l] * scaled[l]
            scaled.append(line * inv[k])
        merged = scaled[0]
        for k in range(1, SUB):
            merged = jnp.where(sub == k, scaled[k], merged)
        work[pl.ds(base, SUB), :] = merged
        shelf += SUB
        for i in range(block + 1, count):
            weights = []
            for l in range(SUB):
                weight = lane_spread(rows[i], base + l)
                for m in range(l):
                    weight = weight - weights[m] * low[l][m]
                weights.append(weight * inv[l])
            if i == block + 1:
                columns = [lane_spread(rows[i], base + SUB + l) for l in range(SUB)]
                for l in range(SUB):
                    board[pl.ds(shelf + SUB * l, SUB), :] = weights[l]
                    for k in range(SUB):
                        across = board[pl.ds(shelf + SUB * l + k, SUB, stride=0), :]
                        columns[k] = columns[k] - weights[l] * across
            rest = jnp.where(here, 0.0, rows[i])
            for l in range(SUB):
                rest = rest - weights[l] * scaled[l]
            rows[i] = rest


def factorize(par, mine_ref, other_ref, gram, work, board):
    half, rows = LANES // 2, mine_ref.shape[0]
    odd = par[1] % 2
    gram[pl.ds(odd * rows, rows), :] = mine_ref[...]
    gram[pl.ds((1 - odd) * rows, rows), :] = other_ref[...]
    packed, diagonal = gram[pl.ds(0, half), :], gram[pl.ds(half, 1), :]
    row = lax.broadcasted_iota(jnp.int32, (half, LANES), 0)
    col = lax.broadcasted_iota(jnp.int32, (half, LANES), 1)
    triangles = jnp.concatenate(
        [
            jnp.where(col < row, pltpu.roll(packed, half, 1), 0.0),
            jnp.where((col < half) | (col - half > row), packed, 0.0),
        ],
        axis=0,
    )
    row = lax.broadcasted_iota(jnp.int32, (LANES, LANES), 0)
    col = lax.broadcasted_iota(jnp.int32, (LANES, LANES), 1)
    size = jnp.broadcast_to(lax.rsqrt(diagonal), (LANES, LANES))
    whole = jnp.where(row == col, diagonal, triangles + jnp.transpose(triangles))
    invert_factor((whole * size) * jnp.transpose(size), work, board)
    inverse = jnp.where(row >= col, work[...], 0.0) * size
    diagonal = jnp.sum(jnp.where(row == col, inverse, 0.0), axis=0, keepdims=True)
    return inverse, diagonal


def paired(inverse):
    high = inverse.astype(jnp.bfloat16)
    low = (inverse - high.astype(jnp.float32)).astype(jnp.bfloat16)
    return jnp.concatenate(
        [jnp.concatenate([high, high], axis=1), jnp.concatenate([low, low], axis=1)], axis=0
    )


def times_factor(pair, factor):
    both = lax.dot_general(
        pair, factor, (((1,), (1,)), ((), ())), preferred_element_type=jnp.float32
    )
    return both[:, :LANES] + both[:, LANES:]


def factor_only(par, mine_ref, other_ref, prior_ref, _, inverse_ref, logs_ref, gram, work, board):
    inverse, diagonal = factorize(par, mine_ref, other_ref, gram, work, board)
    inverse_ref[...] = inverse
    logs_ref[...] = prior_ref[...] - jnp.log(diagonal)


def mend_only(par, start_in, middle_in, state_in, coef_ref, spin_ref, a, b, start, middle, state):
    tall = state.shape[2]
    mend_columns(par, (start, middle, state), coef_ref, spin_ref, ((0, tall, (a, b)),))


def update(scale, par, state, inverse_ref, out_ref, kept, sent, factor, total):
    factor[...] = paired(inverse_ref[...])
    gram = 0.0
    for comp, lon, cells in tiles_of(state):
        new = times_factor(jnp.concatenate(split_halves(cells), axis=1), factor[...])
        out_ref[comp, pl.ds(lon, BATCH)] = new.reshape((BATCH,) + out_ref.shape[2:])
        gram += gram_of(*split_halves(new))
    write_halves(par, gram, scale, kept, sent, total)


def restore_order(turned, out_ref):
    comps, cols, _, _ = turned.shape
    for comp in range(comps):
        for lon in range(0, cols, 2 * SUB):
            cells = jnp.concatenate(
                [
                    jnp.transpose(turned[comp, pl.ds(lon + shift, SUB)], (1, 0, 2))
                    for shift in (0, SUB)
                ],
                axis=1,
            )
            high = cells.astype(jnp.bfloat16)
            low = (cells - high.astype(jnp.float32)).astype(jnp.bfloat16)
            out_ref[comp, :, pl.ds(lon, 2 * SUB), pl.ds(0, LANES)] = high
            out_ref[comp, :, pl.ds(lon, 2 * SUB), pl.ds(LANES, LANES)] = low


def finish(
    par, mine_ref, other_ref, prior_ref, t_ref, out_ref, logs_ref, gram, work, board, factor, fresh, sems
):
    inverse, diagonal = factorize(par, mine_ref, other_ref, gram, work, board)
    factor[...] = paired(inverse)

    def out_copy(tile):
        return pltpu.make_async_copy(fresh.at[tile], out_ref.at[tile], sems.at[tile])

    for tile in range(TILES):
        fresh[tile] = times_factor(t_ref[tile], factor[...])
        out_copy(tile).start(priority=tile % 2)
    logs_ref[...] = prior_ref[...] - jnp.log(diagonal)

    for tile in range(TILES):
        out_copy(tile).wait()


def swap_pairs(near_value, far_value, axis, closed):
    count = lax.axis_size(axis)
    near = [(i, i ^ 1) for i in range(count)]
    far = [(i, (i + 1 if i % 2 else i - 1) % count) for i in range(count)]
    if not closed:
        far = far[1:-1]
    return lax.ppermute(near_value, axis, near), lax.ppermute(far_value, axis, far)


def swapped(value, axis, mask):
    return lax.ppermute(value, axis, [(i, i ^ mask) for i in range(lax.axis_size(axis))])


def add_four(first, second, third, fourth, *rest):
    out_ref = rest[len(rest) // 2]
    out_ref[...] = (first[...] + fourth[...]) + (third[...] + second[...])


def sum_over(value, axis, first_bit, beside=None, held=()):
    bits = lax.axis_size(axis).bit_length() - 1
    while first_bit < bits:
        low = 1 << first_bit
        if first_bit + 1 < bits:
            high = low << 1
            three, two, one = (swapped(value, axis, mask) for mask in (low | high, high, low))
            if beside is None:
                value = (three + two) + (one + value)
            else:
                anywhere = pl.BlockSpec(memory_space=pl.ANY)
                value, *held = pl.pallas_call(
                    add_four,
                    out_shape=[jax.ShapeDtypeStruct(x.shape, x.dtype) for x in (value, *held)],
                    in_specs=[VMEM] * 4 + [anywhere] * (1 + len(held)),
                    out_specs=[VMEM] + [anywhere] * len(held),
                    input_output_aliases={5 + i: 1 + i for i in range(len(held))},
                    compiler_params=params(),
                )(value, three, two, one, beside, *held)
                beside = None
            first_bit += 2
        else:
            value = value + swapped(value, axis, low)
            first_bit += 1
    return value, held


def sum_devices(kept, sent, beside=(None, None), held=()):
    mine = kept + swapped(sent, "col", 1)
    mine, held = sum_over(mine, "col", 1, beside[0], held)
    mine, _ = sum_over(mine, "row", 0, beside[1])
    return mine, swapped(mine, "col", 1), held


def body(tangents, sea_mask, levels, current):
    comps, rows, cols, modes = tangents.shape
    total_rows = rows * lax.axis_size("row")
    total_cells = total_rows * cols * lax.axis_size("col")
    scale = 1.0 / total_cells
    row_at, col_at = lax.axis_index("row"), lax.axis_index("col")
    par = jnp.stack([row_at, col_at]).astype(jnp.int32)

    tall, length = rows + 2 * HALO, cols + 2 * SIDE

    block = shape_of(comps, length, tall, modes)
    coefs = shape_of(FIELDS, length, tall, LANES)
    columns = (shape_of(comps * SIDE * tall, modes),) * 2
    own_columns = (shape_of(comps * SIDE * rows + SUB, modes),) * 2
    corners = (shape_of(comps * SIDE * SUB + SUB, modes),) * 2
    rows_sent = (shape_of(comps * HALO + 1, cols, modes),) * 2
    halves = (shape_of(modes // 4 + SUB, modes),) * 2
    square = pltpu.VMEM((modes, modes), jnp.float32)
    board = pltpu.VMEM((3 * SUB * modes, LANES), jnp.float32)
    factor = pltpu.VMEM((2 * modes, 2 * modes), jnp.bfloat16)

    def call(
        kernel, outs, *operands, specs=None, out_specs=None, scratch=(), aliases=None, cost=1.0
    ):
        return pl.pallas_call(
            kernel,
            out_shape=outs,
            in_specs=specs or [SMEM] + [VMEM] * (len(operands) - 1),
            out_specs=out_specs or (VMEM,) * len(outs),
            scratch_shapes=scratch,
            input_output_aliases=aliases or {},
            compiler_params=params(),
            cost_estimate=pl.CostEstimate(
                flops=int(cost * 1e9), bytes_accessed=int(cost * 3e6), transcendentals=0
            ),
        )(*operands)

    def inside(step, state, chosen=None, partly=()):
        return call(
            functools.partial(apply_inside, step, chosen),
            (block,),
            state,
            coef,
            spin,
            *partly,
            specs=[VMEM] * (3 + len(partly)),
            aliases={3: 0} if partly else None,
            cost=2.0,
        )[0]

    def swap_columns(packed):
        return swap_pairs(*packed, "col", True)

    source, *fields = (
        pltpu.with_memory_space_constraint(x, pltpu.HBM)
        for x in (tangents, sea_mask.T, levels.T, current.T)
    )
    upright = [pltpu.VMEM(x.shape, x.dtype) for x in fields]
    packed = call(
        pack_rows,
        rows_sent,
        par,
        source,
        *fields,
        specs=[SMEM] + [HBM] * 4,
        scratch=upright
        + [
            pltpu.VMEM((cols, LANES), jnp.float32),
            pltpu.SemaphoreType.DMA((2 * comps,)),
            pltpu.SemaphoreType.DMA((FIELDS,)),
        ],
        cost=5.0,
    )
    row_halos = swap_pairs(*packed, "row", False)
    start, coef, spin, *packed = call(
        functools.partial(spread_fields, total_rows),
        (block, coefs, shape_of(tall, LANES)) + own_columns,
        par,
        tangents,
        *fields,
        specs=[SMEM, VMEM] + [HBM] * 3,
        scratch=[pltpu.VMEM((FIELDS, cols, LANES), jnp.float32)]
        + upright
        + [pltpu.SemaphoreType.DMA((FIELDS,))],
        cost=3.0,
    )
    halos = swap_columns(packed)
    middle_tiles = tuple(range(1, rows // SUB - 1))
    outer_tiles = (0,) + tuple(range(rows // SUB - 1, tall // SUB))
    middle = inside(0, start, middle_tiles)
    start, coef, *packed = call(
        join_rows,
        (block, coefs) + corners,
        par,
        start,
        coef,
        *row_halos,
        middle,
        specs=[SMEM] + [VMEM] * 4 + [pl.BlockSpec(memory_space=pl.ANY)],
        aliases={1: 0, 2: 1},
    )
    halos += swap_columns(packed)
    logs = jnp.zeros((1, modes), jnp.float32)

    middle = inside(0, start, outer_tiles, (middle,))
    state = inside(1, middle)
    _, _, start, coef, *packed, kept, sent = call(
        functools.partial(join_gram, scale),
        (block, block, block, coefs) + columns + halves,
        par,
        start,
        middle,
        state,
        coef,
        spin,
        *halos,
        scratch=[square],
        aliases={1: 0, 2: 1, 3: 2, 4: 3},
        cost=2.0,
    )
    middle = inside(0, start)
    state = inside(1, middle)

    mine, other, packed = sum_devices(kept, sent, (middle, state), packed)
    halos = swap_columns(packed)
    _, _, state = call(
        mend_only,
        (block,) * 3,
        par,
        start,
        middle,
        state,
        coef,
        spin,
        *halos,
        aliases={1: 0, 2: 1, 3: 2},
    )
    inverse, logs = call(
        factor_only,
        (shape_of(modes, modes), shape_of(1, modes)),
        par,
        mine,
        other,
        logs,
        state,
        specs=[SMEM] + [VMEM] * 3 + [pl.BlockSpec(memory_space=pl.ANY)],
        scratch=[square, square, board],
        cost=0.01,
    )
    state, kept, sent = call(
        functools.partial(update, scale),
        (shape_of(comps, cols, rows, modes),) + halves,
        par,
        state,
        inverse,
        scratch=[factor, square],
        cost=2.0,
    )
    state = call(
        restore_order,
        (jax.ShapeDtypeStruct((comps, rows, cols, 2 * modes), jnp.bfloat16),),
        state,
        specs=[VMEM],
        cost=1.0,
    )[0]
    height = comps * rows * cols // TILES
    tiled = shape_of(TILES, height, modes)
    mine, other, _ = sum_devices(kept, sent)
    out, logs = call(
        finish,
        (tiled, shape_of(1, modes)),
        par,
        mine,
        other,
        logs,
        state.reshape(TILES, height, 2 * modes),
        out_specs=(HBM, VMEM),
        scratch=[
            square,
            square,
            board,
            factor,
            pltpu.VMEM((TILES, height, modes), jnp.float32),
            pltpu.SemaphoreType.DMA((TILES,)),
        ],
    )
    return out.reshape(tangents.shape), logs.reshape(modes)


def solution(mesh):
    placed = (P(None, "row", "col", None), P("row", "col"), P("row", "col"), P("row", "col"))
    return jax.shard_map(
        body,
        mesh=mesh,
        in_specs=placed,
        out_specs=(P(None, "row", "col", None), P()),
        check_vma=False,
    )
```

```python
import functools

import jax
import jax.numpy as jnp
from jax import lax
from jax.experimental import pallas as pl
from jax.experimental.pallas import tpu as pltpu
from jax.sharding import PartitionSpec as P

STEPS = 2
RENORMS = 2
LEVELS = 50

viscosity = 0.15
gravity = 0.5
rotation = 0.4

SUB = 8
LANES = 128
FIELDS = 3
HALO = STEPS * RENORMS
SIDE = STEPS
TILES = 24
BATCH = 8
GROUP = 4
VMEM_LIMIT = 16 * 1024 * 1024

HBM = pl.BlockSpec(memory_space=pltpu.HBM)
VMEM = pl.BlockSpec(memory_space=pltpu.VMEM)
SMEM = pl.BlockSpec(memory_space=pltpu.SMEM)


def params():
    return pltpu.CompilerParams(vmem_limit_bytes=VMEM_LIMIT)


def shape_of(*dims):
    return jax.ShapeDtypeStruct(dims, jnp.float32)


def lane_spread(block, lane):
    return jnp.broadcast_to(block[:, lane : lane + 1], (block.shape[0], LANES))


def fetch(sources, places, sems):
    copies = [
        pltpu.make_async_copy(source, place, sems.at[i])
        for i, (source, place) in enumerate(zip(sources, places))
    ]
    for copy in copies:
        copy.start()
    return copies


def finish_all(copies):
    for copy in copies:
        copy.wait()


def fields_of(sea_ref, levels_ref, current_ref):
    return (
        sea_ref[...].astype(jnp.float32),
        0.5 * current_ref[...],
        0.5 * ((levels_ref[...] + 1).astype(jnp.float32) / LEVELS),
    )


def sides_of(par):
    odd_row, odd_col = par[0] % 2, par[1] % 2
    return (1 - odd_row, odd_row), (1 - odd_col, odd_col)


def pack_rows(
    par, t_ref, sea_ref, levels_ref, current_ref, row_a, row_b, sea, levels, current, wide, sems, field_sems
):
    comps, rows, cols, _ = t_ref.shape
    norths, _ = sides_of(par)
    field_copies = fetch((sea_ref, levels_ref, current_ref), (sea, levels, current), field_sems)
    slots = [(slot, msg, comp) for slot, msg in ((0, row_a), (1, row_b)) for comp in range(comps)]
    copies = fetch(
        [t_ref.at[comp, pl.ds(norths[slot] * (rows - HALO), HALO)] for slot, _, comp in slots],
        [msg.at[pl.ds(comp * HALO, HALO)] for _, msg, comp in slots],
        sems,
    )
    lane = lax.broadcasted_iota(jnp.int32, (cols, LANES), 1)
    wide[...] = jnp.zeros_like(wide)
    packed = [jnp.zeros((cols, LANES), jnp.float32)] * 2
    finish_all(field_copies)
    for field, value in enumerate(fields_of(sea, levels, current)):
        wide[:, pl.ds(0, rows)] = value
        whole = wide[...]
        for north in (0, 1):
            shift = (field * SUB - north * (rows - HALO)) % LANES
            moved = pltpu.roll(whole, shift, 1) if shift else whole
            here = (lane >= field * SUB) & (lane < field * SUB + HALO)
            packed[north] = jnp.where(here, moved, packed[north])
    for slot, msg in ((0, row_a), (1, row_b)):
        msg[comps * HALO] = jnp.where(norths[slot] == 1, packed[1], packed[0])
    finish_all(copies)


def spread_fields(
    total_rows, par, t_ref, sea_ref, levels_ref, current_ref, state, coef, spin, col_a, col_b, wide, sea, levels, current, field_sems
):
    comps, rows, cols, _ = t_ref.shape
    field_copies = fetch((sea_ref, levels_ref, current_ref), (sea, levels, current), field_sems)
    line = lax.broadcasted_iota(jnp.int32, spin.shape, 0)
    line = jnp.where(line < rows + HALO, line, line - (rows + 2 * HALO))
    latitude = (par[0] * rows + line).astype(jnp.float32)
    angle = (-70.0 + 140.0 * (latitude + 0.5) / total_rows) * (jnp.pi / 180.0)
    spin[...] = rotation * jnp.sin(angle)
    wide[...] = jnp.zeros_like(wide)
    finish_all(field_copies)
    for field, value in enumerate(fields_of(sea, levels, current)):
        wide[field, :, pl.ds(0, rows)] = value
        natural = jnp.transpose(wide[field])[:rows]
        for lon in range(cols):
            coef[field, SIDE + lon, pl.ds(0, rows), :] = lane_spread(natural, lon)
    for comp in range(comps):
        for row in range(0, rows, SUB):
            cells = t_ref[comp, pl.ds(row, SUB)]
            state[comp, pl.ds(SIDE, cols), pl.ds(row, SUB), :] = jnp.transpose(cells, (1, 0, 2))
    send_columns(par, state, (col_a, col_b), 0, rows)
    tail = comps * SIDE * rows
    _, easts = sides_of(par)
    for slot, msg in enumerate((col_a, col_b)):
        msg[pl.ds(tail, SUB), :] = jnp.zeros((SUB, LANES), jnp.float32)
        for field in range(FIELDS):
            msg[pl.ds(tail + field, 1), :] = wide[field, pl.ds(easts[slot] * (cols - 1), 1), :]


def column_at(east, cols, depth):
    return SIDE + depth + east * (cols - 1 - 2 * depth)


def send_columns(par, state, cols_sent, first, count):
    comps, length, _, _ = state.shape
    _, easts = sides_of(par)
    for slot, msg in enumerate(cols_sent):
        for comp in range(comps):
            for j in range(SIDE):
                column = column_at(easts[slot], length - 2 * SIDE, j)
                msg[pl.ds((comp * SIDE + j) * count, count), :] = state[
                    comp, column, pl.ds(first, count), :
                ]


def join_rows(par, state_in, coef_in, row_a, row_b, _, state, coef, col_a, col_b):
    comps, length, tall, _ = state.shape
    cols, rows = length - 2 * SIDE, tall - 2 * HALO
    norths, easts = sides_of(par)
    flat = state.reshape(comps * length * tall, LANES)
    for slot, msg in ((0, row_a), (1, row_b)):
        line = rows + HALO * (1 - norths[slot])
        for comp in range(comps):
            for h in range(HALO):
                for lon in range(0, cols, SUB):
                    at = (comp * length + SIDE + lon) * tall + line + h
                    flat[pl.ds(at, SUB, stride=tall), :] = msg[comp * HALO + h, pl.ds(lon, SUB), :]
    lane = lax.broadcasted_iota(jnp.int32, (cols, LANES), 1)
    north = jnp.where(norths[0] == 1, row_a[comps * HALO], row_b[comps * HALO])
    south = jnp.where(norths[0] == 1, row_b[comps * HALO], row_a[comps * HALO])
    beyond = jnp.where(lane % SUB < HALO, north, pltpu.roll(south, HALO, 1))
    natural = jnp.transpose(beyond)
    for field in range(FIELDS):
        block = natural[field * SUB : (field + 1) * SUB]
        for lon in range(cols):
            coef[field, SIDE + lon, pl.ds(rows, SUB), :] = lane_spread(block, lon)
    send_columns(par, state, (col_a, col_b), rows, SUB)
    tail = comps * SIDE * SUB
    for slot, msg in ((0, col_a), (1, col_b)):
        msg[pl.ds(tail, SUB), :] = jnp.zeros((SUB, LANES), jnp.float32)
        msg[pl.ds(tail, 1), :] = jnp.where(easts[slot] == 1, beyond[cols - 1 :], beyond[:1])


def model(own, x_diff, x_sum, above, below, sea, flow, depth, spin):
    keep, half = 1.0 - 4.0 * viscosity, 0.5 * gravity
    mixed = [
        keep * c + viscosity * (x + (n + s)) - flow * d
        for c, d, x, n, s in zip(own, x_diff, x_sum, above, below)
    ]
    v_y, h_y = above[1] - below[1], above[2] - below[2]
    return (
        sea * (mixed[0] - half * x_diff[2] + spin * own[1]),
        sea * (mixed[1] - half * h_y - spin * own[0]),
        sea * (mixed[2] - depth * (x_diff[0] + v_y)),
    )


def advance_column(source, target, coef_ref, spin_ref, lon, chosen=None):
    comps, length, tall, _ = source.shape
    flat = source.reshape(comps * length * tall, LANES)
    sub = lax.broadcasted_iota(jnp.int32, (SUB, LANES), 0)
    tiles = tall // SUB
    for tile in chosen or range(tiles):
        lines = pl.ds(SUB * tile, SUB)
        own, east, west = (
            [source[comp, lon + shift, lines, :] for comp in range(comps)] for shift in (0, 1, -1)
        )
        starts = [(comp * length + lon) * tall + SUB * tile for comp in range(comps)]
        if tile < tiles - 1:
            above = [flat[pl.ds(start + 1, SUB), :] for start in starts]
        else:
            wrap = [source[comp, lon, pl.ds(0, SUB), :] for comp in range(comps)]
            above = [
                jnp.where(sub == SUB - 1, pltpu.roll(w, SUB - 1, 0), pltpu.roll(o, SUB - 1, 0))
                for w, o in zip(wrap, own)
            ]
        if tile > 0:
            below = [flat[pl.ds(start - 1, SUB), :] for start in starts]
        else:
            wrap = [source[comp, lon, pl.ds(tall - SUB, SUB), :] for comp in range(comps)]
            below = [
                jnp.where(sub == 0, pltpu.roll(w, 1, 0), pltpu.roll(o, 1, 0))
                for w, o in zip(wrap, own)
            ]
        new = model(
            own,
            [e - w for e, w in zip(east, west)],
            [e + w for e, w in zip(east, west)],
            above,
            below,
            *(coef_ref[field, lon, lines, :] for field in range(FIELDS)),
            spin_ref[lines, :],
        )
        for comp in range(comps):
            target[comp, lon, lines, :] = new[comp]


def apply_inside(step, chosen, source, coef_ref, spin_ref, *refs):
    first = SIDE + step + 1
    count = source.shape[1] - 2 * first
    target = refs[-1]

    @pl.loop(0, count // 2)
    def _(pair):
        for lon in (first + 2 * pair, first + 2 * pair + 1):
            advance_column(source, target, coef_ref, spin_ref, lon, chosen)


def mend_columns(par, states, coef_ref, spin_ref, pieces):
    comps, length, _, _ = states[0].shape
    _, easts = sides_of(par)
    for first, count, cols_got in pieces:
        for slot, msg in enumerate(cols_got):
            for comp in range(comps):
                for j in range(SIDE):
                    column = column_at(easts[slot], length - 2 * SIDE, -1 - j)
                    states[0][comp, column, pl.ds(first, count), :] = msg[
                        pl.ds((comp * SIDE + j) * count, count), :
                    ]
    for step in range(STEPS):
        first = step + 1
        skip = length - 2 * first - 2 * SIDE

        @pl.loop(0, 2 * SIDE)
        def _(i):
            lon = first + i + (i // SIDE) * skip
            advance_column(states[step], states[step + 1], coef_ref, spin_ref, lon)


def join_gram(
    scale, par, start_in, middle_in, state_in, coef_in, spin_ref, a, b, c, d, start, middle, state, coef, col_a, col_b, kept, sent, total
):
    _, length, tall, _ = state.shape
    rows = tall - 2 * HALO
    _, easts = sides_of(par)
    for slot, (own, beyond) in enumerate(((a, c), (b, d))):
        own, beyond = (jnp.transpose(x[pl.ds(x.shape[0] - SUB, SUB), :]) for x in (own, beyond))
        column = column_at(easts[slot], length - 2 * SIDE, -1)
        for field in range(FIELDS):
            coef[field, column, pl.ds(0, rows), :] = lane_spread(own[:rows], field)
            coef[field, column, pl.ds(rows, SUB), :] = lane_spread(
                beyond[field * SUB : (field + 1) * SUB], 0
            )
    mend_columns(
        par, (start, middle, state), coef, spin_ref, ((0, rows, (a, b)), (rows, SUB, (c, d)))
    )
    send_columns(par, state, (col_a, col_b), 0, tall)
    gram = sum(gram_of(*split_halves(cells)) for _, _, cells in tiles_of(state))
    write_halves(par, gram, scale, kept, sent, total)


def tiles_of(state):
    comps, length, tall, _ = state.shape
    rows = tall - 2 * HALO
    for comp in range(comps):
        for lon in range(0, length - 2 * SIDE, BATCH):
            cells = state[comp, pl.ds(SIDE + lon, BATCH), pl.ds(0, rows), :]
            yield comp, lon, cells.reshape(BATCH * rows, LANES)


def split_halves(value):
    high = value.astype(jnp.bfloat16)
    return high, (value - high.astype(jnp.float32)).astype(jnp.bfloat16)


def gram_of(high, low):
    return lax.dot_general(
        high,
        jnp.concatenate([high, low], axis=1),
        (((0,), (0,)), ((), ())),
        preferred_element_type=jnp.float32,
    )


def write_halves(par, gram, scale, kept, sent, total):
    half, rows = LANES // 2, kept.shape[0]
    mixed = gram[:, LANES:]
    whole = scale * (gram[:, :LANES] + (mixed + jnp.transpose(mixed)))
    row = lax.broadcasted_iota(jnp.int32, (half, LANES), 0)
    col = lax.broadcasted_iota(jnp.int32, (half, LANES), 1)
    total[pl.ds(0, half), :] = jnp.where(
        (col < half) | (col - half > row), whole[half:], pltpu.roll(whole[:half], half, 1)
    )
    row = lax.broadcasted_iota(jnp.int32, (LANES, LANES), 0)
    col = lax.broadcasted_iota(jnp.int32, (LANES, LANES), 1)
    total[pl.ds(half, 2 * rows - half), :] = jnp.zeros((2 * rows - half, LANES), jnp.float32)
    total[pl.ds(half, 1), :] = jnp.sum(jnp.where(row == col, whole, 0.0), axis=0, keepdims=True)
    odd = par[1] % 2
    kept[...] = total[pl.ds(odd * rows, rows), :]
    sent[...] = total[pl.ds((1 - odd) * rows, rows), :]


def factor_pair(low, p):
    q, size = p + 1, len(low)
    a, b, c = low[p][p], low[q][p], low[q][q]
    root_a, root_det = lax.rsqrt(a), lax.rsqrt(a * c - b * b)
    both = root_a * root_det
    turned = [a * low[i][q] - b * low[i][p] for i in range(q + 1, size)]
    low[q][p] = b * root_a
    for i, value in zip(range(q + 1, size), turned):
        low[i][p] = low[i][p] * root_a
        low[i][q] = value * both
    for i in range(q + 1, size):
        for m in range(q + 1, i + 1):
            low[i][m] = (low[i][m] - low[i][p] * low[m][p]) - low[i][q] * low[m][q]
    return root_a, a * both


def square_of(pivots):
    high = pivots.astype(jnp.bfloat16)
    rest = pivots - high.astype(jnp.float32)
    middle = rest.astype(jnp.bfloat16)
    low = (rest - middle.astype(jnp.float32)).astype(jnp.bfloat16)
    return lax.dot_general(
        jnp.concatenate([high, high, middle, middle, high, low], axis=0),
        jnp.concatenate([high, middle, high, middle, low, high], axis=0),
        (((0,), (0,)), ((), ())),
        preferred_element_type=jnp.float32,
    )


def invert_factor(gram, work, board):
    count = LANES // SUB
    lane = lax.broadcasted_iota(jnp.int32, (SUB, LANES), 1)
    sub = lax.broadcasted_iota(jnp.int32, (SUB, LANES), 0)
    rows = [gram[SUB * i : SUB * (i + 1)] for i in range(count)]
    for block in range(count):
        base = SUB * block
        here = (lane >= base) & (lane < base + SUB)
        shelf = 2 * SUB * base
        for l in range(SUB):
            board[pl.ds(shelf + SUB * l, SUB), :] = lane_spread(rows[block], base + l)
        low = [
            [board[pl.ds(shelf + SUB * l + k, SUB, stride=0), :] for l in range(k + 1)]
            for k in range(SUB)
        ]
        shelf += SUB * SUB
        board[pl.ds(shelf, SUB), :] = jnp.where(
            here, jnp.where(lane - base == sub, 1.0, 0.0), rows[block]
        )
        inv = []
        for p in range(0, SUB, 2):
            inv.extend(factor_pair(low, p))
        scaled = []
        for k in range(SUB):
            line = board[pl.ds(shelf + k, SUB, stride=0), :]
            for l in range(k):
                line = line - low[k][l] * scaled[l]
            scaled.append(line * inv[k])
        merged = scaled[0]
        for k in range(1, SUB):
            merged = jnp.where(sub == k, scaled[k], merged)
        work[pl.ds(base, SUB), :] = merged
        for i in range(block + 1, (block // GROUP + 1) * GROUP):
            weights = []
            rest = jnp.where(here, 0.0, rows[i])
            for l in range(SUB):
                weight = lane_spread(rows[i], base + l)
                for m in range(l):
                    weight = weight - weights[m] * low[l][m]
                weights.append(weight * inv[l])
            for l in range(SUB):
                rest = rest - weights[l] * scaled[l]
            rows[i] = rest
        if block % GROUP == GROUP - 1 and block + 1 < count:
            first = SUB * (block + 1 - GROUP)
            tall = (SUB * GROUP, LANES)
            to_lane = lax.broadcasted_iota(jnp.int32, tall, 1) // SUB - first // SUB
            to_row = lax.broadcasted_iota(jnp.int32, tall, 0) // SUB
            pivots = work[pl.ds(first, SUB * GROUP), :]
            update = square_of(jnp.where((to_lane > to_row) & (to_lane < GROUP), 0.0, pivots))
            here = (lane >= first) & (lane < base + SUB)
            for i in range(block + 1, count):
                rows[i] = jnp.where(here, 0.0, rows[i]) - update[SUB * i : SUB * (i + 1)]


def factorize(par, mine_ref, other_ref, gram, work, board):
    half, rows = LANES // 2, mine_ref.shape[0]
    odd = par[1] % 2
    gram[pl.ds(odd * rows, rows), :] = mine_ref[...]
    gram[pl.ds((1 - odd) * rows, rows), :] = other_ref[...]
    packed, diagonal = gram[pl.ds(0, half), :], gram[pl.ds(half, 1), :]
    row = lax.broadcasted_iota(jnp.int32, (half, LANES), 0)
    col = lax.broadcasted_iota(jnp.int32, (half, LANES), 1)
    triangles = jnp.concatenate(
        [
            jnp.where(col < row, pltpu.roll(packed, half, 1), 0.0),
            jnp.where((col < half) | (col - half > row), packed, 0.0),
        ],
        axis=0,
    )
    row = lax.broadcasted_iota(jnp.int32, (LANES, LANES), 0)
    col = lax.broadcasted_iota(jnp.int32, (LANES, LANES), 1)
    size = jnp.broadcast_to(lax.rsqrt(diagonal), (LANES, LANES))
    whole = jnp.where(row == col, diagonal, triangles + jnp.transpose(triangles))
    invert_factor((whole * size) * jnp.transpose(size), work, board)
    inverse = jnp.where(row >= col, work[...], 0.0) * size
    diagonal = jnp.sum(jnp.where(row == col, inverse, 0.0), axis=0, keepdims=True)
    return inverse, diagonal


def paired(inverse):
    high = inverse.astype(jnp.bfloat16)
    low = (inverse - high.astype(jnp.float32)).astype(jnp.bfloat16)
    return jnp.concatenate(
        [jnp.concatenate([high, high], axis=1), jnp.concatenate([low, low], axis=1)], axis=0
    )


def times_factor(pair, factor):
    both = lax.dot_general(
        pair, factor, (((1,), (1,)), ((), ())), preferred_element_type=jnp.float32
    )
    return both[:, :LANES] + both[:, LANES:]


def factor_only(par, mine_ref, other_ref, prior_ref, _, inverse_ref, logs_ref, gram, work, board):
    inverse, diagonal = factorize(par, mine_ref, other_ref, gram, work, board)
    inverse_ref[...] = inverse
    logs_ref[...] = prior_ref[...] - jnp.log(diagonal)


def mend_only(par, start_in, middle_in, state_in, coef_ref, spin_ref, a, b, start, middle, state):
    tall = state.shape[2]
    mend_columns(par, (start, middle, state), coef_ref, spin_ref, ((0, tall, (a, b)),))


def update(scale, par, state, inverse_ref, out_ref, kept, sent, factor, total):
    factor[...] = paired(inverse_ref[...])
    gram = 0.0
    for comp, lon, cells in tiles_of(state):
        new = times_factor(jnp.concatenate(split_halves(cells), axis=1), factor[...])
        out_ref[comp, pl.ds(lon, BATCH)] = new.reshape((BATCH,) + out_ref.shape[2:])
        gram += gram_of(*split_halves(new))
    write_halves(par, gram, scale, kept, sent, total)


def restore_order(turned, out_ref):
    comps, cols, _, _ = turned.shape
    for comp in range(comps):
        for lon in range(0, cols, 2 * SUB):
            cells = jnp.concatenate(
                [
                    jnp.transpose(turned[comp, pl.ds(lon + shift, SUB)], (1, 0, 2))
                    for shift in (0, SUB)
                ],
                axis=1,
            )
            high = cells.astype(jnp.bfloat16)
            low = (cells - high.astype(jnp.float32)).astype(jnp.bfloat16)
            out_ref[comp, :, pl.ds(lon, 2 * SUB), pl.ds(0, LANES)] = high
            out_ref[comp, :, pl.ds(lon, 2 * SUB), pl.ds(LANES, LANES)] = low


def finish(
    par, mine_ref, other_ref, prior_ref, t_ref, out_ref, logs_ref, gram, work, board, factor, fresh, sems
):
    inverse, diagonal = factorize(par, mine_ref, other_ref, gram, work, board)
    factor[...] = paired(inverse)

    def out_copy(tile):
        return pltpu.make_async_copy(fresh.at[tile], out_ref.at[tile], sems.at[tile])

    for tile in range(TILES):
        fresh[tile] = times_factor(t_ref[tile], factor[...])
        out_copy(tile).start(priority=tile % 2)
    logs_ref[...] = prior_ref[...] - jnp.log(diagonal)

    for tile in range(TILES):
        out_copy(tile).wait()


def swap_pairs(near_value, far_value, axis, closed):
    count = lax.axis_size(axis)
    near = [(i, i ^ 1) for i in range(count)]
    far = [(i, (i + 1 if i % 2 else i - 1) % count) for i in range(count)]
    if not closed:
        far = far[1:-1]
    return lax.ppermute(near_value, axis, near), lax.ppermute(far_value, axis, far)


def swapped(value, axis, mask):
    return lax.ppermute(value, axis, [(i, i ^ mask) for i in range(lax.axis_size(axis))])


def add_four(first, second, third, fourth, *rest):
    out_ref = rest[len(rest) // 2]
    out_ref[...] = (first[...] + fourth[...]) + (third[...] + second[...])


def sum_over(value, axis, first_bit, beside=None, held=()):
    bits = lax.axis_size(axis).bit_length() - 1
    while first_bit < bits:
        low = 1 << first_bit
        if first_bit + 1 < bits:
            high = low << 1
            three, two, one = (swapped(value, axis, mask) for mask in (low | high, high, low))
            if beside is None:
                value = (three + two) + (one + value)
            else:
                anywhere = pl.BlockSpec(memory_space=pl.ANY)
                value, *held = pl.pallas_call(
                    add_four,
                    out_shape=[jax.ShapeDtypeStruct(x.shape, x.dtype) for x in (value, *held)],
                    in_specs=[VMEM] * 4 + [anywhere] * (1 + len(held)),
                    out_specs=[VMEM] + [anywhere] * len(held),
                    input_output_aliases={5 + i: 1 + i for i in range(len(held))},
                    compiler_params=params(),
                )(value, three, two, one, beside, *held)
                beside = None
            first_bit += 2
        else:
            value = value + swapped(value, axis, low)
            first_bit += 1
    return value, held


def sum_devices(kept, sent, beside=(None, None), held=()):
    mine = kept + swapped(sent, "col", 1)
    mine, held = sum_over(mine, "col", 1, beside[0], held)
    mine, _ = sum_over(mine, "row", 0, beside[1])
    return mine, swapped(mine, "col", 1), held


def body(tangents, sea_mask, levels, current):
    comps, rows, cols, modes = tangents.shape
    total_rows = rows * lax.axis_size("row")
    total_cells = total_rows * cols * lax.axis_size("col")
    scale = 1.0 / total_cells
    row_at, col_at = lax.axis_index("row"), lax.axis_index("col")
    par = jnp.stack([row_at, col_at]).astype(jnp.int32)

    tall, length = rows + 2 * HALO, cols + 2 * SIDE

    block = shape_of(comps, length, tall, modes)
    coefs = shape_of(FIELDS, length, tall, LANES)
    columns = (shape_of(comps * SIDE * tall, modes),) * 2
    own_columns = (shape_of(comps * SIDE * rows + SUB, modes),) * 2
    corners = (shape_of(comps * SIDE * SUB + SUB, modes),) * 2
    rows_sent = (shape_of(comps * HALO + 1, cols, modes),) * 2
    halves = (shape_of(modes // 4 + SUB, modes),) * 2
    square = pltpu.VMEM((modes, modes), jnp.float32)
    board = pltpu.VMEM((2 * SUB * modes, LANES), jnp.float32)
    factor = pltpu.VMEM((2 * modes, 2 * modes), jnp.bfloat16)

    def call(
        kernel, outs, *operands, specs=None, out_specs=None, scratch=(), aliases=None, cost=1.0
    ):
        return pl.pallas_call(
            kernel,
            out_shape=outs,
            in_specs=specs or [SMEM] + [VMEM] * (len(operands) - 1),
            out_specs=out_specs or (VMEM,) * len(outs),
            scratch_shapes=scratch,
            input_output_aliases=aliases or {},
            compiler_params=params(),
            cost_estimate=pl.CostEstimate(
                flops=int(cost * 1e9), bytes_accessed=int(cost * 3e6), transcendentals=0
            ),
        )(*operands)

    def inside(step, state, chosen=None, partly=()):
        return call(
            functools.partial(apply_inside, step, chosen),
            (block,),
            state,
            coef,
            spin,
            *partly,
            specs=[VMEM] * (3 + len(partly)),
            aliases={3: 0} if partly else None,
            cost=2.0,
        )[0]

    def swap_columns(packed):
        return swap_pairs(*packed, "col", True)

    source, *fields = (
        pltpu.with_memory_space_constraint(x, pltpu.HBM)
        for x in (tangents, sea_mask.T, levels.T, current.T)
    )
    upright = [pltpu.VMEM(x.shape, x.dtype) for x in fields]
    packed = call(
        pack_rows,
        rows_sent,
        par,
        source,
        *fields,
        specs=[SMEM] + [HBM] * 4,
        scratch=upright
        + [
            pltpu.VMEM((cols, LANES), jnp.float32),
            pltpu.SemaphoreType.DMA((2 * comps,)),
            pltpu.SemaphoreType.DMA((FIELDS,)),
        ],
        cost=5.0,
    )
    row_halos = swap_pairs(*packed, "row", False)
    start, coef, spin, *packed = call(
        functools.partial(spread_fields, total_rows),
        (block, coefs, shape_of(tall, LANES)) + own_columns,
        par,
        tangents,
        *fields,
        specs=[SMEM, VMEM] + [HBM] * 3,
        scratch=[pltpu.VMEM((FIELDS, cols, LANES), jnp.float32)]
        + upright
        + [pltpu.SemaphoreType.DMA((FIELDS,))],
        cost=3.0,
    )
    halos = swap_columns(packed)
    middle_tiles = tuple(range(1, rows // SUB - 1))
    outer_tiles = (0,) + tuple(range(rows // SUB - 1, tall // SUB))
    middle = inside(0, start, middle_tiles)
    start, coef, *packed = call(
        join_rows,
        (block, coefs) + corners,
        par,
        start,
        coef,
        *row_halos,
        middle,
        specs=[SMEM] + [VMEM] * 4 + [pl.BlockSpec(memory_space=pl.ANY)],
        aliases={1: 0, 2: 1},
    )
    halos += swap_columns(packed)
    logs = jnp.zeros((1, modes), jnp.float32)

    middle = inside(0, start, outer_tiles, (middle,))
    state = inside(1, middle)
    _, _, start, coef, *packed, kept, sent = call(
        functools.partial(join_gram, scale),
        (block, block, block, coefs) + columns + halves,
        par,
        start,
        middle,
        state,
        coef,
        spin,
        *halos,
        scratch=[square],
        aliases={1: 0, 2: 1, 3: 2, 4: 3},
        cost=2.0,
    )
    middle = inside(0, start)
    state = inside(1, middle)

    mine, other, packed = sum_devices(kept, sent, (middle, state), packed)
    halos = swap_columns(packed)
    _, _, state = call(
        mend_only,
        (block,) * 3,
        par,
        start,
        middle,
        state,
        coef,
        spin,
        *halos,
        aliases={1: 0, 2: 1, 3: 2},
    )
    inverse, logs = call(
        factor_only,
        (shape_of(modes, modes), shape_of(1, modes)),
        par,
        mine,
        other,
        logs,
        state,
        specs=[SMEM] + [VMEM] * 3 + [pl.BlockSpec(memory_space=pl.ANY)],
        scratch=[square, square, board],
        cost=0.01,
    )
    state, kept, sent = call(
        functools.partial(update, scale),
        (shape_of(comps, cols, rows, modes),) + halves,
        par,
        state,
        inverse,
        scratch=[factor, square],
        cost=2.0,
    )
    state = call(
        restore_order,
        (jax.ShapeDtypeStruct((comps, rows, cols, 2 * modes), jnp.bfloat16),),
        state,
        specs=[VMEM],
        cost=1.0,
    )[0]
    height = comps * rows * cols // TILES
    tiled = shape_of(TILES, height, modes)
    mine, other, _ = sum_devices(kept, sent)
    out, logs = call(
        finish,
        (tiled, shape_of(1, modes)),
        par,
        mine,
        other,
        logs,
        state.reshape(TILES, height, 2 * modes),
        out_specs=(HBM, VMEM),
        scratch=[
            square,
            square,
            board,
            factor,
            pltpu.VMEM((TILES, height, modes), jnp.float32),
            pltpu.SemaphoreType.DMA((TILES,)),
        ],
    )
    return out.reshape(tangents.shape), logs.reshape(modes)


def solution(mesh):
    placed = (P(None, "row", "col", None), P("row", "col"), P("row", "col"), P("row", "col"))
    return jax.shard_map(
        body,
        mesh=mesh,
        in_specs=placed,
        out_specs=(P(None, "row", "col", None), P()),
        check_vma=False,
    )
```

```python
import functools

import jax
import jax.numpy as jnp
from jax import lax
from jax.experimental import pallas as pl
from jax.experimental.pallas import tpu as pltpu
from jax.sharding import PartitionSpec as P

STEPS = 2
RENORMS = 2
LEVELS = 50

viscosity = 0.15
gravity = 0.5
rotation = 0.4

SUB = 8
LANES = 128
FIELDS = 3
HALO = STEPS * RENORMS
SIDE = STEPS
TILES = 24
BATCH = 8
GROUP = 4
VMEM_LIMIT = 16 * 1024 * 1024

HBM = pl.BlockSpec(memory_space=pltpu.HBM)
VMEM = pl.BlockSpec(memory_space=pltpu.VMEM)
SMEM = pl.BlockSpec(memory_space=pltpu.SMEM)


def params():
    return pltpu.CompilerParams(vmem_limit_bytes=VMEM_LIMIT)


def shape_of(*dims):
    return jax.ShapeDtypeStruct(dims, jnp.float32)


def lane_spread(block, lane):
    return jnp.broadcast_to(block[:, lane : lane + 1], (block.shape[0], LANES))


def fetch(sources, places, sems):
    copies = [
        pltpu.make_async_copy(source, place, sems.at[i])
        for i, (source, place) in enumerate(zip(sources, places))
    ]
    for copy in copies:
        copy.start()
    return copies


def finish_all(copies):
    for copy in copies:
        copy.wait()


def fields_of(sea_ref, levels_ref, current_ref):
    return (
        sea_ref[...].astype(jnp.float32),
        0.5 * current_ref[...],
        0.5 * ((levels_ref[...] + 1).astype(jnp.float32) / LEVELS),
    )


def sides_of(par):
    odd_row, odd_col = par[0] % 2, par[1] % 2
    return (1 - odd_row, odd_row), (1 - odd_col, odd_col)


def pack_rows(
    par, t_ref, sea_ref, levels_ref, current_ref, row_a, row_b, sea, levels, current, wide, sems, field_sems
):
    comps, rows, cols, _ = t_ref.shape
    norths, _ = sides_of(par)
    field_copies = fetch((sea_ref, levels_ref, current_ref), (sea, levels, current), field_sems)
    slots = [(slot, msg, comp) for slot, msg in ((0, row_a), (1, row_b)) for comp in range(comps)]
    copies = fetch(
        [t_ref.at[comp, pl.ds(norths[slot] * (rows - HALO), HALO)] for slot, _, comp in slots],
        [msg.at[pl.ds(comp * HALO, HALO)] for _, msg, comp in slots],
        sems,
    )
    lane = lax.broadcasted_iota(jnp.int32, (cols, LANES), 1)
    wide[...] = jnp.zeros_like(wide)
    packed = [jnp.zeros((cols, LANES), jnp.float32)] * 2
    finish_all(field_copies)
    for field, value in enumerate(fields_of(sea, levels, current)):
        wide[:, pl.ds(0, rows)] = value
        whole = wide[...]
        for north in (0, 1):
            shift = (field * SUB - north * (rows - HALO)) % LANES
            moved = pltpu.roll(whole, shift, 1) if shift else whole
            here = (lane >= field * SUB) & (lane < field * SUB + HALO)
            packed[north] = jnp.where(here, moved, packed[north])
    for slot, msg in ((0, row_a), (1, row_b)):
        msg[comps * HALO] = jnp.where(norths[slot] == 1, packed[1], packed[0])
    finish_all(copies)


def spread_fields(
    total_rows, par, t_ref, sea_ref, levels_ref, current_ref, state, coef, spin, col_a, col_b, wide, sea, levels, current, field_sems
):
    comps, rows, cols, _ = t_ref.shape
    field_copies = fetch((sea_ref, levels_ref, current_ref), (sea, levels, current), field_sems)
    line = lax.broadcasted_iota(jnp.int32, spin.shape, 0)
    line = jnp.where(line < rows + HALO, line, line - (rows + 2 * HALO))
    latitude = (par[0] * rows + line).astype(jnp.float32)
    angle = (-70.0 + 140.0 * (latitude + 0.5) / total_rows) * (jnp.pi / 180.0)
    spin[...] = rotation * jnp.sin(angle)
    wide[...] = jnp.zeros_like(wide)
    finish_all(field_copies)
    for field, value in enumerate(fields_of(sea, levels, current)):
        wide[field, :, pl.ds(0, rows)] = value
        natural = jnp.transpose(wide[field])[:rows]
        for lon in range(cols):
            coef[field, SIDE + lon, pl.ds(0, rows), :] = lane_spread(natural, lon)
    for comp in range(comps):
        for row in range(0, rows, SUB):
            cells = t_ref[comp, pl.ds(row, SUB)]
            state[comp, pl.ds(SIDE, cols), pl.ds(row, SUB), :] = jnp.transpose(cells, (1, 0, 2))
    send_columns(par, state, (col_a, col_b), 0, rows)
    tail = comps * SIDE * rows
    _, easts = sides_of(par)
    for slot, msg in enumerate((col_a, col_b)):
        msg[pl.ds(tail, SUB), :] = jnp.zeros((SUB, LANES), jnp.float32)
        for field in range(FIELDS):
            msg[pl.ds(tail + field, 1), :] = wide[field, pl.ds(easts[slot] * (cols - 1), 1), :]


def column_at(east, cols, depth):
    return SIDE + depth + east * (cols - 1 - 2 * depth)


def send_columns(par, state, cols_sent, first, count):
    comps, length, _, _ = state.shape
    _, easts = sides_of(par)
    for slot, msg in enumerate(cols_sent):
        for comp in range(comps):
            for j in range(SIDE):
                column = column_at(easts[slot], length - 2 * SIDE, j)
                msg[pl.ds((comp * SIDE + j) * count, count), :] = state[
                    comp, column, pl.ds(first, count), :
                ]


def join_rows(par, state_in, coef_in, row_a, row_b, _, state, coef, col_a, col_b):
    comps, length, tall, _ = state.shape
    cols, rows = length - 2 * SIDE, tall - 2 * HALO
    norths, easts = sides_of(par)
    flat = state.reshape(comps * length * tall, LANES)
    for slot, msg in ((0, row_a), (1, row_b)):
        line = rows + HALO * (1 - norths[slot])
        for comp in range(comps):
            for h in range(HALO):
                for lon in range(0, cols, SUB):
                    at = (comp * length + SIDE + lon) * tall + line + h
                    flat[pl.ds(at, SUB, stride=tall), :] = msg[comp * HALO + h, pl.ds(lon, SUB), :]
    lane = lax.broadcasted_iota(jnp.int32, (cols, LANES), 1)
    north = jnp.where(norths[0] == 1, row_a[comps * HALO], row_b[comps * HALO])
    south = jnp.where(norths[0] == 1, row_b[comps * HALO], row_a[comps * HALO])
    beyond = jnp.where(lane % SUB < HALO, north, pltpu.roll(south, HALO, 1))
    natural = jnp.transpose(beyond)
    for field in range(FIELDS):
        block = natural[field * SUB : (field + 1) * SUB]
        for lon in range(cols):
            coef[field, SIDE + lon, pl.ds(rows, SUB), :] = lane_spread(block, lon)
    send_columns(par, state, (col_a, col_b), rows, SUB)
    tail = comps * SIDE * SUB
    for slot, msg in ((0, col_a), (1, col_b)):
        msg[pl.ds(tail, SUB), :] = jnp.zeros((SUB, LANES), jnp.float32)
        msg[pl.ds(tail, 1), :] = jnp.where(easts[slot] == 1, beyond[cols - 1 :], beyond[:1])


def model(own, x_diff, x_sum, above, below, sea, flow, depth, spin):
    keep, half = 1.0 - 4.0 * viscosity, 0.5 * gravity
    mixed = [
        keep * c + viscosity * (x + (n + s)) - flow * d
        for c, d, x, n, s in zip(own, x_diff, x_sum, above, below)
    ]
    v_y, h_y = above[1] - below[1], above[2] - below[2]
    return (
        sea * (mixed[0] - half * x_diff[2] + spin * own[1]),
        sea * (mixed[1] - half * h_y - spin * own[0]),
        sea * (mixed[2] - depth * (x_diff[0] + v_y)),
    )


def advance_column(source, target, coef_ref, spin_ref, lon, chosen=None):
    comps, length, tall, _ = source.shape
    flat = source.reshape(comps * length * tall, LANES)
    sub = lax.broadcasted_iota(jnp.int32, (SUB, LANES), 0)
    tiles = tall // SUB
    for tile in chosen or range(tiles):
        lines = pl.ds(SUB * tile, SUB)
        own, east, west = (
            [source[comp, lon + shift, lines, :] for comp in range(comps)] for shift in (0, 1, -1)
        )
        starts = [(comp * length + lon) * tall + SUB * tile for comp in range(comps)]
        if tile < tiles - 1:
            above = [flat[pl.ds(start + 1, SUB), :] for start in starts]
        else:
            wrap = [source[comp, lon, pl.ds(0, SUB), :] for comp in range(comps)]
            above = [
                jnp.where(sub == SUB - 1, pltpu.roll(w, SUB - 1, 0), pltpu.roll(o, SUB - 1, 0))
                for w, o in zip(wrap, own)
            ]
        if tile > 0:
            below = [flat[pl.ds(start - 1, SUB), :] for start in starts]
        else:
            wrap = [source[comp, lon, pl.ds(tall - SUB, SUB), :] for comp in range(comps)]
            below = [
                jnp.where(sub == 0, pltpu.roll(w, 1, 0), pltpu.roll(o, 1, 0))
                for w, o in zip(wrap, own)
            ]
        new = model(
            own,
            [e - w for e, w in zip(east, west)],
            [e + w for e, w in zip(east, west)],
            above,
            below,
            *(coef_ref[field, lon, lines, :] for field in range(FIELDS)),
            spin_ref[lines, :],
        )
        for comp in range(comps):
            target[comp, lon, lines, :] = new[comp]


def apply_inside(step, chosen, source, coef_ref, spin_ref, *refs):
    first = SIDE + step + 1
    count = source.shape[1] - 2 * first
    target = refs[-1]

    @pl.loop(0, count // 2)
    def _(pair):
        for lon in (first + 2 * pair, first + 2 * pair + 1):
            advance_column(source, target, coef_ref, spin_ref, lon, chosen)


def mend_columns(par, states, coef_ref, spin_ref, pieces):
    comps, length, _, _ = states[0].shape
    _, easts = sides_of(par)
    for first, count, cols_got in pieces:
        for slot, msg in enumerate(cols_got):
            for comp in range(comps):
                for j in range(SIDE):
                    column = column_at(easts[slot], length - 2 * SIDE, -1 - j)
                    states[0][comp, column, pl.ds(first, count), :] = msg[
                        pl.ds((comp * SIDE + j) * count, count), :
                    ]
    for step in range(STEPS):
        first = step + 1
        skip = length - 2 * first - 2 * SIDE

        @pl.loop(0, 2 * SIDE)
        def _(i):
            lon = first + i + (i // SIDE) * skip
            advance_column(states[step], states[step + 1], coef_ref, spin_ref, lon)


def join_gram(
    scale, par, start_in, middle_in, state_in, coef_in, spin_ref, a, b, c, d, start, middle, state, coef, col_a, col_b, kept, sent, total
):
    _, length, tall, _ = state.shape
    rows = tall - 2 * HALO
    _, easts = sides_of(par)
    for slot, (own, beyond) in enumerate(((a, c), (b, d))):
        own, beyond = (jnp.transpose(x[pl.ds(x.shape[0] - SUB, SUB), :]) for x in (own, beyond))
        column = column_at(easts[slot], length - 2 * SIDE, -1)
        for field in range(FIELDS):
            coef[field, column, pl.ds(0, rows), :] = lane_spread(own[:rows], field)
            coef[field, column, pl.ds(rows, SUB), :] = lane_spread(
                beyond[field * SUB : (field + 1) * SUB], 0
            )
    mend_columns(
        par, (start, middle, state), coef, spin_ref, ((0, rows, (a, b)), (rows, SUB, (c, d)))
    )
    send_columns(par, state, (col_a, col_b), 0, tall)
    gram = sum(gram_of(*split_halves(cells)) for _, _, cells in tiles_of(state))
    write_halves(par, gram, scale, kept, sent, total)


def tiles_of(state):
    comps, length, tall, _ = state.shape
    rows = tall - 2 * HALO
    for comp in range(comps):
        for lon in range(0, length - 2 * SIDE, BATCH):
            cells = state[comp, pl.ds(SIDE + lon, BATCH), pl.ds(0, rows), :]
            yield comp, lon, cells.reshape(BATCH * rows, LANES)


def split_halves(value):
    high = value.astype(jnp.bfloat16)
    return high, (value - high.astype(jnp.float32)).astype(jnp.bfloat16)


def gram_of(high, low):
    return lax.dot_general(
        high,
        jnp.concatenate([high, low], axis=1),
        (((0,), (0,)), ((), ())),
        preferred_element_type=jnp.float32,
    )


def write_halves(par, gram, scale, kept, sent, total):
    half, rows = LANES // 2, kept.shape[0]
    mixed = gram[:, LANES:]
    whole = scale * (gram[:, :LANES] + (mixed + jnp.transpose(mixed)))
    row = lax.broadcasted_iota(jnp.int32, (half, LANES), 0)
    col = lax.broadcasted_iota(jnp.int32, (half, LANES), 1)
    total[pl.ds(0, half), :] = jnp.where(
        (col < half) | (col - half > row), whole[half:], pltpu.roll(whole[:half], half, 1)
    )
    row = lax.broadcasted_iota(jnp.int32, (LANES, LANES), 0)
    col = lax.broadcasted_iota(jnp.int32, (LANES, LANES), 1)
    total[pl.ds(half, 2 * rows - half), :] = jnp.zeros((2 * rows - half, LANES), jnp.float32)
    total[pl.ds(half, 1), :] = jnp.sum(jnp.where(row == col, whole, 0.0), axis=0, keepdims=True)
    odd = par[1] % 2
    kept[...] = total[pl.ds(odd * rows, rows), :]
    sent[...] = total[pl.ds((1 - odd) * rows, rows), :]


def factor_pair(low, p):
    q, size = p + 1, len(low)
    a, b, c = low[p][p], low[q][p], low[q][q]
    root_a, root_det = lax.rsqrt(a), lax.rsqrt(a * c - b * b)
    both = root_a * root_det
    turned = [a * low[i][q] - b * low[i][p] for i in range(q + 1, size)]
    low[q][p] = b * root_a
    for i, value in zip(range(q + 1, size), turned):
        low[i][p] = low[i][p] * root_a
        low[i][q] = value * both
    for i in range(q + 1, size):
        for m in range(q + 1, i + 1):
            low[i][m] = (low[i][m] - low[i][p] * low[m][p]) - low[i][q] * low[m][q]
    return root_a, a * both


def square_of(pivots):
    high = pivots.astype(jnp.bfloat16)
    rest = pivots - high.astype(jnp.float32)
    middle = rest.astype(jnp.bfloat16)
    low = (rest - middle.astype(jnp.float32)).astype(jnp.bfloat16)
    return lax.dot_general(
        jnp.concatenate([high, high, middle, middle, high, low], axis=0),
        jnp.concatenate([high, middle, high, middle, low, high], axis=0),
        (((0,), (0,)), ((), ())),
        preferred_element_type=jnp.float32,
    )


def invert_factor(gram, work, board):
    count = LANES // SUB
    lane = lax.broadcasted_iota(jnp.int32, (SUB, LANES), 1)
    sub = lax.broadcasted_iota(jnp.int32, (SUB, LANES), 0)
    rows = [gram[SUB * i : SUB * (i + 1)] for i in range(count)]
    columns = [lane_spread(rows[0], l) for l in range(SUB)]
    for block in range(count):
        base = SUB * block
        here = (lane >= base) & (lane < base + SUB)
        shelf = 3 * SUB * base
        for l in range(SUB):
            board[pl.ds(shelf + SUB * l, SUB), :] = columns[l]
        low = [
            [board[pl.ds(shelf + SUB * l + k, SUB, stride=0), :] for l in range(k + 1)]
            for k in range(SUB)
        ]
        shelf += SUB * SUB
        board[pl.ds(shelf, SUB), :] = jnp.where(
            here, jnp.where(lane - base == sub, 1.0, 0.0), rows[block]
        )
        inv = []
        for p in range(0, SUB, 2):
            inv.extend(factor_pair(low, p))
        scaled = []
        for k in range(SUB):
            line = board[pl.ds(shelf + k, SUB, stride=0), :]
            for l in range(k):
                line = line - low[k][l] * scaled[l]
            scaled.append(line * inv[k])
        merged = scaled[0]
        for k in range(1, SUB):
            merged = jnp.where(sub == k, scaled[k], merged)
        work[pl.ds(base, SUB), :] = merged
        shelf += SUB
        for i in range(block + 1, (block // GROUP + 1) * GROUP):
            weights = []
            rest = jnp.where(here, 0.0, rows[i])
            for l in range(SUB):
                weight = lane_spread(rows[i], base + l)
                for m in range(l):
                    weight = weight - weights[m] * low[l][m]
                weights.append(weight * inv[l])
            if i == block + 1:
                columns = [lane_spread(rows[i], base + SUB + l) for l in range(SUB)]
                for l in range(SUB):
                    board[pl.ds(shelf + SUB * l, SUB), :] = weights[l]
                    for k in range(SUB):
                        across = board[pl.ds(shelf + SUB * l + k, SUB, stride=0), :]
                        columns[k] = columns[k] - weights[l] * across
            for l in range(SUB):
                rest = rest - weights[l] * scaled[l]
            rows[i] = rest
        if block % GROUP == GROUP - 1 and block + 1 < count:
            first = SUB * (block + 1 - GROUP)
            tall = (SUB * GROUP, LANES)
            to_lane = lax.broadcasted_iota(jnp.int32, tall, 1) // SUB - first // SUB
            to_row = lax.broadcasted_iota(jnp.int32, tall, 0) // SUB
            pivots = work[pl.ds(first, SUB * GROUP), :]
            update = square_of(jnp.where((to_lane > to_row) & (to_lane < GROUP), 0.0, pivots))
            here = (lane >= first) & (lane < base + SUB)
            for i in range(block + 1, count):
                rows[i] = jnp.where(here, 0.0, rows[i]) - update[SUB * i : SUB * (i + 1)]
            columns = [lane_spread(rows[block + 1], base + SUB + l) for l in range(SUB)]


def factorize(par, mine_ref, other_ref, gram, work, board):
    half, rows = LANES // 2, mine_ref.shape[0]
    odd = par[1] % 2
    gram[pl.ds(odd * rows, rows), :] = mine_ref[...]
    gram[pl.ds((1 - odd) * rows, rows), :] = other_ref[...]
    packed, diagonal = gram[pl.ds(0, half), :], gram[pl.ds(half, 1), :]
    row = lax.broadcasted_iota(jnp.int32, (half, LANES), 0)
    col = lax.broadcasted_iota(jnp.int32, (half, LANES), 1)
    triangles = jnp.concatenate(
        [
            jnp.where(col < row, pltpu.roll(packed, half, 1), 0.0),
            jnp.where((col < half) | (col - half > row), packed, 0.0),
        ],
        axis=0,
    )
    row = lax.broadcasted_iota(jnp.int32, (LANES, LANES), 0)
    col = lax.broadcasted_iota(jnp.int32, (LANES, LANES), 1)
    size = jnp.broadcast_to(lax.rsqrt(diagonal), (LANES, LANES))
    whole = jnp.where(row == col, diagonal, triangles + jnp.transpose(triangles))
    invert_factor((whole * size) * jnp.transpose(size), work, board)
    inverse = jnp.where(row >= col, work[...], 0.0) * size
    diagonal = jnp.sum(jnp.where(row == col, inverse, 0.0), axis=0, keepdims=True)
    return inverse, diagonal


def paired(inverse):
    high = inverse.astype(jnp.bfloat16)
    low = (inverse - high.astype(jnp.float32)).astype(jnp.bfloat16)
    return jnp.concatenate(
        [jnp.concatenate([high, high], axis=1), jnp.concatenate([low, low], axis=1)], axis=0
    )


def times_factor(pair, factor):
    both = lax.dot_general(
        pair, factor, (((1,), (1,)), ((), ())), preferred_element_type=jnp.float32
    )
    return both[:, :LANES] + both[:, LANES:]


def factor_only(par, mine_ref, other_ref, prior_ref, _, inverse_ref, logs_ref, gram, work, board):
    inverse, diagonal = factorize(par, mine_ref, other_ref, gram, work, board)
    inverse_ref[...] = inverse
    logs_ref[...] = prior_ref[...] - jnp.log(diagonal)


def mend_only(par, start_in, middle_in, state_in, coef_ref, spin_ref, a, b, start, middle, state):
    tall = state.shape[2]
    mend_columns(par, (start, middle, state), coef_ref, spin_ref, ((0, tall, (a, b)),))


def update(scale, par, state, inverse_ref, out_ref, kept, sent, factor, total):
    factor[...] = paired(inverse_ref[...])
    gram = 0.0
    for comp, lon, cells in tiles_of(state):
        new = times_factor(jnp.concatenate(split_halves(cells), axis=1), factor[...])
        out_ref[comp, pl.ds(lon, BATCH)] = new.reshape((BATCH,) + out_ref.shape[2:])
        gram += gram_of(*split_halves(new))
    write_halves(par, gram, scale, kept, sent, total)


def restore_order(turned, out_ref):
    comps, cols, _, _ = turned.shape
    for comp in range(comps):
        for lon in range(0, cols, 2 * SUB):
            cells = jnp.concatenate(
                [
                    jnp.transpose(turned[comp, pl.ds(lon + shift, SUB)], (1, 0, 2))
                    for shift in (0, SUB)
                ],
                axis=1,
            )
            high = cells.astype(jnp.bfloat16)
            low = (cells - high.astype(jnp.float32)).astype(jnp.bfloat16)
            out_ref[comp, :, pl.ds(lon, 2 * SUB), pl.ds(0, LANES)] = high
            out_ref[comp, :, pl.ds(lon, 2 * SUB), pl.ds(LANES, LANES)] = low


def finish(
    par, mine_ref, other_ref, prior_ref, t_ref, out_ref, logs_ref, gram, work, board, factor, fresh, sems
):
    inverse, diagonal = factorize(par, mine_ref, other_ref, gram, work, board)
    factor[...] = paired(inverse)

    def out_copy(tile):
        return pltpu.make_async_copy(fresh.at[tile], out_ref.at[tile], sems.at[tile])

    for tile in range(TILES):
        fresh[tile] = times_factor(t_ref[tile], factor[...])
        out_copy(tile).start(priority=tile % 2)
    logs_ref[...] = prior_ref[...] - jnp.log(diagonal)

    for tile in range(TILES):
        out_copy(tile).wait()


def swap_pairs(near_value, far_value, axis, closed):
    count = lax.axis_size(axis)
    near = [(i, i ^ 1) for i in range(count)]
    far = [(i, (i + 1 if i % 2 else i - 1) % count) for i in range(count)]
    if not closed:
        far = far[1:-1]
    return lax.ppermute(near_value, axis, near), lax.ppermute(far_value, axis, far)


def swapped(value, axis, mask):
    return lax.ppermute(value, axis, [(i, i ^ mask) for i in range(lax.axis_size(axis))])


def add_four(first, second, third, fourth, _, out_ref):
    out_ref[...] = (first[...] + fourth[...]) + (third[...] + second[...])


def sum_over(value, axis, first_bit, beside=None):
    bits = lax.axis_size(axis).bit_length() - 1
    while first_bit < bits:
        low = 1 << first_bit
        if first_bit + 1 < bits:
            high = low << 1
            three, two, one = (swapped(value, axis, mask) for mask in (low | high, high, low))
            if beside is None:
                value = (three + two) + (one + value)
            else:
                value = pl.pallas_call(
                    add_four,
                    out_shape=jax.ShapeDtypeStruct(value.shape, value.dtype),
                    in_specs=[VMEM] * 4 + [pl.BlockSpec(memory_space=pl.ANY)],
                    out_specs=VMEM,
                    compiler_params=params(),
                )(value, three, two, one, beside)
                beside = None
            first_bit += 2
        else:
            value = value + swapped(value, axis, low)
            first_bit += 1
    return value


def sum_devices(kept, sent, beside=(None, None)):
    mine = kept + swapped(sent, "col", 1)
    mine = sum_over(mine, "row", 0, beside[0])
    mine = sum_over(mine, "col", 1, beside[1])
    return mine, swapped(mine, "col", 1)


def body(tangents, sea_mask, levels, current):
    comps, rows, cols, modes = tangents.shape
    total_rows = rows * lax.axis_size("row")
    total_cells = total_rows * cols * lax.axis_size("col")
    scale = 1.0 / total_cells
    row_at, col_at = lax.axis_index("row"), lax.axis_index("col")
    par = jnp.stack([row_at, col_at]).astype(jnp.int32)

    tall, length = rows + 2 * HALO, cols + 2 * SIDE

    block = shape_of(comps, length, tall, modes)
    coefs = shape_of(FIELDS, length, tall, LANES)
    columns = (shape_of(comps * SIDE * tall, modes),) * 2
    own_columns = (shape_of(comps * SIDE * rows + SUB, modes),) * 2
    corners = (shape_of(comps * SIDE * SUB + SUB, modes),) * 2
    rows_sent = (shape_of(comps * HALO + 1, cols, modes),) * 2
    halves = (shape_of(modes // 4 + SUB, modes),) * 2
    square = pltpu.VMEM((modes, modes), jnp.float32)
    board = pltpu.VMEM((3 * SUB * modes, LANES), jnp.float32)
    factor = pltpu.VMEM((2 * modes, 2 * modes), jnp.bfloat16)

    def call(
        kernel, outs, *operands, specs=None, out_specs=None, scratch=(), aliases=None, cost=1.0
    ):
        return pl.pallas_call(
            kernel,
            out_shape=outs,
            in_specs=specs or [SMEM] + [VMEM] * (len(operands) - 1),
            out_specs=out_specs or (VMEM,) * len(outs),
            scratch_shapes=scratch,
            input_output_aliases=aliases or {},
            compiler_params=params(),
            cost_estimate=pl.CostEstimate(
                flops=int(cost * 1e9), bytes_accessed=int(cost * 3e6), transcendentals=0
            ),
        )(*operands)

    def inside(step, state, chosen=None, partly=()):
        return call(
            functools.partial(apply_inside, step, chosen),
            (block,),
            state,
            coef,
            spin,
            *partly,
            specs=[VMEM] * (3 + len(partly)),
            aliases={3: 0} if partly else None,
            cost=2.0,
        )[0]

    def swap_columns(packed):
        return swap_pairs(*packed, "col", True)

    source, *fields = (
        pltpu.with_memory_space_constraint(x, pltpu.HBM)
        for x in (tangents, sea_mask.T, levels.T, current.T)
    )
    upright = [pltpu.VMEM(x.shape, x.dtype) for x in fields]
    packed = call(
        pack_rows,
        rows_sent,
        par,
        source,
        *fields,
        specs=[SMEM] + [HBM] * 4,
        scratch=upright
        + [
            pltpu.VMEM((cols, LANES), jnp.float32),
            pltpu.SemaphoreType.DMA((2 * comps,)),
            pltpu.SemaphoreType.DMA((FIELDS,)),
        ],
        cost=5.0,
    )
    row_halos = swap_pairs(*packed, "row", False)
    start, coef, spin, *packed = call(
        functools.partial(spread_fields, total_rows),
        (block, coefs, shape_of(tall, LANES)) + own_columns,
        par,
        tangents,
        *fields,
        specs=[SMEM, VMEM] + [HBM] * 3,
        scratch=[pltpu.VMEM((FIELDS, cols, LANES), jnp.float32)]
        + upright
        + [pltpu.SemaphoreType.DMA((FIELDS,))],
        cost=3.0,
    )
    halos = swap_columns(packed)
    middle_tiles = tuple(range(1, rows // SUB - 1))
    outer_tiles = (0,) + tuple(range(rows // SUB - 1, tall // SUB))
    middle = inside(0, start, middle_tiles)
    start, coef, *packed = call(
        join_rows,
        (block, coefs) + corners,
        par,
        start,
        coef,
        *row_halos,
        middle,
        specs=[SMEM] + [VMEM] * 4 + [pl.BlockSpec(memory_space=pl.ANY)],
        aliases={1: 0, 2: 1},
    )
    halos += swap_columns(packed)
    logs = jnp.zeros((1, modes), jnp.float32)

    middle = inside(0, start, outer_tiles, (middle,))
    state = inside(1, middle)
    _, _, start, coef, *packed, kept, sent = call(
        functools.partial(join_gram, scale),
        (block, block, block, coefs) + columns + halves,
        par,
        start,
        middle,
        state,
        coef,
        spin,
        *halos,
        scratch=[square],
        aliases={1: 0, 2: 1, 3: 2, 4: 3},
        cost=2.0,
    )
    middle = inside(0, start)
    state = inside(1, middle)

    halos = swap_columns(packed)
    mine, other = sum_devices(kept, sent, (middle, state))
    _, _, state = call(
        mend_only,
        (block,) * 3,
        par,
        start,
        middle,
        state,
        coef,
        spin,
        *halos,
        aliases={1: 0, 2: 1, 3: 2},
    )
    inverse, logs = call(
        factor_only,
        (shape_of(modes, modes), shape_of(1, modes)),
        par,
        mine,
        other,
        logs,
        state,
        specs=[SMEM] + [VMEM] * 3 + [pl.BlockSpec(memory_space=pl.ANY)],
        scratch=[square, square, board],
        cost=0.01,
    )
    state, kept, sent = call(
        functools.partial(update, scale),
        (shape_of(comps, cols, rows, modes),) + halves,
        par,
        state,
        inverse,
        scratch=[factor, square],
        cost=2.0,
    )
    state = call(
        restore_order,
        (jax.ShapeDtypeStruct((comps, rows, cols, 2 * modes), jnp.bfloat16),),
        state,
        specs=[VMEM],
        cost=1.0,
    )[0]
    height = comps * rows * cols // TILES
    tiled = shape_of(TILES, height, modes)
    mine, other = sum_devices(kept, sent)
    out, logs = call(
        finish,
        (tiled, shape_of(1, modes)),
        par,
        mine,
        other,
        logs,
        state.reshape(TILES, height, 2 * modes),
        out_specs=(HBM, VMEM),
        scratch=[
            square,
            square,
            board,
            factor,
            pltpu.VMEM((TILES, height, modes), jnp.float32),
            pltpu.SemaphoreType.DMA((TILES,)),
        ],
    )
    return out.reshape(tangents.shape), logs.reshape(modes)


def solution(mesh):
    placed = (P(None, "row", "col", None), P("row", "col"), P("row", "col"), P("row", "col"))
    return jax.shard_map(
        body,
        mesh=mesh,
        in_specs=placed,
        out_specs=(P(None, "row", "col", None), P()),
        check_vma=False,
    )
```

```python
import functools

import jax
import jax.numpy as jnp
from jax import lax
from jax.experimental import pallas as pl
from jax.experimental.pallas import tpu as pltpu
from jax.sharding import PartitionSpec as P

STEPS = 2
RENORMS = 2
LEVELS = 50

viscosity = 0.15
gravity = 0.5
rotation = 0.4

SUB = 8
LANES = 128
FIELDS = 3
HALO = STEPS * RENORMS
SIDE = STEPS
TILES = 24
BATCH = 8
GROUP = 8
VMEM_LIMIT = 16 * 1024 * 1024

HBM = pl.BlockSpec(memory_space=pltpu.HBM)
VMEM = pl.BlockSpec(memory_space=pltpu.VMEM)
SMEM = pl.BlockSpec(memory_space=pltpu.SMEM)


def params():
    return pltpu.CompilerParams(vmem_limit_bytes=VMEM_LIMIT)


def shape_of(*dims):
    return jax.ShapeDtypeStruct(dims, jnp.float32)


def lane_spread(block, lane):
    return jnp.broadcast_to(block[:, lane : lane + 1], (block.shape[0], LANES))


def fetch(sources, places, sems, priority=0):
    copies = [
        pltpu.make_async_copy(source, place, sems.at[i])
        for i, (source, place) in enumerate(zip(sources, places))
    ]
    for copy in copies:
        copy.start(priority=priority)
    return copies


def finish_all(copies):
    for copy in copies:
        copy.wait()


def fields_of(sea_ref, levels_ref, current_ref):
    return (
        sea_ref[...].astype(jnp.float32),
        0.5 * current_ref[...],
        0.5 * ((levels_ref[...] + 1).astype(jnp.float32) / LEVELS),
    )


def sides_of(par):
    odd_row, odd_col = par[0] % 2, par[1] % 2
    return (1 - odd_row, odd_row), (1 - odd_col, odd_col)


def pack_rows(
    par, t_ref, sea_ref, levels_ref, current_ref, row_a, row_b, sea, levels, current, wide, sems, field_sems
):
    comps, rows, cols, _ = t_ref.shape
    norths, _ = sides_of(par)
    field_copies = fetch((sea_ref, levels_ref, current_ref), (sea, levels, current), field_sems)
    slots = [(slot, msg, comp) for slot, msg in ((0, row_a), (1, row_b)) for comp in range(comps)]
    copies = fetch(
        [t_ref.at[comp, pl.ds(norths[slot] * (rows - HALO), HALO)] for slot, _, comp in slots],
        [msg.at[pl.ds(comp * HALO, HALO)] for _, msg, comp in slots],
        sems,
        1,
    )
    lane = lax.broadcasted_iota(jnp.int32, (cols, LANES), 1)
    wide[...] = jnp.zeros_like(wide)
    packed = [jnp.zeros((cols, LANES), jnp.float32)] * 2
    finish_all(field_copies)
    for field, value in enumerate(fields_of(sea, levels, current)):
        wide[:, pl.ds(0, rows)] = value
        whole = wide[...]
        for north in (0, 1):
            shift = (field * SUB - north * (rows - HALO)) % LANES
            moved = pltpu.roll(whole, shift, 1) if shift else whole
            here = (lane >= field * SUB) & (lane < field * SUB + HALO)
            packed[north] = jnp.where(here, moved, packed[north])
    for slot, msg in ((0, row_a), (1, row_b)):
        msg[comps * HALO] = jnp.where(norths[slot] == 1, packed[1], packed[0])
    finish_all(copies)


def spread_fields(
    total_rows, par, t_ref, sea_ref, levels_ref, current_ref, state, coef, spin, col_a, col_b, wide, sea, levels, current, field_sems
):
    comps, rows, cols, _ = t_ref.shape
    field_copies = fetch((sea_ref, levels_ref, current_ref), (sea, levels, current), field_sems)
    line = lax.broadcasted_iota(jnp.int32, spin.shape, 0)
    line = jnp.where(line < rows + HALO, line, line - (rows + 2 * HALO))
    latitude = (par[0] * rows + line).astype(jnp.float32)
    angle = (-70.0 + 140.0 * (latitude + 0.5) / total_rows) * (jnp.pi / 180.0)
    spin[...] = rotation * jnp.sin(angle)
    wide[...] = jnp.zeros_like(wide)
    finish_all(field_copies)
    for field, value in enumerate(fields_of(sea, levels, current)):
        wide[field, :, pl.ds(0, rows)] = value
        natural = jnp.transpose(wide[field])[:rows]
        for lon in range(cols):
            coef[field, SIDE + lon, pl.ds(0, rows), :] = lane_spread(natural, lon)
    for comp in range(comps):
        for row in range(0, rows, SUB):
            cells = t_ref[comp, pl.ds(row, SUB)]
            state[comp, pl.ds(SIDE, cols), pl.ds(row, SUB), :] = jnp.transpose(cells, (1, 0, 2))
    send_columns(par, state, (col_a, col_b), 0, rows)
    tail = comps * SIDE * rows
    _, easts = sides_of(par)
    for slot, msg in enumerate((col_a, col_b)):
        msg[pl.ds(tail, SUB), :] = jnp.zeros((SUB, LANES), jnp.float32)
        for field in range(FIELDS):
            msg[pl.ds(tail + field, 1), :] = wide[field, pl.ds(easts[slot] * (cols - 1), 1), :]


def column_at(east, cols, depth):
    return SIDE + depth + east * (cols - 1 - 2 * depth)


def send_columns(par, state, cols_sent, first, count):
    comps, length, _, _ = state.shape
    _, easts = sides_of(par)
    for slot, msg in enumerate(cols_sent):
        for comp in range(comps):
            for j in range(SIDE):
                column = column_at(easts[slot], length - 2 * SIDE, j)
                msg[pl.ds((comp * SIDE + j) * count, count), :] = state[
                    comp, column, pl.ds(first, count), :
                ]


def join_rows(par, state_in, coef_in, row_a, row_b, _, state, coef, col_a, col_b):
    comps, length, tall, _ = state.shape
    cols, rows = length - 2 * SIDE, tall - 2 * HALO
    norths, easts = sides_of(par)
    flat = state.reshape(comps * length * tall, LANES)
    for slot, msg in ((0, row_a), (1, row_b)):
        line = rows + HALO * (1 - norths[slot])
        for comp in range(comps):
            for h in range(HALO):
                for lon in range(0, cols, SUB):
                    at = (comp * length + SIDE + lon) * tall + line + h
                    flat[pl.ds(at, SUB, stride=tall), :] = msg[comp * HALO + h, pl.ds(lon, SUB), :]
    lane = lax.broadcasted_iota(jnp.int32, (cols, LANES), 1)
    north = jnp.where(norths[0] == 1, row_a[comps * HALO], row_b[comps * HALO])
    south = jnp.where(norths[0] == 1, row_b[comps * HALO], row_a[comps * HALO])
    beyond = jnp.where(lane % SUB < HALO, north, pltpu.roll(south, HALO, 1))
    natural = jnp.transpose(beyond)
    for field in range(FIELDS):
        block = natural[field * SUB : (field + 1) * SUB]
        for lon in range(cols):
            coef[field, SIDE + lon, pl.ds(rows, SUB), :] = lane_spread(block, lon)
    send_columns(par, state, (col_a, col_b), rows, SUB)
    tail = comps * SIDE * SUB
    for slot, msg in ((0, col_a), (1, col_b)):
        msg[pl.ds(tail, SUB), :] = jnp.zeros((SUB, LANES), jnp.float32)
        msg[pl.ds(tail, 1), :] = jnp.where(easts[slot] == 1, beyond[cols - 1 :], beyond[:1])


def model(own, x_diff, x_sum, above, below, sea, flow, depth, spin):
    keep, half = 1.0 - 4.0 * viscosity, 0.5 * gravity
    mixed = [
        keep * c + viscosity * (x + (n + s)) - flow * d
        for c, d, x, n, s in zip(own, x_diff, x_sum, above, below)
    ]
    v_y, h_y = above[1] - below[1], above[2] - below[2]
    return (
        sea * (mixed[0] - half * x_diff[2] + spin * own[1]),
        sea * (mixed[1] - half * h_y - spin * own[0]),
        sea * (mixed[2] - depth * (x_diff[0] + v_y)),
    )


def advance_column(source, target, coef_ref, spin_ref, lon, chosen=None):
    comps, length, tall, _ = source.shape
    flat = source.reshape(comps * length * tall, LANES)
    sub = lax.broadcasted_iota(jnp.int32, (SUB, LANES), 0)
    tiles = tall // SUB
    for tile in chosen or range(tiles):
        lines = pl.ds(SUB * tile, SUB)
        own, east, west = (
            [source[comp, lon + shift, lines, :] for comp in range(comps)] for shift in (0, 1, -1)
        )
        starts = [(comp * length + lon) * tall + SUB * tile for comp in range(comps)]
        if tile < tiles - 1:
            above = [flat[pl.ds(start + 1, SUB), :] for start in starts]
        else:
            wrap = [source[comp, lon, pl.ds(0, SUB), :] for comp in range(comps)]
            above = [
                jnp.where(sub == SUB - 1, pltpu.roll(w, SUB - 1, 0), pltpu.roll(o, SUB - 1, 0))
                for w, o in zip(wrap, own)
            ]
        if tile > 0:
            below = [flat[pl.ds(start - 1, SUB), :] for start in starts]
        else:
            wrap = [source[comp, lon, pl.ds(tall - SUB, SUB), :] for comp in range(comps)]
            below = [
                jnp.where(sub == 0, pltpu.roll(w, 1, 0), pltpu.roll(o, 1, 0))
                for w, o in zip(wrap, own)
            ]
        new = model(
            own,
            [e - w for e, w in zip(east, west)],
            [e + w for e, w in zip(east, west)],
            above,
            below,
            *(coef_ref[field, lon, lines, :] for field in range(FIELDS)),
            spin_ref[lines, :],
        )
        for comp in range(comps):
            target[comp, lon, lines, :] = new[comp]


def apply_inside(step, chosen, source, coef_ref, spin_ref, *refs):
    first = SIDE + step + 1
    count = source.shape[1] - 2 * first
    target = refs[-1]

    @pl.loop(0, count // 2)
    def _(pair):
        for lon in (first + 2 * pair, first + 2 * pair + 1):
            advance_column(source, target, coef_ref, spin_ref, lon, chosen)


def mend_columns(par, states, coef_ref, spin_ref, pieces):
    comps, length, _, _ = states[0].shape
    _, easts = sides_of(par)
    for first, count, cols_got in pieces:
        for slot, msg in enumerate(cols_got):
            for comp in range(comps):
                for j in range(SIDE):
                    column = column_at(easts[slot], length - 2 * SIDE, -1 - j)
                    states[0][comp, column, pl.ds(first, count), :] = msg[
                        pl.ds((comp * SIDE + j) * count, count), :
                    ]
    for step in range(STEPS):
        first = step + 1
        skip = length - 2 * first - 2 * SIDE

        @pl.loop(0, 2 * SIDE)
        def _(i):
            lon = first + i + (i // SIDE) * skip
            advance_column(states[step], states[step + 1], coef_ref, spin_ref, lon)


def join_gram(
    scale, par, start_in, middle_in, state_in, coef_in, spin_ref, a, b, c, d, start, middle, state, coef, col_a, col_b, kept, sent, total
):
    _, length, tall, _ = state.shape
    rows = tall - 2 * HALO
    _, easts = sides_of(par)
    for slot, (own, beyond) in enumerate(((a, c), (b, d))):
        own, beyond = (jnp.transpose(x[pl.ds(x.shape[0] - SUB, SUB), :]) for x in (own, beyond))
        column = column_at(easts[slot], length - 2 * SIDE, -1)
        for field in range(FIELDS):
            coef[field, column, pl.ds(0, rows), :] = lane_spread(own[:rows], field)
            coef[field, column, pl.ds(rows, SUB), :] = lane_spread(
                beyond[field * SUB : (field + 1) * SUB], 0
            )
    mend_columns(
        par, (start, middle, state), coef, spin_ref, ((0, rows, (a, b)), (rows, SUB, (c, d)))
    )
    send_columns(par, state, (col_a, col_b), 0, tall)
    gram = sum(gram_of(*split_halves(cells)) for _, _, cells in tiles_of(state))
    write_halves(par, gram, scale, kept, sent, total)


def tiles_of(state):
    comps, length, tall, _ = state.shape
    rows = tall - 2 * HALO
    for comp in range(comps):
        for lon in range(0, length - 2 * SIDE, BATCH):
            cells = state[comp, pl.ds(SIDE + lon, BATCH), pl.ds(0, rows), :]
            yield comp, lon, cells.reshape(BATCH * rows, LANES)


def split_halves(value):
    high = value.astype(jnp.bfloat16)
    return high, (value - high.astype(jnp.float32)).astype(jnp.bfloat16)


def gram_of(high, low):
    return lax.dot_general(
        high,
        jnp.concatenate([high, low], axis=1),
        (((0,), (0,)), ((), ())),
        preferred_element_type=jnp.float32,
    )


def write_halves(par, gram, scale, kept, sent, total):
    half, rows = LANES // 2, kept.shape[0]
    mixed = gram[:, LANES:]
    whole = scale * (gram[:, :LANES] + (mixed + jnp.transpose(mixed)))
    row = lax.broadcasted_iota(jnp.int32, (half, LANES), 0)
    col = lax.broadcasted_iota(jnp.int32, (half, LANES), 1)
    total[pl.ds(0, half), :] = jnp.where(
        (col < half) | (col - half > row), whole[half:], pltpu.roll(whole[:half], half, 1)
    )
    row = lax.broadcasted_iota(jnp.int32, (LANES, LANES), 0)
    col = lax.broadcasted_iota(jnp.int32, (LANES, LANES), 1)
    total[pl.ds(half, 2 * rows - half), :] = jnp.zeros((2 * rows - half, LANES), jnp.float32)
    total[pl.ds(half, 1), :] = jnp.sum(jnp.where(row == col, whole, 0.0), axis=0, keepdims=True)
    odd = par[1] % 2
    kept[...] = total[pl.ds(odd * rows, rows), :]
    sent[...] = total[pl.ds((1 - odd) * rows, rows), :]


def factor_pair(low, p):
    q, size = p + 1, len(low)
    a, b, c = low[p][p], low[q][p], low[q][q]
    root_a, root_det = lax.rsqrt(a), lax.rsqrt(a * c - b * b)
    both = root_a * root_det
    turned = [a * low[i][q] - b * low[i][p] for i in range(q + 1, size)]
    low[q][p] = b * root_a
    for i, value in zip(range(q + 1, size), turned):
        low[i][p] = low[i][p] * root_a
        low[i][q] = value * both
    for i in range(q + 1, size):
        for m in range(q + 1, i + 1):
            low[i][m] = (low[i][m] - low[i][p] * low[m][p]) - low[i][q] * low[m][q]
    return root_a, a * both


def square_of(pivots):
    high = pivots.astype(jnp.bfloat16)
    rest = pivots - high.astype(jnp.float32)
    middle = rest.astype(jnp.bfloat16)
    low = (rest - middle.astype(jnp.float32)).astype(jnp.bfloat16)
    return lax.dot_general(
        jnp.concatenate([high, high, middle, middle, high, low], axis=0),
        jnp.concatenate([high, middle, high, middle, low, high], axis=0),
        (((0,), (0,)), ((), ())),
        preferred_element_type=jnp.float32,
    )


def invert_factor(gram, work, board):
    count = LANES // SUB
    lane = lax.broadcasted_iota(jnp.int32, (SUB, LANES), 1)
    sub = lax.broadcasted_iota(jnp.int32, (SUB, LANES), 0)
    rows = [gram[SUB * i : SUB * (i + 1)] for i in range(count)]
    columns = [lane_spread(rows[0], l) for l in range(SUB)]
    for block in range(count):
        base = SUB * block
        here = (lane >= base) & (lane < base + SUB)
        shelf = 3 * SUB * base
        for l in range(SUB):
            board[pl.ds(shelf + SUB * l, SUB), :] = columns[l]
        low = [
            [board[pl.ds(shelf + SUB * l + k, SUB, stride=0), :] for l in range(k + 1)]
            for k in range(SUB)
        ]
        shelf += SUB * SUB
        board[pl.ds(shelf, SUB), :] = jnp.where(
            here, jnp.where(lane - base == sub, 1.0, 0.0), rows[block]
        )
        inv = []
        for p in range(0, SUB, 2):
            inv.extend(factor_pair(low, p))
        scaled = []
        for k in range(SUB):
            line = board[pl.ds(shelf + k, SUB, stride=0), :]
            for l in range(k):
                line = line - low[k][l] * scaled[l]
            scaled.append(line * inv[k])
        merged = scaled[0]
        for k in range(1, SUB):
            merged = jnp.where(sub == k, scaled[k], merged)
        work[pl.ds(base, SUB), :] = merged
        shelf += SUB
        for i in range(block + 1, (block // GROUP + 1) * GROUP):
            weights = []
            rest = jnp.where(here, 0.0, rows[i])
            for l in range(SUB):
                weight = lane_spread(rows[i], base + l)
                for m in range(l):
                    weight = weight - weights[m] * low[l][m]
                weights.append(weight * inv[l])
            if i == block + 1:
                columns = [lane_spread(rows[i], base + SUB + l) for l in range(SUB)]
                for l in range(SUB):
                    board[pl.ds(shelf + SUB * l, SUB), :] = weights[l]
                    for k in range(SUB):
                        across = board[pl.ds(shelf + SUB * l + k, SUB, stride=0), :]
                        columns[k] = columns[k] - weights[l] * across
            for l in range(SUB):
                rest = rest - weights[l] * scaled[l]
            rows[i] = rest
        if block % GROUP == GROUP - 1 and block + 1 < count:
            first = SUB * (block + 1 - GROUP)
            tall = (SUB * GROUP, LANES)
            to_lane = lax.broadcasted_iota(jnp.int32, tall, 1) // SUB - first // SUB
            to_row = lax.broadcasted_iota(jnp.int32, tall, 0) // SUB
            pivots = work[pl.ds(first, SUB * GROUP), :]
            update = square_of(jnp.where((to_lane > to_row) & (to_lane < GROUP), 0.0, pivots))
            here = (lane >= first) & (lane < base + SUB)
            for i in range(block + 1, count):
                rows[i] = jnp.where(here, 0.0, rows[i]) - update[SUB * i : SUB * (i + 1)]
            columns = [lane_spread(rows[block + 1], base + SUB + l) for l in range(SUB)]


def factorize(par, mine_ref, other_ref, gram, work, board):
    half, rows = LANES // 2, mine_ref.shape[0]
    odd = par[1] % 2
    gram[pl.ds(odd * rows, rows), :] = mine_ref[...]
    gram[pl.ds((1 - odd) * rows, rows), :] = other_ref[...]
    packed, diagonal = gram[pl.ds(0, half), :], gram[pl.ds(half, 1), :]
    row = lax.broadcasted_iota(jnp.int32, (half, LANES), 0)
    col = lax.broadcasted_iota(jnp.int32, (half, LANES), 1)
    triangles = jnp.concatenate(
        [
            jnp.where(col < row, pltpu.roll(packed, half, 1), 0.0),
            jnp.where((col < half) | (col - half > row), packed, 0.0),
        ],
        axis=0,
    )
    row = lax.broadcasted_iota(jnp.int32, (LANES, LANES), 0)
    col = lax.broadcasted_iota(jnp.int32, (LANES, LANES), 1)
    size = jnp.broadcast_to(lax.rsqrt(diagonal), (LANES, LANES))
    whole = jnp.where(row == col, diagonal, triangles + jnp.transpose(triangles))
    invert_factor((whole * size) * jnp.transpose(size), work, board)
    inverse = jnp.where(row >= col, work[...], 0.0) * size
    diagonal = jnp.sum(jnp.where(row == col, inverse, 0.0), axis=0, keepdims=True)
    return inverse, diagonal


def paired(inverse):
    high = inverse.astype(jnp.bfloat16)
    low = (inverse - high.astype(jnp.float32)).astype(jnp.bfloat16)
    return jnp.concatenate(
        [jnp.concatenate([high, high], axis=1), jnp.concatenate([low, low], axis=1)], axis=0
    )


def times_factor(pair, factor):
    both = lax.dot_general(
        pair, factor, (((1,), (1,)), ((), ())), preferred_element_type=jnp.float32
    )
    return both[:, :LANES] + both[:, LANES:]


def factor_only(par, mine_ref, other_ref, prior_ref, _, inverse_ref, logs_ref, gram, work, board):
    inverse, diagonal = factorize(par, mine_ref, other_ref, gram, work, board)
    inverse_ref[...] = inverse
    logs_ref[...] = prior_ref[...] - jnp.log(diagonal)


def mend_only(par, start_in, middle_in, state_in, coef_ref, spin_ref, a, b, start, middle, state):
    tall = state.shape[2]
    mend_columns(par, (start, middle, state), coef_ref, spin_ref, ((0, tall, (a, b)),))


def update(scale, par, state, inverse_ref, out_ref, kept, sent, factor, total):
    factor[...] = paired(inverse_ref[...])
    gram = 0.0
    for comp, lon, cells in tiles_of(state):
        new = times_factor(jnp.concatenate(split_halves(cells), axis=1), factor[...])
        out_ref[comp, pl.ds(lon, BATCH)] = new.reshape((BATCH,) + out_ref.shape[2:])
        gram += gram_of(*split_halves(new))
    write_halves(par, gram, scale, kept, sent, total)


def restore_order(turned, out_ref):
    comps, cols, _, _ = turned.shape
    for comp in range(comps):
        for lon in range(0, cols, 2 * SUB):
            cells = jnp.concatenate(
                [
                    jnp.transpose(turned[comp, pl.ds(lon + shift, SUB)], (1, 0, 2))
                    for shift in (0, SUB)
                ],
                axis=1,
            )
            high = cells.astype(jnp.bfloat16)
            low = (cells - high.astype(jnp.float32)).astype(jnp.bfloat16)
            out_ref[comp, :, pl.ds(lon, 2 * SUB), pl.ds(0, LANES)] = high
            out_ref[comp, :, pl.ds(lon, 2 * SUB), pl.ds(LANES, LANES)] = low


def finish(
    par, mine_ref, other_ref, prior_ref, t_ref, out_ref, logs_ref, gram, work, board, factor, fresh, sems
):
    inverse, diagonal = factorize(par, mine_ref, other_ref, gram, work, board)
    factor[...] = paired(inverse)

    def out_copy(tile):
        return pltpu.make_async_copy(fresh.at[tile], out_ref.at[tile], sems.at[tile])

    for tile in range(TILES):
        fresh[tile] = times_factor(t_ref[tile], factor[...])
        out_copy(tile).start(priority=tile % 2)
    logs_ref[...] = prior_ref[...] - jnp.log(diagonal)

    for tile in range(TILES):
        out_copy(tile).wait()


def swap_pairs(near_value, far_value, axis, closed):
    count = lax.axis_size(axis)
    near = [(i, i ^ 1) for i in range(count)]
    far = [(i, (i + 1 if i % 2 else i - 1) % count) for i in range(count)]
    if not closed:
        far = far[1:-1]
    return lax.ppermute(near_value, axis, near), lax.ppermute(far_value, axis, far)


def swapped(value, axis, mask):
    return lax.ppermute(value, axis, [(i, i ^ mask) for i in range(lax.axis_size(axis))])


def add_four(first, second, third, fourth, _, out_ref):
    out_ref[...] = (first[...] + fourth[...]) + (third[...] + second[...])


def sum_over(value, axis, first_bit, beside=None):
    bits = lax.axis_size(axis).bit_length() - 1
    while first_bit < bits:
        low = 1 << first_bit
        if first_bit + 1 < bits:
            high = low << 1
            three, two, one = (swapped(value, axis, mask) for mask in (low | high, high, low))
            if beside is None:
                value = (three + two) + (one + value)
            else:
                value = pl.pallas_call(
                    add_four,
                    out_shape=jax.ShapeDtypeStruct(value.shape, value.dtype),
                    in_specs=[VMEM] * 4 + [pl.BlockSpec(memory_space=pl.ANY)],
                    out_specs=VMEM,
                    compiler_params=params(),
                )(value, three, two, one, beside)
                beside = None
            first_bit += 2
        else:
            value = value + swapped(value, axis, low)
            first_bit += 1
    return value


def sum_devices(kept, sent, order, beside=(None, None)):
    mine = kept + swapped(sent, "col", 1)
    for axis, work in zip(order, beside):
        mine = sum_over(mine, axis, 1 if axis == "col" else 0, work)
    return mine, swapped(mine, "col", 1)


def body(tangents, sea_mask, levels, current):
    comps, rows, cols, modes = tangents.shape
    total_rows = rows * lax.axis_size("row")
    total_cells = total_rows * cols * lax.axis_size("col")
    scale = 1.0 / total_cells
    row_at, col_at = lax.axis_index("row"), lax.axis_index("col")
    par = jnp.stack([row_at, col_at]).astype(jnp.int32)

    tall, length = rows + 2 * HALO, cols + 2 * SIDE

    block = shape_of(comps, length, tall, modes)
    coefs = shape_of(FIELDS, length, tall, LANES)
    columns = (shape_of(comps * SIDE * tall, modes),) * 2
    own_columns = (shape_of(comps * SIDE * rows + SUB, modes),) * 2
    corners = (shape_of(comps * SIDE * SUB + SUB, modes),) * 2
    rows_sent = (shape_of(comps * HALO + 1, cols, modes),) * 2
    halves = (shape_of(modes // 4 + SUB, modes),) * 2
    square = pltpu.VMEM((modes, modes), jnp.float32)
    board = pltpu.VMEM((3 * SUB * modes, LANES), jnp.float32)
    factor = pltpu.VMEM((2 * modes, 2 * modes), jnp.bfloat16)

    def call(
        kernel, outs, *operands, specs=None, out_specs=None, scratch=(), aliases=None, cost=1.0
    ):
        return pl.pallas_call(
            kernel,
            out_shape=outs,
            in_specs=specs or [SMEM] + [VMEM] * (len(operands) - 1),
            out_specs=out_specs or (VMEM,) * len(outs),
            scratch_shapes=scratch,
            input_output_aliases=aliases or {},
            compiler_params=params(),
            cost_estimate=pl.CostEstimate(
                flops=int(cost * 1e9), bytes_accessed=int(cost * 3e6), transcendentals=0
            ),
        )(*operands)

    def inside(step, state, chosen=None, partly=()):
        return call(
            functools.partial(apply_inside, step, chosen),
            (block,),
            state,
            coef,
            spin,
            *partly,
            specs=[VMEM] * (3 + len(partly)),
            aliases={3: 0} if partly else None,
            cost=2.0,
        )[0]

    def swap_columns(packed):
        return swap_pairs(*packed, "col", True)

    source, *fields = (
        pltpu.with_memory_space_constraint(x, pltpu.HBM)
        for x in (tangents, sea_mask.T, levels.T, current.T)
    )
    upright = [pltpu.VMEM(x.shape, x.dtype) for x in fields]
    packed = call(
        pack_rows,
        rows_sent,
        par,
        source,
        *fields,
        specs=[SMEM] + [HBM] * 4,
        scratch=upright
        + [
            pltpu.VMEM((cols, LANES), jnp.float32),
            pltpu.SemaphoreType.DMA((2 * comps,)),
            pltpu.SemaphoreType.DMA((FIELDS,)),
        ],
        cost=5.0,
    )
    row_halos = swap_pairs(*packed, "row", False)
    start, coef, spin, *packed = call(
        functools.partial(spread_fields, total_rows),
        (block, coefs, shape_of(tall, LANES)) + own_columns,
        par,
        tangents,
        *fields,
        specs=[SMEM, VMEM] + [HBM] * 3,
        scratch=[pltpu.VMEM((FIELDS, cols, LANES), jnp.float32)]
        + upright
        + [pltpu.SemaphoreType.DMA((FIELDS,))],
        cost=3.0,
    )
    halos = swap_columns(packed)
    middle_tiles = tuple(range(1, rows // SUB - 1))
    outer_tiles = (0,) + tuple(range(rows // SUB - 1, tall // SUB))
    middle = inside(0, start, middle_tiles)
    start, coef, *packed = call(
        join_rows,
        (block, coefs) + corners,
        par,
        start,
        coef,
        *row_halos,
        middle,
        specs=[SMEM] + [VMEM] * 4 + [pl.BlockSpec(memory_space=pl.ANY)],
        aliases={1: 0, 2: 1},
    )
    halos += swap_columns(packed)
    logs = jnp.zeros((1, modes), jnp.float32)

    middle = inside(0, start, outer_tiles, (middle,))
    state = inside(1, middle)
    _, _, start, coef, *packed, kept, sent = call(
        functools.partial(join_gram, scale),
        (block, block, block, coefs) + columns + halves,
        par,
        start,
        middle,
        state,
        coef,
        spin,
        *halos,
        scratch=[square],
        aliases={1: 0, 2: 1, 3: 2, 4: 3},
        cost=2.0,
    )
    middle = inside(0, start)
    state = inside(1, middle)

    halos = swap_columns(packed)
    mine, other = sum_devices(kept, sent, ("row", "col"), (middle, state))
    _, _, state = call(
        mend_only,
        (block,) * 3,
        par,
        start,
        middle,
        state,
        coef,
        spin,
        *halos,
        aliases={1: 0, 2: 1, 3: 2},
    )
    inverse, logs = call(
        factor_only,
        (shape_of(modes, modes), shape_of(1, modes)),
        par,
        mine,
        other,
        logs,
        state,
        specs=[SMEM] + [VMEM] * 3 + [pl.BlockSpec(memory_space=pl.ANY)],
        scratch=[square, square, board],
        cost=0.01,
    )
    state, kept, sent = call(
        functools.partial(update, scale),
        (shape_of(comps, cols, rows, modes),) + halves,
        par,
        state,
        inverse,
        scratch=[factor, square],
        cost=2.0,
    )
    state = call(
        restore_order,
        (jax.ShapeDtypeStruct((comps, rows, cols, 2 * modes), jnp.bfloat16),),
        state,
        specs=[VMEM],
        cost=1.0,
    )[0]
    height = comps * rows * cols // TILES
    tiled = shape_of(TILES, height, modes)
    mine, other = sum_devices(kept, sent, ("col", "row"))
    out, logs = call(
        finish,
        (tiled, shape_of(1, modes)),
        par,
        mine,
        other,
        logs,
        state.reshape(TILES, height, 2 * modes),
        out_specs=(HBM, VMEM),
        scratch=[
            square,
            square,
            board,
            factor,
            pltpu.VMEM((TILES, height, modes), jnp.float32),
            pltpu.SemaphoreType.DMA((TILES,)),
        ],
    )
    return out.reshape(tangents.shape), logs.reshape(modes)


def solution(mesh):
    placed = (P(None, "row", "col", None), P("row", "col"), P("row", "col"), P("row", "col"))
    return jax.shard_map(
        body,
        mesh=mesh,
        in_specs=placed,
        out_specs=(P(None, "row", "col", None), P()),
        check_vma=False,
    )
```

```python
import functools

import jax
import jax.numpy as jnp
from jax import lax
from jax.experimental import pallas as pl
from jax.experimental.pallas import tpu as pltpu
from jax.sharding import PartitionSpec as P

STEPS = 2
RENORMS = 2
LEVELS = 50

viscosity = 0.15
gravity = 0.5
rotation = 0.4

SUB = 8
LANES = 128
FIELDS = 3
HALO = STEPS * RENORMS
SIDE = STEPS
TILES = 24
BATCH = 8
GROUP = 8
VMEM_LIMIT = 16 * 1024 * 1024

HBM = pl.BlockSpec(memory_space=pltpu.HBM)
VMEM = pl.BlockSpec(memory_space=pltpu.VMEM)
SMEM = pl.BlockSpec(memory_space=pltpu.SMEM)


def params():
    return pltpu.CompilerParams(vmem_limit_bytes=VMEM_LIMIT)


def shape_of(*dims):
    return jax.ShapeDtypeStruct(dims, jnp.float32)


def lane_spread(block, lane):
    return jnp.broadcast_to(block[:, lane : lane + 1], (block.shape[0], LANES))


def fetch(sources, places, sems, priority=0):
    copies = [
        pltpu.make_async_copy(source, place, sems.at[i])
        for i, (source, place) in enumerate(zip(sources, places))
    ]
    for copy in copies:
        copy.start(priority=priority)
    return copies


def finish_all(copies):
    for copy in copies:
        copy.wait()


def fields_of(sea_ref, levels_ref, current_ref):
    return (
        sea_ref[...].astype(jnp.float32),
        0.5 * current_ref[...],
        0.5 * ((levels_ref[...] + 1).astype(jnp.float32) / LEVELS),
    )


def sides_of(par):
    odd_row, odd_col = par[0] % 2, par[1] % 2
    return (1 - odd_row, odd_row), (1 - odd_col, odd_col)


def pack_rows(
    par, t_ref, sea_ref, levels_ref, current_ref, row_a, row_b, sea, levels, current, wide, sems, field_sems
):
    comps, rows, cols, _ = t_ref.shape
    norths, _ = sides_of(par)
    field_copies = fetch((sea_ref, levels_ref, current_ref), (sea, levels, current), field_sems)
    slots = [(slot, msg, comp) for slot, msg in ((0, row_a), (1, row_b)) for comp in range(comps)]
    copies = fetch(
        [t_ref.at[comp, pl.ds(norths[slot] * (rows - HALO), HALO)] for slot, _, comp in slots],
        [msg.at[pl.ds(comp * HALO, HALO)] for _, msg, comp in slots],
        sems,
        1,
    )
    lane = lax.broadcasted_iota(jnp.int32, (cols, LANES), 1)
    wide[...] = jnp.zeros_like(wide)
    packed = [jnp.zeros((cols, LANES), jnp.float32)] * 2
    finish_all(field_copies)
    for field, value in enumerate(fields_of(sea, levels, current)):
        wide[:, pl.ds(0, rows)] = value
        whole = wide[...]
        for north in (0, 1):
            shift = (field * SUB - north * (rows - HALO)) % LANES
            moved = pltpu.roll(whole, shift, 1) if shift else whole
            here = (lane >= field * SUB) & (lane < field * SUB + HALO)
            packed[north] = jnp.where(here, moved, packed[north])
    for slot, msg in ((0, row_a), (1, row_b)):
        msg[comps * HALO] = jnp.where(norths[slot] == 1, packed[1], packed[0])
    finish_all(copies)


def spread_fields(
    total_rows, par, t_ref, sea_ref, levels_ref, current_ref, state, coef, spin, col_a, col_b, wide, sea, levels, current, field_sems
):
    comps, rows, cols, _ = t_ref.shape
    field_copies = fetch((sea_ref, levels_ref, current_ref), (sea, levels, current), field_sems)
    line = lax.broadcasted_iota(jnp.int32, spin.shape, 0)
    line = jnp.where(line < rows + HALO, line, line - (rows + 2 * HALO))
    latitude = (par[0] * rows + line).astype(jnp.float32)
    angle = (-70.0 + 140.0 * (latitude + 0.5) / total_rows) * (jnp.pi / 180.0)
    spin[...] = rotation * jnp.sin(angle)
    wide[...] = jnp.zeros_like(wide)
    finish_all(field_copies)
    for field, value in enumerate(fields_of(sea, levels, current)):
        wide[field, :, pl.ds(0, rows)] = value
        natural = jnp.transpose(wide[field])[:rows]
        for lon in range(cols):
            coef[field, SIDE + lon, pl.ds(0, rows), :] = lane_spread(natural, lon)
    for comp in range(comps):
        for row in range(0, rows, SUB):
            cells = t_ref[comp, pl.ds(row, SUB)]
            state[comp, pl.ds(SIDE, cols), pl.ds(row, SUB), :] = jnp.transpose(cells, (1, 0, 2))
    send_columns(par, state, (col_a, col_b), 0, rows)
    tail = comps * SIDE * rows
    _, easts = sides_of(par)
    for slot, msg in enumerate((col_a, col_b)):
        msg[pl.ds(tail, SUB), :] = jnp.zeros((SUB, LANES), jnp.float32)
        for field in range(FIELDS):
            msg[pl.ds(tail + field, 1), :] = wide[field, pl.ds(easts[slot] * (cols - 1), 1), :]


def column_at(east, cols, depth):
    return SIDE + depth + east * (cols - 1 - 2 * depth)


def send_columns(par, state, cols_sent, first, count):
    comps, length, _, _ = state.shape
    _, easts = sides_of(par)
    for slot, msg in enumerate(cols_sent):
        for comp in range(comps):
            for j in range(SIDE):
                column = column_at(easts[slot], length - 2 * SIDE, j)
                msg[pl.ds((comp * SIDE + j) * count, count), :] = state[
                    comp, column, pl.ds(first, count), :
                ]


def join_rows(par, state_in, coef_in, row_b, row_a, _, state, coef, col_a, col_b):
    comps, length, tall, _ = state.shape
    cols, rows = length - 2 * SIDE, tall - 2 * HALO
    norths, easts = sides_of(par)
    flat = state.reshape(comps * length * tall, LANES)
    for slot, msg in ((0, row_a), (1, row_b)):
        line = rows + HALO * (1 - norths[slot])
        for comp in range(comps):
            for h in range(HALO):
                for lon in range(0, cols, SUB):
                    at = (comp * length + SIDE + lon) * tall + line + h
                    flat[pl.ds(at, SUB, stride=tall), :] = msg[comp * HALO + h, pl.ds(lon, SUB), :]
    lane = lax.broadcasted_iota(jnp.int32, (cols, LANES), 1)
    north = jnp.where(norths[0] == 1, row_a[comps * HALO], row_b[comps * HALO])
    south = jnp.where(norths[0] == 1, row_b[comps * HALO], row_a[comps * HALO])
    beyond = jnp.where(lane % SUB < HALO, north, pltpu.roll(south, HALO, 1))
    natural = jnp.transpose(beyond)
    for field in range(FIELDS):
        block = natural[field * SUB : (field + 1) * SUB]
        for lon in range(cols):
            coef[field, SIDE + lon, pl.ds(rows, SUB), :] = lane_spread(block, lon)
    send_columns(par, state, (col_a, col_b), rows, SUB)
    tail = comps * SIDE * SUB
    for slot, msg in ((0, col_a), (1, col_b)):
        msg[pl.ds(tail, SUB), :] = jnp.zeros((SUB, LANES), jnp.float32)
        msg[pl.ds(tail, 1), :] = jnp.where(easts[slot] == 1, beyond[cols - 1 :], beyond[:1])


def model(own, x_diff, x_sum, above, below, sea, flow, depth, spin):
    keep, half = 1.0 - 4.0 * viscosity, 0.5 * gravity
    mixed = [
        keep * c + viscosity * (x + (n + s)) - flow * d
        for c, d, x, n, s in zip(own, x_diff, x_sum, above, below)
    ]
    v_y, h_y = above[1] - below[1], above[2] - below[2]
    return (
        sea * (mixed[0] - half * x_diff[2] + spin * own[1]),
        sea * (mixed[1] - half * h_y - spin * own[0]),
        sea * (mixed[2] - depth * (x_diff[0] + v_y)),
    )


def advance_column(source, target, coef_ref, spin_ref, lon, chosen=None):
    comps, length, tall, _ = source.shape
    flat = source.reshape(comps * length * tall, LANES)
    sub = lax.broadcasted_iota(jnp.int32, (SUB, LANES), 0)
    tiles = tall // SUB
    for tile in chosen or range(tiles):
        lines = pl.ds(SUB * tile, SUB)
        own, east, west = (
            [source[comp, lon + shift, lines, :] for comp in range(comps)] for shift in (0, 1, -1)
        )
        starts = [(comp * length + lon) * tall + SUB * tile for comp in range(comps)]
        if tile < tiles - 1:
            above = [flat[pl.ds(start + 1, SUB), :] for start in starts]
        else:
            wrap = [source[comp, lon, pl.ds(0, SUB), :] for comp in range(comps)]
            above = [
                jnp.where(sub == SUB - 1, pltpu.roll(w, SUB - 1, 0), pltpu.roll(o, SUB - 1, 0))
                for w, o in zip(wrap, own)
            ]
        if tile > 0:
            below = [flat[pl.ds(start - 1, SUB), :] for start in starts]
        else:
            wrap = [source[comp, lon, pl.ds(tall - SUB, SUB), :] for comp in range(comps)]
            below = [
                jnp.where(sub == 0, pltpu.roll(w, 1, 0), pltpu.roll(o, 1, 0))
                for w, o in zip(wrap, own)
            ]
        new = model(
            own,
            [e - w for e, w in zip(east, west)],
            [e + w for e, w in zip(east, west)],
            above,
            below,
            *(coef_ref[field, lon, lines, :] for field in range(FIELDS)),
            spin_ref[lines, :],
        )
        for comp in range(comps):
            target[comp, lon, lines, :] = new[comp]


def apply_inside(step, chosen, source, coef_ref, spin_ref, *refs):
    first = SIDE + step + 1
    count = source.shape[1] - 2 * first
    target = refs[-1]

    @pl.loop(0, count // 2)
    def _(pair):
        for lon in (first + 2 * pair, first + 2 * pair + 1):
            advance_column(source, target, coef_ref, spin_ref, lon, chosen)


def mend_columns(par, states, coef_ref, spin_ref, pieces):
    comps, length, _, _ = states[0].shape
    _, easts = sides_of(par)
    for first, count, cols_got in pieces:
        for slot, msg in enumerate(cols_got):
            for comp in range(comps):
                for j in range(SIDE):
                    column = column_at(easts[slot], length - 2 * SIDE, -1 - j)
                    states[0][comp, column, pl.ds(first, count), :] = msg[
                        pl.ds((comp * SIDE + j) * count, count), :
                    ]
    for step in range(STEPS):
        first = step + 1
        skip = length - 2 * first - 2 * SIDE

        @pl.loop(0, 2 * SIDE)
        def _(i):
            lon = first + i + (i // SIDE) * skip
            advance_column(states[step], states[step + 1], coef_ref, spin_ref, lon)


def join_gram(
    scale, par, start_in, middle_in, state_in, coef_in, spin_ref, a, b, c, d, start, middle, state, coef, col_a, col_b, kept, sent, total
):
    _, length, tall, _ = state.shape
    rows = tall - 2 * HALO
    _, easts = sides_of(par)
    for slot, (own, beyond) in enumerate(((a, c), (b, d))):
        own, beyond = (jnp.transpose(x[pl.ds(x.shape[0] - SUB, SUB), :]) for x in (own, beyond))
        column = column_at(easts[slot], length - 2 * SIDE, -1)
        for field in range(FIELDS):
            coef[field, column, pl.ds(0, rows), :] = lane_spread(own[:rows], field)
            coef[field, column, pl.ds(rows, SUB), :] = lane_spread(
                beyond[field * SUB : (field + 1) * SUB], 0
            )
    mend_columns(
        par, (start, middle, state), coef, spin_ref, ((0, rows, (a, b)), (rows, SUB, (c, d)))
    )
    send_columns(par, state, (col_a, col_b), 0, tall)
    gram = sum(gram_of(*split_halves(cells)) for _, _, cells in tiles_of(state))
    write_halves(par, gram, scale, kept, sent, total)


def tiles_of(state):
    comps, length, tall, _ = state.shape
    rows = tall - 2 * HALO
    for comp in range(comps):
        for lon in range(0, length - 2 * SIDE, BATCH):
            cells = state[comp, pl.ds(SIDE + lon, BATCH), pl.ds(0, rows), :]
            yield comp, lon, cells.reshape(BATCH * rows, LANES)


def split_halves(value):
    high = value.astype(jnp.bfloat16)
    return high, (value - high.astype(jnp.float32)).astype(jnp.bfloat16)


def gram_of(high, low):
    return lax.dot_general(
        high,
        jnp.concatenate([high, low], axis=1),
        (((0,), (0,)), ((), ())),
        preferred_element_type=jnp.float32,
    )


def write_halves(par, gram, scale, kept, sent, total):
    half, rows = LANES // 2, kept.shape[0]
    mixed = gram[:, LANES:]
    whole = scale * (gram[:, :LANES] + (mixed + jnp.transpose(mixed)))
    row = lax.broadcasted_iota(jnp.int32, (half, LANES), 0)
    col = lax.broadcasted_iota(jnp.int32, (half, LANES), 1)
    total[pl.ds(0, half), :] = jnp.where(
        (col < half) | (col - half > row), whole[half:], pltpu.roll(whole[:half], half, 1)
    )
    row = lax.broadcasted_iota(jnp.int32, (LANES, LANES), 0)
    col = lax.broadcasted_iota(jnp.int32, (LANES, LANES), 1)
    total[pl.ds(half, 2 * rows - half), :] = jnp.zeros((2 * rows - half, LANES), jnp.float32)
    total[pl.ds(half, 1), :] = jnp.sum(jnp.where(row == col, whole, 0.0), axis=0, keepdims=True)
    odd = par[1] % 2
    kept[...] = total[pl.ds(odd * rows, rows), :]
    sent[...] = total[pl.ds((1 - odd) * rows, rows), :]


def factor_pair(low, p):
    q, size = p + 1, len(low)
    a, b, c = low[p][p], low[q][p], low[q][q]
    root_a, root_det = lax.rsqrt(a), lax.rsqrt(a * c - b * b)
    both = root_a * root_det
    turned = [a * low[i][q] - b * low[i][p] for i in range(q + 1, size)]
    low[q][p] = b * root_a
    for i, value in zip(range(q + 1, size), turned):
        low[i][p] = low[i][p] * root_a
        low[i][q] = value * both
    for i in range(q + 1, size):
        for m in range(q + 1, i + 1):
            low[i][m] = (low[i][m] - low[i][p] * low[m][p]) - low[i][q] * low[m][q]
    return root_a, a * both


def square_of(pivots):
    high = pivots.astype(jnp.bfloat16)
    rest = pivots - high.astype(jnp.float32)
    middle = rest.astype(jnp.bfloat16)
    low = (rest - middle.astype(jnp.float32)).astype(jnp.bfloat16)
    return lax.dot_general(
        jnp.concatenate([high, high, middle, middle, high, low], axis=0),
        jnp.concatenate([high, middle, high, middle, low, high], axis=0),
        (((0,), (0,)), ((), ())),
        preferred_element_type=jnp.float32,
    )


def invert_factor(gram, work, board):
    count = LANES // SUB
    lane = lax.broadcasted_iota(jnp.int32, (SUB, LANES), 1)
    sub = lax.broadcasted_iota(jnp.int32, (SUB, LANES), 0)
    rows = [gram[SUB * i : SUB * (i + 1)] for i in range(count)]
    columns = [lane_spread(rows[0], l) for l in range(SUB)]
    for block in range(count):
        base = SUB * block
        here = (lane >= base) & (lane < base + SUB)
        shelf = 3 * SUB * base
        for l in range(SUB):
            board[pl.ds(shelf + SUB * l, SUB), :] = columns[l]
        low = [
            [board[pl.ds(shelf + SUB * l + k, SUB, stride=0), :] for l in range(k + 1)]
            for k in range(SUB)
        ]
        shelf += SUB * SUB
        board[pl.ds(shelf, SUB), :] = jnp.where(
            here, jnp.where(lane - base == sub, 1.0, 0.0), rows[block]
        )
        inv = []
        for p in range(0, SUB, 2):
            inv.extend(factor_pair(low, p))
        scaled = []
        for k in range(SUB):
            line = board[pl.ds(shelf + k, SUB, stride=0), :]
            for l in range(k):
                line = line - low[k][l] * scaled[l]
            scaled.append(line * inv[k])
        merged = scaled[0]
        for k in range(1, SUB):
            merged = jnp.where(sub == k, scaled[k], merged)
        work[pl.ds(base, SUB), :] = merged
        shelf += SUB
        for i in range(block + 1, (block // GROUP + 1) * GROUP):
            weights = []
            rest = jnp.where(here, 0.0, rows[i])
            for l in range(SUB):
                weight = lane_spread(rows[i], base + l)
                for m in range(l):
                    weight = weight - weights[m] * low[l][m]
                weights.append(weight * inv[l])
            if i == block + 1:
                columns = [lane_spread(rows[i], base + SUB + l) for l in range(SUB)]
                for l in range(SUB):
                    board[pl.ds(shelf + SUB * l, SUB), :] = weights[l]
                    for k in range(SUB):
                        across = board[pl.ds(shelf + SUB * l + k, SUB, stride=0), :]
                        columns[k] = columns[k] - weights[l] * across
            for l in range(SUB):
                rest = rest - weights[l] * scaled[l]
            rows[i] = rest
        if block % GROUP == GROUP - 1 and block + 1 < count:
            first = SUB * (block + 1 - GROUP)
            tall = (SUB * GROUP, LANES)
            to_lane = lax.broadcasted_iota(jnp.int32, tall, 1) // SUB - first // SUB
            to_row = lax.broadcasted_iota(jnp.int32, tall, 0) // SUB
            pivots = work[pl.ds(first, SUB * GROUP), :]
            update = square_of(jnp.where((to_lane > to_row) & (to_lane < GROUP), 0.0, pivots))
            here = (lane >= first) & (lane < base + SUB)
            for i in range(block + 1, count):
                rows[i] = jnp.where(here, 0.0, rows[i]) - update[SUB * i : SUB * (i + 1)]
            columns = [lane_spread(rows[block + 1], base + SUB + l) for l in range(SUB)]


def factorize(par, mine_ref, other_ref, gram, work, board):
    half, rows = LANES // 2, mine_ref.shape[0]
    odd = par[1] % 2
    gram[pl.ds(odd * rows, rows), :] = mine_ref[...]
    gram[pl.ds((1 - odd) * rows, rows), :] = other_ref[...]
    packed, diagonal = gram[pl.ds(0, half), :], gram[pl.ds(half, 1), :]
    row = lax.broadcasted_iota(jnp.int32, (half, LANES), 0)
    col = lax.broadcasted_iota(jnp.int32, (half, LANES), 1)
    triangles = jnp.concatenate(
        [
            jnp.where(col < row, pltpu.roll(packed, half, 1), 0.0),
            jnp.where((col < half) | (col - half > row), packed, 0.0),
        ],
        axis=0,
    )
    row = lax.broadcasted_iota(jnp.int32, (LANES, LANES), 0)
    col = lax.broadcasted_iota(jnp.int32, (LANES, LANES), 1)
    size = jnp.broadcast_to(lax.rsqrt(diagonal), (LANES, LANES))
    whole = jnp.where(row == col, diagonal, triangles + jnp.transpose(triangles))
    invert_factor((whole * size) * jnp.transpose(size), work, board)
    inverse = jnp.where(row >= col, work[...], 0.0) * size
    diagonal = jnp.sum(jnp.where(row == col, inverse, 0.0), axis=0, keepdims=True)
    return inverse, diagonal


def paired(inverse):
    high = inverse.astype(jnp.bfloat16)
    low = (inverse - high.astype(jnp.float32)).astype(jnp.bfloat16)
    return jnp.concatenate(
        [jnp.concatenate([high, high], axis=1), jnp.concatenate([low, low], axis=1)], axis=0
    )


def times_factor(pair, factor):
    both = lax.dot_general(
        pair, factor, (((1,), (1,)), ((), ())), preferred_element_type=jnp.float32
    )
    return both[:, :LANES] + both[:, LANES:]


def factor_only(par, mine_ref, other_ref, prior_ref, _, inverse_ref, logs_ref, gram, work, board):
    inverse, diagonal = factorize(par, mine_ref, other_ref, gram, work, board)
    inverse_ref[...] = inverse
    logs_ref[...] = prior_ref[...] - jnp.log(diagonal)


def mend_only(par, start_in, middle_in, state_in, coef_ref, spin_ref, a, b, start, middle, state):
    tall = state.shape[2]
    mend_columns(par, (start, middle, state), coef_ref, spin_ref, ((0, tall, (a, b)),))


def update(scale, par, state, inverse_ref, out_ref, kept, sent, factor, total):
    factor[...] = paired(inverse_ref[...])
    gram = 0.0
    for comp, lon, cells in tiles_of(state):
        new = times_factor(jnp.concatenate(split_halves(cells), axis=1), factor[...])
        out_ref[comp, pl.ds(lon, BATCH)] = new.reshape((BATCH,) + out_ref.shape[2:])
        gram += gram_of(*split_halves(new))
    write_halves(par, gram, scale, kept, sent, total)


def restore_order(turned, out_ref):
    comps, cols, _, _ = turned.shape
    for comp in range(comps):
        for lon in range(0, cols, 2 * SUB):
            cells = jnp.concatenate(
                [
                    jnp.transpose(turned[comp, pl.ds(lon + shift, SUB)], (1, 0, 2))
                    for shift in (0, SUB)
                ],
                axis=1,
            )
            high = cells.astype(jnp.bfloat16)
            low = (cells - high.astype(jnp.float32)).astype(jnp.bfloat16)
            out_ref[comp, :, pl.ds(lon, 2 * SUB), pl.ds(0, LANES)] = high
            out_ref[comp, :, pl.ds(lon, 2 * SUB), pl.ds(LANES, LANES)] = low


def finish(
    par, mine_ref, other_ref, prior_ref, t_ref, out_ref, logs_ref, gram, work, board, factor, fresh, sems
):
    inverse, diagonal = factorize(par, mine_ref, other_ref, gram, work, board)
    factor[...] = paired(inverse)

    def out_copy(tile):
        return pltpu.make_async_copy(fresh.at[tile], out_ref.at[tile], sems.at[tile])

    for tile in range(TILES):
        fresh[tile] = times_factor(t_ref[tile], factor[...])
        out_copy(tile).start(priority=tile % 2)
    logs_ref[...] = prior_ref[...] - jnp.log(diagonal)

    for tile in range(TILES):
        out_copy(tile).wait()


def swap_pairs(near_value, far_value, axis, closed):
    count = lax.axis_size(axis)
    near = [(i, i ^ 1) for i in range(count)]
    far = [(i, (i + 1 if i % 2 else i - 1) % count) for i in range(count)]
    if not closed:
        far = far[1:-1]
    from_far = lax.ppermute(far_value, axis, far)
    return lax.ppermute(near_value, axis, near), from_far


def swapped(value, axis, mask):
    return lax.ppermute(value, axis, [(i, i ^ mask) for i in range(lax.axis_size(axis))])


def add_four(first, second, third, fourth, _, out_ref):
    out_ref[...] = (first[...] + fourth[...]) + (third[...] + second[...])


def sum_over(value, axis, first_bit, beside=None):
    bits = lax.axis_size(axis).bit_length() - 1
    while first_bit < bits:
        low = 1 << first_bit
        if first_bit + 1 < bits:
            high = low << 1
            three, two, one = (swapped(value, axis, mask) for mask in (low | high, high, low))
            if beside is None:
                value = (three + two) + (one + value)
            else:
                value = pl.pallas_call(
                    add_four,
                    out_shape=jax.ShapeDtypeStruct(value.shape, value.dtype),
                    in_specs=[VMEM] * 4 + [pl.BlockSpec(memory_space=pl.ANY)],
                    out_specs=VMEM,
                    compiler_params=params(),
                )(value, three, two, one, beside)
                beside = None
            first_bit += 2
        else:
            value = value + swapped(value, axis, low)
            first_bit += 1
    return value


def sum_devices(kept, sent, order, beside=(None, None)):
    mine = kept + swapped(sent, "col", 1)
    for axis, work in zip(order, beside):
        mine = sum_over(mine, axis, 1 if axis == "col" else 0, work)
    return mine, swapped(mine, "col", 1)


def body(tangents, sea_mask, levels, current):
    comps, rows, cols, modes = tangents.shape
    total_rows = rows * lax.axis_size("row")
    total_cells = total_rows * cols * lax.axis_size("col")
    scale = 1.0 / total_cells
    row_at, col_at = lax.axis_index("row"), lax.axis_index("col")
    par = jnp.stack([row_at, col_at]).astype(jnp.int32)

    tall, length = rows + 2 * HALO, cols + 2 * SIDE

    block = shape_of(comps, length, tall, modes)
    coefs = shape_of(FIELDS, length, tall, LANES)
    columns = (shape_of(comps * SIDE * tall, modes),) * 2
    own_columns = (shape_of(comps * SIDE * rows + SUB, modes),) * 2
    corners = (shape_of(comps * SIDE * SUB + SUB, modes),) * 2
    rows_sent = (shape_of(comps * HALO + 1, cols, modes),) * 2
    halves = (shape_of(modes // 4 + SUB, modes),) * 2
    square = pltpu.VMEM((modes, modes), jnp.float32)
    board = pltpu.VMEM((3 * SUB * modes, LANES), jnp.float32)
    factor = pltpu.VMEM((2 * modes, 2 * modes), jnp.bfloat16)

    def call(
        kernel, outs, *operands, specs=None, out_specs=None, scratch=(), aliases=None, cost=1.0
    ):
        return pl.pallas_call(
            kernel,
            out_shape=outs,
            in_specs=specs or [SMEM] + [VMEM] * (len(operands) - 1),
            out_specs=out_specs or (VMEM,) * len(outs),
            scratch_shapes=scratch,
            input_output_aliases=aliases or {},
            compiler_params=params(),
            cost_estimate=pl.CostEstimate(
                flops=int(cost * 1e9), bytes_accessed=int(cost * 3e6), transcendentals=0
            ),
        )(*operands)

    def inside(step, state, chosen=None, partly=()):
        return call(
            functools.partial(apply_inside, step, chosen),
            (block,),
            state,
            coef,
            spin,
            *partly,
            specs=[VMEM] * (3 + len(partly)),
            aliases={3: 0} if partly else None,
            cost=2.0,
        )[0]

    def swap_columns(packed):
        return swap_pairs(*packed, "col", True)

    source, *fields = (
        pltpu.with_memory_space_constraint(x, pltpu.HBM)
        for x in (tangents, sea_mask.T, levels.T, current.T)
    )
    upright = [pltpu.VMEM(x.shape, x.dtype) for x in fields]
    packed = call(
        pack_rows,
        rows_sent,
        par,
        source,
        *fields,
        specs=[SMEM] + [HBM] * 4,
        scratch=upright
        + [
            pltpu.VMEM((cols, LANES), jnp.float32),
            pltpu.SemaphoreType.DMA((2 * comps,)),
            pltpu.SemaphoreType.DMA((FIELDS,)),
        ],
        cost=5.0,
    )
    row_halos = swap_pairs(*packed, "row", False)
    start, coef, spin, *packed = call(
        functools.partial(spread_fields, total_rows),
        (block, coefs, shape_of(tall, LANES)) + own_columns,
        par,
        tangents,
        *fields,
        specs=[SMEM, VMEM] + [HBM] * 3,
        scratch=[pltpu.VMEM((FIELDS, cols, LANES), jnp.float32)]
        + upright
        + [pltpu.SemaphoreType.DMA((FIELDS,))],
        cost=3.0,
    )
    halos = swap_columns(packed)
    middle_tiles = tuple(range(1, rows // SUB - 1))
    outer_tiles = (0,) + tuple(range(rows // SUB - 1, tall // SUB))
    middle = inside(0, start, middle_tiles)
    start, coef, *packed = call(
        join_rows,
        (block, coefs) + corners,
        par,
        start,
        coef,
        *reversed(row_halos),
        middle,
        specs=[SMEM] + [VMEM] * 4 + [pl.BlockSpec(memory_space=pl.ANY)],
        aliases={1: 0, 2: 1},
    )
    halos += swap_columns(packed)
    logs = jnp.zeros((1, modes), jnp.float32)

    middle = inside(0, start, outer_tiles, (middle,))
    state = inside(1, middle)
    _, _, start, coef, *packed, kept, sent = call(
        functools.partial(join_gram, scale),
        (block, block, block, coefs) + columns + halves,
        par,
        start,
        middle,
        state,
        coef,
        spin,
        *halos,
        scratch=[square],
        aliases={1: 0, 2: 1, 3: 2, 4: 3},
        cost=2.0,
    )
    middle = inside(0, start)
    state = inside(1, middle)

    halos = swap_columns(packed)
    mine, other = sum_devices(kept, sent, ("row", "col"), (middle, state))
    _, _, state = call(
        mend_only,
        (block,) * 3,
        par,
        start,
        middle,
        state,
        coef,
        spin,
        *halos,
        aliases={1: 0, 2: 1, 3: 2},
    )
    inverse, logs = call(
        factor_only,
        (shape_of(modes, modes), shape_of(1, modes)),
        par,
        mine,
        other,
        logs,
        state,
        specs=[SMEM] + [VMEM] * 3 + [pl.BlockSpec(memory_space=pl.ANY)],
        scratch=[square, square, board],
        cost=0.01,
    )
    state, kept, sent = call(
        functools.partial(update, scale),
        (shape_of(comps, cols, rows, modes),) + halves,
        par,
        state,
        inverse,
        scratch=[factor, square],
        cost=2.0,
    )
    state = call(
        restore_order,
        (jax.ShapeDtypeStruct((comps, rows, cols, 2 * modes), jnp.bfloat16),),
        state,
        specs=[VMEM],
        cost=1.0,
    )[0]
    height = comps * rows * cols // TILES
    tiled = shape_of(TILES, height, modes)
    mine, other = sum_devices(kept, sent, ("col", "row"))
    out, logs = call(
        finish,
        (tiled, shape_of(1, modes)),
        par,
        mine,
        other,
        logs,
        state.reshape(TILES, height, 2 * modes),
        out_specs=(HBM, VMEM),
        scratch=[
            square,
            square,
            board,
            factor,
            pltpu.VMEM((TILES, height, modes), jnp.float32),
            pltpu.SemaphoreType.DMA((TILES,)),
        ],
    )
    return out.reshape(tangents.shape), logs.reshape(modes)


def solution(mesh):
    placed = (P(None, "row", "col", None), P("row", "col"), P("row", "col"), P("row", "col"))
    return jax.shard_map(
        body,
        mesh=mesh,
        in_specs=placed,
        out_specs=(P(None, "row", "col", None), P()),
        check_vma=False,
    )
```

```python
import functools

import jax
import jax.numpy as jnp
from jax import lax
from jax.experimental import pallas as pl
from jax.experimental.pallas import tpu as pltpu
from jax.sharding import PartitionSpec as P

STEPS = 2
RENORMS = 2
LEVELS = 50

viscosity = 0.15
gravity = 0.5
rotation = 0.4

SUB = 8
LANES = 128
FIELDS = 3
HALO = STEPS * RENORMS
SIDE = STEPS
TILES = 32
BATCH = 4
GROUP = 8
VMEM_LIMIT = 16 * 1024 * 1024

HBM = pl.BlockSpec(memory_space=pltpu.HBM)
VMEM = pl.BlockSpec(memory_space=pltpu.VMEM)
SMEM = pl.BlockSpec(memory_space=pltpu.SMEM)


def params():
    return pltpu.CompilerParams(vmem_limit_bytes=VMEM_LIMIT)


def shape_of(*dims):
    return jax.ShapeDtypeStruct(dims, jnp.float32)


def lane_spread(block, lane):
    return jnp.broadcast_to(block[:, lane : lane + 1], (block.shape[0], LANES))


def fetch(sources, places, sems, priority=0):
    copies = [
        pltpu.make_async_copy(source, place, sems.at[i])
        for i, (source, place) in enumerate(zip(sources, places))
    ]
    for copy in copies:
        copy.start(priority=priority)
    return copies


def finish_all(copies):
    for copy in copies:
        copy.wait()


def fields_of(sea_ref, levels_ref, current_ref):
    return (
        sea_ref[...].astype(jnp.float32),
        0.5 * current_ref[...],
        0.5 * ((levels_ref[...] + 1).astype(jnp.float32) / LEVELS),
    )


def sides_of(par):
    odd_row, odd_col = par[0] % 2, par[1] % 2
    return (1 - odd_row, odd_row), (1 - odd_col, odd_col)


def pack_rows(
    par, t_ref, sea_ref, levels_ref, current_ref, row_a, row_b, sea, levels, current, wide, sems, field_sems
):
    comps, rows, cols, _ = t_ref.shape
    norths, _ = sides_of(par)
    field_copies = fetch((sea_ref, levels_ref, current_ref), (sea, levels, current), field_sems)
    slots = [(slot, msg, comp) for slot, msg in ((0, row_a), (1, row_b)) for comp in range(comps)]
    copies = fetch(
        [t_ref.at[comp, pl.ds(norths[slot] * (rows - HALO), HALO)] for slot, _, comp in slots],
        [msg.at[pl.ds(comp * HALO, HALO)] for _, msg, comp in slots],
        sems,
        1,
    )
    lane = lax.broadcasted_iota(jnp.int32, (cols, LANES), 1)
    wide[...] = jnp.zeros_like(wide)
    packed = [jnp.zeros((cols, LANES), jnp.float32)] * 2
    finish_all(field_copies)
    for field, value in enumerate(fields_of(sea, levels, current)):
        wide[:, pl.ds(0, rows)] = value
        whole = wide[...]
        for north in (0, 1):
            shift = (field * SUB - north * (rows - HALO)) % LANES
            moved = pltpu.roll(whole, shift, 1) if shift else whole
            here = (lane >= field * SUB) & (lane < field * SUB + HALO)
            packed[north] = jnp.where(here, moved, packed[north])
    for slot, msg in ((0, row_a), (1, row_b)):
        msg[comps * HALO] = jnp.where(norths[slot] == 1, packed[1], packed[0])
    finish_all(copies)


def spread_fields(
    total_rows, par, t_ref, sea_ref, levels_ref, current_ref, state, coef, spin, col_a, col_b, wide, sea, levels, current, field_sems
):
    comps, rows, cols, _ = t_ref.shape
    field_copies = fetch((sea_ref, levels_ref, current_ref), (sea, levels, current), field_sems)
    line = lax.broadcasted_iota(jnp.int32, spin.shape, 0)
    line = jnp.where(line < rows + HALO, line, line - (rows + 2 * HALO))
    latitude = (par[0] * rows + line).astype(jnp.float32)
    angle = (-70.0 + 140.0 * (latitude + 0.5) / total_rows) * (jnp.pi / 180.0)
    spin[...] = rotation * jnp.sin(angle)
    wide[...] = jnp.zeros_like(wide)
    finish_all(field_copies)
    for field, value in enumerate(fields_of(sea, levels, current)):
        wide[field, :, pl.ds(0, rows)] = value
        natural = jnp.transpose(wide[field])[:rows]
        for lon in range(cols):
            coef[field, SIDE + lon, pl.ds(0, rows), :] = lane_spread(natural, lon)
    for comp in range(comps):
        for row in range(0, rows, SUB):
            cells = t_ref[comp, pl.ds(row, SUB)]
            state[comp, pl.ds(SIDE, cols), pl.ds(row, SUB), :] = jnp.transpose(cells, (1, 0, 2))
    send_columns(par, state, (col_a, col_b), 0, rows)
    tail = comps * SIDE * rows
    _, easts = sides_of(par)
    for slot, msg in enumerate((col_a, col_b)):
        msg[pl.ds(tail, SUB), :] = jnp.zeros((SUB, LANES), jnp.float32)
        for field in range(FIELDS):
            msg[pl.ds(tail + field, 1), :] = wide[field, pl.ds(easts[slot] * (cols - 1), 1), :]


def column_at(east, cols, depth):
    return SIDE + depth + east * (cols - 1 - 2 * depth)


def send_columns(par, state, cols_sent, first, count):
    comps, length, _, _ = state.shape
    _, easts = sides_of(par)
    for slot, msg in enumerate(cols_sent):
        for comp in range(comps):
            for j in range(SIDE):
                column = column_at(easts[slot], length - 2 * SIDE, j)
                msg[pl.ds((comp * SIDE + j) * count, count), :] = state[
                    comp, column, pl.ds(first, count), :
                ]


def join_rows(par, state_in, coef_in, row_a, row_b, _, state, coef, col_a, col_b):
    comps, length, tall, _ = state.shape
    cols, rows = length - 2 * SIDE, tall - 2 * HALO
    norths, easts = sides_of(par)
    flat = state.reshape(comps * length * tall, LANES)
    for slot, msg in ((0, row_a), (1, row_b)):
        line = rows + HALO * (1 - norths[slot])
        for comp in range(comps):
            for h in range(HALO):
                for lon in range(0, cols, SUB):
                    at = (comp * length + SIDE + lon) * tall + line + h
                    flat[pl.ds(at, SUB, stride=tall), :] = msg[comp * HALO + h, pl.ds(lon, SUB), :]
    lane = lax.broadcasted_iota(jnp.int32, (cols, LANES), 1)
    north = jnp.where(norths[0] == 1, row_a[comps * HALO], row_b[comps * HALO])
    south = jnp.where(norths[0] == 1, row_b[comps * HALO], row_a[comps * HALO])
    beyond = jnp.where(lane % SUB < HALO, north, pltpu.roll(south, HALO, 1))
    natural = jnp.transpose(beyond)
    for field in range(FIELDS):
        block = natural[field * SUB : (field + 1) * SUB]
        for lon in range(cols):
            coef[field, SIDE + lon, pl.ds(rows, SUB), :] = lane_spread(block, lon)
    send_columns(par, state, (col_a, col_b), rows, SUB)
    tail = comps * SIDE * SUB
    for slot, msg in ((0, col_a), (1, col_b)):
        msg[pl.ds(tail, SUB), :] = jnp.zeros((SUB, LANES), jnp.float32)
        msg[pl.ds(tail, 1), :] = jnp.where(easts[slot] == 1, beyond[cols - 1 :], beyond[:1])


def model(own, x_diff, x_sum, above, below, sea, flow, depth, spin):
    keep, half = 1.0 - 4.0 * viscosity, 0.5 * gravity
    mixed = [
        keep * c + viscosity * (x + (n + s)) - flow * d
        for c, d, x, n, s in zip(own, x_diff, x_sum, above, below)
    ]
    v_y, h_y = above[1] - below[1], above[2] - below[2]
    return (
        sea * (mixed[0] - half * x_diff[2] + spin * own[1]),
        sea * (mixed[1] - half * h_y - spin * own[0]),
        sea * (mixed[2] - depth * (x_diff[0] + v_y)),
    )


def advance_column(source, target, coef_ref, spin_ref, lon, chosen=None):
    comps, length, tall, _ = source.shape
    flat = source.reshape(comps * length * tall, LANES)
    sub = lax.broadcasted_iota(jnp.int32, (SUB, LANES), 0)
    tiles = tall // SUB
    for tile in chosen or range(tiles):
        lines = pl.ds(SUB * tile, SUB)
        own, east, west = (
            [source[comp, lon + shift, lines, :] for comp in range(comps)] for shift in (0, 1, -1)
        )
        starts = [(comp * length + lon) * tall + SUB * tile for comp in range(comps)]
        if tile < tiles - 1:
            above = [flat[pl.ds(start + 1, SUB), :] for start in starts]
        else:
            wrap = [source[comp, lon, pl.ds(0, SUB), :] for comp in range(comps)]
            above = [
                jnp.where(sub == SUB - 1, pltpu.roll(w, SUB - 1, 0), pltpu.roll(o, SUB - 1, 0))
                for w, o in zip(wrap, own)
            ]
        if tile > 0:
            below = [flat[pl.ds(start - 1, SUB), :] for start in starts]
        else:
            wrap = [source[comp, lon, pl.ds(tall - SUB, SUB), :] for comp in range(comps)]
            below = [
                jnp.where(sub == 0, pltpu.roll(w, 1, 0), pltpu.roll(o, 1, 0))
                for w, o in zip(wrap, own)
            ]
        new = model(
            own,
            [e - w for e, w in zip(east, west)],
            [e + w for e, w in zip(east, west)],
            above,
            below,
            *(coef_ref[field, lon, lines, :] for field in range(FIELDS)),
            spin_ref[lines, :],
        )
        for comp in range(comps):
            target[comp, lon, lines, :] = new[comp]


def apply_inside(step, chosen, source, coef_ref, spin_ref, *refs):
    first = SIDE + step + 1
    count = source.shape[1] - 2 * first
    target = refs[-1]

    @pl.loop(0, count // 2)
    def _(pair):
        for lon in (first + 2 * pair, first + 2 * pair + 1):
            advance_column(source, target, coef_ref, spin_ref, lon, chosen)


def mend_columns(par, states, coef_ref, spin_ref, pieces):
    comps, length, _, _ = states[0].shape
    _, easts = sides_of(par)
    for first, count, cols_got in pieces:
        for slot, msg in enumerate(cols_got):
            for comp in range(comps):
                for j in range(SIDE):
                    column = column_at(easts[slot], length - 2 * SIDE, -1 - j)
                    states[0][comp, column, pl.ds(first, count), :] = msg[
                        pl.ds((comp * SIDE + j) * count, count), :
                    ]
    for step in range(STEPS):
        first = step + 1
        skip = length - 2 * first - 2 * SIDE

        @pl.loop(0, 2 * SIDE)
        def _(i):
            lon = first + i + (i // SIDE) * skip
            advance_column(states[step], states[step + 1], coef_ref, spin_ref, lon)


def join_gram(
    scale, par, start_in, middle_in, state_in, coef_in, spin_ref, a, b, c, d, start, middle, state, coef, col_a, col_b, kept, sent, total
):
    _, length, tall, _ = state.shape
    rows = tall - 2 * HALO
    _, easts = sides_of(par)
    for slot, (own, beyond) in enumerate(((a, c), (b, d))):
        own, beyond = (jnp.transpose(x[pl.ds(x.shape[0] - SUB, SUB), :]) for x in (own, beyond))
        column = column_at(easts[slot], length - 2 * SIDE, -1)
        for field in range(FIELDS):
            coef[field, column, pl.ds(0, rows), :] = lane_spread(own[:rows], field)
            coef[field, column, pl.ds(rows, SUB), :] = lane_spread(
                beyond[field * SUB : (field + 1) * SUB], 0
            )
    mend_columns(
        par, (start, middle, state), coef, spin_ref, ((0, rows, (a, b)), (rows, SUB, (c, d)))
    )
    send_columns(par, state, (col_a, col_b), 0, tall)
    gram = sum(gram_of(*split_halves(cells)) for _, _, cells in tiles_of(state))
    write_halves(par, gram, scale, kept, sent, total)


def tiles_of(state):
    comps, length, tall, _ = state.shape
    rows = tall - 2 * HALO
    for comp in range(comps):
        for lon in range(0, length - 2 * SIDE, BATCH):
            cells = state[comp, pl.ds(SIDE + lon, BATCH), pl.ds(0, rows), :]
            yield comp, lon, cells.reshape(BATCH * rows, LANES)


def split_halves(value):
    high = value.astype(jnp.bfloat16)
    return high, (value - high.astype(jnp.float32)).astype(jnp.bfloat16)


def gram_of(high, low):
    return lax.dot_general(
        high,
        jnp.concatenate([high, low], axis=1),
        (((0,), (0,)), ((), ())),
        preferred_element_type=jnp.float32,
    )


def write_halves(par, gram, scale, kept, sent, total):
    half, rows = LANES // 2, kept.shape[0]
    mixed = gram[:, LANES:]
    whole = scale * (gram[:, :LANES] + (mixed + jnp.transpose(mixed)))
    row = lax.broadcasted_iota(jnp.int32, (half, LANES), 0)
    col = lax.broadcasted_iota(jnp.int32, (half, LANES), 1)
    total[pl.ds(0, half), :] = jnp.where(
        (col < half) | (col - half > row), whole[half:], pltpu.roll(whole[:half], half, 1)
    )
    row = lax.broadcasted_iota(jnp.int32, (LANES, LANES), 0)
    col = lax.broadcasted_iota(jnp.int32, (LANES, LANES), 1)
    total[pl.ds(half, 2 * rows - half), :] = jnp.zeros((2 * rows - half, LANES), jnp.float32)
    total[pl.ds(half, 1), :] = jnp.sum(jnp.where(row == col, whole, 0.0), axis=0, keepdims=True)
    odd = par[1] % 2
    kept[...] = total[pl.ds(odd * rows, rows), :]
    sent[...] = total[pl.ds((1 - odd) * rows, rows), :]


def factor_pair(low, p):
    q, size = p + 1, len(low)
    a, b, c = low[p][p], low[q][p], low[q][q]
    root_a, root_det = lax.rsqrt(a), lax.rsqrt(a * c - b * b)
    both = root_a * root_det
    turned = [a * low[i][q] - b * low[i][p] for i in range(q + 1, size)]
    low[q][p] = b * root_a
    for i, value in zip(range(q + 1, size), turned):
        low[i][p] = low[i][p] * root_a
        low[i][q] = value * both
    for i in range(q + 1, size):
        for m in range(q + 1, i + 1):
            low[i][m] = (low[i][m] - low[i][p] * low[m][p]) - low[i][q] * low[m][q]
    return root_a, a * both


def square_of(pivots):
    high = pivots.astype(jnp.bfloat16)
    rest = pivots - high.astype(jnp.float32)
    middle = rest.astype(jnp.bfloat16)
    low = (rest - middle.astype(jnp.float32)).astype(jnp.bfloat16)
    return lax.dot_general(
        jnp.concatenate([high, high, middle, middle, high, low], axis=0),
        jnp.concatenate([high, middle, high, middle, low, high], axis=0),
        (((0,), (0,)), ((), ())),
        preferred_element_type=jnp.float32,
    )


def invert_factor(gram, work, board):
    count = LANES // SUB
    lane = lax.broadcasted_iota(jnp.int32, (SUB, LANES), 1)
    sub = lax.broadcasted_iota(jnp.int32, (SUB, LANES), 0)
    rows = [gram[SUB * i : SUB * (i + 1)] for i in range(count)]
    columns = [lane_spread(rows[0], l) for l in range(SUB)]
    for block in range(count):
        base = SUB * block
        here = (lane >= base) & (lane < base + SUB)
        shelf = 3 * SUB * base
        for l in range(SUB):
            board[pl.ds(shelf + SUB * l, SUB), :] = columns[l]
        low = [
            [board[pl.ds(shelf + SUB * l + k, SUB, stride=0), :] for l in range(k + 1)]
            for k in range(SUB)
        ]
        shelf += SUB * SUB
        board[pl.ds(shelf, SUB), :] = jnp.where(
            here, jnp.where(lane - base == sub, 1.0, 0.0), rows[block]
        )
        inv = []
        for p in range(0, SUB, 2):
            inv.extend(factor_pair(low, p))
        scaled = []
        for k in range(SUB):
            line = board[pl.ds(shelf + k, SUB, stride=0), :]
            for l in range(k):
                line = line - low[k][l] * scaled[l]
            scaled.append(line * inv[k])
        merged = scaled[0]
        for k in range(1, SUB):
            merged = jnp.where(sub == k, scaled[k], merged)
        work[pl.ds(base, SUB), :] = merged
        shelf += SUB
        for i in range(block + 1, (block // GROUP + 1) * GROUP):
            weights = []
            rest = jnp.where(here, 0.0, rows[i])
            for l in range(SUB):
                weight = lane_spread(rows[i], base + l)
                for m in range(l):
                    weight = weight - weights[m] * low[l][m]
                weights.append(weight * inv[l])
            if i == block + 1:
                columns = [lane_spread(rows[i], base + SUB + l) for l in range(SUB)]
                for l in range(SUB):
                    board[pl.ds(shelf + SUB * l, SUB), :] = weights[l]
                    for k in range(SUB):
                        across = board[pl.ds(shelf + SUB * l + k, SUB, stride=0), :]
                        columns[k] = columns[k] - weights[l] * across
            for l in range(SUB):
                rest = rest - weights[l] * scaled[l]
            rows[i] = rest
        if block % GROUP == GROUP - 1 and block + 1 < count:
            first = SUB * (block + 1 - GROUP)
            tall = (SUB * GROUP, LANES)
            to_lane = lax.broadcasted_iota(jnp.int32, tall, 1) // SUB - first // SUB
            to_row = lax.broadcasted_iota(jnp.int32, tall, 0) // SUB
            pivots = work[pl.ds(first, SUB * GROUP), :]
            update = square_of(jnp.where((to_lane > to_row) & (to_lane < GROUP), 0.0, pivots))
            here = (lane >= first) & (lane < base + SUB)
            for i in range(block + 1, count):
                rows[i] = jnp.where(here, 0.0, rows[i]) - update[SUB * i : SUB * (i + 1)]
            columns = [lane_spread(rows[block + 1], base + SUB + l) for l in range(SUB)]


def factorize(par, mine_ref, other_ref, gram, work, board):
    half, rows = LANES // 2, mine_ref.shape[0]
    odd = par[1] % 2
    gram[pl.ds(odd * rows, rows), :] = mine_ref[...]
    gram[pl.ds((1 - odd) * rows, rows), :] = other_ref[...]
    packed, diagonal = gram[pl.ds(0, half), :], gram[pl.ds(half, 1), :]
    row = lax.broadcasted_iota(jnp.int32, (half, LANES), 0)
    col = lax.broadcasted_iota(jnp.int32, (half, LANES), 1)
    triangles = jnp.concatenate(
        [
            jnp.where(col < row, pltpu.roll(packed, half, 1), 0.0),
            jnp.where((col < half) | (col - half > row), packed, 0.0),
        ],
        axis=0,
    )
    row = lax.broadcasted_iota(jnp.int32, (LANES, LANES), 0)
    col = lax.broadcasted_iota(jnp.int32, (LANES, LANES), 1)
    size = jnp.broadcast_to(lax.rsqrt(diagonal), (LANES, LANES))
    whole = jnp.where(row == col, diagonal, triangles + jnp.transpose(triangles))
    invert_factor((whole * size) * jnp.transpose(size), work, board)
    inverse = jnp.where(row >= col, work[...], 0.0) * size
    diagonal = jnp.sum(jnp.where(row == col, inverse, 0.0), axis=0, keepdims=True)
    return inverse, diagonal


def paired(inverse):
    high = inverse.astype(jnp.bfloat16)
    low = (inverse - high.astype(jnp.float32)).astype(jnp.bfloat16)
    return jnp.concatenate(
        [jnp.concatenate([high, high], axis=1), jnp.concatenate([low, low], axis=1)], axis=0
    )


def times_factor(pair, factor):
    both = lax.dot_general(
        pair, factor, (((1,), (1,)), ((), ())), preferred_element_type=jnp.float32
    )
    return both[:, :LANES] + both[:, LANES:]


def factor_only(par, mine_ref, other_ref, prior_ref, _, inverse_ref, logs_ref, gram, work, board):
    inverse, diagonal = factorize(par, mine_ref, other_ref, gram, work, board)
    inverse_ref[...] = inverse
    logs_ref[...] = prior_ref[...] - jnp.log(diagonal)


def mend_only(par, start_in, middle_in, state_in, coef_ref, spin_ref, a, b, start, middle, state):
    tall = state.shape[2]
    mend_columns(par, (start, middle, state), coef_ref, spin_ref, ((0, tall, (a, b)),))


def update(scale, par, state, inverse_ref, out_ref, kept, sent, factor, total):
    factor[...] = paired(inverse_ref[...])
    gram = 0.0
    for comp, lon, cells in tiles_of(state):
        new = times_factor(jnp.concatenate(split_halves(cells), axis=1), factor[...])
        out_ref[comp, pl.ds(lon, BATCH)] = new.reshape((BATCH,) + out_ref.shape[2:])
        gram += gram_of(*split_halves(new))
    write_halves(par, gram, scale, kept, sent, total)


def restore_order(turned, out_ref):
    comps, cols, _, _ = turned.shape
    for comp in range(comps):
        for lon in range(0, cols, 2 * SUB):
            cells = jnp.concatenate(
                [
                    jnp.transpose(turned[comp, pl.ds(lon + shift, SUB)], (1, 0, 2))
                    for shift in (0, SUB)
                ],
                axis=1,
            )
            high = cells.astype(jnp.bfloat16)
            low = (cells - high.astype(jnp.float32)).astype(jnp.bfloat16)
            out_ref[comp, :, pl.ds(lon, 2 * SUB), pl.ds(0, LANES)] = high
            out_ref[comp, :, pl.ds(lon, 2 * SUB), pl.ds(LANES, LANES)] = low


def finish(
    par, mine_ref, other_ref, prior_ref, t_ref, out_ref, logs_ref, gram, work, board, factor, fresh, sems
):
    inverse, diagonal = factorize(par, mine_ref, other_ref, gram, work, board)
    factor[...] = paired(inverse)

    def out_copy(tile):
        return pltpu.make_async_copy(fresh.at[tile], out_ref.at[tile], sems.at[tile])

    for tile in range(TILES):
        fresh[tile] = times_factor(t_ref[tile], factor[...])
        out_copy(tile).start(priority=tile % 2)
    logs_ref[...] = prior_ref[...] - jnp.log(diagonal)

    for tile in range(TILES):
        out_copy(tile).wait()


def swap_pairs(near_value, far_value, axis, closed):
    count = lax.axis_size(axis)
    near = [(i, i ^ 1) for i in range(count)]
    far = [(i, (i + 1 if i % 2 else i - 1) % count) for i in range(count)]
    if not closed:
        far = far[1:-1]
    return lax.ppermute(near_value, axis, near), lax.ppermute(far_value, axis, far)


def swapped(value, axis, mask):
    return lax.ppermute(value, axis, [(i, i ^ mask) for i in range(lax.axis_size(axis))])


def add_four(first, second, third, fourth, _, out_ref):
    out_ref[...] = (first[...] + fourth[...]) + (third[...] + second[...])


def sum_over(value, axis, first_bit, beside=None):
    bits = lax.axis_size(axis).bit_length() - 1
    while first_bit < bits:
        low = 1 << first_bit
        if first_bit + 1 < bits:
            high = low << 1
            three, two, one = (swapped(value, axis, mask) for mask in (low | high, high, low))
            if beside is None:
                value = (three + two) + (one + value)
            else:
                value = pl.pallas_call(
                    add_four,
                    out_shape=jax.ShapeDtypeStruct(value.shape, value.dtype),
                    in_specs=[VMEM] * 4 + [pl.BlockSpec(memory_space=pl.ANY)],
                    out_specs=VMEM,
                    compiler_params=params(),
                )(value, three, two, one, beside)
                beside = None
            first_bit += 2
        else:
            value = value + swapped(value, axis, low)
            first_bit += 1
    return value


def sum_devices(kept, sent, order, beside=(None, None)):
    mine = kept + swapped(sent, "col", 1)
    for axis, work in zip(order, beside):
        mine = sum_over(mine, axis, 1 if axis == "col" else 0, work)
    return mine, swapped(mine, "col", 1)


def body(tangents, sea_mask, levels, current):
    comps, rows, cols, modes = tangents.shape
    total_rows = rows * lax.axis_size("row")
    total_cells = total_rows * cols * lax.axis_size("col")
    scale = 1.0 / total_cells
    row_at, col_at = lax.axis_index("row"), lax.axis_index("col")
    par = jnp.stack([row_at, col_at]).astype(jnp.int32)

    tall, length = rows + 2 * HALO, cols + 2 * SIDE

    block = shape_of(comps, length, tall, modes)
    coefs = shape_of(FIELDS, length, tall, LANES)
    columns = (shape_of(comps * SIDE * tall, modes),) * 2
    own_columns = (shape_of(comps * SIDE * rows + SUB, modes),) * 2
    corners = (shape_of(comps * SIDE * SUB + SUB, modes),) * 2
    rows_sent = (shape_of(comps * HALO + 1, cols, modes),) * 2
    halves = (shape_of(modes // 4 + SUB, modes),) * 2
    square = pltpu.VMEM((modes, modes), jnp.float32)
    board = pltpu.VMEM((3 * SUB * modes, LANES), jnp.float32)
    factor = pltpu.VMEM((2 * modes, 2 * modes), jnp.bfloat16)

    def call(
        kernel, outs, *operands, specs=None, out_specs=None, scratch=(), aliases=None, cost=1.0
    ):
        return pl.pallas_call(
            kernel,
            out_shape=outs,
            in_specs=specs or [SMEM] + [VMEM] * (len(operands) - 1),
            out_specs=out_specs or (VMEM,) * len(outs),
            scratch_shapes=scratch,
            input_output_aliases=aliases or {},
            compiler_params=params(),
            cost_estimate=pl.CostEstimate(
                flops=int(cost * 1e9), bytes_accessed=int(cost * 3e6), transcendentals=0
            ),
        )(*operands)

    def inside(step, state, chosen=None, partly=()):
        return call(
            functools.partial(apply_inside, step, chosen),
            (block,),
            state,
            coef,
            spin,
            *partly,
            specs=[VMEM] * (3 + len(partly)),
            aliases={3: 0} if partly else None,
            cost=2.0,
        )[0]

    def swap_columns(packed):
        return swap_pairs(*packed, "col", True)

    source, *fields = (
        pltpu.with_memory_space_constraint(x, pltpu.HBM)
        for x in (tangents, sea_mask.T, levels.T, current.T)
    )
    upright = [pltpu.VMEM(x.shape, x.dtype) for x in fields]
    packed = call(
        pack_rows,
        rows_sent,
        par,
        source,
        *fields,
        specs=[SMEM] + [HBM] * 4,
        scratch=upright
        + [
            pltpu.VMEM((cols, LANES), jnp.float32),
            pltpu.SemaphoreType.DMA((2 * comps,)),
            pltpu.SemaphoreType.DMA((FIELDS,)),
        ],
        cost=5.0,
    )
    row_halos = swap_pairs(*packed, "row", False)
    start, coef, spin, *packed = call(
        functools.partial(spread_fields, total_rows),
        (block, coefs, shape_of(tall, LANES)) + own_columns,
        par,
        tangents,
        *fields,
        specs=[SMEM, VMEM] + [HBM] * 3,
        scratch=[pltpu.VMEM((FIELDS, cols, LANES), jnp.float32)]
        + upright
        + [pltpu.SemaphoreType.DMA((FIELDS,))],
        cost=3.0,
    )
    halos = swap_columns(packed)
    middle_tiles = tuple(range(1, rows // SUB - 1))
    outer_tiles = (0,) + tuple(range(rows // SUB - 1, tall // SUB))
    middle = inside(0, start, middle_tiles)
    start, coef, *packed = call(
        join_rows,
        (block, coefs) + corners,
        par,
        start,
        coef,
        *row_halos,
        middle,
        specs=[SMEM] + [VMEM] * 4 + [pl.BlockSpec(memory_space=pl.ANY)],
        aliases={1: 0, 2: 1},
    )
    halos += swap_columns(packed)
    logs = jnp.zeros((1, modes), jnp.float32)

    middle = inside(0, start, outer_tiles, (middle,))
    state = inside(1, middle)
    _, _, start, coef, *packed, kept, sent = call(
        functools.partial(join_gram, scale),
        (block, block, block, coefs) + columns + halves,
        par,
        start,
        middle,
        state,
        coef,
        spin,
        *halos,
        scratch=[square],
        aliases={1: 0, 2: 1, 3: 2, 4: 3},
        cost=2.0,
    )
    middle = inside(0, start)
    state = inside(1, middle)

    halos = swap_columns(packed)
    mine, other = sum_devices(kept, sent, ("row", "col"), (middle, state))
    _, _, state = call(
        mend_only,
        (block,) * 3,
        par,
        start,
        middle,
        state,
        coef,
        spin,
        *halos,
        aliases={1: 0, 2: 1, 3: 2},
    )
    inverse, logs = call(
        factor_only,
        (shape_of(modes, modes), shape_of(1, modes)),
        par,
        mine,
        other,
        logs,
        state,
        specs=[SMEM] + [VMEM] * 3 + [pl.BlockSpec(memory_space=pl.ANY)],
        scratch=[square, square, board],
        cost=0.01,
    )
    state, kept, sent = call(
        functools.partial(update, scale),
        (shape_of(comps, cols, rows, modes),) + halves,
        par,
        state,
        inverse,
        scratch=[factor, square],
        cost=2.0,
    )
    state = call(
        restore_order,
        (jax.ShapeDtypeStruct((comps, rows, cols, 2 * modes), jnp.bfloat16),),
        state,
        specs=[VMEM],
        cost=1.0,
    )[0]
    height = comps * rows * cols // TILES
    tiled = shape_of(TILES, height, modes)
    mine, other = sum_devices(kept, sent, ("col", "row"))
    out, logs = call(
        finish,
        (tiled, shape_of(1, modes)),
        par,
        mine,
        other,
        logs,
        state.reshape(TILES, height, 2 * modes),
        out_specs=(HBM, VMEM),
        scratch=[
            square,
            square,
            board,
            factor,
            pltpu.VMEM((TILES, height, modes), jnp.float32),
            pltpu.SemaphoreType.DMA((TILES,)),
        ],
    )
    return out.reshape(tangents.shape), logs.reshape(modes)


def solution(mesh):
    placed = (P(None, "row", "col", None), P("row", "col"), P("row", "col"), P("row", "col"))
    return jax.shard_map(
        body,
        mesh=mesh,
        in_specs=placed,
        out_specs=(P(None, "row", "col", None), P()),
        check_vma=False,
    )
```
